32 devices in a mesh: branch: 2 (over x), series: 16 (over z, y, core).
Axes of the slice: x: 2, y: 2, z: 4, core: 2. Of those that a mesh axis runs over, the one named last changes fastest.
Arguments:
- series_in: bfloat16 [16, 816, 512], P('series'), may hold values from -6 to 6
- target: bfloat16 [16, 816, 512], P('series', 'branch'), may hold values from -6 to 6
- horizons: int32 [16], P('series'), may hold values from 96 to 720, as said below
- observed: int32 [16, 816], P('series'), may hold values 0 or 1
- down_short: bfloat16 [6144, 512], P('series'), may hold values from -0.078125 to 0.078125
- iso_short: bfloat16 [35328, 512], P('series'), may hold values from -0.046875 to 0.046875
- trans_short: bfloat16 [6144, 512], P('series'), may hold values from -0.25 to 0.25
- down_long: bfloat16 [8192, 512], P('series'), may hold values from -0.0625 to 0.0625
- iso_long: bfloat16 [26624, 512], P('series'), may hold values from -0.0546875 to 0.0546875
- trans_long: bfloat16 [8192, 512], P('series'), may hold values from -0.25 to 0.25
- branch_bias: float32 [2, 4, 512], P('branch'), may hold values from -2 to 2
- branch_gain: float32 [2, 512], P('branch'), may hold values from 0.5 to 1.5
- merge_weight: bfloat16 [2, 512, 512], replicated, may hold values from -0.1875 to 0.1875
- head_bias: float32 [4, 512], replicated, may hold values from -2 to 2
- head_gain: float32 [2, 512], replicated, may hold values from 0.5 to 1.5
- ff_in: bfloat16 [512, 2048], replicated, may hold values from -0.25 to 0.25
- ff_in_bias: float32 [2048], replicated, may hold values from -2 to 2
- ff_out: bfloat16 [2048, 512], replicated, may hold values from -0.125 to 0.125
Outputs:
- out: bfloat16 [16, 816, 512], P('series', 'branch')
- series_loss: float32 [16], P('series')
- grad_input: float32 [16, 816, 512], P('series')
- grad_down_short: float32 [6144, 512], P('series')
- grad_iso_short: float32 [35328, 512], P('series')
- grad_trans_short: float32 [6144, 512], P('series')
- grad_down_long: float32 [8192, 512], P('series')
- grad_iso_long: float32 [26624, 512], P('series')
- grad_trans_long: float32 [8192, 512], P('series')
- grad_branch_bias: float32 [2, 4, 512], replicated
- grad_branch_gain: float32 [2, 512], replicated
- grad_merge: float32 [2, 512, 512], replicated
- grad_head_bias: float32 [4, 512], replicated
- grad_head_gain: float32 [2, 512], replicated
- grad_ff_in: float32 [512, 2048], P(None, 'series')
- grad_ff_in_bias: float32 [2048], replicated
- grad_ff_out: float32 [2048, 512], P('series')
The draws below stay inside these ranges and needn't reach their ends.
Inputs may be any that keep to these rules, and one draw needn't show every extreme that they name: `horizons`: each horizon is one of 96, 192, 336 and 720; the shortest and the longest occur in every draw.
All inputs are finite; a program needn't handle non-finite values. No bound on the sum of `observed` on one device may be relied on, other than what follows from the above.
Results may differ from the reference program's by a relative error of at most 0.018.
Values may be sent and summed in bfloat16 or wider, within the bound.
No kernel may reach another device: no remote copies, remote signals or barrier semaphores. Data moves between devices by JAX's collectives and lax.ppermute only.
A program may use at most 448 MiB of HBM per device.

```python
import jax
import jax.numpy as jnp
from jax import lax

D = 512
FF = 2048
SCALE_S = 12
SCALE_L = 16
SEQ_IN = 96
MAX_H = 720
LEN = 816
ISO_S = 69
ISO_L = 52
SERIES = 16


def draw_horizons(key, part):
    key = jax.random.fold_in(key, 11)
    first_key, second_key, third_key = jax.random.split(key, 3)
    table = jnp.array([MAX_H * 2 // 15, MAX_H * 4 // 15, MAX_H * 7 // 15, MAX_H], jnp.int32)
    picks = jax.random.randint(first_key, (SERIES,), 0, 4)
    longest = jax.random.randint(second_key, (), 0, SERIES)
    shortest = (longest + 1 + jax.random.randint(third_key, (), 0, SERIES - 1)) % SERIES
    index_row = jnp.arange(SERIES, dtype=jnp.int32)
    picks = jnp.where(index_row == longest, 3, jnp.where(index_row == shortest, 0, picks))
    return table[picks]


def plant(values, stream_key, least, top_value):
    index_at = [jax.random.randint(jax.random.fold_in(stream_key, axis), (), 0, length) for axis, length in enumerate(values.shape)]
    widest = values.shape.index(max(values.shape))
    beside = index_at[:widest] + [(index_at[widest] + 1) % values.shape[widest]] + index_at[widest + 1:]
    return values.at[tuple(index_at)].set(least).at[tuple(beside)].set(top_value)


def level_of(rng, dims, cuts, low, high):
    def one(position, blocks):
        draws = jax.random.uniform(jax.random.fold_in(jax.random.fold_in(rng, 6), position), (blocks,), jnp.float32, low / len(cuts), high / len(cuts))
        return jnp.repeat(jnp.exp(draws), dims[position] // blocks).reshape((-1,) + (1,) * (len(dims) - position - 1))

    level = one(*cuts[0])
    for cut in cuts[1:]:
        level = level * one(*cut)
    return level


def bell_draw(own_key, dims, scale, limit, cuts=(), kind=jnp.bfloat16):
    factor_of = level_of(own_key, dims, cuts, -0.22, 0.18) if cuts else 1.0
    drawn = jax.random.normal(own_key, dims, jnp.float32) * scale * factor_of
    return jnp.minimum(jnp.maximum(drawn, -limit), limit).astype(kind)


def setup_inputs(seed: int = 0) -> dict:
    splits = jax.random.split(jax.random.key(seed), 19)
    return {
        "series_in": bell_draw(splits[0], (SERIES, LEN, D), 1.0, 6.0, ((0, 16),)),
        "target": bell_draw(splits[1], (SERIES, LEN, D), 1.0, 6.0, ((0, 16), (1, 2))),
        "horizons": draw_horizons(jax.random.fold_in(splits[18], 71), 0),
        "observed": plant((jax.random.randint(splits[3], (SERIES, LEN), 0, 10) < 9).astype(jnp.int32), jax.random.fold_in(splits[3], 1), 0, 1),
        "down_short": bell_draw(splits[4], (SCALE_S * D, D), (SCALE_S * D) ** -0.5, 0.078125, ((0, 16),)),
        "iso_short": bell_draw(splits[5], (ISO_S * D, D), (ISO_S * D // 2) ** -0.5, 0.046875, ((0, 16),)),
        "trans_short": bell_draw(splits[6], (SCALE_S * D, D), D ** -0.5, 0.25, ((0, 16),)),
        "down_long": bell_draw(splits[7], (SCALE_L * D, D), (SCALE_L * D) ** -0.5, 0.0625, ((0, 16),)),
        "iso_long": bell_draw(splits[8], (ISO_L * D, D), (ISO_L * D // 2) ** -0.5, 0.0546875, ((0, 16),)),
        "trans_long": bell_draw(splits[9], (SCALE_L * D, D), D ** -0.5, 0.25, ((0, 16),)),
        "branch_bias": bell_draw(splits[10], (2, 4, D), 0.3, 2.0, ((0, 2),), jnp.float32),
        "branch_gain": jnp.clip(1.0 + 0.1 * jax.random.normal(splits[11], (2, D), jnp.float32), 0.5, 1.5),
        "merge_weight": bell_draw(splits[12], (2, D, D), (2 * D) ** -0.5, 0.1875),
        "head_bias": bell_draw(splits[13], (4, D), 0.3, 2.0, (), jnp.float32),
        "head_gain": jnp.clip(1.0 + 0.1 * jax.random.normal(splits[14], (2, D), jnp.float32), 0.5, 1.5),
        "ff_in": bell_draw(splits[15], (D, FF), D ** -0.5, 0.25),
        "ff_in_bias": bell_draw(splits[16], (FF,), 0.3, 2.0, (), jnp.float32),
        "ff_out": bell_draw(splits[17], (FF, D), FF ** -0.5, 0.125),
    }


@jax.custom_vjp
def low(v):
    return lax.optimization_barrier(v.astype(jnp.bfloat16)).astype(jnp.float32)

@jax.custom_vjp
def low_back(v):
    return v

def low_keep(v):
    return (low(v), None)

def low_pass(kept, grad):
    return (grad,)

def back_keep(v):
    return (v, None)

def back_low(kept, grad):
    return (low(grad),)
low.defvjp(low_keep, low_pass)
low_back.defvjp(back_keep, back_low)
EPSILON = 1e-05
HIGHEST = lax.Precision.HIGHEST

def layer_norm(values, gain_row, shift_row):
    center = values - lax.optimization_barrier(jnp.mean(values, axis=-1, keepdims=True))
    spread = lax.optimization_barrier(jnp.mean(center * center, axis=-1, keepdims=True))
    return center * lax.rsqrt(spread + EPSILON) * gain_row + shift_row

def product(first_operand, second_operand):
    return jnp.dot(first_operand, second_operand, precision=HIGHEST, preferred_element_type=jnp.float32)

def branch_ref(series, down_weight, iso_weight, trans_weight, biases, gain_row, factor):
    length, features = series.shape
    step_count = (length + factor) // factor
    margin = factor // 2
    blocks = jnp.pad(series, ((margin, step_count * factor - length - margin), (0, 0))).reshape(step_count, factor * features)
    pre_down = low_back(product(blocks, down_weight) + biases[0])
    low_down = low(jnp.tanh(pre_down))
    padded = jnp.concatenate([jnp.zeros((step_count - 1, features), jnp.float32), low_down], axis=0)
    unfolded = jnp.concatenate([padded[offset:offset + step_count] for offset in range(step_count)], axis=1)
    pre_iso = low_back(product(unfolded, iso_weight) + biases[1])
    inner_norm = low(layer_norm(jnp.tanh(pre_iso) + low_down, gain_row, biases[3]))
    spread_out = jnp.einsum('mi,jio->mjo', inner_norm, trans_weight.reshape(factor, features, features), precision=HIGHEST)
    pre_trans = low_back(spread_out.reshape(step_count * factor, features)[:length] + biases[2])
    return low_back(low(layer_norm(jnp.tanh(pre_trans) + series, gain_row, biases[3])))

def forward(params, series, target_rows, valid_mask):
    down_short, iso_short, trans_short, down_long, iso_long, trans_long, branch_bias, branch_gain, merge_weight, head_bias, head_gain, ff_in, ff_in_bias, ff_out = params
    out_short = branch_ref(series, down_short, iso_short, trans_short, branch_bias[0], branch_gain[0], SCALE_S)
    out_long = branch_ref(series, down_long, iso_long, trans_long, branch_bias[1], branch_gain[1], SCALE_L)
    merged = low_back(product(out_short, merge_weight[0]) + product(out_long, merge_weight[1]) + head_bias[0])
    normed = low(layer_norm(merged, head_gain[0], head_bias[2]))
    pre_ff = low_back(product(normed, ff_in) + ff_in_bias)
    activated = low(jax.nn.gelu(pre_ff, approximate=False))
    ff_result = low_back(product(activated, ff_out) + head_bias[1])
    final_out = layer_norm(merged + ff_result, head_gain[1], head_bias[3])
    error_rows = final_out - target_rows
    return (0.5 * jnp.sum(valid_mask[:, None] * error_rows * error_rows), final_out)

def reference(series_in, target, horizons, observed, down_short, iso_short, trans_short, down_long, iso_long, trans_long, branch_bias, branch_gain, merge_weight, head_bias, head_gain, ff_in, ff_in_bias, ff_out):
    weights = (down_short.astype(jnp.float32), iso_short.astype(jnp.float32), trans_short.astype(jnp.float32), down_long.astype(jnp.float32), iso_long.astype(jnp.float32), trans_long.astype(jnp.float32), branch_bias.astype(jnp.float32), branch_gain.astype(jnp.float32), merge_weight.astype(jnp.float32), head_bias.astype(jnp.float32), head_gain.astype(jnp.float32), ff_in.astype(jnp.float32), ff_in_bias.astype(jnp.float32), ff_out.astype(jnp.float32))

    def one_series(sums, series_item):
        series, target_row, horizon, observed_row = series_item
        positions = jnp.arange(LEN, dtype=jnp.int32)
        valid_mask = observed_row.astype(jnp.float32) * (positions >= SEQ_IN).astype(jnp.float32) * (positions < SEQ_IN + horizon).astype(jnp.float32)

        def objective(params, values):
            return forward(params, values, target_row.astype(jnp.float32), valid_mask)
        loss_value, backward, final_out = jax.vjp(objective, weights, series.astype(jnp.float32), has_aux=True)
        grad_params, grad_series = backward(jnp.ones((), loss_value.dtype))
        sums = jax.tree.map(jnp.add, sums, grad_params)
        return (sums, (final_out.astype(jnp.bfloat16), loss_value / (D * LEN), grad_series))
    zeros_start = jax.tree.map(jnp.zeros_like, weights)
    sums, (out_rows, losses, grad_rows) = lax.scan(one_series, zeros_start, (series_in, target, horizons, observed))
    return (out_rows, losses, grad_rows, sums[0], sums[1], sums[2], sums[3], sums[4], sums[5], sums[6], sums[7], sums[8], sums[9], sums[10], sums[11], sums[12], sums[13])
```

```python
import functools

import jax
import jax.numpy as jnp
from jax import lax
from jax.experimental import pallas as pl
from jax.experimental.pallas import tpu as pltpu
from jax.sharding import PartitionSpec as P

SCALE_S = 12
SCALE_L = 16
SEQ_IN = 96
EPSILON = 1e-05
LANE = 128

BF = jnp.bfloat16
F32 = jnp.float32


def up8(count, base=8):
    return -(-count // base) * base


class Plan:
    def __init__(self, shards, length, features, down_rows, iso_rows):
        self.shards, self.length, self.features = shards, length, features
        self.factors = (SCALE_S, SCALE_L)
        self.steps = tuple((length + k) // k for k in self.factors)
        self.rows = up8(max(self.steps))
        self.down_rows = down_rows
        self.iso_rows = iso_rows
        self.down_max, self.iso_max = max(down_rows), max(iso_rows)
        self.groups = tuple(r // LANE for r in down_rows)
        self.pack = up8(max(g * n for g, n in zip(self.groups, self.steps)), 16)
        self.taps = tuple(
            max(-(-((d * r) % features + r) // features) for d in range(shards)) for r in iso_rows
        )
        self.taps_max = max(self.taps)
        self.quarter = shards // 4
        self.stage_rows = max(k * up8(n) for k, n in zip(self.factors, self.steps))

    def mask(self, slot):
        core, rest = divmod(slot, 2 * self.quarter)
        side, line = divmod(rest, self.quarter)
        return core | (side << 1) | (line << 2)


def vmem(count):
    return [pl.BlockSpec(memory_space=pltpu.VMEM) for _ in range(count)]


SMEM = pl.BlockSpec(memory_space=pltpu.SMEM)
ANY = pl.BlockSpec(memory_space=pl.ANY)


def call(body, in_specs, outs, scratch, flops=0, moved=0, limit=56):
    return pl.pallas_call(
        body,
        out_shape=[jax.ShapeDtypeStruct(s, d) for s, d in outs],
        in_specs=in_specs,
        out_specs=vmem(len(outs)),
        scratch_shapes=scratch,
        compiler_params=pltpu.CompilerParams(vmem_limit_bytes=limit << 20),
        cost_estimate=pl.CostEstimate(flops=flops, bytes_accessed=moved, transcendentals=0),
    )


def dot(a, b, dims=((1,), (0,))):
    return lax.dot_general(a, b, (dims, ((), ())), preferred_element_type=F32)


def norm_parts(values):
    center = values - jnp.mean(values, axis=-1, keepdims=True)
    spread = jnp.mean(center * center, axis=-1, keepdims=True)
    scale = lax.rsqrt(spread + EPSILON)
    return center * scale, scale


def norm_back(upstream, unit, scale, gain):
    inner = upstream * gain
    first = jnp.mean(inner, axis=-1, keepdims=True)
    second = jnp.mean(inner * unit, axis=-1, keepdims=True)
    return scale * (inner - first - unit * second)


def keep_rows(values, count):
    index = lax.broadcasted_iota(jnp.int32, values.shape, 0)
    return jnp.where(index < count, values, 0.0)


def both(meta, short, long):
    pl.when(meta[0] == 0)(short)
    pl.when(meta[0] == 1)(long)


def split(rows, features):
    return pltpu.VMEM((features // LANE, rows, LANE), F32)


def put(ref, start, values, stride=1):
    count = values.shape[0]
    where = pl.ds(start, count) if stride == 1 else pl.ds(start, count, stride=stride)
    for c in range(ref.shape[0]):
        ref[c, where, :] = values[:, c * LANE : (c + 1) * LANE]


def get(ref, start, count, stride=1):
    where = pl.ds(start, count) if stride == 1 else pl.ds(start, count, stride=stride)
    return jnp.concatenate([ref[c, where, :] for c in range(ref.shape[0])], axis=1)


def prep_blocks(plan, meta, series):
    length, features = plan.length, plan.features
    per_tap = features // LANE
    shape = (plan.shards, plan.pack, LANE)

    def kernel(meta_ref, x_ref, out_ref, wide, packed):
        def run(b):
            k, n, groups = plan.factors[b], plan.steps[b], plan.groups[b]
            margin = k // 2
            wide[...] = jnp.zeros_like(wide)
            put(wide, margin, x_ref[...].astype(F32))
            packed[...] = jnp.zeros_like(packed)
            for d in range(plan.shards):
                for r in range(groups):
                    j, c = divmod(d * groups + r, per_tap)
                    packed[r * n : (r + 1) * n, :] = wide[c, pl.ds(j, n, stride=k), :]
                out_ref[d] = packed[...].astype(BF)

        both(meta_ref, lambda: run(0), lambda: run(1))

    return call(
        kernel,
        [SMEM] + vmem(1),
        [(shape, BF)],
        [split(plan.stage_rows, features), pltpu.VMEM((plan.pack, LANE), F32)],
        moved=2 * length * features * 2,
        limit=16,
    )(meta, series)[0]


def down_partial(plan, meta, blocks, w_short, w_long):
    shards, rows, features = plan.shards, plan.rows, plan.features
    half = shards // 2
    chunk = 4

    def kernel(meta_ref, in_ref, ws_ref, wl_ref, keep_ref, send_ref, a_ref, wide, packed):
        me = meta_ref[1]

        def run(b, w_ref):
            n, groups = plan.steps[b], plan.groups[b]
            width = groups * LANE
            wide[...] = jnp.zeros_like(wide)
            for start in range(0, shards, chunk):
                for i in range(chunk):
                    packed[...] = in_ref[me ^ plan.mask(start + i)].astype(F32)
                    for r in range(groups):
                        wide[i * rows : i * rows + n, r * LANE : (r + 1) * LANE] = packed[
                            r * n : (r + 1) * n, :
                        ]
                matrix = wide[...].astype(BF)
                a_ref[start * rows : (start + chunk) * rows, :] = matrix
                part = dot(matrix[:, :width], w_ref[...])
                for i in range(chunk):
                    slot = start + i
                    piece = part[i * rows : (i + 1) * rows]
                    if slot < half:
                        keep_ref[slot] = piece
                    else:
                        send_ref[slot - half] = piece.astype(BF)

        both(meta_ref, lambda: run(0, ws_ref), lambda: run(1, wl_ref))

    return call(
        kernel,
        [SMEM] + vmem(3),
        [
            ((half, rows, features), F32),
            ((half, rows, features), BF),
            ((shards * rows, plan.down_max), BF),
        ],
        [
            pltpu.VMEM((chunk * rows, plan.down_max), F32),
            pltpu.VMEM((plan.pack, LANE), F32),
        ],
        flops=2 * shards * rows * features * plan.down_max,
        moved=6 << 20,
        limit=32,
    )(meta, blocks, w_short, w_long)


def low_rows(plan, meta, pieces, biases):
    rows, features = plan.rows, plan.features

    def kernel(meta_ref, *refs):
        parts, bias_ref, low_ref, act_ref = refs[:-3], refs[-3], refs[-2], refs[-1]
        total = parts[0][...]
        for piece in parts[1:]:
            total = total + piece[...].astype(F32)
        act = keep_rows(jnp.tanh(total + bias_ref[0:1, :]), meta_ref[4])
        act_ref[...] = act
        low_ref[...] = act.astype(BF)

    return call(
        kernel,
        [SMEM] + vmem(len(pieces) + 1),
        [((rows, features), BF), ((rows, features), F32)],
        [],
        moved=1 << 19,
        limit=16,
    )(meta, *pieces, biases)


def time_major(plan, slots, stage, target, lead, tail_from):
    shards, rows = plan.shards, plan.rows
    for q, slot in enumerate(slots):
        put(stage, q, slot[...].astype(F32), shards)
    body = shards * rows
    if lead:
        target[0 : lead * shards, :] = jnp.zeros((lead * shards, target.shape[1]), BF)
    target[lead * shards : lead * shards + body, :] = get(stage, 0, body).astype(BF)
    rest = target.shape[0] - lead * shards - body
    if rest:
        target[lead * shards + body :, :] = jnp.zeros((rest, target.shape[1]), BF)


def slot_list(refs, plan):
    singles = refs[:-1]
    return list(singles) + [refs[-1].at[i] for i in range(plan.shards // 2)]


def pad_weight(plan, b, meta_ref, w_ref, target):
    target[...] = jnp.zeros_like(target)
    shift = pl.multiple_of(meta_ref[3], 16)
    target[pl.ds(shift, plan.iso_rows[b]), :] = w_ref[...]


def iso_partial(plan, meta, slots, w_short, w_long, backward):
    shards, rows, features = plan.shards, plan.rows, plan.features
    half = shards // 2
    steps_max = max(plan.steps)
    extra = plan.taps_max + 2
    buffer = (steps_max + rows + extra) * shards
    count = len(slots)

    def kernel(meta_ref, *refs):
        slot_refs = slot_list(refs[:count], plan)
        ws_ref, wl_ref, keep_ref, send_ref, stage, lined, padded = refs[count:]
        first = meta_ref[2]

        def run(b, w_ref):
            n, taps = plan.steps[b], plan.taps[b]
            pad_weight(plan, b, meta_ref, w_ref, padded)
            if backward:
                time_major(plan, slot_refs, stage, lined, extra, 0)
            else:
                time_major(plan, slot_refs, stage, lined, n - 1, 0)
            for m in range(taps):
                if backward:
                    start = extra + n - 1 - first - m
                else:
                    start = first + m
                start = pl.multiple_of(start * shards, 16)
                window = lined[pl.ds(start, rows * shards), :]
                weight = padded[m * features : (m + 1) * features, :]
                part = dot(window, weight, ((1,), (1,)) if backward else ((1,), (0,)))
                total = part if m == 0 else total + part
            put(stage, 0, total)
            for q in range(shards):
                piece = get(stage, q, rows, shards)
                if q < half:
                    keep_ref[q] = piece
                else:
                    send_ref[q - half] = piece.astype(BF)

        both(meta_ref, lambda: run(0, ws_ref), lambda: run(1, wl_ref))

    return call(
        kernel,
        [SMEM] + vmem(count + 2),
        [((half, rows, features), F32), ((half, rows, features), BF)],
        [
            split(rows * shards, features),
            pltpu.VMEM((buffer, features), BF),
            pltpu.VMEM((plan.taps_max * features, features), BF),
        ],
        flops=2 * shards * rows * features * features * plan.taps_max,
        moved=10 << 20,
        limit=40,
    )(meta, *slots, w_short, w_long)


def iso_weight(plan, meta, low_slots, delta_slots):
    shards, rows, features = plan.shards, plan.rows, plan.features
    steps_max = max(plan.steps)
    extra = plan.taps_max + 2
    buffer = (steps_max + rows + extra) * shards
    count = len(low_slots)

    def kernel(meta_ref, *refs):
        low_refs = slot_list(refs[:count], plan)
        delta_refs = slot_list(refs[count : 2 * count], plan)
        grad_ref, sum_ref, stage, lined, delta, total, ordered = refs[2 * count :]
        first = meta_ref[2]
        me = meta_ref[1]
        for q in range(shards):
            ordered[pl.ds(me ^ plan.mask(q), 1), :] = jnp.sum(
                delta_refs[q][...].astype(F32), axis=0, keepdims=True
            )
        sum_ref[...] = jnp.sum(ordered[...], axis=0, keepdims=True)
        time_major(plan, delta_refs, stage, delta, 0, 0)

        def run(b):
            n, taps = plan.steps[b], plan.taps[b]
            time_major(plan, low_refs, stage, lined, n - 1, 0)
            for m in range(taps):
                start = pl.multiple_of((first + m) * shards, 16)
                window = lined[pl.ds(start, rows * shards), :]
                total[m * features : (m + 1) * features, :] = dot(window, delta[...], ((0,), (0,)))
            shift = pl.multiple_of(meta_ref[3], 16)
            grad_ref[0 : plan.iso_rows[b], :] = total[pl.ds(shift, plan.iso_rows[b]), :].astype(BF)

        both(meta_ref, lambda: run(0), lambda: run(1))

    return call(
        kernel,
        [SMEM] + vmem(2 * count),
        [((plan.iso_max, features), BF), ((1, features), F32)],
        [
            split(rows * shards, features),
            pltpu.VMEM((buffer, features), BF),
            pltpu.VMEM((rows * shards, features), BF),
            pltpu.VMEM((plan.taps_max * features, features), F32),
            pltpu.VMEM((shards, features), F32),
        ],
        flops=2 * shards * rows * features * features * plan.taps_max,
        moved=10 << 20,
        limit=48,
    )(meta, *low_slots, *delta_slots)


def fetch_weight(plan, b, source, target, sems):
    own = plan.down_rows[b]
    copies = [
        pltpu.make_async_copy(
            source.at[d, pl.ds(0, own)], target.at[pl.ds(d * own, own)], sems.at[d]
        )
        for d in range(plan.shards)
    ]
    for copy in copies:
        copy.start()
    return copies


def branch_forward(plan, meta, pieces, low, series, trans, biases, gain):
    rows, features, length = plan.rows, plan.features, plan.length
    count = len(pieces)
    half_rows = length // 2

    def kernel(meta_ref, *refs):
        parts = refs[:count]
        (low_ref, x_ref, w_hbm, bias_ref, gain_ref) = refs[count : count + 5]
        (keep_ref, send_ref, act_ref, inner_ref, iso_ref, weight, stage, sems) = refs[count + 5 :]

        def run(b):
            k, n = plan.factors[b], plan.steps[b]
            copies = fetch_weight(plan, b, w_hbm, weight, sems)
            pre = parts[0][...]
            for piece in parts[1:]:
                pre = pre + piece[...].astype(F32)
            act_iso = jnp.tanh(pre + bias_ref[1:2, :])
            iso_ref[...] = act_iso
            unit, _ = norm_parts(act_iso + low_ref[...].astype(F32))
            inner = keep_rows(unit * gain_ref[...] + bias_ref[3:4, :], n).astype(BF)
            inner_ref[...] = inner
            for copy in copies:
                copy.wait()
            fit = up8(n)
            for j in range(k):
                pre_trans = dot(inner, weight[j * features : (j + 1) * features, :])
                put(stage, j, pre_trans[:fit], k)
            act = jnp.tanh(get(stage, 0, length) + bias_ref[2:3, :])
            act_ref[...] = act
            unit_out, _ = norm_parts(act + x_ref[...].astype(F32))
            put(stage, 0, unit_out * gain_ref[...] + bias_ref[3:4, :])
            mine = pl.multiple_of(meta_ref[0] * half_rows, 8)
            other = pl.multiple_of((1 - meta_ref[0]) * half_rows, 8)
            keep_ref[...] = get(stage, mine, half_rows).astype(BF)
            send_ref[...] = get(stage, other, half_rows).astype(BF)

        both(meta_ref, lambda: run(0), lambda: run(1))

    return call(
        kernel,
        [SMEM] + vmem(count + 2) + [ANY] + vmem(2),
        [
            ((half_rows, features), BF),
            ((half_rows, features), BF),
            ((length, features), F32),
            ((rows, features), BF),
            ((rows, features), F32),
        ],
        [
            pltpu.VMEM((plan.shards * plan.down_max, features), BF),
            split(plan.stage_rows, features),
            pltpu.SemaphoreType.DMA((plan.shards,)),
        ],
        flops=2 * rows * features * features * SCALE_L,
        moved=14 << 20,
        limit=48,
    )(meta, *pieces, low, series, trans, biases, gain)


def branch_backward(plan, meta, up_keep, up_recv, series, act, act_iso, low, trans, biases, gain):
    rows, features, length, shards = plan.rows, plan.features, plan.length, plan.shards
    half_rows = length // 2

    def kernel(
        meta_ref, uk_ref, ur_ref, x_ref, act_ref, iso_ref, low_ref, w_hbm, bias_ref, gain_ref,
        outer_ref, taps_ref, delta_iso_ref, delta_inner_ref, vec_ref, weight, stage, upstream, sems,
    ):
        def run(b):
            k, n = plan.factors[b], plan.steps[b]
            copies = fetch_weight(plan, b, w_hbm, weight, sems)
            mine = pl.multiple_of(meta_ref[0] * half_rows, 8)
            other = pl.multiple_of((1 - meta_ref[0]) * half_rows, 8)
            upstream[pl.ds(mine, half_rows), :] = uk_ref[...].astype(F32)
            upstream[pl.ds(other, half_rows), :] = ur_ref[...].astype(F32)
            act_value = act_ref[...]
            unit, scale = norm_parts(act_value + x_ref[...].astype(F32))
            above = upstream[...]
            vec_ref[...] = jnp.zeros_like(vec_ref)
            shift_sum = jnp.sum(above, axis=0, keepdims=True)
            gain_sum = jnp.sum(above * unit, axis=0, keepdims=True)
            outer = norm_back(above, unit, scale, gain_ref[...])
            outer_ref[...] = outer
            delta = (outer * (1.0 - act_value * act_value)).astype(BF).astype(F32)
            vec_ref[0:1, :] = jnp.sum(delta, axis=0, keepdims=True)
            put(stage, 0, delta)
            put(stage, length, jnp.zeros((plan.stage_rows - length, features), F32))
            for copy in copies:
                copy.wait()
            fit = up8(n)
            total = jnp.zeros((fit, features), F32)
            pieces = []
            for j in range(k):
                piece = get(stage, j, fit, k).astype(BF)
                total = total + dot(
                    piece, weight[j * features : (j + 1) * features, :], ((1,), (1,))
                )
            own = plan.down_rows[b]
            for d in range(shards):
                tap = (2 * own * (d // 2)) // features + d % 2
                piece = get(stage, tap, fit, k)
                if fit < rows:
                    piece = jnp.concatenate([piece, jnp.zeros((rows - fit, features), F32)], axis=0)
                taps_ref[d] = piece.astype(BF)
            if fit < rows:
                total = jnp.concatenate([total, jnp.zeros((rows - fit, features), F32)], axis=0)
            total = keep_rows(total, n)
            act_in = iso_ref[...]
            unit_in, scale_in = norm_parts(act_in + low_ref[...].astype(F32))
            vec_ref[1:2, :] = shift_sum + jnp.sum(total, axis=0, keepdims=True)
            vec_ref[2:3, :] = gain_sum + jnp.sum(total * unit_in, axis=0, keepdims=True)
            delta_inner = norm_back(total, unit_in, scale_in, gain_ref[...])
            delta_inner_ref[...] = delta_inner
            delta_iso_ref[...] = keep_rows(delta_inner * (1.0 - act_in * act_in), n).astype(BF)

        both(meta_ref, lambda: run(0), lambda: run(1))

    return call(
        kernel,
        [SMEM] + vmem(6) + [ANY] + vmem(2),
        [
            ((length, features), F32),
            ((shards, rows, features), BF),
            ((rows, features), BF),
            ((rows, features), F32),
            ((8, features), F32),
        ],
        [
            pltpu.VMEM((shards * plan.down_max, features), BF),
            split(plan.stage_rows, features),
            pltpu.VMEM((length, features), F32),
            pltpu.SemaphoreType.DMA((shards,)),
        ],
        flops=2 * rows * features * features * SCALE_L,
        moved=16 << 20,
        limit=52,
    )(meta, up_keep, up_recv, series, act, act_iso, low, trans, biases, gain)


def trans_weight(plan, meta, inner_all, own_taps, other_taps):
    shards, rows, features = plan.shards, plan.rows, plan.features

    def kernel(meta_ref, inner_ref, own_ref, other_ref, grad_ref, total):
        lhs = inner_ref[...]

        def run(b):
            own = plan.down_rows[b]
            odd = meta_ref[5]
            first = dot(lhs, own_ref[...], ((0,), (0,)))
            total[pl.ds(pl.multiple_of(odd * features, 8), features), :] = first
            if own != features:
                second = dot(lhs, other_ref[...], ((0,), (0,)))
                total[pl.ds(pl.multiple_of((1 - odd) * features, 8), features), :] = second
            start = pl.multiple_of(meta_ref[6], 8)
            grad_ref[0:own, :] = total[pl.ds(start, own), :].astype(BF)

        both(meta_ref, lambda: run(0), lambda: run(1))

    flat = (shards * rows, features)
    return call(
        kernel,
        [SMEM] + vmem(3),
        [((plan.down_max, features), BF)],
        [pltpu.VMEM((2 * features, features), F32)],
        flops=4 * shards * rows * features * features,
        moved=5 << 20,
        limit=32,
    )(meta, inner_all.reshape(flat), own_taps.reshape(flat), other_taps.reshape(flat))[0]


def down_delta(plan, meta, pieces, delta_inner, act):
    rows, features = plan.rows, plan.features
    count = len(pieces)

    def kernel(meta_ref, *refs):
        parts = refs[:count]
        inner_ref, act_ref, out_ref = refs[count:]
        total = parts[0][...] + inner_ref[...]
        for piece in parts[1:]:
            total = total + piece[...].astype(F32)
        value = act_ref[...]
        out_ref[...] = keep_rows(total * (1.0 - value * value), meta_ref[4]).astype(BF)

    return call(
        kernel,
        [SMEM] + vmem(count + 2),
        [((rows, features), BF)],
        [],
        moved=1 << 19,
        limit=16,
    )(meta, *pieces, delta_inner, act)[0]


def input_delta(plan, meta, delta_down, outer, down):
    features, length = plan.features, plan.length

    def kernel(meta_ref, delta_ref, outer_ref, w_hbm, out_ref, weight, stage, sems):
        def run(b):
            k, n = plan.factors[b], plan.steps[b]
            copies = fetch_weight(plan, b, w_hbm, weight, sems)
            for copy in copies:
                copy.wait()
            fit = up8(n)
            value = delta_ref[...]
            for j in range(k):
                part = dot(value, weight[j * features : (j + 1) * features, :], ((1,), (1,)))
                put(stage, j, part[:fit], k)
            margin = k // 2
            out_ref[...] = (get(stage, margin, length) + outer_ref[...]).astype(BF)

        both(meta_ref, lambda: run(0), lambda: run(1))

    return call(
        kernel,
        [SMEM] + vmem(2) + [ANY],
        [((length, features), BF)],
        [
            pltpu.VMEM((plan.shards * plan.down_max, features), BF),
            split(plan.stage_rows, features),
            pltpu.SemaphoreType.DMA((plan.shards,)),
        ],
        flops=2 * plan.rows * features * features * SCALE_L,
        moved=12 << 20,
        limit=40,
    )(meta, delta_down, outer, down)[0]


def down_weight(plan, meta, matrix, delta_slots):
    shards, rows, features = plan.shards, plan.rows, plan.features
    count = len(delta_slots)

    def kernel(meta_ref, a_ref, *refs):
        delta_refs = slot_list(refs[:count], plan)
        grad_ref, sum_ref, delta, ordered = refs[count:]
        me = meta_ref[1]
        for q in range(shards):
            value = delta_refs[q][...].astype(F32)
            ordered[pl.ds(me ^ plan.mask(q), 1), :] = jnp.sum(value, axis=0, keepdims=True)
            delta[q * rows : (q + 1) * rows, :] = value
        sum_ref[...] = jnp.sum(ordered[...], axis=0, keepdims=True)
        grad_ref[...] = dot(a_ref[...], delta[...].astype(BF), ((0,), (0,))).astype(BF)

    return call(
        kernel,
        [SMEM] + vmem(1 + count),
        [((plan.down_max, features), BF), ((1, features), F32)],
        [pltpu.VMEM((shards * rows, features), F32), pltpu.VMEM((shards, features), F32)],
        flops=2 * shards * rows * features * features,
        moved=4 << 20,
        limit=32,
    )(meta, matrix, *delta_slots)


def hop(values, distance, shards):
    return lax.ppermute(values, "series", [(i, i ^ distance) for i in range(shards)])


def swap(values):
    return lax.ppermute(values, "branch", [(0, 1), (1, 0)])


def gather_slots(plan, own):
    shards = plan.shards
    line = [own] + [hop(own, i << 2, shards) for i in range(1, plan.quarter)]
    side = [hop(value, 2, shards) for value in line]
    return line + side + [hop(jnp.stack(line + side), 1, shards)]


def scatter_sum(plan, keep, send):
    shards, quarter = plan.shards, plan.quarter
    first = keep + hop(send, 1, shards).astype(F32)
    second = first[:quarter] + hop(first[quarter:].astype(BF), 2, shards).astype(F32)
    pieces = [second[0]]
    for i in range(1, quarter):
        pieces.append(hop(second[i].astype(BF), i << 2, shards))
    return pieces


def rounded(values):
    return lax.reduce_precision(values, exponent_bits=8, mantissa_bits=7)


def layer_norm(values, gain_row, shift_row):
    center = values - jnp.mean(values, axis=-1, keepdims=True)
    spread = jnp.mean(center * center, axis=-1, keepdims=True)
    return center * lax.rsqrt(spread + EPSILON) * gain_row + shift_row


def gelu_exact(values):
    return jax.nn.gelu(values, approximate=False)


def product(a, b):
    return jnp.dot(a, b, preferred_element_type=F32)


def left_product(a, b):
    return jnp.einsum("mi,mo->io", a, b, preferred_element_type=F32)


def right_product(a, b):
    return jnp.einsum("mo,io->mi", a, b, preferred_element_type=F32)


def body(
    series_in, target, horizons, observed,
    down_short, iso_short, trans_short, down_long, iso_long, trans_long,
    branch_bias, branch_gain, merge_weight, head_bias, head_gain, ff_in, ff_in_bias, ff_out,
):
    shards = lax.axis_size("series")
    _, length, features = series_in.shape
    plan = Plan(
        shards,
        length,
        features,
        (down_short.shape[0], down_long.shape[0]),
        (iso_short.shape[0], iso_long.shape[0]),
    )
    half_rows = length // 2
    branch = lax.axis_index("branch")
    me = lax.axis_index("series")
    is_short = branch == 0
    iso_rows = jnp.where(is_short, plan.iso_rows[0], plan.iso_rows[1])
    down_rows = jnp.where(is_short, plan.down_rows[0], plan.down_rows[1])
    meta = jnp.stack(
        [
            branch,
            me,
            (me * iso_rows) // features,
            (me * iso_rows) % features,
            jnp.where(is_short, plan.steps[0], plan.steps[1]),
            me % 2,
            (2 * down_rows * (me // 2)) % features + (me % 2) * down_rows,
            0,
        ]
    ).astype(jnp.int32)
    series = series_in[0]
    biases, gain = branch_bias[0], branch_gain

    def chosen(short, long):
        rows = max(short.shape[0], long.shape[0])
        short = jnp.pad(short, ((0, rows - short.shape[0]), (0, 0)))
        long = jnp.pad(long, ((0, rows - long.shape[0]), (0, 0)))
        return jnp.where(is_short, short, long)

    own_trans = chosen(trans_short, trans_long)
    trans_all = lax.all_gather(own_trans, "series", axis=0)

    blocks = lax.all_to_all(
        prep_blocks(plan, meta, series), "series", split_axis=0, concat_axis=0, tiled=True
    )
    keep, send, matrix = down_partial(plan, meta, blocks, down_short, down_long)
    low, act_down = low_rows(plan, meta, scatter_sum(plan, keep, send), biases)
    low_slots = gather_slots(plan, low)
    keep, send = iso_partial(plan, meta, low_slots, iso_short, iso_long, False)
    pieces = scatter_sum(plan, keep, send)
    out_keep, out_send, act_trans, inner, act_iso = branch_forward(
        plan, meta, pieces, low, series, trans_all, biases, gain
    )
    out_recv = swap(out_send)
    own_down, _ = lax.optimization_barrier((chosen(down_short, down_long), out_keep))
    down_all = lax.all_gather(own_down, "series", axis=0)

    merge_own = lax.dynamic_index_in_dim(merge_weight, branch, 0, keepdims=False)
    merge_other = lax.dynamic_index_in_dim(merge_weight, 1 - branch, 0, keepdims=False)
    merged = product(out_keep, merge_own) + product(out_recv, merge_other) + head_bias[0]
    normed, first_back = jax.vjp(layer_norm, merged, head_gain[0], head_bias[2])
    low_normed = normed.astype(BF)
    pre_ff = product(low_normed, ff_in) + ff_in_bias
    activated, gelu_back = jax.vjp(gelu_exact, pre_ff)
    low_act = activated.astype(BF)
    ff_result = product(low_act, ff_out) + head_bias[1]
    final_out, second_back = jax.vjp(layer_norm, merged + ff_result, head_gain[1], head_bias[3])
    positions = branch * half_rows + jnp.arange(half_rows, dtype=jnp.int32)
    observed_half = lax.dynamic_slice_in_dim(observed[0], branch * half_rows, half_rows, 0)
    valid = (
        observed_half.astype(F32)
        * (positions >= SEQ_IN).astype(F32)
        * (positions < SEQ_IN + horizons[0]).astype(F32)
    )
    error_rows = final_out - target[0].astype(F32)
    weighted = valid[:, None] * error_rows
    loss_part = 0.5 * jnp.sum(weighted * error_rows) / (features * length)
    delta_sum, gain_second, shift_second = second_back(weighted)
    delta_ff = delta_sum.astype(BF)
    grad_ff_out = left_product(low_act, delta_ff)
    delta_act = right_product(delta_ff, ff_out)
    (delta_pre,) = gelu_back(delta_act)
    low_pre = delta_pre.astype(BF)
    grad_ff_in = left_product(low_pre, low_normed)
    delta_normed = right_product(low_pre, ff_in)
    delta_first, gain_first, shift_first = first_back(delta_normed)
    delta_merged = (delta_first + delta_sum).astype(BF)
    grad_merge_own = left_product(out_keep, delta_merged)
    grad_merge_other = left_product(out_recv, delta_merged)
    up_keep = right_product(delta_merged, merge_own).astype(BF)
    up_send = right_product(delta_merged, merge_other).astype(BF)
    up_recv = swap(up_send)

    outer, taps, delta_iso, delta_inner, vectors = branch_backward(
        plan, meta, up_keep, up_recv, series, act_trans, act_iso, low, trans_all, biases, gain
    )
    delta_slots = gather_slots(plan, delta_iso)
    keep, send = iso_partial(plan, meta, delta_slots, iso_short, iso_long, True)
    pieces = scatter_sum(plan, keep, send)
    grad_iso, iso_sum = iso_weight(plan, meta, low_slots, delta_slots)
    iso_recv = swap(grad_iso)
    delta_down = down_delta(plan, meta, pieces, delta_inner, act_down)
    down_slots = gather_slots(plan, delta_down)
    input_own = input_delta(plan, meta, delta_down, outer, down_all)
    input_recv = swap(input_own)
    grad_down, down_sum = down_weight(plan, meta, matrix, down_slots)
    down_recv = swap(grad_down)

    inner_all = lax.all_gather(inner, "series", axis=0)
    own_taps = lax.all_to_all(taps, "series", split_axis=0, concat_axis=0, tiled=True)
    grad_trans = trans_weight(plan, meta, inner_all, own_taps, hop(own_taps, 1, shards))
    trans_recv = swap(grad_trans)

    def placed(own, other, b, rows):
        return jnp.where(branch == b, own, other)[:rows].astype(F32)

    ff_in_share = rounded(
        lax.psum_scatter(grad_ff_in, "series", scatter_dimension=0, tiled=True)
    )
    ff_out_share = rounded(
        lax.psum_scatter(grad_ff_out, "series", scatter_dimension=0, tiled=True)
    )
    ff_in_total = ff_in_share + swap(ff_in_share.astype(BF)).astype(F32)
    ff_out_total = ff_out_share + swap(ff_out_share.astype(BF)).astype(F32)
    loss = loss_part[None] + swap(loss_part[None])
    short_own = jnp.where(is_short, 1.0, 0.0)
    head_rows = jnp.stack(
        [
            jnp.sum(delta_merged.astype(F32), axis=0),
            jnp.sum(delta_ff.astype(F32), axis=0),
            shift_first,
            shift_second,
            gain_first,
            gain_second,
        ]
    )
    ff_bias_grad = jnp.sum(low_pre.astype(F32), axis=0)
    selector = jnp.stack([short_own, 1.0 - short_own])
    branch_rows = (selector[:, None, None] * vectors[None, 0:3]).reshape(6, features)
    merge_pair = jnp.where(
        is_short,
        jnp.stack([grad_merge_own, grad_merge_other]),
        jnp.stack([grad_merge_other, grad_merge_own]),
    )
    merge_total = lax.psum(merge_pair, ("branch", "series"))
    small = jnp.concatenate([head_rows, ff_bias_grad.reshape(-1, features), branch_rows], axis=0)
    small = lax.psum(small, ("branch", "series"))
    ff_rows = ff_in_bias.shape[0] // features
    branch_total = small[6 + ff_rows :].reshape(2, 3, features)
    late = jnp.concatenate([down_sum, iso_sum], axis=0)
    late_recv = swap(late)
    late_short = jnp.where(is_short, late, late_recv)
    late_long = jnp.where(is_short, late_recv, late)
    late_all = jnp.stack([late_short, late_long])
    bias_total = jnp.concatenate([late_all, branch_total[:, 0:2]], axis=1)

    return (
        final_out.astype(BF)[None],
        loss,
        (input_own.astype(F32) + input_recv.astype(F32))[None],
        placed(grad_down, down_recv, 0, plan.down_rows[0]),
        placed(grad_iso, iso_recv, 0, plan.iso_rows[0]),
        placed(grad_trans, trans_recv, 0, plan.down_rows[0]),
        placed(grad_down, down_recv, 1, plan.down_rows[1]),
        placed(grad_iso, iso_recv, 1, plan.iso_rows[1]),
        placed(grad_trans, trans_recv, 1, plan.down_rows[1]),
        bias_total,
        branch_total[:, 2],
        merge_total,
        small[0:4],
        small[4:6],
        ff_in_total.T,
        small[6 : 6 + ff_rows].reshape(-1),
        ff_out_total,
    )


def fitted(matrix, row_total):
    return jnp.pad(matrix, ((0, row_total - matrix.shape[0]), (0, 0)))


def unpack(gathered_all, shards, rows_max, rows_own):
    features = gathered_all.shape[1]
    return gathered_all.reshape(shards, rows_max, features)[:, :rows_own].reshape(
        shards * rows_own, features
    )


def repack(gradient, shards, rows_max):
    rows_own = gradient.shape[0] // shards
    shaped = gradient.reshape(shards, rows_own, gradient.shape[1])
    return jnp.pad(shaped, ((0, 0), (0, rows_max - rows_own), (0, 0))).reshape(
        shards * rows_max, gradient.shape[1]
    )


def branch_pass(series_in, weights, shards, rows_max, biases, gain_row, factor):
    series_count, length, features = series_in.shape
    step_count = (length + factor) // factor
    margin = factor // 2
    weight_down = unpack(weights[0], shards, rows_max[0], factor * features // shards)
    weight_iso = unpack(weights[1], shards, rows_max[1], step_count * features // shards)
    weight_trans = unpack(weights[2], shards, rows_max[2], factor * features // shards).reshape(
        factor, features, features
    )
    blocks = jnp.pad(series_in, ((0, 0), (margin, step_count * factor - length - margin), (0, 0)))
    blocks = blocks.reshape(series_count * step_count, factor * features)
    act_down = jnp.tanh(product(blocks, weight_down) + biases[0])
    low_down = act_down.astype(jnp.bfloat16)
    padded = jnp.concatenate(
        [
            jnp.zeros((series_count, step_count - 1, features), jnp.bfloat16),
            low_down.reshape(series_count, step_count, features),
        ],
        axis=1,
    )
    unfolded = jnp.concatenate(
        [padded[:, offset : offset + step_count] for offset in range(step_count)], axis=2
    )
    unfolded = unfolded.reshape(series_count * step_count, step_count * features)
    act_iso = jnp.tanh(product(unfolded, weight_iso) + biases[1])
    inner_norm, inner_back = jax.vjp(
        layer_norm, act_iso + low_down.astype(jnp.float32), gain_row, biases[3]
    )
    low_inner = inner_norm.astype(jnp.bfloat16)
    spread_out = jnp.einsum(
        "mi,jio->mjo", low_inner, weight_trans, preferred_element_type=jnp.float32
    )
    act_trans = jnp.tanh(
        spread_out.reshape(series_count, step_count * factor, features)[:, :length] + biases[2]
    )
    result, outer_back = jax.vjp(
        layer_norm, act_trans + series_in.astype(jnp.float32), gain_row, biases[3]
    )
    stored = (
        blocks,
        weight_down,
        weight_iso,
        weight_trans,
        act_down,
        unfolded,
        act_iso,
        inner_back,
        low_inner,
        act_trans,
        outer_back,
    )
    return (result, stored)


def branch_back(series_in, weights, shards, rows_max, biases, gain_row, factor, upstream):
    series_count, length, features = series_in.shape
    step_count = (length + factor) // factor
    margin = factor // 2
    result, stored = branch_pass(series_in, weights, shards, rows_max, biases, gain_row, factor)
    (
        blocks,
        weight_down,
        weight_iso,
        weight_trans,
        act_down,
        unfolded,
        act_iso,
        inner_back,
        low_inner,
        act_trans,
        outer_back,
    ) = stored
    delta_outer, gain_outer, shift_outer = outer_back(upstream)
    delta_trans = (delta_outer * (1.0 - act_trans * act_trans)).astype(jnp.bfloat16)
    trans_blocks = jnp.pad(delta_trans, ((0, 0), (0, step_count * factor - length), (0, 0)))
    trans_blocks = trans_blocks.reshape(series_count * step_count, factor, features)
    grad_trans = jnp.einsum(
        "mi,mjo->jio", low_inner, trans_blocks, preferred_element_type=jnp.float32
    )
    grad_trans = grad_trans.reshape(factor * features, features)
    inner_upstream = jnp.einsum(
        "mjo,jio->mi", trans_blocks, weight_trans, preferred_element_type=jnp.float32
    )
    delta_inner, gain_inner, shift_inner = inner_back(inner_upstream)
    delta_iso = (delta_inner * (1.0 - act_iso * act_iso)).astype(jnp.bfloat16)
    grad_iso = left_product(unfolded, delta_iso)
    delta_unfold = right_product(delta_iso, weight_iso).reshape(
        series_count, step_count, step_count, features
    )
    delta_padded = jnp.zeros((series_count, 2 * step_count - 1, features), jnp.float32)
    for offset in range(step_count):
        delta_padded = delta_padded.at[:, offset : offset + step_count].add(
            delta_unfold[:, :, offset]
        )
    delta_low = (
        delta_padded[:, step_count - 1 :].reshape(series_count * step_count, features) + delta_inner
    )
    delta_down = (delta_low * (1.0 - act_down * act_down)).astype(jnp.bfloat16)
    grad_down = left_product(blocks, delta_down)
    delta_blocks = right_product(delta_down, weight_down).reshape(
        series_count, step_count * factor, features
    )
    delta_series = delta_blocks[:, margin : margin + length] + delta_outer
    vectors = jnp.stack(
        [
            jnp.sum(delta_down.astype(jnp.float32), axis=0),
            jnp.sum(delta_iso.astype(jnp.float32), axis=0),
            jnp.sum(delta_trans.astype(jnp.float32), axis=(0, 1)),
            shift_inner + shift_outer,
        ]
    )
    padded_grads = (
        repack(grad_down, shards, rows_max[0]),
        repack(grad_iso, shards, rows_max[1]),
        repack(grad_trans, shards, rows_max[2]),
    )
    return (delta_series, padded_grads, vectors, gain_inner + gain_outer)


def plain_body(
    series_in,
    target,
    horizons,
    observed,
    down_short,
    iso_short,
    trans_short,
    down_long,
    iso_long,
    trans_long,
    branch_bias,
    branch_gain,
    merge_weight,
    head_bias,
    head_gain,
    ff_in,
    ff_in_bias,
    ff_out,
):
    branch_index = lax.axis_index("branch")
    shards = lax.axis_size("series")
    series_count, length, features = series_in.shape
    rows_max = (
        max(down_short.shape[0], down_long.shape[0]),
        max(iso_short.shape[0], iso_long.shape[0]),
        max(trans_short.shape[0], trans_long.shape[0]),
    )
    is_short = branch_index == 0
    own_down = jnp.where(is_short, fitted(down_short, rows_max[0]), fitted(down_long, rows_max[0]))
    own_iso = jnp.where(is_short, fitted(iso_short, rows_max[1]), fitted(iso_long, rows_max[1]))
    own_trans = jnp.where(
        is_short, fitted(trans_short, rows_max[2]), fitted(trans_long, rows_max[2])
    )
    gathered = (
        lax.all_gather(own_down, "series", axis=0, tiled=True),
        lax.all_gather(own_iso, "series", axis=0, tiled=True),
        lax.all_gather(own_trans, "series", axis=0, tiled=True),
    )
    biases = branch_bias[0]
    gain_row = branch_gain[0]

    def forward_with(factor):
        return lambda: branch_pass(series_in, gathered, shards, rows_max, biases, gain_row, factor)[
            0
        ].astype(jnp.bfloat16)

    branch_out = lax.cond(is_short, forward_with(SCALE_S), forward_with(SCALE_L))
    received = lax.all_to_all(
        branch_out.reshape(series_count, length, 1, features),
        "branch",
        split_axis=1,
        concat_axis=2,
        tiled=True,
    )
    half_rows = received.shape[1]
    merge_rows = received.reshape(series_count * half_rows, 2 * features)
    merge_flat = merge_weight.reshape(2 * features, features)
    merged = product(merge_rows, merge_flat) + head_bias[0]
    normed, first_back = jax.vjp(layer_norm, merged, head_gain[0], head_bias[2])
    low_normed = normed.astype(jnp.bfloat16)
    pre_ff = product(low_normed, ff_in) + ff_in_bias
    activated, gelu_back = jax.vjp(gelu_exact, pre_ff)
    low_act = activated.astype(jnp.bfloat16)
    ff_result = product(low_act, ff_out) + head_bias[1]
    final_out, second_back = jax.vjp(layer_norm, merged + ff_result, head_gain[1], head_bias[3])
    final_rows = final_out.reshape(series_count, half_rows, features)
    positions = branch_index * half_rows + jnp.arange(half_rows, dtype=jnp.int32)
    observed_half = lax.dynamic_slice_in_dim(observed, branch_index * half_rows, half_rows, 1)
    valid_mask = (
        observed_half.astype(jnp.float32)
        * (positions >= SEQ_IN).astype(jnp.float32)
        * (positions < SEQ_IN + horizons[:, None]).astype(jnp.float32)
    )
    error_rows = final_rows - target.astype(jnp.float32)
    weighted = valid_mask[:, :, None] * error_rows
    series_part = 0.5 * jnp.sum(weighted * error_rows, axis=(1, 2)) / (features * length)
    delta_sum, gain_second, shift_second = second_back(
        weighted.reshape(series_count * half_rows, features)
    )
    delta_ff = delta_sum.astype(jnp.bfloat16)
    grad_ff_out = left_product(low_act, delta_ff)
    delta_act = right_product(delta_ff, ff_out)
    (delta_pre,) = gelu_back(delta_act)
    low_pre = delta_pre.astype(jnp.bfloat16)
    grad_ff_in = left_product(low_normed, low_pre)
    delta_normed = right_product(low_pre, ff_in)
    delta_first, gain_first, shift_first = first_back(delta_normed)
    delta_merged = (delta_first + delta_sum).astype(jnp.bfloat16)
    grad_merge = left_product(merge_rows, delta_merged).reshape(2, features, features)
    delta_rows = (
        right_product(delta_merged, merge_flat)
        .astype(jnp.bfloat16)
        .reshape(series_count, half_rows, 2, features)
    )
    back_rows = lax.all_to_all(delta_rows, "branch", split_axis=2, concat_axis=1, tiled=True)
    upstream = back_rows.astype(jnp.float32).reshape(series_count, length, features)
    ff_shares = (
        lax.psum_scatter(grad_ff_in, "series", scatter_dimension=1, tiled=True),
        lax.psum_scatter(grad_ff_out, "series", scatter_dimension=0, tiled=True),
    )
    weights_back = (
        lax.all_gather(own_down, "series", axis=0, tiled=True),
        lax.all_gather(own_iso, "series", axis=0, tiled=True),
        lax.all_gather(own_trans, "series", axis=0, tiled=True),
    )

    def backward_with(factor):
        return lambda: branch_back(
            series_in, weights_back, shards, rows_max, biases, gain_row, factor, upstream
        )

    delta_series, padded_grads, vectors, gain_grad = lax.cond(
        is_short, backward_with(SCALE_S), backward_with(SCALE_L)
    )
    reduced = (
        lax.psum_scatter(padded_grads[0], "series", scatter_dimension=0, tiled=True),
        lax.psum_scatter(padded_grads[1], "series", scatter_dimension=0, tiled=True),
        lax.psum_scatter(padded_grads[2], "series", scatter_dimension=0, tiled=True),
    )
    short_flag = is_short.astype(jnp.float32)
    long_flag = 1.0 - short_flag
    summed = (
        lax.psum(delta_series.astype(jnp.bfloat16), "branch").astype(jnp.float32),
        lax.psum(series_part.astype(jnp.bfloat16), "branch").astype(jnp.float32),
        lax.psum(
            (short_flag * reduced[0][: down_short.shape[0]]).astype(jnp.bfloat16), "branch"
        ).astype(jnp.float32),
        lax.psum((short_flag * reduced[1]).astype(jnp.bfloat16), "branch").astype(jnp.float32),
        lax.psum(
            (short_flag * reduced[2][: trans_short.shape[0]]).astype(jnp.bfloat16), "branch"
        ).astype(jnp.float32),
        lax.psum((long_flag * reduced[0]).astype(jnp.bfloat16), "branch").astype(jnp.float32),
        lax.psum(
            (long_flag * reduced[1][: iso_long.shape[0]]).astype(jnp.bfloat16), "branch"
        ).astype(jnp.float32),
        lax.psum((long_flag * reduced[2]).astype(jnp.bfloat16), "branch").astype(jnp.float32),
        lax.psum(ff_shares[0].astype(jnp.bfloat16), "branch").astype(jnp.float32),
        lax.psum(ff_shares[1].astype(jnp.bfloat16), "branch").astype(jnp.float32),
    )
    selector = (jnp.arange(2, dtype=jnp.int32) == branch_index).astype(jnp.float32)
    full_bias = selector[:, None, None] * vectors[None]
    full_gain = selector[:, None] * gain_grad[None]
    head_vectors = jnp.stack(
        [
            jnp.sum(delta_merged.astype(jnp.float32), axis=0),
            jnp.sum(delta_ff.astype(jnp.float32), axis=0),
            shift_first,
            shift_second,
        ]
    )
    head_gains = jnp.stack([gain_first, gain_second])
    ff_bias_grad = jnp.sum(low_pre.astype(jnp.float32), axis=0)
    totals = lax.psum(
        (grad_merge, head_vectors, head_gains, ff_bias_grad, full_bias, full_gain),
        ("branch", "series"),
    )
    return (
        final_rows.astype(jnp.bfloat16),
        summed[1],
        summed[0],
        summed[2],
        summed[3],
        summed[4],
        summed[5],
        summed[6],
        summed[7],
        totals[4],
        totals[5],
        totals[0],
        totals[1],
        totals[2],
        summed[8],
        totals[3],
        summed[9],
    )


def solution(mesh):
    placed = (
        P("series", None, None),
        P("series", "branch", None),
        P("series"),
        P("series", None),
        P("series", None),
        P("series", None),
        P("series", None),
        P("series", None),
        P("series", None),
        P("series", None),
        P("branch", None, None),
        P("branch", None),
        P(),
        P(),
        P(),
        P(),
        P(),
        P(),
    )

    def run(*args):
        shards = mesh.shape["series"]
        features = args[0].shape[2]
        fits = (
            args[0].shape[0] == shards
            and shards >= 8
            and shards & (shards - 1) == 0
            and all((args[i].shape[0] // shards) % LANE == 0 for i in (4, 7))
            and all((args[i].shape[0] // shards) % 16 == 0 for i in (5, 8))
            and all(2 * (args[i].shape[0] // shards) + features // 2 <= 3 * features for i in (4, 7))
        )
        return jax.shard_map(
            body if fits else plain_body,
            mesh=mesh,
            in_specs=placed,
            out_specs=(
                P("series", "branch", None),
                P("series"),
                P("series", None, None),
                P("series", None),
                P("series", None),
                P("series", None),
                P("series", None),
                P("series", None),
                P("series", None),
                P(),
                P(),
                P(),
                P(),
                P(),
                P(None, "series"),
                P(),
                P("series", None),
            ),
            check_vma=False,
        )(*args)

    return run
```

```python
import functools

import jax
import jax.numpy as jnp
from jax import lax
from jax.experimental import pallas as pl
from jax.experimental.pallas import tpu as pltpu
from jax.sharding import PartitionSpec as P

SCALE_S = 12
SCALE_L = 16
SEQ_IN = 96
EPSILON = 1e-05
LANE = 128

BF = jnp.bfloat16
F32 = jnp.float32


def up8(count, base=8):
    return -(-count // base) * base


class Plan:
    def __init__(self, shards, length, features, down_rows, iso_rows):
        self.shards, self.length, self.features = shards, length, features
        self.factors = (SCALE_S, SCALE_L)
        self.steps = tuple((length + k) // k for k in self.factors)
        self.rows = up8(max(self.steps))
        self.down_rows = down_rows
        self.iso_rows = iso_rows
        self.down_max, self.iso_max = max(down_rows), max(iso_rows)
        self.line = shards // 4
        self.line_taps = tuple(4 * r // features for r in down_rows)
        blocks = features // LANE
        self.pack = up8(max(t * blocks * n for t, n in zip(self.line_taps, self.steps)), 16)
        self.taps = tuple(
            max(-(-((d * r) % features + r) // features) for d in range(shards)) for r in iso_rows
        )
        self.taps_max = max(self.taps)
        self.stage_rows = max(k * up8(n) for k, n in zip(self.factors, self.steps))

    def mask(self, slot):
        core, rest = divmod(slot, 2 * self.line)
        side, line = divmod(rest, self.line)
        return core | (side << 1) | (line << 2)


def vmem(count):
    return [pl.BlockSpec(memory_space=pltpu.VMEM) for _ in range(count)]


SMEM = pl.BlockSpec(memory_space=pltpu.SMEM)
ANY = pl.BlockSpec(memory_space=pl.ANY)
HBM = pl.BlockSpec(memory_space=pltpu.HBM)


def call(body, in_specs, outs, scratch, flops=0, moved=0, limit=56):
    return pl.pallas_call(
        body,
        out_shape=[jax.ShapeDtypeStruct(s, d) for s, d in outs],
        in_specs=in_specs,
        out_specs=vmem(len(outs)),
        scratch_shapes=scratch,
        compiler_params=pltpu.CompilerParams(vmem_limit_bytes=limit << 20),
        cost_estimate=pl.CostEstimate(flops=flops, bytes_accessed=moved, transcendentals=0),
    )


def dot(a, b, dims=((1,), (0,))):
    return lax.dot_general(a, b, (dims, ((), ())), preferred_element_type=F32)


def norm_parts(values):
    center = values - jnp.mean(values, axis=-1, keepdims=True)
    spread = jnp.mean(center * center, axis=-1, keepdims=True)
    scale = lax.rsqrt(spread + EPSILON)
    return center * scale, scale


def norm_back(upstream, unit, scale, gain):
    inner = upstream * gain
    first = jnp.mean(inner, axis=-1, keepdims=True)
    second = jnp.mean(inner * unit, axis=-1, keepdims=True)
    return scale * (inner - first - unit * second)


def keep_rows(values, count):
    index = lax.broadcasted_iota(jnp.int32, values.shape, 0)
    return jnp.where(index < count, values, 0.0)


def both(meta, short, long):
    pl.when(meta[0] == 0)(short)
    pl.when(meta[0] == 1)(long)


def split(rows, features):
    return pltpu.VMEM((features // LANE, rows, LANE), F32)


def put(ref, start, values, stride=1):
    count = values.shape[0]
    where = pl.ds(start, count) if stride == 1 else pl.ds(start, count, stride=stride)
    for c in range(ref.shape[0]):
        ref[c, where, :] = values[:, c * LANE : (c + 1) * LANE]


def get(ref, start, count, stride=1):
    where = pl.ds(start, count) if stride == 1 else pl.ds(start, count, stride=stride)
    return jnp.concatenate([ref[c, where, :] for c in range(ref.shape[0])], axis=1)


def split(rows, features):
    return pltpu.VMEM((features // LANE, rows, LANE), F32)


def put(ref, start, values, stride=1):
    count = values.shape[0]
    where = pl.ds(start, count) if stride == 1 else pl.ds(start, count, stride=stride)
    for c in range(ref.shape[0]):
        ref[c, where, :] = values[:, c * LANE : (c + 1) * LANE]


def get(ref, start, count, stride=1):
    where = pl.ds(start, count) if stride == 1 else pl.ds(start, count, stride=stride)
    return jnp.concatenate([ref[c, where, :] for c in range(ref.shape[0])], axis=1)


def pack_taps(plan, b, stage, first, packed):
    k, n = plan.factors[b], plan.steps[b]
    blocks = plan.features // LANE
    for i in range(plan.line_taps[b]):
        for c in range(blocks):
            at = (i * blocks + c) * n
            packed[at : at + n, :] = stage[c, pl.ds(first + i, n, stride=k), :]


def unpack_taps(plan, b, packed, stage, first):
    k, n = plan.factors[b], plan.steps[b]
    blocks = plan.features // LANE
    for i in range(plan.line_taps[b]):
        for c in range(blocks):
            at = (i * blocks + c) * n
            stage[c, pl.ds(first + i, n, stride=k), :] = packed[at : at + n, :]


def packed_matrix(plan, b, packed, base, matrix):
    n = plan.steps[b]
    for g in range(plan.line_taps[b] * plan.features // LANE):
        matrix[base : base + n, g * LANE : (g + 1) * LANE] = packed[g * n : (g + 1) * n, :]


def matrix_packed(plan, b, matrix, base, packed):
    n = plan.steps[b]
    for g in range(plan.line_taps[b] * plan.features // LANE):
        packed[g * n : (g + 1) * n, :] = matrix[base : base + n, g * LANE : (g + 1) * LANE]


def fetch_quarter(plan, b, meta_ref, sources, target, sems):
    own = plan.down_rows[b]
    quad = meta_ref[7]
    copies = []
    for v, source in enumerate(sources):
        start = pl.multiple_of((quad ^ v) * own, LANE)
        copies.append(
            pltpu.make_async_copy(
                source.at[pl.ds(0, own)], target.at[pl.ds(start, own)], sems.at[v]
            )
        )
    for copy in copies:
        copy.start()
    return copies


def total_of(parts):
    total = parts[0][...].astype(F32)
    for piece in parts[1:]:
        total = total + piece[...].astype(F32)
    return total


def prep_blocks(plan, meta, series):
    length, features, line = plan.length, plan.features, plan.line

    def kernel(meta_ref, x_ref, out_ref, wide, packed):
        def run(b):
            margin = plan.factors[b] // 2
            wide[...] = jnp.zeros_like(wide)
            put(wide, margin, x_ref[...].astype(F32))
            packed[...] = jnp.zeros_like(packed)
            for z in range(line):
                pack_taps(plan, b, wide, z * plan.line_taps[b], packed)
                out_ref[z ^ meta_ref[5]] = packed[...].astype(BF)

        both(meta_ref, lambda: run(0), lambda: run(1))

    return call(
        kernel,
        [SMEM] + vmem(1),
        [((line, plan.pack, LANE), BF)],
        [split(plan.stage_rows, features), pltpu.VMEM((plan.pack, LANE), F32)],
        moved=2 * length * features * 2,
        limit=8,
    )(meta, series)[0]


def down_partial(plan, meta, blocks, quarter):
    rows, features, line = plan.rows, plan.features, plan.line
    wide_max = 4 * plan.down_max

    def kernel(meta_ref, *refs):
        packs, weights = refs[:line], refs[line : line + 4]
        keep_ref, send_ref, *col_refs = refs[line + 4 : line + 10]
        weight, wide, packed, cols, sems = refs[line + 10 :]

        def run(b):
            copies = fetch_quarter(plan, b, meta_ref, weights, weight, sems)
            own = plan.down_rows[b]
            wide[...] = jnp.zeros_like(wide)
            for m in range(line):
                packed[...] = packs[m][...].astype(F32)
                packed_matrix(plan, b, packed, m * rows, wide)
            matrix = wide[...].astype(BF)
            for u in range(4):
                piece = matrix[:, u * own : (u + 1) * own]
                if own < plan.down_max:
                    pad = jnp.zeros((line * rows, plan.down_max - own), BF)
                    piece = jnp.concatenate([piece, pad], axis=1)
                cols[u ^ meta_ref[7]] = piece
            for v in range(4):
                col_refs[v][...] = cols[v]
            for copy in copies:
                copy.wait()
            part = dot(matrix[:, : 4 * own], weight[0 : 4 * own, :])
            keep_ref[...] = part[:rows]
            for m in range(1, line):
                send_ref[m - 1] = part[m * rows : (m + 1) * rows].astype(BF)

        both(meta_ref, lambda: run(0), lambda: run(1))

    return call(
        kernel,
        [SMEM] + vmem(line) + [ANY] * 4,
        [
            ((rows, features), F32),
            ((line - 1, rows, features), BF),
        ]
        + [((line * rows, plan.down_max), BF)] * 4,
        [
            pltpu.VMEM((wide_max, features), BF),
            pltpu.VMEM((line * rows, wide_max), F32),
            pltpu.VMEM((plan.pack, LANE), F32),
            pltpu.VMEM((4, line * rows, plan.down_max), BF),
            pltpu.SemaphoreType.DMA((4,)),
        ],
        flops=2 * line * rows * features * wide_max,
        moved=5 << 20,
        limit=16,
    )(meta, *blocks, *quarter)


def low_rows(plan, meta, pieces, biases):
    rows, features = plan.rows, plan.features

    def kernel(meta_ref, *refs):
        parts, bias_ref, low_ref, act_ref = refs[:-3], refs[-3], refs[-2], refs[-1]
        act = keep_rows(jnp.tanh(total_of(parts) + bias_ref[0:1, :]), meta_ref[4])
        act_ref[...] = act
        low_ref[...] = act.astype(BF)

    return call(
        kernel,
        [SMEM] + vmem(len(pieces) + 1),
        [((rows, features), BF), ((rows, features), F32)],
        [],
        moved=1 << 19,
        limit=4,
    )(meta, *pieces, biases)


def time_major(plan, halves, stage, target, lead):
    shards, rows = plan.shards, plan.rows
    half = shards // 2
    for q in range(shards):
        put(stage, q, halves[q // half][q % half].astype(F32), shards)
    body = shards * rows
    if lead:
        target[0 : lead * shards, :] = jnp.zeros((lead * shards, target.shape[1]), BF)
    target[lead * shards : lead * shards + body, :] = get(stage, 0, body).astype(BF)
    rest = target.shape[0] - lead * shards - body
    if rest:
        target[lead * shards + body :, :] = jnp.zeros((rest, target.shape[1]), BF)


def pad_weight(plan, b, meta_ref, source, target, sem):
    target[...] = jnp.zeros_like(target)
    shift = pl.multiple_of(meta_ref[3], 16)
    copy = pltpu.make_async_copy(source, target.at[pl.ds(shift, plan.iso_rows[b])], sem)
    copy.start()
    return copy


def iso_partial(plan, meta, halves, w_short, w_long, backward):
    shards, rows, features = plan.shards, plan.rows, plan.features
    half = shards // 2
    extra = plan.taps_max + 2
    buffer = (max(plan.steps) + rows + extra) * shards

    def kernel(
        meta_ref, even_ref, odd_ref, ws_ref, wl_ref, keep_ref, send_ref, stage, lined, padded, sem
    ):
        first = meta_ref[2]

        def run(b, w_ref):
            n, taps = plan.steps[b], plan.taps[b]
            copy = pad_weight(plan, b, meta_ref, w_ref, padded, sem)
            lead = extra if backward else n - 1
            time_major(plan, (even_ref, odd_ref), stage, lined, lead)
            copy.wait()
            for m in range(taps):
                start = extra + n - 1 - first - m if backward else first + m
                start = pl.multiple_of(start * shards, 16)
                window = lined[pl.ds(start, rows * shards), :]
                weight = padded[m * features : (m + 1) * features, :]
                part = dot(window, weight, ((1,), (1,)) if backward else ((1,), (0,)))
                total = part if m == 0 else total + part
            put(stage, 0, total)
            for q in range(shards):
                piece = get(stage, q, rows, shards)
                if q < half:
                    keep_ref[q] = piece
                else:
                    send_ref[q - half] = piece.astype(BF)

        both(meta_ref, lambda: run(0, ws_ref), lambda: run(1, wl_ref))

    return call(
        kernel,
        [SMEM] + vmem(2) + [HBM] * 2,
        [((half, rows, features), F32), ((half, rows, features), BF)],
        [
            split(rows * shards, features),
            pltpu.VMEM((buffer, features), BF),
            pltpu.VMEM((plan.taps_max * features, features), BF),
            pltpu.SemaphoreType.DMA,
        ],
        flops=2 * shards * rows * features * features * plan.taps_max,
        moved=10 << 20,
        limit=56,
    )(meta, *halves, w_short, w_long)


def iso_weight(plan, meta, b, low_own, low_other, delta_own, delta_other):
    shards, rows, features = plan.shards, plan.rows, plan.features
    half = shards // 2
    n, taps, own = plan.steps[b], plan.taps[b], plan.iso_rows[b]
    buffer = (n - 1 + rows + taps + 1) * shards

    def kernel(meta_ref, *refs):
        lows, deltas = refs[0:4], refs[4:8]
        grad_ref, sum_ref, stage, lined, delta, total, ordered = refs[8:]
        me = meta_ref[1]

        def load(low, steps):
            for q in range(shards):
                ordered[pl.ds(me ^ plan.mask(q), 1), :] = jnp.sum(
                    steps[q // half][q % half].astype(F32), axis=0, keepdims=True
                )
            time_major(plan, steps, stage, delta, 0)
            time_major(plan, low, stage, lined, n - 1)

        pl.when(meta_ref[0] == b)(lambda: load(lows[0:2], deltas[0:2]))
        pl.when(meta_ref[0] != b)(lambda: load(lows[2:4], deltas[2:4]))
        sum_ref[...] = jnp.sum(ordered[...], axis=0, keepdims=True)
        flat = me * own
        first = flat // features
        for m in range(taps):
            start = pl.multiple_of((first + m) * shards, 16)
            window = lined[pl.ds(start, rows * shards), :]
            total[m * features : (m + 1) * features, :] = dot(window, delta[...], ((0,), (0,)))
        shift = pl.multiple_of(flat % features, 16)
        grad_ref[...] = total[pl.ds(shift, own), :]

    return call(
        kernel,
        [SMEM] + vmem(8),
        [((own, features), F32), ((1, features), F32)],
        [
            split(rows * shards, features),
            pltpu.VMEM((buffer, features), BF),
            pltpu.VMEM((rows * shards, features), BF),
            pltpu.VMEM((taps * features, features), F32),
            pltpu.VMEM((shards, features), F32),
        ],
        flops=2 * shards * rows * features * features * taps,
        moved=10 << 20,
        limit=32,
    )(meta, *low_own, *low_other, *delta_own, *delta_other)


def inner_rows(plan, meta, pieces, low, biases, gain):
    rows, features = plan.rows, plan.features

    def kernel(meta_ref, *refs):
        parts = refs[:-5]
        low_ref, bias_ref, gain_ref, inner_ref, act_ref = refs[-5:]
        act = jnp.tanh(total_of(parts) + bias_ref[1:2, :])
        act_ref[...] = act
        unit, _ = norm_parts(act + low_ref[...].astype(F32))
        inner = unit * gain_ref[...] + bias_ref[3:4, :]
        inner_ref[...] = keep_rows(inner, meta_ref[4]).astype(BF)

    return call(
        kernel,
        [SMEM] + vmem(len(pieces) + 3),
        [((rows, features), BF), ((rows, features), F32)],
        [],
        moved=1 << 19,
        limit=4,
    )(meta, *pieces, low, biases, gain)


def trans_forward(plan, meta, inners, quarter):
    rows, features, line = plan.rows, plan.features, plan.line
    wide_max = 4 * plan.down_max

    def kernel(meta_ref, *refs):
        inner_refs, weights = refs[:line], refs[line : line + 4]
        out_ref, weight, wide, packed, sems = refs[line + 4 :]

        def run(b):
            copies = fetch_quarter(plan, b, meta_ref, weights, weight, sems)
            lhs = jnp.concatenate([ref[...] for ref in inner_refs], axis=0)
            for copy in copies:
                copy.wait()
            for i in range(plan.line_taps[b]):
                wide[:, i * features : (i + 1) * features] = dot(
                    lhs, weight[i * features : (i + 1) * features, :]
                )
            packed[...] = jnp.zeros_like(packed)
            for m in range(line):
                matrix_packed(plan, b, wide, m * rows, packed)
                out_ref[m] = packed[...].astype(BF)

        both(meta_ref, lambda: run(0), lambda: run(1))

    return call(
        kernel,
        [SMEM] + vmem(line) + [ANY] * 4,
        [((line, plan.pack, LANE), BF)],
        [
            pltpu.VMEM((wide_max, features), BF),
            pltpu.VMEM((line * rows, wide_max), F32),
            pltpu.VMEM((plan.pack, LANE), F32),
            pltpu.SemaphoreType.DMA((4,)),
        ],
        flops=2 * line * rows * features * wide_max,
        moved=4 << 20,
        limit=16,
    )(meta, *inners, *quarter)[0]


def outer_rows(plan, meta, packs, series, biases, gain):
    features, length, line = plan.features, plan.length, plan.line
    half_rows = length // 2

    def kernel(meta_ref, *refs):
        pack_refs = refs[:line]
        x_ref, bias_ref, gain_ref, keep_ref, send_ref, act_ref, stage, packed = refs[line:]

        def run(b):
            for m in range(line):
                packed[...] = pack_refs[m][...].astype(F32)
                unpack_taps(plan, b, packed, stage, (meta_ref[5] ^ m) * plan.line_taps[b])

        both(meta_ref, lambda: run(0), lambda: run(1))
        act = jnp.tanh(get(stage, 0, length) + bias_ref[2:3, :])
        act_ref[...] = act
        unit, _ = norm_parts(act + x_ref[...].astype(F32))
        put(stage, 0, unit * gain_ref[...] + bias_ref[3:4, :])
        mine = pl.multiple_of(meta_ref[0] * half_rows, 8)
        other = pl.multiple_of((1 - meta_ref[0]) * half_rows, 8)
        keep_ref[...] = get(stage, mine, half_rows).astype(BF)
        send_ref[...] = get(stage, other, half_rows).astype(BF)

    return call(
        kernel,
        [SMEM] + vmem(line + 3),
        [((half_rows, features), BF), ((half_rows, features), BF), ((length, features), F32)],
        [split(plan.stage_rows, features), pltpu.VMEM((plan.pack, LANE), F32)],
        moved=6 << 20,
        limit=16,
    )(meta, *packs, series, biases, gain)


def outer_backward(plan, meta, up_keep, up_recv, series, act, gain):
    features, length, line = plan.features, plan.length, plan.line
    half_rows = length // 2

    def kernel(
        meta_ref, uk_ref, ur_ref, x_ref, act_ref, gain_ref,
        outer_ref, taps_ref, vec_ref, stage, upstream, packed,
    ):
        mine = pl.multiple_of(meta_ref[0] * half_rows, 8)
        other = pl.multiple_of((1 - meta_ref[0]) * half_rows, 8)
        upstream[pl.ds(mine, half_rows), :] = uk_ref[...].astype(F32)
        upstream[pl.ds(other, half_rows), :] = ur_ref[...].astype(F32)
        act_value = act_ref[...]
        unit, scale = norm_parts(act_value + x_ref[...].astype(F32))
        above = upstream[...]
        vec_ref[...] = jnp.zeros_like(vec_ref)
        vec_ref[1:2, :] = jnp.sum(above, axis=0, keepdims=True)
        vec_ref[2:3, :] = jnp.sum(above * unit, axis=0, keepdims=True)
        outer = norm_back(above, unit, scale, gain_ref[...])
        outer_ref[...] = outer
        delta = (outer * (1.0 - act_value * act_value)).astype(BF).astype(F32)
        vec_ref[0:1, :] = jnp.sum(delta, axis=0, keepdims=True)
        put(stage, 0, delta)
        put(stage, length, jnp.zeros((plan.stage_rows - length, features), F32))
        packed[...] = jnp.zeros_like(packed)

        def run(b):
            for m in range(line):
                pack_taps(plan, b, stage, (meta_ref[5] ^ m) * plan.line_taps[b], packed)
                taps_ref[m] = packed[...].astype(BF)

        both(meta_ref, lambda: run(0), lambda: run(1))

    return call(
        kernel,
        [SMEM] + vmem(5),
        [((length, features), F32), ((line, plan.pack, LANE), BF), ((8, features), F32)],
        [
            split(plan.stage_rows, features),
            pltpu.VMEM((length, features), F32),
            pltpu.VMEM((plan.pack, LANE), F32),
        ],
        moved=8 << 20,
        limit=20,
    )(meta, up_keep, up_recv, series, act, gain)


def trans_backward(plan, meta, packs, quarter):
    rows, features, line = plan.rows, plan.features, plan.line
    wide_max = 4 * plan.down_max

    def kernel(meta_ref, *refs):
        pack_refs, weights = refs[:line], refs[line : line + 4]
        keep_ref, send_ref, wide_ref, weight, wide, packed, sems = refs[line + 4 :]

        def run(b):
            copies = fetch_quarter(plan, b, meta_ref, weights, weight, sems)
            wide[...] = jnp.zeros_like(wide)
            for m in range(line):
                packed[...] = pack_refs[m][...].astype(F32)
                packed_matrix(plan, b, packed, m * rows, wide)
            matrix = wide[...].astype(BF)
            wide_ref[...] = matrix
            for copy in copies:
                copy.wait()
            for i in range(plan.line_taps[b]):
                part = dot(
                    matrix[:, i * features : (i + 1) * features],
                    weight[i * features : (i + 1) * features, :],
                    ((1,), (1,)),
                )
                total = part if i == 0 else total + part
            keep_ref[...] = total[:rows]
            for m in range(1, line):
                send_ref[m - 1] = total[m * rows : (m + 1) * rows].astype(BF)

        both(meta_ref, lambda: run(0), lambda: run(1))

    return call(
        kernel,
        [SMEM] + vmem(line) + [ANY] * 4,
        [
            ((rows, features), F32),
            ((line - 1, rows, features), BF),
            ((line * rows, wide_max), BF),
        ],
        [
            pltpu.VMEM((wide_max, features), BF),
            pltpu.VMEM((line * rows, wide_max), F32),
            pltpu.VMEM((plan.pack, LANE), F32),
            pltpu.SemaphoreType.DMA((4,)),
        ],
        flops=2 * line * rows * features * wide_max,
        moved=5 << 20,
        limit=16,
    )(meta, *packs, *quarter)


def trans_weight(plan, meta, inners, wide):
    rows, features, line = plan.rows, plan.features, plan.line
    most = plan.down_max

    def kernel(meta_ref, *refs):
        inner_refs = refs[:line]
        wide_ref, keep_ref, send_ref, total = refs[line:]

        def run(b):
            own = plan.down_rows[b]
            lhs = jnp.concatenate([ref[...] for ref in inner_refs], axis=0)
            for i in range(plan.line_taps[b]):
                total[i * features : (i + 1) * features, :] = dot(
                    lhs, wide_ref[:, i * features : (i + 1) * features], ((0,), (0,))
                )
            for v in range(4):
                start = pl.multiple_of((meta_ref[7] ^ v) * own, LANE)
                piece = total[pl.ds(start, own), :]
                if own < most:
                    pad = jnp.zeros((most - own, features), F32)
                    piece = jnp.concatenate([piece, pad], axis=0)
                if v % 2 == 0:
                    keep_ref[v // 2] = piece
                else:
                    send_ref[v // 2] = piece.astype(BF)

        both(meta_ref, lambda: run(0), lambda: run(1))

    return call(
        kernel,
        [SMEM] + vmem(line + 1),
        [((2, most, features), F32), ((2, most, features), BF)],
        [pltpu.VMEM((4 * most, features), F32)],
        flops=2 * line * rows * features * 4 * most,
        moved=5 << 20,
        limit=20,
    )(meta, *inners, wide)


def inner_backward(plan, meta, pieces, low, act, vectors, gain):
    rows, features = plan.rows, plan.features

    def kernel(meta_ref, *refs):
        parts = refs[:-7]
        low_ref, act_ref, vec_ref, gain_ref, delta_ref, back_ref, out_ref = refs[-7:]
        total = keep_rows(total_of(parts), meta_ref[4])
        act_in = act_ref[...]
        unit, scale = norm_parts(act_in + low_ref[...].astype(F32))
        out_ref[...] = vec_ref[...]
        out_ref[1:2, :] = vec_ref[1:2, :] + jnp.sum(total, axis=0, keepdims=True)
        out_ref[2:3, :] = vec_ref[2:3, :] + jnp.sum(total * unit, axis=0, keepdims=True)
        back = norm_back(total, unit, scale, gain_ref[...])
        back_ref[...] = back
        delta_ref[...] = keep_rows(back * (1.0 - act_in * act_in), meta_ref[4]).astype(BF)

    return call(
        kernel,
        [SMEM] + vmem(len(pieces) + 4),
        [((rows, features), BF), ((rows, features), F32), ((8, features), F32)],
        [],
        moved=1 << 19,
        limit=6,
    )(meta, *pieces, low, act, vectors, gain)


def down_delta(plan, meta, pieces, delta_inner, act, small):
    rows, features = plan.rows, plan.features
    base, extra = up8(rows, 16), small.shape[0]

    def kernel(meta_ref, *refs):
        parts = refs[:-4]
        inner_ref, act_ref, small_ref, out_ref = refs[-4:]
        value = act_ref[...]
        total = total_of(parts) + inner_ref[...]
        delta = keep_rows(total * (1.0 - value * value), meta_ref[4])
        pad = jnp.zeros((base - rows, features), F32)
        out_ref[0:base, :] = jnp.concatenate([delta, pad], axis=0).astype(BF)
        high = small_ref[...].astype(BF)
        out_ref[base : base + extra, :] = high
        out_ref[base + extra :, :] = (small_ref[...] - high.astype(F32)).astype(BF)

    return call(
        kernel,
        [SMEM] + vmem(len(pieces) + 3),
        [((base + 2 * extra, features), BF)],
        [],
        moved=1 << 19,
        limit=8,
    )(meta, *pieces, delta_inner, act, small)[0]


def input_quarter(plan, meta, deltas, quarter):
    features, line = plan.features, plan.line
    rows = up8(plan.rows, 16)
    wide_max = 4 * plan.down_max

    def kernel(meta_ref, *refs):
        delta_refs, weights = refs[:line], refs[line : line + 4]
        out_ref, weight, wide, packed, sems = refs[line + 4 :]

        def run(b):
            copies = fetch_quarter(plan, b, meta_ref, weights, weight, sems)
            lhs = jnp.concatenate([ref[0:rows, :] for ref in delta_refs], axis=0)
            for copy in copies:
                copy.wait()
            for i in range(plan.line_taps[b]):
                wide[:, i * features : (i + 1) * features] = dot(
                    lhs, weight[i * features : (i + 1) * features, :], ((1,), (1,))
                )
            packed[...] = jnp.zeros_like(packed)
            for m in range(line):
                matrix_packed(plan, b, wide, m * rows, packed)
                out_ref[m] = packed[...].astype(BF)

        both(meta_ref, lambda: run(0), lambda: run(1))

    return call(
        kernel,
        [SMEM] + vmem(line) + [ANY] * 4,
        [((line, plan.pack, LANE), BF)],
        [
            pltpu.VMEM((wide_max, features), BF),
            pltpu.VMEM((line * rows, wide_max), F32),
            pltpu.VMEM((plan.pack, LANE), F32),
            pltpu.SemaphoreType.DMA((4,)),
        ],
        flops=2 * line * rows * features * wide_max,
        moved=4 << 20,
        limit=16,
    )(meta, *deltas, *quarter)[0]


def input_rows(plan, meta, packs, outer):
    features, length, line = plan.features, plan.length, plan.line

    def kernel(meta_ref, *refs):
        pack_refs = refs[:line]
        outer_ref, out_ref, stage, packed = refs[line:]

        def run(b):
            for m in range(line):
                packed[...] = pack_refs[m][...].astype(F32)
                unpack_taps(plan, b, packed, stage, (meta_ref[5] ^ m) * plan.line_taps[b])
            inner = get(stage, plan.factors[b] // 2, length)
            out_ref[...] = (inner + outer_ref[...]).astype(BF)

        both(meta_ref, lambda: run(0), lambda: run(1))

    return call(
        kernel,
        [SMEM] + vmem(line + 1),
        [((length, features), BF)],
        [split(plan.stage_rows, features), pltpu.VMEM((plan.pack, LANE), F32)],
        moved=3 << 20,
        limit=12,
    )(meta, *packs, outer)[0]


def down_weight(plan, meta, columns, even, odd, extra):
    shards, rows, features, line = plan.shards, plan.rows, plan.features, plan.line
    half = shards // 2
    base = up8(rows, 16)

    def kernel(meta_ref, *refs):
        col_refs = refs[:4]
        even_ref, odd_ref, grad_ref, sum_ref, small_ref, delta, ordered, small = refs[4:]
        me = meta_ref[1]
        for q in range(shards):
            source = (even_ref, odd_ref)[q // half]
            value = source[q % half, 0:base, :].astype(F32)
            at = me ^ plan.mask(q)
            ordered[pl.ds(at, 1), :] = jnp.sum(value, axis=0, keepdims=True)
            delta[q * rows : (q + 1) * rows, :] = value[:rows]
            high = source[q % half, base : base + extra, :].astype(F32)
            low = source[q % half, base + extra : base + 2 * extra, :].astype(F32)
            small[at] = high + low
        sum_ref[...] = jnp.sum(ordered[...], axis=0, keepdims=True)
        total = small[0]
        for i in range(1, shards):
            total = total + small[i]
        small_ref[...] = total
        for at, v in enumerate((0, 2, 1, 3)):
            steps = delta[at * line * rows : (at + 1) * line * rows, :].astype(BF)
            part = dot(col_refs[v][...], steps, ((0,), (0,)))
            total = part if at == 0 else total + part
        grad_ref[...] = total.astype(BF)

    return call(
        kernel,
        [SMEM] + vmem(6),
        [((plan.down_max, features), BF), ((1, features), F32), ((extra, features), F32)],
        [
            pltpu.VMEM((shards * rows, features), F32),
            pltpu.VMEM((shards, features), F32),
            pltpu.VMEM((shards, extra, features), F32),
        ],
        flops=2 * shards * rows * features * features,
        moved=4 << 20,
        limit=20,
    )(meta, *columns, even, odd)


ROOT_HALF = 0.7071067811865476
ROOT_TWO_PI = 0.3989422804014327


def head_rows(plan, meta, keep, recv, target, valid, merge, bias, gain, ff_in, ff_bias, ff_out):
    half_rows, features = keep.shape
    hidden = ff_in.shape[1]
    parts = hidden // features
    dims = (half_rows, features)

    def kernel(
        meta_ref, keep_ref, recv_ref, target_ref, valid_ref, merge_ref, bias_ref, gain_ref,
        in_bias_ref, in_hbm, out_hbm,
        out_ref, up_keep_ref, up_send_ref, normed_ref, act_ref, pre_delta_ref, ff_delta_ref,
        merged_delta_ref, vec_ref, loss_ref, slope_ref, in_ref, out_w_ref, sems,
    ):
        fetch_in = pltpu.make_async_copy(in_hbm, in_ref, sems.at[0])
        fetch_out = pltpu.make_async_copy(out_hbm, out_w_ref, sems.at[1])
        fetch_in.start()
        fetch_out.start()
        branch = meta_ref[0]
        merged = dot(keep_ref[...], merge_ref[branch]) + dot(recv_ref[...], merge_ref[1 - branch])
        merged = merged + bias_ref[0:1, :]
        unit, scale = norm_parts(merged)
        normed = (unit * gain_ref[0:1, :] + bias_ref[2:3, :]).astype(BF)
        normed_ref[...] = normed
        fetch_in.wait()
        fetch_out.wait()
        for c in range(parts):
            cols = slice(c * features, (c + 1) * features)
            pre = dot(normed, in_ref[:, cols]) + in_bias_ref[:, cols]
            share = 0.5 * (1.0 + lax.erf(pre * ROOT_HALF))
            slope_ref[:, cols] = share + pre * (jnp.exp(-0.5 * pre * pre) * ROOT_TWO_PI)
            act = (pre * share).astype(BF)
            act_ref[:, cols] = act
            part = dot(act, out_w_ref[cols, :])
            total = part if c == 0 else total + part
        unit_end, scale_end = norm_parts(merged + total + bias_ref[1:2, :])
        final = unit_end * gain_ref[1:2, :] + bias_ref[3:4, :]
        out_ref[...] = final.astype(BF)
        error = final - target_ref[...].astype(F32)
        weighted = valid_ref[...] * error
        loss = jnp.sum(jnp.sum(weighted * error, axis=0, keepdims=True), axis=1, keepdims=True)
        loss_ref[...] = jnp.broadcast_to(loss, loss_ref.shape)
        vec_ref[...] = jnp.zeros_like(vec_ref)
        vec_ref[3:4, :] = jnp.sum(weighted, axis=0, keepdims=True)
        vec_ref[5:6, :] = jnp.sum(weighted * unit_end, axis=0, keepdims=True)
        delta_sum = norm_back(weighted, unit_end, scale_end, gain_ref[1:2, :])
        delta_ff = delta_sum.astype(BF)
        ff_delta_ref[...] = delta_ff
        vec_ref[1:2, :] = jnp.sum(delta_ff.astype(F32), axis=0, keepdims=True)
        for c in range(parts):
            cols = slice(c * features, (c + 1) * features)
            pre_delta = dot(delta_ff, out_w_ref[cols, :], ((1,), (1,))) * slope_ref[:, cols]
            pre_delta = pre_delta.astype(BF)
            pre_delta_ref[:, cols] = pre_delta
            vec_ref[6 + c : 7 + c, :] = jnp.sum(pre_delta.astype(F32), axis=0, keepdims=True)
            part = dot(pre_delta, in_ref[:, cols], ((1,), (1,)))
            above = part if c == 0 else above + part
        vec_ref[2:3, :] = jnp.sum(above, axis=0, keepdims=True)
        vec_ref[4:5, :] = jnp.sum(above * unit, axis=0, keepdims=True)
        delta = norm_back(above, unit, scale, gain_ref[0:1, :]) + delta_sum
        delta = delta.astype(BF)
        merged_delta_ref[...] = delta
        vec_ref[0:1, :] = jnp.sum(delta.astype(F32), axis=0, keepdims=True)
        up_keep_ref[...] = dot(delta, merge_ref[branch], ((1,), (1,))).astype(BF)
        up_send_ref[...] = dot(delta, merge_ref[1 - branch], ((1,), (1,))).astype(BF)

    vec_rows = up8(6 + parts + 6)
    return call(
        kernel,
        [SMEM] + vmem(8) + [HBM] * 2,
        [
            (dims, BF), (dims, BF), (dims, BF), (dims, BF),
            ((half_rows, hidden), BF), ((half_rows, hidden), BF), (dims, BF), (dims, BF),
            ((vec_rows, features), F32), ((8, LANE), F32),
        ],
        [
            pltpu.VMEM((half_rows, hidden), F32),
            pltpu.VMEM((features, hidden), BF),
            pltpu.VMEM((hidden, features), BF),
            pltpu.SemaphoreType.DMA((2,)),
        ],
        flops=10 * half_rows * features * hidden,
        moved=14 << 20,
        limit=56,
    )(meta, keep, recv, target, valid, merge, bias, gain, ff_bias, ff_in, ff_out)


def head_weights(plan, meta, keep, recv, normed, act, pre_delta, ff_delta, merged_delta):
    shards = plan.shards
    half_rows, features = keep.shape
    hidden = act.shape[1]
    ff_rows, merge_rows = hidden // shards // 2, features // shards
    parts, half = hidden // features, shards // 2
    own = 2 * ff_rows + merge_rows

    def kernel(
        meta_ref, keep_ref, recv_ref, normed_ref, act_ref, pre_ref, ff_ref, merged_ref,
        stay_ref, send_ref, first, second, third,
    ):
        branch = meta_ref[0]
        for c in range(parts):
            cols = slice(c * features, (c + 1) * features)
            first[cols, :] = dot(pre_ref[:, cols], normed_ref[...], ((0,), (0,))).astype(BF)
            second[cols, :] = dot(act_ref[:, cols], ff_ref[...], ((0,), (0,))).astype(BF)
        for side, ref in enumerate((keep_ref, recv_ref)):
            part = dot(ref[...], merged_ref[...], ((0,), (0,))).astype(BF)
            start = pl.multiple_of((branch ^ side) * features, 16)
            third[pl.ds(start, features), :] = part
        for q in range(shards):
            device = meta_ref[1] ^ plan.mask(q)
            target = stay_ref if q < half else send_ref
            for h in range(2):
                at = 2 * device + (branch ^ h)
                for start, count, source in (
                    (0, ff_rows, first),
                    (ff_rows, ff_rows, second),
                    (2 * ff_rows, merge_rows, third),
                ):
                    rows = pl.ds(pl.multiple_of(at * count, 16), count)
                    target[h, q % half, start : start + count, :] = source[rows, :]

    return call(
        kernel,
        [SMEM] + vmem(7),
        [((2, half, own, features), BF), ((2, half, own, features), BF)],
        [
            pltpu.VMEM((hidden, features), BF),
            pltpu.VMEM((hidden, features), BF),
            pltpu.VMEM((2 * features, features), BF),
        ],
        flops=4 * half_rows * features * hidden,
        moved=12 << 20,
        limit=24,
    )(meta, keep, recv, normed, act, pre_delta, ff_delta, merged_delta)


def hop(values, distance, shards):
    return lax.ppermute(values, "series", [(i, i ^ distance) for i in range(shards)])


def swap(values):
    return lax.ppermute(values, "branch", [(0, 1), (1, 0)])


def after(value, *others):
    return lax.optimization_barrier((value, others))[0]


def along_line(plan, own):
    return [own] + [hop(own, i << 2, plan.shards) for i in range(1, plan.line)]


def line_parts(plan, first, rest):
    return [first] + [hop(rest[i - 1], i << 2, plan.shards) for i in range(1, plan.line)]


def quad_gather(plan, own, later):
    side = hop(own, 2, plan.shards)
    return [own, hop(own, 1, plan.shards), side, hop(after(side, later), 1, plan.shards)]


def settle(value, *others):
    return lax.optimization_barrier((value,) + others)


def gather_slots(plan, line):
    even = jnp.stack(line + [hop(value, 2, plan.shards) for value in line])
    return even, hop(even, 1, plan.shards)


def scatter_sum(plan, keep, send, *others):
    shards, line = plan.shards, plan.line
    first = keep + hop(send, 1, shards).astype(F32)
    second = first[:line] + hop(first[line:].astype(BF), 2, shards).astype(F32)
    if others:
        second, *others = settle(second, *others)
    pieces = line_parts(plan, second[0], [second[i].astype(BF) for i in range(1, line)])
    return (pieces, *others) if others else pieces


def rounded(values):
    return lax.reduce_precision(values, exponent_bits=8, mantissa_bits=7)


def layer_norm(values, gain_row, shift_row):
    center = values - jnp.mean(values, axis=-1, keepdims=True)
    spread = jnp.mean(center * center, axis=-1, keepdims=True)
    return center * lax.rsqrt(spread + EPSILON) * gain_row + shift_row


def gelu_exact(values):
    return jax.nn.gelu(values, approximate=False)


def product(a, b):
    return jnp.dot(a, b, preferred_element_type=F32)


def left_product(a, b):
    return jnp.einsum("mi,mo->io", a, b, preferred_element_type=F32)


def right_product(a, b):
    return jnp.einsum("mo,io->mi", a, b, preferred_element_type=F32)


def body(
    series_in, target, horizons, observed,
    down_short, iso_short, trans_short, down_long, iso_long, trans_long,
    branch_bias, branch_gain, merge_weight, head_bias, head_gain, ff_in, ff_in_bias, ff_out,
):
    shards = lax.axis_size("series")
    _, length, features = series_in.shape
    plan = Plan(
        shards,
        length,
        features,
        (down_short.shape[0], down_long.shape[0]),
        (iso_short.shape[0], iso_long.shape[0]),
    )
    line = plan.line
    half_rows = length // 2
    branch = lax.axis_index("branch")
    me = lax.axis_index("series")
    is_short = branch == 0
    iso_rows = jnp.where(is_short, plan.iso_rows[0], plan.iso_rows[1])
    meta = jnp.stack(
        [
            branch,
            me,
            (me * iso_rows) // features,
            (me * iso_rows) % features,
            jnp.where(is_short, plan.steps[0], plan.steps[1]),
            me // 4,
            me % 2,
            me % 4,
        ]
    ).astype(jnp.int32)
    series = series_in[0]
    biases, gain = branch_bias[0], branch_gain

    def chosen(short, long):
        rows = max(short.shape[0], long.shape[0])
        short = jnp.pad(short, ((0, rows - short.shape[0]), (0, 0)))
        long = jnp.pad(long, ((0, rows - long.shape[0]), (0, 0)))
        return jnp.where(is_short, short, long)

    blocks = prep_blocks(plan, meta, series)
    own_down = after(chosen(down_short, down_long), blocks)
    blocks = line_parts(plan, blocks[0], [blocks[i] for i in range(1, line)])
    down_quarter = quad_gather(plan, own_down, blocks)
    own_trans = after(chosen(trans_short, trans_long), blocks)
    keep, send, *columns = down_partial(plan, meta, blocks, down_quarter)
    pieces = line_parts(plan, keep, send)
    trans_quarter = quad_gather(plan, own_trans, pieces)
    low, act_down = low_rows(plan, meta, pieces, biases)
    low_own = gather_slots(plan, along_line(plan, low))
    low_own, trans_quarter = settle(low_own, trans_quarter)
    keep, send = iso_partial(plan, meta, low_own, iso_short, iso_long, False)
    low_other = swap(after(low_own[0], low_own[1]))
    pieces = scatter_sum(plan, keep, send)
    inner, act_iso = inner_rows(plan, meta, pieces, low, biases, gain)
    columns[2] = hop(after(columns[2], inner), 2, shards)
    inners, columns = settle(along_line(plan, inner), columns)
    packs = trans_forward(plan, meta, inners, trans_quarter)
    columns[3] = hop(after(columns[3], packs), 3, shards)
    packs = line_parts(plan, packs[0], [packs[i] for i in range(1, line)])
    packs, columns, low_other = settle(packs, columns, low_other)
    out_keep, out_send, act_trans = outer_rows(plan, meta, packs, series, biases, gain)
    out_recv = swap(out_send)
    columns[1] = hop(after(columns[1], out_keep), 1, shards)
    low_other = (low_other, hop(after(low_other, out_keep), 1, shards))
    out_recv, columns, low_other = settle(out_recv, columns, low_other)

    positions = branch * half_rows + jnp.arange(half_rows, dtype=jnp.int32)
    observed_half = lax.dynamic_slice_in_dim(observed[0], branch * half_rows, half_rows, 0)
    valid = (
        observed_half.astype(F32)
        * (positions >= SEQ_IN).astype(F32)
        * (positions < SEQ_IN + horizons[0]).astype(F32)
    )
    (
        out, up_keep, up_send, normed, act_ff, pre_delta, ff_delta, merged_delta, vec_head, loss_part
    ) = head_rows(
        plan, meta, out_keep, out_recv, target[0], valid[:, None], merge_weight, head_bias,
        head_gain, ff_in, ff_in_bias[None], ff_out,
    )
    up_recv = swap(up_send)
    shares, share_send = head_weights(
        plan, meta, out_keep, out_recv, normed, act_ff, pre_delta, ff_delta, merged_delta
    )

    outer, packs, vectors = outer_backward(plan, meta, up_keep, up_recv, series, act_trans, gain)
    share_recv = hop(after(share_send, packs), 1, shards)
    shares = shares.astype(F32) + share_recv.astype(F32)
    share_recv = hop(shares[:, line:].astype(BF), 2, shards)
    packs = line_parts(plan, packs[0], [packs[i] for i in range(1, line)])
    keep, send, wide = trans_backward(plan, meta, packs, trans_quarter)
    trans_keep, trans_send = trans_weight(plan, meta, inners, wide)
    pieces, trans_send, share_recv = settle(line_parts(plan, keep, send), trans_send, share_recv)
    shares = shares[:, :line] + share_recv.astype(F32)
    share_recv = swap(shares[1].astype(BF))
    shares = shares[0]
    delta_iso, delta_inner, vectors = inner_backward(
        plan, meta, pieces, low, act_iso, vectors, gain
    )
    ff_parts = ff_in_bias.shape[0] // features
    selector = jnp.stack([is_short, branch == 1]).astype(F32)
    branch_rows = (selector[:, None, None] * vectors[None, 0:3]).reshape(6, features)
    small = jnp.concatenate([vec_head[: 6 + ff_parts], branch_rows], axis=0)
    count = small.shape[0]
    small = jnp.pad(small, ((0, up8(count, 16) - count), (0, 0)))
    trans_recv = hop(trans_send, 1, shards)
    deltas, trans_recv = settle(along_line(plan, delta_iso), trans_recv)
    trans_sum = trans_keep + trans_recv.astype(F32)
    trans_next = trans_sum[1].astype(BF)
    delta_own = gather_slots(plan, deltas)
    delta_own, trans_next, share_recv = settle(delta_own, trans_next, share_recv)
    shares = shares + share_recv.astype(F32)
    spread = line // 2
    share_recv = hop(shares[spread:].astype(BF), 4 * spread, shards)
    keep, send = iso_partial(plan, meta, delta_own, iso_short, iso_long, True)
    delta_other = swap(delta_own[0])
    pieces, delta_other, share_recv = scatter_sum(plan, keep, send, delta_other, share_recv)
    delta_other = (delta_other, hop(delta_other, 1, shards))
    pieces, delta_other = settle(pieces, delta_other)
    shares = shares[:spread] + share_recv.astype(F32)
    payload = down_delta(plan, meta, pieces, delta_inner, act_down, small)
    first_grad = iso_weight(
        plan, meta, 0, after(low_own, payload), low_other, delta_own, delta_other
    )
    trans_recv = hop(after(trans_next, payload), 2, shards)
    share_recv = hop(after(shares[1:].astype(BF), payload), 4, shards)
    deltas, trans_recv, share_recv, first_grad = settle(
        along_line(plan, payload), trans_recv, share_recv, first_grad
    )
    shares = rounded(shares[0] + share_recv[0].astype(F32))
    grad_trans = (trans_sum[0] + trans_recv.astype(F32)).astype(BF)
    share_recv = swap(shares.astype(BF))
    packs = input_quarter(plan, meta, deltas, down_quarter)
    even = jnp.stack(deltas)
    odd = hop(after(even, packs), 2, shards)
    packs = line_parts(plan, packs[0], [packs[i] for i in range(1, line)])
    trans_recv = swap(grad_trans)
    packs, odd, share_recv, trans_recv = settle(packs, odd, share_recv, trans_recv)
    share_recv = share_recv.astype(F32)
    ff_rows = ff_in_bias.shape[0] // shards // 2
    halves = [
        jnp.where(is_short, shares, share_recv),
        jnp.where(is_short, share_recv, shares),
    ]
    merge_own = jnp.concatenate([half[2 * ff_rows :] for half in halves], axis=0)
    merge_all = lax.all_gather(merge_own.astype(BF), "series", axis=0)
    even = jnp.concatenate([even, odd], axis=0)
    delta_halves = (even, hop(even, 1, shards))
    input_own = input_rows(plan, meta, packs, outer)
    input_recv = swap(input_own)
    grad_down, down_sum, small = down_weight(
        plan, meta, columns, *after(delta_halves, input_own), small.shape[0]
    )
    down_recv = swap(grad_down)
    loss_row = jnp.broadcast_to(loss_part[0:1, 0:1], (1, features))
    mine = jnp.concatenate([small[:count], down_sum, loss_row], axis=0)
    theirs = swap(mine)
    second_grad = iso_weight(
        plan, meta, 1, after(low_own, grad_down), low_other, delta_own, delta_other
    )
    input_recv = after(input_recv, second_grad)
    iso_grads = [first_grad, second_grad]

    def placed(own, other, b, rows):
        return jnp.where(branch == b, own, other)[:rows].astype(F32)

    merge_total = merge_all.astype(F32).reshape(2, features, features)
    both_sums = mine + theirs
    loss = (0.5 / (features * length)) * both_sums[count + 1, 0:1]
    small = both_sums[:count]
    down_sum, down_other = mine[count : count + 1], theirs[count : count + 1]
    branch_total = small[6 + ff_parts :].reshape(2, 3, features)
    down_sums = jnp.stack(
        [jnp.where(is_short, down_sum, down_other), jnp.where(is_short, down_other, down_sum)]
    )
    iso_sums = jnp.stack([iso_grads[0][1], iso_grads[1][1]])
    bias_total = jnp.concatenate([down_sums, iso_sums, branch_total[:, 0:2]], axis=1)

    others = (
        iso_grads[0][0],
        placed(grad_trans, trans_recv, 0, plan.down_rows[0]),
        iso_grads[1][0],
        placed(grad_trans, trans_recv, 1, plan.down_rows[1]),
        merge_total,
        jnp.concatenate([half[:ff_rows] for half in halves], axis=0).T,
        jnp.concatenate([half[ff_rows : 2 * ff_rows] for half in halves], axis=0),
    )
    input_recv, others = settle(input_recv, others)
    short_iso, short_trans, long_iso, long_trans, merge_total, ff_in_total, ff_out_total = others
    return (
        out[None],
        loss,
        (input_own.astype(F32) + input_recv.astype(F32))[None],
        placed(grad_down, down_recv, 0, plan.down_rows[0]),
        short_iso,
        short_trans,
        placed(grad_down, down_recv, 1, plan.down_rows[1]),
        long_iso,
        long_trans,
        bias_total,
        branch_total[:, 2],
        merge_total,
        small[0:4],
        small[4:6],
        ff_in_total,
        small[6 : 6 + ff_parts].reshape(-1),
        ff_out_total,
    )


def fitted(matrix, row_total):
    return jnp.pad(matrix, ((0, row_total - matrix.shape[0]), (0, 0)))


def unpack(gathered_all, shards, rows_max, rows_own):
    features = gathered_all.shape[1]
    return gathered_all.reshape(shards, rows_max, features)[:, :rows_own].reshape(
        shards * rows_own, features
    )


def repack(gradient, shards, rows_max):
    rows_own = gradient.shape[0] // shards
    shaped = gradient.reshape(shards, rows_own, gradient.shape[1])
    return jnp.pad(shaped, ((0, 0), (0, rows_max - rows_own), (0, 0))).reshape(
        shards * rows_max, gradient.shape[1]
    )


def branch_pass(series_in, weights, shards, rows_max, biases, gain_row, factor):
    series_count, length, features = series_in.shape
    step_count = (length + factor) // factor
    margin = factor // 2
    weight_down = unpack(weights[0], shards, rows_max[0], factor * features // shards)
    weight_iso = unpack(weights[1], shards, rows_max[1], step_count * features // shards)
    weight_trans = unpack(weights[2], shards, rows_max[2], factor * features // shards).reshape(
        factor, features, features
    )
    blocks = jnp.pad(series_in, ((0, 0), (margin, step_count * factor - length - margin), (0, 0)))
    blocks = blocks.reshape(series_count * step_count, factor * features)
    act_down = jnp.tanh(product(blocks, weight_down) + biases[0])
    low_down = act_down.astype(jnp.bfloat16)
    padded = jnp.concatenate(
        [
            jnp.zeros((series_count, step_count - 1, features), jnp.bfloat16),
            low_down.reshape(series_count, step_count, features),
        ],
        axis=1,
    )
    unfolded = jnp.concatenate(
        [padded[:, offset : offset + step_count] for offset in range(step_count)], axis=2
    )
    unfolded = unfolded.reshape(series_count * step_count, step_count * features)
    act_iso = jnp.tanh(product(unfolded, weight_iso) + biases[1])
    inner_norm, inner_back = jax.vjp(
        layer_norm, act_iso + low_down.astype(jnp.float32), gain_row, biases[3]
    )
    low_inner = inner_norm.astype(jnp.bfloat16)
    spread_out = jnp.einsum(
        "mi,jio->mjo", low_inner, weight_trans, preferred_element_type=jnp.float32
    )
    act_trans = jnp.tanh(
        spread_out.reshape(series_count, step_count * factor, features)[:, :length] + biases[2]
    )
    result, outer_back = jax.vjp(
        layer_norm, act_trans + series_in.astype(jnp.float32), gain_row, biases[3]
    )
    stored = (
        blocks,
        weight_down,
        weight_iso,
        weight_trans,
        act_down,
        unfolded,
        act_iso,
        inner_back,
        low_inner,
        act_trans,
        outer_back,
    )
    return (result, stored)


def branch_back(series_in, weights, shards, rows_max, biases, gain_row, factor, upstream):
    series_count, length, features = series_in.shape
    step_count = (length + factor) // factor
    margin = factor // 2
    result, stored = branch_pass(series_in, weights, shards, rows_max, biases, gain_row, factor)
    (
        blocks,
        weight_down,
        weight_iso,
        weight_trans,
        act_down,
        unfolded,
        act_iso,
        inner_back,
        low_inner,
        act_trans,
        outer_back,
    ) = stored
    delta_outer, gain_outer, shift_outer = outer_back(upstream)
    delta_trans = (delta_outer * (1.0 - act_trans * act_trans)).astype(jnp.bfloat16)
    trans_blocks = jnp.pad(delta_trans, ((0, 0), (0, step_count * factor - length), (0, 0)))
    trans_blocks = trans_blocks.reshape(series_count * step_count, factor, features)
    grad_trans = jnp.einsum(
        "mi,mjo->jio", low_inner, trans_blocks, preferred_element_type=jnp.float32
    )
    grad_trans = grad_trans.reshape(factor * features, features)
    inner_upstream = jnp.einsum(
        "mjo,jio->mi", trans_blocks, weight_trans, preferred_element_type=jnp.float32
    )
    delta_inner, gain_inner, shift_inner = inner_back(inner_upstream)
    delta_iso = (delta_inner * (1.0 - act_iso * act_iso)).astype(jnp.bfloat16)
    grad_iso = left_product(unfolded, delta_iso)
    delta_unfold = right_product(delta_iso, weight_iso).reshape(
        series_count, step_count, step_count, features
    )
    delta_padded = jnp.zeros((series_count, 2 * step_count - 1, features), jnp.float32)
    for offset in range(step_count):
        delta_padded = delta_padded.at[:, offset : offset + step_count].add(
            delta_unfold[:, :, offset]
        )
    delta_low = (
        delta_padded[:, step_count - 1 :].reshape(series_count * step_count, features) + delta_inner
    )
    delta_down = (delta_low * (1.0 - act_down * act_down)).astype(jnp.bfloat16)
    grad_down = left_product(blocks, delta_down)
    delta_blocks = right_product(delta_down, weight_down).reshape(
        series_count, step_count * factor, features
    )
    delta_series = delta_blocks[:, margin : margin + length] + delta_outer
    vectors = jnp.stack(
        [
            jnp.sum(delta_down.astype(jnp.float32), axis=0),
            jnp.sum(delta_iso.astype(jnp.float32), axis=0),
            jnp.sum(delta_trans.astype(jnp.float32), axis=(0, 1)),
            shift_inner + shift_outer,
        ]
    )
    padded_grads = (
        repack(grad_down, shards, rows_max[0]),
        repack(grad_iso, shards, rows_max[1]),
        repack(grad_trans, shards, rows_max[2]),
    )
    return (delta_series, padded_grads, vectors, gain_inner + gain_outer)


def plain_body(
    series_in,
    target,
    horizons,
    observed,
    down_short,
    iso_short,
    trans_short,
    down_long,
    iso_long,
    trans_long,
    branch_bias,
    branch_gain,
    merge_weight,
    head_bias,
    head_gain,
    ff_in,
    ff_in_bias,
    ff_out,
):
    branch_index = lax.axis_index("branch")
    shards = lax.axis_size("series")
    series_count, length, features = series_in.shape
    rows_max = (
        max(down_short.shape[0], down_long.shape[0]),
        max(iso_short.shape[0], iso_long.shape[0]),
        max(trans_short.shape[0], trans_long.shape[0]),
    )
    is_short = branch_index == 0
    own_down = jnp.where(is_short, fitted(down_short, rows_max[0]), fitted(down_long, rows_max[0]))
    own_iso = jnp.where(is_short, fitted(iso_short, rows_max[1]), fitted(iso_long, rows_max[1]))
    own_trans = jnp.where(
        is_short, fitted(trans_short, rows_max[2]), fitted(trans_long, rows_max[2])
    )
    gathered = (
        lax.all_gather(own_down, "series", axis=0, tiled=True),
        lax.all_gather(own_iso, "series", axis=0, tiled=True),
        lax.all_gather(own_trans, "series", axis=0, tiled=True),
    )
    biases = branch_bias[0]
    gain_row = branch_gain[0]

    def forward_with(factor):
        return lambda: branch_pass(series_in, gathered, shards, rows_max, biases, gain_row, factor)[
            0
        ].astype(jnp.bfloat16)

    branch_out = lax.cond(is_short, forward_with(SCALE_S), forward_with(SCALE_L))
    received = lax.all_to_all(
        branch_out.reshape(series_count, length, 1, features),
        "branch",
        split_axis=1,
        concat_axis=2,
        tiled=True,
    )
    half_rows = received.shape[1]
    merge_rows = received.reshape(series_count * half_rows, 2 * features)
    merge_flat = merge_weight.reshape(2 * features, features)
    merged = product(merge_rows, merge_flat) + head_bias[0]
    normed, first_back = jax.vjp(layer_norm, merged, head_gain[0], head_bias[2])
    low_normed = normed.astype(jnp.bfloat16)
    pre_ff = product(low_normed, ff_in) + ff_in_bias
    activated, gelu_back = jax.vjp(gelu_exact, pre_ff)
    low_act = activated.astype(jnp.bfloat16)
    ff_result = product(low_act, ff_out) + head_bias[1]
    final_out, second_back = jax.vjp(layer_norm, merged + ff_result, head_gain[1], head_bias[3])
    final_rows = final_out.reshape(series_count, half_rows, features)
    positions = branch_index * half_rows + jnp.arange(half_rows, dtype=jnp.int32)
    observed_half = lax.dynamic_slice_in_dim(observed, branch_index * half_rows, half_rows, 1)
    valid_mask = (
        observed_half.astype(jnp.float32)
        * (positions >= SEQ_IN).astype(jnp.float32)
        * (positions < SEQ_IN + horizons[:, None]).astype(jnp.float32)
    )
    error_rows = final_rows - target.astype(jnp.float32)
    weighted = valid_mask[:, :, None] * error_rows
    series_part = 0.5 * jnp.sum(weighted * error_rows, axis=(1, 2)) / (features * length)
    delta_sum, gain_second, shift_second = second_back(
        weighted.reshape(series_count * half_rows, features)
    )
    delta_ff = delta_sum.astype(jnp.bfloat16)
    grad_ff_out = left_product(low_act, delta_ff)
    delta_act = right_product(delta_ff, ff_out)
    (delta_pre,) = gelu_back(delta_act)
    low_pre = delta_pre.astype(jnp.bfloat16)
    grad_ff_in = left_product(low_normed, low_pre)
    delta_normed = right_product(low_pre, ff_in)
    delta_first, gain_first, shift_first = first_back(delta_normed)
    delta_merged = (delta_first + delta_sum).astype(jnp.bfloat16)
    grad_merge = left_product(merge_rows, delta_merged).reshape(2, features, features)
    delta_rows = (
        right_product(delta_merged, merge_flat)
        .astype(jnp.bfloat16)
        .reshape(series_count, half_rows, 2, features)
    )
    back_rows = lax.all_to_all(delta_rows, "branch", split_axis=2, concat_axis=1, tiled=True)
    upstream = back_rows.astype(jnp.float32).reshape(series_count, length, features)
    ff_shares = (
        lax.psum_scatter(grad_ff_in, "series", scatter_dimension=1, tiled=True),
        lax.psum_scatter(grad_ff_out, "series", scatter_dimension=0, tiled=True),
    )
    weights_back = (
        lax.all_gather(own_down, "series", axis=0, tiled=True),
        lax.all_gather(own_iso, "series", axis=0, tiled=True),
        lax.all_gather(own_trans, "series", axis=0, tiled=True),
    )

    def backward_with(factor):
        return lambda: branch_back(
            series_in, weights_back, shards, rows_max, biases, gain_row, factor, upstream
        )

    delta_series, padded_grads, vectors, gain_grad = lax.cond(
        is_short, backward_with(SCALE_S), backward_with(SCALE_L)
    )
    reduced = (
        lax.psum_scatter(padded_grads[0], "series", scatter_dimension=0, tiled=True),
        lax.psum_scatter(padded_grads[1], "series", scatter_dimension=0, tiled=True),
        lax.psum_scatter(padded_grads[2], "series", scatter_dimension=0, tiled=True),
    )
    short_flag = is_short.astype(jnp.float32)
    long_flag = 1.0 - short_flag
    summed = (
        lax.psum(delta_series.astype(jnp.bfloat16), "branch").astype(jnp.float32),
        lax.psum(series_part.astype(jnp.bfloat16), "branch").astype(jnp.float32),
        lax.psum(
            (short_flag * reduced[0][: down_short.shape[0]]).astype(jnp.bfloat16), "branch"
        ).astype(jnp.float32),
        lax.psum((short_flag * reduced[1]).astype(jnp.bfloat16), "branch").astype(jnp.float32),
        lax.psum(
            (short_flag * reduced[2][: trans_short.shape[0]]).astype(jnp.bfloat16), "branch"
        ).astype(jnp.float32),
        lax.psum((long_flag * reduced[0]).astype(jnp.bfloat16), "branch").astype(jnp.float32),
        lax.psum(
            (long_flag * reduced[1][: iso_long.shape[0]]).astype(jnp.bfloat16), "branch"
        ).astype(jnp.float32),
        lax.psum((long_flag * reduced[2]).astype(jnp.bfloat16), "branch").astype(jnp.float32),
        lax.psum(ff_shares[0].astype(jnp.bfloat16), "branch").astype(jnp.float32),
        lax.psum(ff_shares[1].astype(jnp.bfloat16), "branch").astype(jnp.float32),
    )
    selector = (jnp.arange(2, dtype=jnp.int32) == branch_index).astype(jnp.float32)
    full_bias = selector[:, None, None] * vectors[None]
    full_gain = selector[:, None] * gain_grad[None]
    head_vectors = jnp.stack(
        [
            jnp.sum(delta_merged.astype(jnp.float32), axis=0),
            jnp.sum(delta_ff.astype(jnp.float32), axis=0),
            shift_first,
            shift_second,
        ]
    )
    head_gains = jnp.stack([gain_first, gain_second])
    ff_bias_grad = jnp.sum(low_pre.astype(jnp.float32), axis=0)
    totals = lax.psum(
        (grad_merge, head_vectors, head_gains, ff_bias_grad, full_bias, full_gain),
        ("branch", "series"),
    )
    return (
        final_rows.astype(jnp.bfloat16),
        summed[1],
        summed[0],
        summed[2],
        summed[3],
        summed[4],
        summed[5],
        summed[6],
        summed[7],
        totals[4],
        totals[5],
        totals[0],
        totals[1],
        totals[2],
        summed[8],
        totals[3],
        summed[9],
    )


def solution(mesh):
    placed = (
        P("series", None, None),
        P("series", "branch", None),
        P("series"),
        P("series", None),
        P("series", None),
        P("series", None),
        P("series", None),
        P("series", None),
        P("series", None),
        P("series", None),
        P("branch", None, None),
        P("branch", None),
        P(),
        P(),
        P(),
        P(),
        P(),
        P(),
    )

    def run(*args):
        shards = mesh.shape["series"]
        features = args[0].shape[2]
        down_rows = [args[i].shape[0] // shards for i in (4, 7)]
        iso_rows = [args[i].shape[0] // shards for i in (5, 8)]
        fits = (
            args[0].shape[0] == shards
            and shards == 16
            and shards & (shards - 1) == 0
            and all(r % LANE == 0 and r <= features and 4 * r % features == 0 for r in down_rows)
            and all(r % 16 == 0 for r in iso_rows)
        )
        return jax.shard_map(
            body if fits else plain_body,
            mesh=mesh,
            in_specs=placed,
            out_specs=(
                P("series", "branch", None),
                P("series"),
                P("series", None, None),
                P("series", None),
                P("series", None),
                P("series", None),
                P("series", None),
                P("series", None),
                P("series", None),
                P(),
                P(),
                P(),
                P(),
                P(),
                P(None, "series"),
                P(),
                P("series", None),
            ),
            check_vma=False,
        )(*args)

    return run
```

```python
import functools

import jax
import jax.numpy as jnp
from jax import lax
from jax.experimental import pallas as pl
from jax.experimental.pallas import tpu as pltpu
from jax.sharding import PartitionSpec as P

SCALE_S = 12
SCALE_L = 16
SEQ_IN = 96
EPSILON = 1e-05
LANE = 128

BF = jnp.bfloat16
F32 = jnp.float32


def up8(count, base=8):
    return -(-count // base) * base


class Plan:
    def __init__(self, shards, length, features, down_rows, iso_rows):
        self.shards, self.length, self.features = shards, length, features
        self.factors = (SCALE_S, SCALE_L)
        self.steps = tuple((length + k) // k for k in self.factors)
        self.rows = up8(max(self.steps))
        self.down_rows = down_rows
        self.iso_rows = iso_rows
        self.down_max, self.iso_max = max(down_rows), max(iso_rows)
        self.line = shards // 4
        self.line_taps = tuple(4 * r // features for r in down_rows)
        blocks = features // LANE
        self.pack = up8(max(t * blocks * n for t, n in zip(self.line_taps, self.steps)), 16)
        self.taps = tuple(
            max(-(-((d * r) % features + r) // features) for d in range(shards)) for r in iso_rows
        )
        self.taps_max = max(self.taps)
        self.stage_rows = max(k * up8(n) for k, n in zip(self.factors, self.steps))

    def mask(self, slot):
        core, rest = divmod(slot, 2 * self.line)
        side, line = divmod(rest, self.line)
        return core | (side << 1) | (line << 2)


def vmem(count):
    return [pl.BlockSpec(memory_space=pltpu.VMEM) for _ in range(count)]


SMEM = pl.BlockSpec(memory_space=pltpu.SMEM)
ANY = pl.BlockSpec(memory_space=pl.ANY)
HBM = pl.BlockSpec(memory_space=pltpu.HBM)


def call(body, in_specs, outs, scratch, flops=0, moved=0, limit=56):
    return pl.pallas_call(
        body,
        out_shape=[jax.ShapeDtypeStruct(s, d) for s, d in outs],
        in_specs=in_specs,
        out_specs=vmem(len(outs)),
        scratch_shapes=scratch,
        compiler_params=pltpu.CompilerParams(vmem_limit_bytes=limit << 20),
        cost_estimate=pl.CostEstimate(flops=flops, bytes_accessed=moved, transcendentals=0),
    )


def dot(a, b, dims=((1,), (0,))):
    return lax.dot_general(a, b, (dims, ((), ())), preferred_element_type=F32)


def norm_parts(values):
    center = values - jnp.mean(values, axis=-1, keepdims=True)
    spread = jnp.mean(center * center, axis=-1, keepdims=True)
    scale = lax.rsqrt(spread + EPSILON)
    return center * scale, scale


def norm_back(upstream, unit, scale, gain):
    inner = upstream * gain
    first = jnp.mean(inner, axis=-1, keepdims=True)
    second = jnp.mean(inner * unit, axis=-1, keepdims=True)
    return scale * (inner - first - unit * second)


def keep_rows(values, count):
    index = lax.broadcasted_iota(jnp.int32, values.shape, 0)
    return jnp.where(index < count, values, 0.0)


def both(meta, short, long):
    pl.when(meta[0] == 0)(short)
    pl.when(meta[0] == 1)(long)


def split(rows, features):
    return pltpu.VMEM((features // LANE, rows, LANE), F32)


def put(ref, start, values, stride=1):
    count = values.shape[0]
    where = pl.ds(start, count) if stride == 1 else pl.ds(start, count, stride=stride)
    for c in range(ref.shape[0]):
        ref[c, where, :] = values[:, c * LANE : (c + 1) * LANE]


def get(ref, start, count, stride=1):
    where = pl.ds(start, count) if stride == 1 else pl.ds(start, count, stride=stride)
    return jnp.concatenate([ref[c, where, :] for c in range(ref.shape[0])], axis=1)


def split(rows, features):
    return pltpu.VMEM((features // LANE, rows, LANE), F32)


def put(ref, start, values, stride=1):
    count = values.shape[0]
    where = pl.ds(start, count) if stride == 1 else pl.ds(start, count, stride=stride)
    for c in range(ref.shape[0]):
        ref[c, where, :] = values[:, c * LANE : (c + 1) * LANE]


def get(ref, start, count, stride=1):
    where = pl.ds(start, count) if stride == 1 else pl.ds(start, count, stride=stride)
    return jnp.concatenate([ref[c, where, :] for c in range(ref.shape[0])], axis=1)


def pack_taps(plan, b, stage, first, packed):
    k, n = plan.factors[b], plan.steps[b]
    blocks = plan.features // LANE
    for i in range(plan.line_taps[b]):
        for c in range(blocks):
            at = (i * blocks + c) * n
            packed[at : at + n, :] = stage[c, pl.ds(first + i, n, stride=k), :]


def unpack_taps(plan, b, packed, stage, first):
    k, n = plan.factors[b], plan.steps[b]
    blocks = plan.features // LANE
    for i in range(plan.line_taps[b]):
        for c in range(blocks):
            at = (i * blocks + c) * n
            stage[c, pl.ds(first + i, n, stride=k), :] = packed[at : at + n, :]


def packed_matrix(plan, b, packed, base, matrix):
    n = plan.steps[b]
    for g in range(plan.line_taps[b] * plan.features // LANE):
        matrix[base : base + n, g * LANE : (g + 1) * LANE] = packed[g * n : (g + 1) * n, :]


def matrix_packed(plan, b, matrix, base, packed):
    n = plan.steps[b]
    for g in range(plan.line_taps[b] * plan.features // LANE):
        packed[g * n : (g + 1) * n, :] = matrix[base : base + n, g * LANE : (g + 1) * LANE]


def fetch_quarter(plan, b, meta_ref, sources, target, sems):
    own = plan.down_rows[b]
    quad = meta_ref[7]
    copies = []
    for v, source in enumerate(sources):
        start = pl.multiple_of((quad ^ v) * own, LANE)
        copies.append(
            pltpu.make_async_copy(
                source.at[pl.ds(0, own)], target.at[pl.ds(start, own)], sems.at[v]
            )
        )
    for copy in copies:
        copy.start()
    return copies


def total_of(parts):
    total = parts[0][...].astype(F32)
    for piece in parts[1:]:
        total = total + piece[...].astype(F32)
    return total


def prep_blocks(plan, meta, series):
    length, features, line = plan.length, plan.features, plan.line

    def kernel(meta_ref, x_ref, out_ref, wide, packed):
        def run(b):
            margin = plan.factors[b] // 2
            wide[...] = jnp.zeros_like(wide)
            put(wide, margin, x_ref[...].astype(F32))
            packed[...] = jnp.zeros_like(packed)
            for z in range(line):
                pack_taps(plan, b, wide, z * plan.line_taps[b], packed)
                out_ref[z ^ meta_ref[5]] = packed[...].astype(BF)

        both(meta_ref, lambda: run(0), lambda: run(1))

    return call(
        kernel,
        [SMEM] + vmem(1),
        [((line, plan.pack, LANE), BF)],
        [split(plan.stage_rows, features), pltpu.VMEM((plan.pack, LANE), F32)],
        moved=2 * length * features * 2,
        limit=8,
    )(meta, series)[0]


def down_partial(plan, meta, blocks, quarter):
    rows, features, line = plan.rows, plan.features, plan.line
    wide_max = 4 * plan.down_max

    def kernel(meta_ref, *refs):
        packs, weights = refs[:line], refs[line : line + 4]
        keep_ref, send_ref, *col_refs = refs[line + 4 : line + 10]
        weight, wide, packed, cols, sems = refs[line + 10 :]

        def run(b):
            copies = fetch_quarter(plan, b, meta_ref, weights, weight, sems)
            own = plan.down_rows[b]
            wide[...] = jnp.zeros_like(wide)
            for m in range(line):
                packed[...] = packs[m][...].astype(F32)
                packed_matrix(plan, b, packed, m * rows, wide)
            matrix = wide[...].astype(BF)
            for u in range(4):
                piece = matrix[:, u * own : (u + 1) * own]
                if own < plan.down_max:
                    pad = jnp.zeros((line * rows, plan.down_max - own), BF)
                    piece = jnp.concatenate([piece, pad], axis=1)
                cols[u ^ meta_ref[7]] = piece
            for v in range(4):
                col_refs[v][...] = cols[v]
            for copy in copies:
                copy.wait()
            part = dot(matrix[:, : 4 * own], weight[0 : 4 * own, :])
            keep_ref[...] = part[:rows]
            for m in range(1, line):
                send_ref[m - 1] = part[m * rows : (m + 1) * rows].astype(BF)

        both(meta_ref, lambda: run(0), lambda: run(1))

    return call(
        kernel,
        [SMEM] + vmem(line) + [ANY] * 4,
        [
            ((rows, features), F32),
            ((line - 1, rows, features), BF),
        ]
        + [((line * rows, plan.down_max), BF)] * 4,
        [
            pltpu.VMEM((wide_max, features), BF),
            pltpu.VMEM((line * rows, wide_max), F32),
            pltpu.VMEM((plan.pack, LANE), F32),
            pltpu.VMEM((4, line * rows, plan.down_max), BF),
            pltpu.SemaphoreType.DMA((4,)),
        ],
        flops=2 * line * rows * features * wide_max,
        moved=5 << 20,
        limit=16,
    )(meta, *blocks, *quarter)


def low_rows(plan, meta, pieces, biases):
    rows, features = plan.rows, plan.features

    def kernel(meta_ref, *refs):
        parts, bias_ref, low_ref, act_ref = refs[:-3], refs[-3], refs[-2], refs[-1]
        act = keep_rows(jnp.tanh(total_of(parts) + bias_ref[0:1, :]), meta_ref[4])
        act_ref[...] = act
        low_ref[...] = act.astype(BF)

    return call(
        kernel,
        [SMEM] + vmem(len(pieces) + 1),
        [((rows, features), BF), ((rows, features), F32)],
        [],
        moved=1 << 19,
        limit=4,
    )(meta, *pieces, biases)


def time_major(plan, halves, stage, target, lead):
    shards, rows = plan.shards, plan.rows
    half = shards // 2
    for q in range(shards):
        put(stage, q, halves[q // half][q % half].astype(F32), shards)
    body = shards * rows
    if lead:
        target[0 : lead * shards, :] = jnp.zeros((lead * shards, target.shape[1]), BF)
    target[lead * shards : lead * shards + body, :] = get(stage, 0, body).astype(BF)
    rest = target.shape[0] - lead * shards - body
    if rest:
        target[lead * shards + body :, :] = jnp.zeros((rest, target.shape[1]), BF)


def pad_weight(plan, b, meta_ref, source, target, sem):
    target[...] = jnp.zeros_like(target)
    shift = pl.multiple_of(meta_ref[3], 16)
    copy = pltpu.make_async_copy(source, target.at[pl.ds(shift, plan.iso_rows[b])], sem)
    copy.start()
    return copy


def iso_partial(plan, meta, halves, w_short, w_long, backward):
    shards, rows, features = plan.shards, plan.rows, plan.features
    half = shards // 2
    extra = plan.taps_max + 2
    buffer = (max(plan.steps) + rows + extra) * shards

    def kernel(
        meta_ref, even_ref, odd_ref, ws_ref, wl_ref, keep_ref, send_ref, stage, lined, padded, sem
    ):
        first = meta_ref[2]

        def run(b, w_ref):
            n, taps = plan.steps[b], plan.taps[b]
            copy = pad_weight(plan, b, meta_ref, w_ref, padded, sem)
            lead = extra if backward else n - 1
            time_major(plan, (even_ref, odd_ref), stage, lined, lead)
            copy.wait()
            for m in range(taps):
                start = extra + n - 1 - first - m if backward else first + m
                start = pl.multiple_of(start * shards, 16)
                window = lined[pl.ds(start, rows * shards), :]
                weight = padded[m * features : (m + 1) * features, :]
                part = dot(window, weight, ((1,), (1,)) if backward else ((1,), (0,)))
                total = part if m == 0 else total + part
            put(stage, 0, total)
            for q in range(shards):
                piece = get(stage, q, rows, shards)
                if q < half:
                    keep_ref[q] = piece
                else:
                    send_ref[q - half] = piece.astype(BF)

        both(meta_ref, lambda: run(0, ws_ref), lambda: run(1, wl_ref))

    return call(
        kernel,
        [SMEM] + vmem(2) + [HBM] * 2,
        [((half, rows, features), F32), ((half, rows, features), BF)],
        [
            split(rows * shards, features),
            pltpu.VMEM((buffer, features), BF),
            pltpu.VMEM((plan.taps_max * features, features), BF),
            pltpu.SemaphoreType.DMA,
        ],
        flops=2 * shards * rows * features * features * plan.taps_max,
        moved=10 << 20,
        limit=56,
    )(meta, *halves, w_short, w_long)


def iso_weight(plan, meta, b, low_own, low_other, delta_own, delta_other):
    shards, rows, features = plan.shards, plan.rows, plan.features
    half = shards // 2
    n, taps, own = plan.steps[b], plan.taps[b], plan.iso_rows[b]
    buffer = (n - 1 + rows + taps + 1) * shards

    def kernel(meta_ref, *refs):
        lows, deltas = refs[0:4], refs[4:8]
        grad_ref, sum_ref, stage, lined, delta, total, ordered = refs[8:]
        me = meta_ref[1]

        def load(low, steps):
            for q in range(shards):
                ordered[pl.ds(me ^ plan.mask(q), 1), :] = jnp.sum(
                    steps[q // half][q % half].astype(F32), axis=0, keepdims=True
                )
            time_major(plan, steps, stage, delta, 0)
            time_major(plan, low, stage, lined, n - 1)

        pl.when(meta_ref[0] == b)(lambda: load(lows[0:2], deltas[0:2]))
        pl.when(meta_ref[0] != b)(lambda: load(lows[2:4], deltas[2:4]))
        sum_ref[...] = jnp.sum(ordered[...], axis=0, keepdims=True)
        flat = me * own
        first = flat // features
        for m in range(taps):
            start = pl.multiple_of((first + m) * shards, 16)
            window = lined[pl.ds(start, rows * shards), :]
            total[m * features : (m + 1) * features, :] = dot(window, delta[...], ((0,), (0,)))
        shift = pl.multiple_of(flat % features, 16)
        grad_ref[...] = total[pl.ds(shift, own), :]

    return call(
        kernel,
        [SMEM] + vmem(8),
        [((own, features), F32), ((1, features), F32)],
        [
            split(rows * shards, features),
            pltpu.VMEM((buffer, features), BF),
            pltpu.VMEM((rows * shards, features), BF),
            pltpu.VMEM((taps * features, features), F32),
            pltpu.VMEM((shards, features), F32),
        ],
        flops=2 * shards * rows * features * features * taps,
        moved=10 << 20,
        limit=32,
    )(meta, *low_own, *low_other, *delta_own, *delta_other)


def inner_rows(plan, meta, pieces, low, biases, gain):
    rows, features = plan.rows, plan.features

    def kernel(meta_ref, *refs):
        parts = refs[:-5]
        low_ref, bias_ref, gain_ref, inner_ref, act_ref = refs[-5:]
        act = jnp.tanh(total_of(parts) + bias_ref[1:2, :])
        act_ref[...] = act
        unit, _ = norm_parts(act + low_ref[...].astype(F32))
        inner = unit * gain_ref[...] + bias_ref[3:4, :]
        inner_ref[...] = keep_rows(inner, meta_ref[4]).astype(BF)

    return call(
        kernel,
        [SMEM] + vmem(len(pieces) + 3),
        [((rows, features), BF), ((rows, features), F32)],
        [],
        moved=1 << 19,
        limit=4,
    )(meta, *pieces, low, biases, gain)


def trans_forward(plan, meta, inners, quarter):
    rows, features, line = plan.rows, plan.features, plan.line
    wide_max = 4 * plan.down_max

    def kernel(meta_ref, *refs):
        inner_refs, weights = refs[:line], refs[line : line + 4]
        out_ref, weight, wide, packed, sems = refs[line + 4 :]

        def run(b):
            copies = fetch_quarter(plan, b, meta_ref, weights, weight, sems)
            lhs = jnp.concatenate([ref[...] for ref in inner_refs], axis=0)
            for copy in copies:
                copy.wait()
            for i in range(plan.line_taps[b]):
                wide[:, i * features : (i + 1) * features] = dot(
                    lhs, weight[i * features : (i + 1) * features, :]
                )
            packed[...] = jnp.zeros_like(packed)
            for m in range(line):
                matrix_packed(plan, b, wide, m * rows, packed)
                out_ref[m] = packed[...].astype(BF)

        both(meta_ref, lambda: run(0), lambda: run(1))

    return call(
        kernel,
        [SMEM] + vmem(line) + [ANY] * 4,
        [((line, plan.pack, LANE), BF)],
        [
            pltpu.VMEM((wide_max, features), BF),
            pltpu.VMEM((line * rows, wide_max), F32),
            pltpu.VMEM((plan.pack, LANE), F32),
            pltpu.SemaphoreType.DMA((4,)),
        ],
        flops=2 * line * rows * features * wide_max,
        moved=4 << 20,
        limit=16,
    )(meta, *inners, *quarter)[0]


def outer_rows(plan, meta, packs, series, biases, gain):
    features, length, line = plan.features, plan.length, plan.line
    half_rows = length // 2

    def kernel(meta_ref, *refs):
        pack_refs = refs[:line]
        x_ref, bias_ref, gain_ref, keep_ref, send_ref, act_ref, stage, packed = refs[line:]

        def run(b):
            for m in range(line):
                packed[...] = pack_refs[m][...].astype(F32)
                unpack_taps(plan, b, packed, stage, (meta_ref[5] ^ m) * plan.line_taps[b])

        both(meta_ref, lambda: run(0), lambda: run(1))
        act = jnp.tanh(get(stage, 0, length) + bias_ref[2:3, :])
        act_ref[...] = act
        unit, _ = norm_parts(act + x_ref[...].astype(F32))
        put(stage, 0, unit * gain_ref[...] + bias_ref[3:4, :])
        mine = pl.multiple_of(meta_ref[0] * half_rows, 8)
        other = pl.multiple_of((1 - meta_ref[0]) * half_rows, 8)
        keep_ref[...] = get(stage, mine, half_rows).astype(BF)
        send_ref[...] = get(stage, other, half_rows).astype(BF)

    return call(
        kernel,
        [SMEM] + vmem(line + 3),
        [((half_rows, features), BF), ((half_rows, features), BF), ((length, features), F32)],
        [split(plan.stage_rows, features), pltpu.VMEM((plan.pack, LANE), F32)],
        moved=6 << 20,
        limit=16,
    )(meta, *packs, series, biases, gain)


def outer_backward(plan, meta, up_keep, up_recv, series, act, gain):
    features, length, line = plan.features, plan.length, plan.line
    half_rows = length // 2

    def kernel(
        meta_ref, uk_ref, ur_ref, x_ref, act_ref, gain_ref,
        outer_ref, taps_ref, vec_ref, stage, upstream, packed,
    ):
        mine = pl.multiple_of(meta_ref[0] * half_rows, 8)
        other = pl.multiple_of((1 - meta_ref[0]) * half_rows, 8)
        upstream[pl.ds(mine, half_rows), :] = uk_ref[...].astype(F32)
        upstream[pl.ds(other, half_rows), :] = ur_ref[...].astype(F32)
        act_value = act_ref[...]
        unit, scale = norm_parts(act_value + x_ref[...].astype(F32))
        above = upstream[...]
        vec_ref[...] = jnp.zeros_like(vec_ref)
        vec_ref[1:2, :] = jnp.sum(above, axis=0, keepdims=True)
        vec_ref[2:3, :] = jnp.sum(above * unit, axis=0, keepdims=True)
        outer = norm_back(above, unit, scale, gain_ref[...])
        outer_ref[...] = outer
        delta = (outer * (1.0 - act_value * act_value)).astype(BF).astype(F32)
        vec_ref[0:1, :] = jnp.sum(delta, axis=0, keepdims=True)
        put(stage, 0, delta)
        put(stage, length, jnp.zeros((plan.stage_rows - length, features), F32))
        packed[...] = jnp.zeros_like(packed)

        def run(b):
            for m in range(line):
                pack_taps(plan, b, stage, (meta_ref[5] ^ m) * plan.line_taps[b], packed)
                taps_ref[m] = packed[...].astype(BF)

        both(meta_ref, lambda: run(0), lambda: run(1))

    return call(
        kernel,
        [SMEM] + vmem(5),
        [((length, features), F32), ((line, plan.pack, LANE), BF), ((8, features), F32)],
        [
            split(plan.stage_rows, features),
            pltpu.VMEM((length, features), F32),
            pltpu.VMEM((plan.pack, LANE), F32),
        ],
        moved=8 << 20,
        limit=20,
    )(meta, up_keep, up_recv, series, act, gain)


def trans_backward(plan, meta, packs, quarter):
    rows, features, line = plan.rows, plan.features, plan.line
    wide_max = 4 * plan.down_max

    def kernel(meta_ref, *refs):
        pack_refs, weights = refs[:line], refs[line : line + 4]
        keep_ref, send_ref, wide_ref, weight, wide, packed, sems = refs[line + 4 :]

        def run(b):
            copies = fetch_quarter(plan, b, meta_ref, weights, weight, sems)
            wide[...] = jnp.zeros_like(wide)
            for m in range(line):
                packed[...] = pack_refs[m][...].astype(F32)
                packed_matrix(plan, b, packed, m * rows, wide)
            matrix = wide[...].astype(BF)
            wide_ref[...] = matrix
            for copy in copies:
                copy.wait()
            for i in range(plan.line_taps[b]):
                part = dot(
                    matrix[:, i * features : (i + 1) * features],
                    weight[i * features : (i + 1) * features, :],
                    ((1,), (1,)),
                )
                total = part if i == 0 else total + part
            keep_ref[...] = total[:rows]
            for m in range(1, line):
                send_ref[m - 1] = total[m * rows : (m + 1) * rows].astype(BF)

        both(meta_ref, lambda: run(0), lambda: run(1))

    return call(
        kernel,
        [SMEM] + vmem(line) + [ANY] * 4,
        [
            ((rows, features), F32),
            ((line - 1, rows, features), BF),
            ((line * rows, wide_max), BF),
        ],
        [
            pltpu.VMEM((wide_max, features), BF),
            pltpu.VMEM((line * rows, wide_max), F32),
            pltpu.VMEM((plan.pack, LANE), F32),
            pltpu.SemaphoreType.DMA((4,)),
        ],
        flops=2 * line * rows * features * wide_max,
        moved=5 << 20,
        limit=16,
    )(meta, *packs, *quarter)


def trans_weight(plan, meta, inners, wide):
    rows, features, line = plan.rows, plan.features, plan.line
    most = plan.down_max

    def kernel(meta_ref, *refs):
        inner_refs = refs[:line]
        wide_ref, keep_ref, send_ref, total = refs[line:]

        def run(b):
            own = plan.down_rows[b]
            lhs = jnp.concatenate([ref[...] for ref in inner_refs], axis=0)
            for i in range(plan.line_taps[b]):
                total[i * features : (i + 1) * features, :] = dot(
                    lhs, wide_ref[:, i * features : (i + 1) * features], ((0,), (0,))
                )
            for v in range(4):
                start = pl.multiple_of((meta_ref[7] ^ v) * own, LANE)
                piece = total[pl.ds(start, own), :]
                if own < most:
                    pad = jnp.zeros((most - own, features), F32)
                    piece = jnp.concatenate([piece, pad], axis=0)
                if v % 2 == 0:
                    keep_ref[v // 2] = piece
                else:
                    send_ref[v // 2] = piece.astype(BF)

        both(meta_ref, lambda: run(0), lambda: run(1))

    return call(
        kernel,
        [SMEM] + vmem(line + 1),
        [((2, most, features), F32), ((2, most, features), BF)],
        [pltpu.VMEM((4 * most, features), F32)],
        flops=2 * line * rows * features * 4 * most,
        moved=5 << 20,
        limit=20,
    )(meta, *inners, wide)


def inner_backward(plan, meta, pieces, low, act, vectors, gain):
    rows, features = plan.rows, plan.features

    def kernel(meta_ref, *refs):
        parts = refs[:-7]
        low_ref, act_ref, vec_ref, gain_ref, delta_ref, back_ref, out_ref = refs[-7:]
        total = keep_rows(total_of(parts), meta_ref[4])
        act_in = act_ref[...]
        unit, scale = norm_parts(act_in + low_ref[...].astype(F32))
        out_ref[...] = vec_ref[...]
        out_ref[1:2, :] = vec_ref[1:2, :] + jnp.sum(total, axis=0, keepdims=True)
        out_ref[2:3, :] = vec_ref[2:3, :] + jnp.sum(total * unit, axis=0, keepdims=True)
        back = norm_back(total, unit, scale, gain_ref[...])
        back_ref[...] = back
        delta_ref[...] = keep_rows(back * (1.0 - act_in * act_in), meta_ref[4]).astype(BF)

    return call(
        kernel,
        [SMEM] + vmem(len(pieces) + 4),
        [((rows, features), BF), ((rows, features), F32), ((8, features), F32)],
        [],
        moved=1 << 19,
        limit=6,
    )(meta, *pieces, low, act, vectors, gain)


def down_delta(plan, meta, pieces, delta_inner, act, small):
    rows, features = plan.rows, plan.features
    base, extra = up8(rows, 16), small.shape[0]

    def kernel(meta_ref, *refs):
        parts = refs[:-4]
        inner_ref, act_ref, small_ref, out_ref = refs[-4:]
        value = act_ref[...]
        total = total_of(parts) + inner_ref[...]
        delta = keep_rows(total * (1.0 - value * value), meta_ref[4])
        pad = jnp.zeros((base - rows, features), F32)
        out_ref[0:base, :] = jnp.concatenate([delta, pad], axis=0).astype(BF)
        high = small_ref[...].astype(BF)
        out_ref[base : base + extra, :] = high
        out_ref[base + extra :, :] = (small_ref[...] - high.astype(F32)).astype(BF)

    return call(
        kernel,
        [SMEM] + vmem(len(pieces) + 3),
        [((base + 2 * extra, features), BF)],
        [],
        moved=1 << 19,
        limit=8,
    )(meta, *pieces, delta_inner, act, small)[0]


def input_quarter(plan, meta, deltas, quarter):
    features, line = plan.features, plan.line
    rows = up8(plan.rows, 16)
    wide_max = 4 * plan.down_max

    def kernel(meta_ref, *refs):
        delta_refs, weights = refs[:line], refs[line : line + 4]
        out_ref, weight, wide, packed, sems = refs[line + 4 :]

        def run(b):
            copies = fetch_quarter(plan, b, meta_ref, weights, weight, sems)
            lhs = jnp.concatenate([ref[0:rows, :] for ref in delta_refs], axis=0)
            for copy in copies:
                copy.wait()
            for i in range(plan.line_taps[b]):
                wide[:, i * features : (i + 1) * features] = dot(
                    lhs, weight[i * features : (i + 1) * features, :], ((1,), (1,))
                )
            packed[...] = jnp.zeros_like(packed)
            for m in range(line):
                matrix_packed(plan, b, wide, m * rows, packed)
                out_ref[m] = packed[...].astype(BF)

        both(meta_ref, lambda: run(0), lambda: run(1))

    return call(
        kernel,
        [SMEM] + vmem(line) + [ANY] * 4,
        [((line, plan.pack, LANE), BF)],
        [
            pltpu.VMEM((wide_max, features), BF),
            pltpu.VMEM((line * rows, wide_max), F32),
            pltpu.VMEM((plan.pack, LANE), F32),
            pltpu.SemaphoreType.DMA((4,)),
        ],
        flops=2 * line * rows * features * wide_max,
        moved=4 << 20,
        limit=16,
    )(meta, *deltas, *quarter)[0]


def input_rows(plan, meta, packs, outer):
    features, length, line = plan.features, plan.length, plan.line

    def kernel(meta_ref, *refs):
        pack_refs = refs[:line]
        outer_ref, out_ref, stage, packed = refs[line:]

        def run(b):
            for m in range(line):
                packed[...] = pack_refs[m][...].astype(F32)
                unpack_taps(plan, b, packed, stage, (meta_ref[5] ^ m) * plan.line_taps[b])
            inner = get(stage, plan.factors[b] // 2, length)
            out_ref[...] = (inner + outer_ref[...]).astype(BF)

        both(meta_ref, lambda: run(0), lambda: run(1))

    return call(
        kernel,
        [SMEM] + vmem(line + 1),
        [((length, features), BF)],
        [split(plan.stage_rows, features), pltpu.VMEM((plan.pack, LANE), F32)],
        moved=3 << 20,
        limit=12,
    )(meta, *packs, outer)[0]


def down_weight(plan, meta, columns, even, odd, extra, loss_part):
    shards, rows, features, line = plan.shards, plan.rows, plan.features, plan.line
    half = shards // 2
    base = up8(rows, 16)
    most, tail = plan.down_max, up8(extra + 2, 16)

    def kernel(meta_ref, *refs):
        col_refs = refs[:4]
        even_ref, odd_ref, loss_ref, grad_ref, sums_ref, delta, ordered, small = refs[4:]
        me = meta_ref[1]
        for q in range(shards):
            source = (even_ref, odd_ref)[q // half]
            value = source[q % half, 0:base, :].astype(F32)
            at = me ^ plan.mask(q)
            ordered[pl.ds(at, 1), :] = jnp.sum(value, axis=0, keepdims=True)
            delta[q * rows : (q + 1) * rows, :] = value[:rows]
            high = source[q % half, base : base + extra, :].astype(F32)
            low = source[q % half, base + extra : base + 2 * extra, :].astype(F32)
            small[at] = high + low
        total = small[0]
        for i in range(1, shards):
            total = total + small[i]
        sums_ref[...] = jnp.zeros_like(sums_ref)
        sums_ref[0:extra, :] = total
        sums_ref[extra : extra + 1, :] = jnp.sum(ordered[...], axis=0, keepdims=True)
        sums_ref[extra + 1 : extra + 2, :] = jnp.broadcast_to(loss_ref[0:1, 0:1], (1, features))
        sums = sums_ref[...]
        high = sums.astype(BF)
        low = (sums - high.astype(F32)).astype(BF)
        grad_ref[most : most + tail, :] = high
        grad_ref[most + tail :, :] = low
        sums_ref[...] = high.astype(F32) + low.astype(F32)
        for at, v in enumerate((0, 2, 1, 3)):
            steps = delta[at * line * rows : (at + 1) * line * rows, :].astype(BF)
            part = dot(col_refs[v][...], steps, ((0,), (0,)))
            total = part if at == 0 else total + part
        grad_ref[0:most, :] = total.astype(BF)

    return call(
        kernel,
        [SMEM] + vmem(7),
        [((most + 2 * tail, features), BF), ((tail, features), F32)],
        [
            pltpu.VMEM((shards * rows, features), F32),
            pltpu.VMEM((shards, features), F32),
            pltpu.VMEM((shards, extra, features), F32),
        ],
        flops=2 * shards * rows * features * features,
        moved=4 << 20,
        limit=20,
    )(meta, *columns, even, odd, loss_part)


def natural_order(plan, meta, own, halves):
    shards = plan.shards
    half = shards // 2
    rows, features = own

    def kernel(meta_ref, even_ref, odd_ref, out_ref):
        for q in range(shards):
            out_ref[meta_ref[1] ^ plan.mask(q)] = (even_ref, odd_ref)[q // half][q % half].astype(
                F32
            )

    return call(
        kernel,
        [SMEM] + vmem(2),
        [((shards, rows, features), F32)],
        [],
        moved=3 << 20,
        limit=16,
    )(meta, *halves)[0]


ROOT_HALF = 0.7071067811865476
ROOT_TWO_PI = 0.3989422804014327


def head_rows(plan, meta, keep, recv, target, valid, merge, bias, gain, ff_in, ff_bias, ff_out):
    half_rows, features = keep.shape
    hidden = ff_in.shape[1]
    parts = hidden // features
    dims = (half_rows, features)

    def kernel(
        meta_ref, keep_ref, recv_ref, target_ref, valid_ref, merge_ref, bias_ref, gain_ref,
        in_bias_ref, in_hbm, out_hbm,
        out_ref, up_keep_ref, up_send_ref, normed_ref, act_ref, pre_delta_ref, ff_delta_ref,
        merged_delta_ref, vec_ref, loss_ref, slope_ref, in_ref, out_w_ref, sems,
    ):
        fetch_in = pltpu.make_async_copy(in_hbm, in_ref, sems.at[0])
        fetch_out = pltpu.make_async_copy(out_hbm, out_w_ref, sems.at[1])
        fetch_in.start()
        fetch_out.start()
        branch = meta_ref[0]
        merged = dot(keep_ref[...], merge_ref[branch]) + dot(recv_ref[...], merge_ref[1 - branch])
        merged = merged + bias_ref[0:1, :]
        unit, scale = norm_parts(merged)
        normed = (unit * gain_ref[0:1, :] + bias_ref[2:3, :]).astype(BF)
        normed_ref[...] = normed
        fetch_in.wait()
        fetch_out.wait()
        for c in range(parts):
            cols = slice(c * features, (c + 1) * features)
            pre = dot(normed, in_ref[:, cols]) + in_bias_ref[:, cols]
            share = 0.5 * (1.0 + lax.erf(pre * ROOT_HALF))
            slope_ref[:, cols] = share + pre * (jnp.exp(-0.5 * pre * pre) * ROOT_TWO_PI)
            act = (pre * share).astype(BF)
            act_ref[:, cols] = act
            part = dot(act, out_w_ref[cols, :])
            total = part if c == 0 else total + part
        unit_end, scale_end = norm_parts(merged + total + bias_ref[1:2, :])
        final = unit_end * gain_ref[1:2, :] + bias_ref[3:4, :]
        out_ref[...] = final.astype(BF)
        error = final - target_ref[...].astype(F32)
        weighted = valid_ref[...] * error
        loss = jnp.sum(jnp.sum(weighted * error, axis=0, keepdims=True), axis=1, keepdims=True)
        loss_ref[...] = jnp.broadcast_to(loss, loss_ref.shape)
        vec_ref[...] = jnp.zeros_like(vec_ref)
        vec_ref[3:4, :] = jnp.sum(weighted, axis=0, keepdims=True)
        vec_ref[5:6, :] = jnp.sum(weighted * unit_end, axis=0, keepdims=True)
        delta_sum = norm_back(weighted, unit_end, scale_end, gain_ref[1:2, :])
        delta_ff = delta_sum.astype(BF)
        ff_delta_ref[...] = delta_ff
        vec_ref[1:2, :] = jnp.sum(delta_ff.astype(F32), axis=0, keepdims=True)
        for c in range(parts):
            cols = slice(c * features, (c + 1) * features)
            pre_delta = dot(delta_ff, out_w_ref[cols, :], ((1,), (1,))) * slope_ref[:, cols]
            pre_delta = pre_delta.astype(BF)
            pre_delta_ref[:, cols] = pre_delta
            vec_ref[6 + c : 7 + c, :] = jnp.sum(pre_delta.astype(F32), axis=0, keepdims=True)
            part = dot(pre_delta, in_ref[:, cols], ((1,), (1,)))
            above = part if c == 0 else above + part
        vec_ref[2:3, :] = jnp.sum(above, axis=0, keepdims=True)
        vec_ref[4:5, :] = jnp.sum(above * unit, axis=0, keepdims=True)
        delta = norm_back(above, unit, scale, gain_ref[0:1, :]) + delta_sum
        delta = delta.astype(BF)
        merged_delta_ref[...] = delta
        vec_ref[0:1, :] = jnp.sum(delta.astype(F32), axis=0, keepdims=True)
        up_keep_ref[...] = dot(delta, merge_ref[branch], ((1,), (1,))).astype(BF)
        up_send_ref[...] = dot(delta, merge_ref[1 - branch], ((1,), (1,))).astype(BF)

    vec_rows = up8(6 + parts + 6)
    return call(
        kernel,
        [SMEM] + vmem(8) + [HBM] * 2,
        [
            (dims, BF), (dims, BF), (dims, BF), (dims, BF),
            ((half_rows, hidden), BF), ((half_rows, hidden), BF), (dims, BF), (dims, BF),
            ((vec_rows, features), F32), ((8, LANE), F32),
        ],
        [
            pltpu.VMEM((half_rows, hidden), F32),
            pltpu.VMEM((features, hidden), BF),
            pltpu.VMEM((hidden, features), BF),
            pltpu.SemaphoreType.DMA((2,)),
        ],
        flops=10 * half_rows * features * hidden,
        moved=14 << 20,
        limit=56,
    )(meta, keep, recv, target, valid, merge, bias, gain, ff_bias, ff_in, ff_out)


def head_weights(plan, meta, keep, recv, normed, act, pre_delta, ff_delta, merged_delta):
    shards = plan.shards
    half_rows, features = keep.shape
    hidden = act.shape[1]
    ff_rows, merge_rows = hidden // shards // 2, features // shards
    parts = hidden // features
    own = 2 * ff_rows + merge_rows

    def kernel(
        meta_ref, keep_hbm, recv_hbm, normed_hbm, act_hbm, pre_hbm, ff_hbm, merged_hbm,
        stay_near, stay_far, send_near, send_far, first, second, third,
        keep_ref, recv_ref, normed_ref, act_ref, pre_ref, ff_ref, merged_ref, sems,
    ):
        pairs = (
            (normed_hbm, normed_ref), (pre_hbm, pre_ref), (ff_hbm, ff_ref), (act_hbm, act_ref),
            (merged_hbm, merged_ref), (keep_hbm, keep_ref), (recv_hbm, recv_ref),
        )
        copies = [
            pltpu.make_async_copy(source, target, sems.at[i])
            for i, (source, target) in enumerate(pairs)
        ]
        for copy in copies:
            copy.start()
        branch = meta_ref[0]
        copies[0].wait()
        copies[1].wait()
        for c in range(parts):
            cols = slice(c * features, (c + 1) * features)
            first[cols, :] = dot(pre_ref[:, cols], normed_ref[...], ((0,), (0,))).astype(BF)
        copies[2].wait()
        copies[3].wait()
        for c in range(parts):
            cols = slice(c * features, (c + 1) * features)
            second[cols, :] = dot(act_ref[:, cols], ff_ref[...], ((0,), (0,))).astype(BF)
        for copy in copies[4:]:
            copy.wait()
        for side, ref in enumerate((keep_ref, recv_ref)):
            part = dot(ref[...], merged_ref[...], ((0,), (0,))).astype(BF)
            start = pl.multiple_of((branch ^ side) * features, 16)
            third[pl.ds(start, features), :] = part
        for q in range(shards):
            device = meta_ref[1] ^ plan.mask(q)
            targets = (stay_near, stay_far, send_near, send_far)
            target = targets[q // plan.line]
            for h in range(2):
                at = 2 * device + (branch ^ h)
                for start, count, source in (
                    (0, ff_rows, first),
                    (ff_rows, ff_rows, second),
                    (2 * ff_rows, merge_rows, third),
                ):
                    rows = pl.ds(pl.multiple_of(at * count, 16), count)
                    target[h, q % plan.line, start : start + count, :] = source[rows, :]

    return call(
        kernel,
        [SMEM] + [HBM] * 7,
        [((2, plan.line, own, features), BF)] * 4,
        [
            pltpu.VMEM((hidden, features), BF),
            pltpu.VMEM((hidden, features), BF),
            pltpu.VMEM((2 * features, features), BF),
        ]
        + [
            pltpu.VMEM(ref.shape, BF)
            for ref in (keep, recv, normed, act, pre_delta, ff_delta, merged_delta)
        ]
        + [pltpu.SemaphoreType.DMA((7,))],
        flops=4 * half_rows * features * hidden,
        moved=12 << 20,
        limit=56,
    )(meta, keep, recv, normed, act, pre_delta, ff_delta, merged_delta)


def hop(values, distance, shards):
    return lax.ppermute(values, "series", [(i, i ^ distance) for i in range(shards)])


def swap(values):
    return lax.ppermute(values, "branch", [(0, 1), (1, 0)])


def after(value, *others):
    return lax.optimization_barrier((value, others))[0]


def along_line(plan, own):
    return [own] + [hop(own, i << 2, plan.shards) for i in range(1, plan.line)]


def line_parts(plan, first, rest):
    return [first] + [hop(rest[i - 1], i << 2, plan.shards) for i in range(1, plan.line)]


def quad_gather(plan, own, later):
    side = hop(own, 2, plan.shards)
    return [own, hop(own, 1, plan.shards), side, hop(after(side, later), 1, plan.shards)]


def settle(value, *others):
    return lax.optimization_barrier((value,) + others)


def gather_slots(plan, line):
    even = jnp.stack(line + [hop(value, 2, plan.shards) for value in line])
    return even, hop(even, 1, plan.shards)


def scatter_sum(plan, keep, send, *others):
    shards, line = plan.shards, plan.line
    first = keep + hop(send, 1, shards).astype(F32)
    second = first[:line] + hop(first[line:].astype(BF), 2, shards).astype(F32)
    if others:
        second, *others = settle(second, *others)
    pieces = line_parts(plan, second[0], [second[i].astype(BF) for i in range(1, line)])
    return (pieces, *others) if others else pieces


def rounded(values):
    return lax.reduce_precision(values, exponent_bits=8, mantissa_bits=7)


def layer_norm(values, gain_row, shift_row):
    center = values - jnp.mean(values, axis=-1, keepdims=True)
    spread = jnp.mean(center * center, axis=-1, keepdims=True)
    return center * lax.rsqrt(spread + EPSILON) * gain_row + shift_row


def gelu_exact(values):
    return jax.nn.gelu(values, approximate=False)


def product(a, b):
    return jnp.dot(a, b, preferred_element_type=F32)


def left_product(a, b):
    return jnp.einsum("mi,mo->io", a, b, preferred_element_type=F32)


def right_product(a, b):
    return jnp.einsum("mo,io->mi", a, b, preferred_element_type=F32)


def body(
    series_in, target, horizons, observed,
    down_short, iso_short, trans_short, down_long, iso_long, trans_long,
    branch_bias, branch_gain, merge_weight, head_bias, head_gain, ff_in, ff_in_bias, ff_out,
):
    shards = lax.axis_size("series")
    _, length, features = series_in.shape
    plan = Plan(
        shards,
        length,
        features,
        (down_short.shape[0], down_long.shape[0]),
        (iso_short.shape[0], iso_long.shape[0]),
    )
    line = plan.line
    half_rows = length // 2
    branch = lax.axis_index("branch")
    me = lax.axis_index("series")
    is_short = branch == 0
    iso_rows = jnp.where(is_short, plan.iso_rows[0], plan.iso_rows[1])
    meta = jnp.stack(
        [
            branch,
            me,
            (me * iso_rows) // features,
            (me * iso_rows) % features,
            jnp.where(is_short, plan.steps[0], plan.steps[1]),
            me // 4,
            me % 2,
            me % 4,
        ]
    ).astype(jnp.int32)
    series = series_in[0]
    biases, gain = branch_bias[0], branch_gain

    def chosen(short, long):
        rows = max(short.shape[0], long.shape[0])
        short = jnp.pad(short, ((0, rows - short.shape[0]), (0, 0)))
        long = jnp.pad(long, ((0, rows - long.shape[0]), (0, 0)))
        return jnp.where(is_short, short, long)

    def placed(own, other, b, rows):
        return jnp.where(branch == b, own, other)[:rows].astype(F32)

    blocks = prep_blocks(plan, meta, series)
    own_down = after(chosen(down_short, down_long), blocks)
    blocks = line_parts(plan, blocks[0], [blocks[i] for i in range(1, line)])
    down_quarter = quad_gather(plan, own_down, blocks)
    own_trans = after(chosen(trans_short, trans_long), blocks)
    keep, send, *columns = down_partial(plan, meta, blocks, down_quarter)
    pieces = line_parts(plan, keep, send)
    trans_quarter = quad_gather(plan, own_trans, pieces)
    low, act_down = low_rows(plan, meta, pieces, biases)
    low_own = gather_slots(plan, along_line(plan, low))
    low_own, trans_quarter = settle(low_own, trans_quarter)
    keep, send = iso_partial(plan, meta, low_own, iso_short, iso_long, False)
    low_other = swap(after(low_own[0], low_own[1]))
    pieces = scatter_sum(plan, keep, send)
    inner, act_iso = inner_rows(plan, meta, pieces, low, biases, gain)
    columns[2] = hop(after(columns[2], inner), 2, shards)
    inners, columns = settle(along_line(plan, inner), columns)
    packs = trans_forward(plan, meta, inners, trans_quarter)
    columns[3] = hop(after(columns[3], packs), 3, shards)
    packs = line_parts(plan, packs[0], [packs[i] for i in range(1, line)])
    packs, columns, low_other = settle(packs, columns, low_other)
    out_keep, out_send, act_trans = outer_rows(plan, meta, packs, series, biases, gain)
    out_recv = swap(out_send)
    columns[1] = hop(after(columns[1], out_keep), 1, shards)
    low_other = (low_other, hop(after(low_other, out_keep), 1, shards))
    out_recv, columns, low_other = settle(out_recv, columns, low_other)

    positions = branch * half_rows + jnp.arange(half_rows, dtype=jnp.int32)
    observed_half = lax.dynamic_slice_in_dim(observed[0], branch * half_rows, half_rows, 0)
    valid = (
        observed_half.astype(F32)
        * (positions >= SEQ_IN).astype(F32)
        * (positions < SEQ_IN + horizons[0]).astype(F32)
    )
    (
        out, up_keep, up_send, normed, act_ff, pre_delta, ff_delta, merged_delta, vec_head, loss_part
    ) = head_rows(
        plan, meta, out_keep, out_recv, target[0], valid[:, None], merge_weight, head_bias,
        head_gain, ff_in, ff_in_bias[None], ff_out,
    )
    up_recv = swap(up_send)
    near, far, near_send, far_send = head_weights(
        plan, meta, out_keep, out_recv, normed, act_ff, pre_delta, ff_delta, merged_delta
    )

    far_recv = hop(after(far_send, up_recv), 1, shards)
    outer, packs, vectors = outer_backward(plan, meta, up_keep, up_recv, series, act_trans, gain)
    far = (far.astype(F32) + after(far_recv, packs).astype(F32)).astype(BF)
    near_recv = hop(after(near_send, packs), 1, shards)
    share_recv = hop(far, 2, shards)
    packs = line_parts(plan, packs[0], [packs[i] for i in range(1, line)])
    keep, send, wide = trans_backward(plan, meta, packs, trans_quarter)
    trans_keep, trans_send = trans_weight(plan, meta, inners, wide)
    pieces, trans_send, share_recv, near_recv = settle(
        line_parts(plan, keep, send), trans_send, share_recv, near_recv
    )
    shares = near.astype(F32) + near_recv.astype(F32) + share_recv.astype(F32)
    share_recv = swap(shares[1].astype(BF))
    shares = shares[0]
    delta_iso, delta_inner, vectors = inner_backward(
        plan, meta, pieces, low, act_iso, vectors, gain
    )
    ff_parts = ff_in_bias.shape[0] // features
    selector = jnp.stack([is_short, branch == 1]).astype(F32)
    branch_rows = (selector[:, None, None] * vectors[None, 0:3]).reshape(6, features)
    small = jnp.concatenate([vec_head[: 6 + ff_parts], branch_rows], axis=0)
    count = small.shape[0]
    small = jnp.pad(small, ((0, up8(count, 16) - count), (0, 0)))
    trans_recv = hop(trans_send, 1, shards)
    deltas, trans_recv = settle(along_line(plan, delta_iso), trans_recv)
    trans_sum = trans_keep + trans_recv.astype(F32)
    trans_next = trans_sum[1].astype(BF)
    delta_own = gather_slots(plan, deltas)
    delta_own, trans_next, share_recv = settle(delta_own, trans_next, share_recv)
    shares = shares + share_recv.astype(F32)
    spread = line // 2
    share_recv = hop(shares[spread:].astype(BF), 4 * spread, shards)
    keep, send = iso_partial(plan, meta, delta_own, iso_short, iso_long, True)
    delta_other = swap(delta_own[0])
    pieces, delta_other = scatter_sum(plan, keep, send, delta_other)
    pieces, share_recv = settle(pieces, share_recv)
    shares = shares[:spread] + share_recv.astype(F32)
    payload = down_delta(plan, meta, pieces, delta_inner, act_down, small)
    delta_other = (delta_other, hop(after(delta_other, payload), 1, shards))
    trans_recv = hop(after(trans_next, payload), 2, shards)
    share_recv = hop(after(shares[1:].astype(BF), payload), 4, shards)
    first_grad = iso_weight(plan, meta, 0, low_own, low_other, delta_own, delta_other)
    deltas, trans_recv, share_recv, first_grad = settle(
        along_line(plan, payload), trans_recv, share_recv, first_grad
    )
    shares = rounded(shares[0] + share_recv[0].astype(F32))
    grad_trans = (trans_sum[0] + trans_recv.astype(F32)).astype(BF)
    packs = input_quarter(plan, meta, deltas, down_quarter)
    even = jnp.stack(deltas)
    odd = hop(after(even, packs), 2, shards)
    packs = line_parts(plan, packs[0], [packs[i] for i in range(1, line)])
    crossing = swap(after(jnp.concatenate([grad_trans, shares.astype(BF)], axis=0), odd))
    second_grad = iso_weight(
        plan, meta, 1, after(low_own, odd), low_other, delta_own, delta_other
    )
    packs, second_grad = settle(packs, second_grad)
    input_own = input_rows(plan, meta, packs, outer)
    input_own, crossing = settle(input_own, crossing)
    trans_recv, share_recv = crossing[: plan.down_max], crossing[plan.down_max :]
    input_recv = swap(input_own)
    even = jnp.concatenate([even, odd], axis=0)
    delta_halves = (even, hop(after(even, input_own), 1, shards))
    share_recv = share_recv.astype(F32)
    ff_rows = ff_in_bias.shape[0] // shards // 2
    halves = [
        jnp.where(is_short, shares, share_recv),
        jnp.where(is_short, share_recv, shares),
    ]
    merge_own = jnp.concatenate([half[2 * ff_rows :] for half in halves], axis=0)
    extra = small.shape[0]
    grad_down, mine = down_weight(
        plan, meta, columns, *after(delta_halves, input_own), extra, loss_part
    )
    down_recv = swap(grad_down)
    merge_even = jnp.stack(along_line(plan, after(merge_own.astype(BF), delta_halves[1])))
    merge_odd = hop(after(merge_even, grad_down), 2, shards)
    trans_grads = [placed(grad_trans, trans_recv, b, plan.down_rows[b]) for b in range(2)]
    merge_odd, trans_grads = settle(merge_odd, trans_grads)
    merge_even = jnp.concatenate([merge_even, merge_odd], axis=0)
    merge_core = hop(merge_even, 1, shards)
    input_total = input_own.astype(F32) + after(input_recv, merge_odd).astype(F32)
    merge_core, input_total = settle(merge_core, input_total)
    merge_total = natural_order(
        plan, meta, merge_own.shape, (merge_even, merge_core)
    ).reshape(2, features, features)
    down_recv = after(down_recv, merge_total)
    tail = mine.shape[0]
    theirs = down_recv[plan.down_max :].astype(F32)
    theirs = theirs[:tail] + theirs[tail:]
    down_recv = down_recv[: plan.down_max]
    grad_down = grad_down[: plan.down_max]
    iso_grads = [first_grad, second_grad]
    both_sums = mine + theirs
    loss = (0.5 / (features * length)) * both_sums[extra + 1, 0:1]
    small = both_sums[:count]
    down_sum, down_other = mine[extra : extra + 1], theirs[extra : extra + 1]
    branch_total = small[6 + ff_parts :].reshape(2, 3, features)
    down_sums = jnp.stack(
        [jnp.where(is_short, down_sum, down_other), jnp.where(is_short, down_other, down_sum)]
    )
    iso_sums = jnp.stack([iso_grads[0][1], iso_grads[1][1]])
    bias_total = jnp.concatenate([down_sums, iso_sums, branch_total[:, 0:2]], axis=1)

    return (
        out[None],
        loss,
        input_total[None],
        placed(grad_down, down_recv, 0, plan.down_rows[0]),
        iso_grads[0][0],
        trans_grads[0],
        placed(grad_down, down_recv, 1, plan.down_rows[1]),
        iso_grads[1][0],
        trans_grads[1],
        bias_total,
        branch_total[:, 2],
        merge_total,
        small[0:4],
        small[4:6],
        jnp.concatenate([half[:ff_rows] for half in halves], axis=0).T,
        small[6 : 6 + ff_parts].reshape(-1),
        jnp.concatenate([half[ff_rows : 2 * ff_rows] for half in halves], axis=0),
    )


def fitted(matrix, row_total):
    return jnp.pad(matrix, ((0, row_total - matrix.shape[0]), (0, 0)))


def unpack(gathered_all, shards, rows_max, rows_own):
    features = gathered_all.shape[1]
    return gathered_all.reshape(shards, rows_max, features)[:, :rows_own].reshape(
        shards * rows_own, features
    )


def repack(gradient, shards, rows_max):
    rows_own = gradient.shape[0] // shards
    shaped = gradient.reshape(shards, rows_own, gradient.shape[1])
    return jnp.pad(shaped, ((0, 0), (0, rows_max - rows_own), (0, 0))).reshape(
        shards * rows_max, gradient.shape[1]
    )


def branch_pass(series_in, weights, shards, rows_max, biases, gain_row, factor):
    series_count, length, features = series_in.shape
    step_count = (length + factor) // factor
    margin = factor // 2
    weight_down = unpack(weights[0], shards, rows_max[0], factor * features // shards)
    weight_iso = unpack(weights[1], shards, rows_max[1], step_count * features // shards)
    weight_trans = unpack(weights[2], shards, rows_max[2], factor * features // shards).reshape(
        factor, features, features
    )
    blocks = jnp.pad(series_in, ((0, 0), (margin, step_count * factor - length - margin), (0, 0)))
    blocks = blocks.reshape(series_count * step_count, factor * features)
    act_down = jnp.tanh(product(blocks, weight_down) + biases[0])
    low_down = act_down.astype(jnp.bfloat16)
    padded = jnp.concatenate(
        [
            jnp.zeros((series_count, step_count - 1, features), jnp.bfloat16),
            low_down.reshape(series_count, step_count, features),
        ],
        axis=1,
    )
    unfolded = jnp.concatenate(
        [padded[:, offset : offset + step_count] for offset in range(step_count)], axis=2
    )
    unfolded = unfolded.reshape(series_count * step_count, step_count * features)
    act_iso = jnp.tanh(product(unfolded, weight_iso) + biases[1])
    inner_norm, inner_back = jax.vjp(
        layer_norm, act_iso + low_down.astype(jnp.float32), gain_row, biases[3]
    )
    low_inner = inner_norm.astype(jnp.bfloat16)
    spread_out = jnp.einsum(
        "mi,jio->mjo", low_inner, weight_trans, preferred_element_type=jnp.float32
    )
    act_trans = jnp.tanh(
        spread_out.reshape(series_count, step_count * factor, features)[:, :length] + biases[2]
    )
    result, outer_back = jax.vjp(
        layer_norm, act_trans + series_in.astype(jnp.float32), gain_row, biases[3]
    )
    stored = (
        blocks,
        weight_down,
        weight_iso,
        weight_trans,
        act_down,
        unfolded,
        act_iso,
        inner_back,
        low_inner,
        act_trans,
        outer_back,
    )
    return (result, stored)


def branch_back(series_in, weights, shards, rows_max, biases, gain_row, factor, upstream):
    series_count, length, features = series_in.shape
    step_count = (length + factor) // factor
    margin = factor // 2
    result, stored = branch_pass(series_in, weights, shards, rows_max, biases, gain_row, factor)
    (
        blocks,
        weight_down,
        weight_iso,
        weight_trans,
        act_down,
        unfolded,
        act_iso,
        inner_back,
        low_inner,
        act_trans,
        outer_back,
    ) = stored
    delta_outer, gain_outer, shift_outer = outer_back(upstream)
    delta_trans = (delta_outer * (1.0 - act_trans * act_trans)).astype(jnp.bfloat16)
    trans_blocks = jnp.pad(delta_trans, ((0, 0), (0, step_count * factor - length), (0, 0)))
    trans_blocks = trans_blocks.reshape(series_count * step_count, factor, features)
    grad_trans = jnp.einsum(
        "mi,mjo->jio", low_inner, trans_blocks, preferred_element_type=jnp.float32
    )
    grad_trans = grad_trans.reshape(factor * features, features)
    inner_upstream = jnp.einsum(
        "mjo,jio->mi", trans_blocks, weight_trans, preferred_element_type=jnp.float32
    )
    delta_inner, gain_inner, shift_inner = inner_back(inner_upstream)
    delta_iso = (delta_inner * (1.0 - act_iso * act_iso)).astype(jnp.bfloat16)
    grad_iso = left_product(unfolded, delta_iso)
    delta_unfold = right_product(delta_iso, weight_iso).reshape(
        series_count, step_count, step_count, features
    )
    delta_padded = jnp.zeros((series_count, 2 * step_count - 1, features), jnp.float32)
    for offset in range(step_count):
        delta_padded = delta_padded.at[:, offset : offset + step_count].add(
            delta_unfold[:, :, offset]
        )
    delta_low = (
        delta_padded[:, step_count - 1 :].reshape(series_count * step_count, features) + delta_inner
    )
    delta_down = (delta_low * (1.0 - act_down * act_down)).astype(jnp.bfloat16)
    grad_down = left_product(blocks, delta_down)
    delta_blocks = right_product(delta_down, weight_down).reshape(
        series_count, step_count * factor, features
    )
    delta_series = delta_blocks[:, margin : margin + length] + delta_outer
    vectors = jnp.stack(
        [
            jnp.sum(delta_down.astype(jnp.float32), axis=0),
            jnp.sum(delta_iso.astype(jnp.float32), axis=0),
            jnp.sum(delta_trans.astype(jnp.float32), axis=(0, 1)),
            shift_inner + shift_outer,
        ]
    )
    padded_grads = (
        repack(grad_down, shards, rows_max[0]),
        repack(grad_iso, shards, rows_max[1]),
        repack(grad_trans, shards, rows_max[2]),
    )
    return (delta_series, padded_grads, vectors, gain_inner + gain_outer)


def plain_body(
    series_in,
    target,
    horizons,
    observed,
    down_short,
    iso_short,
    trans_short,
    down_long,
    iso_long,
    trans_long,
    branch_bias,
    branch_gain,
    merge_weight,
    head_bias,
    head_gain,
    ff_in,
    ff_in_bias,
    ff_out,
):
    branch_index = lax.axis_index("branch")
    shards = lax.axis_size("series")
    series_count, length, features = series_in.shape
    rows_max = (
        max(down_short.shape[0], down_long.shape[0]),
        max(iso_short.shape[0], iso_long.shape[0]),
        max(trans_short.shape[0], trans_long.shape[0]),
    )
    is_short = branch_index == 0
    own_down = jnp.where(is_short, fitted(down_short, rows_max[0]), fitted(down_long, rows_max[0]))
    own_iso = jnp.where(is_short, fitted(iso_short, rows_max[1]), fitted(iso_long, rows_max[1]))
    own_trans = jnp.where(
        is_short, fitted(trans_short, rows_max[2]), fitted(trans_long, rows_max[2])
    )
    gathered = (
        lax.all_gather(own_down, "series", axis=0, tiled=True),
        lax.all_gather(own_iso, "series", axis=0, tiled=True),
        lax.all_gather(own_trans, "series", axis=0, tiled=True),
    )
    biases = branch_bias[0]
    gain_row = branch_gain[0]

    def forward_with(factor):
        return lambda: branch_pass(series_in, gathered, shards, rows_max, biases, gain_row, factor)[
            0
        ].astype(jnp.bfloat16)

    branch_out = lax.cond(is_short, forward_with(SCALE_S), forward_with(SCALE_L))
    received = lax.all_to_all(
        branch_out.reshape(series_count, length, 1, features),
        "branch",
        split_axis=1,
        concat_axis=2,
        tiled=True,
    )
    half_rows = received.shape[1]
    merge_rows = received.reshape(series_count * half_rows, 2 * features)
    merge_flat = merge_weight.reshape(2 * features, features)
    merged = product(merge_rows, merge_flat) + head_bias[0]
    normed, first_back = jax.vjp(layer_norm, merged, head_gain[0], head_bias[2])
    low_normed = normed.astype(jnp.bfloat16)
    pre_ff = product(low_normed, ff_in) + ff_in_bias
    activated, gelu_back = jax.vjp(gelu_exact, pre_ff)
    low_act = activated.astype(jnp.bfloat16)
    ff_result = product(low_act, ff_out) + head_bias[1]
    final_out, second_back = jax.vjp(layer_norm, merged + ff_result, head_gain[1], head_bias[3])
    final_rows = final_out.reshape(series_count, half_rows, features)
    positions = branch_index * half_rows + jnp.arange(half_rows, dtype=jnp.int32)
    observed_half = lax.dynamic_slice_in_dim(observed, branch_index * half_rows, half_rows, 1)
    valid_mask = (
        observed_half.astype(jnp.float32)
        * (positions >= SEQ_IN).astype(jnp.float32)
        * (positions < SEQ_IN + horizons[:, None]).astype(jnp.float32)
    )
    error_rows = final_rows - target.astype(jnp.float32)
    weighted = valid_mask[:, :, None] * error_rows
    series_part = 0.5 * jnp.sum(weighted * error_rows, axis=(1, 2)) / (features * length)
    delta_sum, gain_second, shift_second = second_back(
        weighted.reshape(series_count * half_rows, features)
    )
    delta_ff = delta_sum.astype(jnp.bfloat16)
    grad_ff_out = left_product(low_act, delta_ff)
    delta_act = right_product(delta_ff, ff_out)
    (delta_pre,) = gelu_back(delta_act)
    low_pre = delta_pre.astype(jnp.bfloat16)
    grad_ff_in = left_product(low_normed, low_pre)
    delta_normed = right_product(low_pre, ff_in)
    delta_first, gain_first, shift_first = first_back(delta_normed)
    delta_merged = (delta_first + delta_sum).astype(jnp.bfloat16)
    grad_merge = left_product(merge_rows, delta_merged).reshape(2, features, features)
    delta_rows = (
        right_product(delta_merged, merge_flat)
        .astype(jnp.bfloat16)
        .reshape(series_count, half_rows, 2, features)
    )
    back_rows = lax.all_to_all(delta_rows, "branch", split_axis=2, concat_axis=1, tiled=True)
    upstream = back_rows.astype(jnp.float32).reshape(series_count, length, features)
    ff_shares = (
        lax.psum_scatter(grad_ff_in, "series", scatter_dimension=1, tiled=True),
        lax.psum_scatter(grad_ff_out, "series", scatter_dimension=0, tiled=True),
    )
    weights_back = (
        lax.all_gather(own_down, "series", axis=0, tiled=True),
        lax.all_gather(own_iso, "series", axis=0, tiled=True),
        lax.all_gather(own_trans, "series", axis=0, tiled=True),
    )

    def backward_with(factor):
        return lambda: branch_back(
            series_in, weights_back, shards, rows_max, biases, gain_row, factor, upstream
        )

    delta_series, padded_grads, vectors, gain_grad = lax.cond(
        is_short, backward_with(SCALE_S), backward_with(SCALE_L)
    )
    reduced = (
        lax.psum_scatter(padded_grads[0], "series", scatter_dimension=0, tiled=True),
        lax.psum_scatter(padded_grads[1], "series", scatter_dimension=0, tiled=True),
        lax.psum_scatter(padded_grads[2], "series", scatter_dimension=0, tiled=True),
    )
    short_flag = is_short.astype(jnp.float32)
    long_flag = 1.0 - short_flag
    summed = (
        lax.psum(delta_series.astype(jnp.bfloat16), "branch").astype(jnp.float32),
        lax.psum(series_part.astype(jnp.bfloat16), "branch").astype(jnp.float32),
        lax.psum(
            (short_flag * reduced[0][: down_short.shape[0]]).astype(jnp.bfloat16), "branch"
        ).astype(jnp.float32),
        lax.psum((short_flag * reduced[1]).astype(jnp.bfloat16), "branch").astype(jnp.float32),
        lax.psum(
            (short_flag * reduced[2][: trans_short.shape[0]]).astype(jnp.bfloat16), "branch"
        ).astype(jnp.float32),
        lax.psum((long_flag * reduced[0]).astype(jnp.bfloat16), "branch").astype(jnp.float32),
        lax.psum(
            (long_flag * reduced[1][: iso_long.shape[0]]).astype(jnp.bfloat16), "branch"
        ).astype(jnp.float32),
        lax.psum((long_flag * reduced[2]).astype(jnp.bfloat16), "branch").astype(jnp.float32),
        lax.psum(ff_shares[0].astype(jnp.bfloat16), "branch").astype(jnp.float32),
        lax.psum(ff_shares[1].astype(jnp.bfloat16), "branch").astype(jnp.float32),
    )
    selector = (jnp.arange(2, dtype=jnp.int32) == branch_index).astype(jnp.float32)
    full_bias = selector[:, None, None] * vectors[None]
    full_gain = selector[:, None] * gain_grad[None]
    head_vectors = jnp.stack(
        [
            jnp.sum(delta_merged.astype(jnp.float32), axis=0),
            jnp.sum(delta_ff.astype(jnp.float32), axis=0),
            shift_first,
            shift_second,
        ]
    )
    head_gains = jnp.stack([gain_first, gain_second])
    ff_bias_grad = jnp.sum(low_pre.astype(jnp.float32), axis=0)
    totals = lax.psum(
        (grad_merge, head_vectors, head_gains, ff_bias_grad, full_bias, full_gain),
        ("branch", "series"),
    )
    return (
        final_rows.astype(jnp.bfloat16),
        summed[1],
        summed[0],
        summed[2],
        summed[3],
        summed[4],
        summed[5],
        summed[6],
        summed[7],
        totals[4],
        totals[5],
        totals[0],
        totals[1],
        totals[2],
        summed[8],
        totals[3],
        summed[9],
    )


def solution(mesh):
    placed = (
        P("series", None, None),
        P("series", "branch", None),
        P("series"),
        P("series", None),
        P("series", None),
        P("series", None),
        P("series", None),
        P("series", None),
        P("series", None),
        P("series", None),
        P("branch", None, None),
        P("branch", None),
        P(),
        P(),
        P(),
        P(),
        P(),
        P(),
    )

    def run(*args):
        shards = mesh.shape["series"]
        features = args[0].shape[2]
        down_rows = [args[i].shape[0] // shards for i in (4, 7)]
        iso_rows = [args[i].shape[0] // shards for i in (5, 8)]
        fits = (
            args[0].shape[0] == shards
            and shards == 16
            and shards & (shards - 1) == 0
            and all(r % LANE == 0 and r <= features and 4 * r % features == 0 for r in down_rows)
            and all(r % 16 == 0 for r in iso_rows)
        )
        return jax.shard_map(
            body if fits else plain_body,
            mesh=mesh,
            in_specs=placed,
            out_specs=(
                P("series", "branch", None),
                P("series"),
                P("series", None, None),
                P("series", None),
                P("series", None),
                P("series", None),
                P("series", None),
                P("series", None),
                P("series", None),
                P(),
                P(),
                P(),
                P(),
                P(),
                P(None, "series"),
                P(),
                P("series", None),
            ),
            check_vma=False,
        )(*args)

    return run
```

```python
import functools

import jax
import jax.numpy as jnp
from jax import lax
from jax.experimental import pallas as pl
from jax.experimental.pallas import tpu as pltpu
from jax.sharding import PartitionSpec as P

SCALE_S = 12
SCALE_L = 16
SEQ_IN = 96
EPSILON = 1e-05
LANE = 128

BF = jnp.bfloat16
F32 = jnp.float32


def up8(count, base=8):
    return -(-count // base) * base


class Plan:
    def __init__(self, shards, length, features, down_rows, iso_rows):
        self.shards, self.length, self.features = shards, length, features
        self.factors = (SCALE_S, SCALE_L)
        self.steps = tuple((length + k) // k for k in self.factors)
        self.rows = up8(max(self.steps))
        self.down_rows = down_rows
        self.iso_rows = iso_rows
        self.down_max, self.iso_max = max(down_rows), max(iso_rows)
        self.line = shards // 4
        self.line_taps = tuple(4 * r // features for r in down_rows)
        blocks = features // LANE
        self.pack = up8(max(t * blocks * n for t, n in zip(self.line_taps, self.steps)), 16)
        self.taps = tuple(
            max(-(-((d * r) % features + r) // features) for d in range(shards)) for r in iso_rows
        )
        self.taps_max = max(self.taps)
        self.stage_rows = max(k * up8(n) for k, n in zip(self.factors, self.steps))

    def mask(self, slot):
        core, rest = divmod(slot, 2 * self.line)
        side, line = divmod(rest, self.line)
        return core | (side << 1) | (line << 2)


def vmem(count):
    return [pl.BlockSpec(memory_space=pltpu.VMEM) for _ in range(count)]


SMEM = pl.BlockSpec(memory_space=pltpu.SMEM)
ANY = pl.BlockSpec(memory_space=pl.ANY)
HBM = pl.BlockSpec(memory_space=pltpu.HBM)


def call(body, in_specs, outs, scratch, flops=0, moved=0, limit=56):
    return pl.pallas_call(
        body,
        out_shape=[jax.ShapeDtypeStruct(s, d) for s, d in outs],
        in_specs=in_specs,
        out_specs=vmem(len(outs)),
        scratch_shapes=scratch,
        compiler_params=pltpu.CompilerParams(vmem_limit_bytes=limit << 20),
        cost_estimate=pl.CostEstimate(flops=flops, bytes_accessed=moved, transcendentals=0),
    )


def dot(a, b, dims=((1,), (0,))):
    return lax.dot_general(a, b, (dims, ((), ())), preferred_element_type=F32)


def norm_parts(values):
    center = values - jnp.mean(values, axis=-1, keepdims=True)
    spread = jnp.mean(center * center, axis=-1, keepdims=True)
    scale = lax.rsqrt(spread + EPSILON)
    return center * scale, scale


def norm_back(upstream, unit, scale, gain):
    inner = upstream * gain
    first = jnp.mean(inner, axis=-1, keepdims=True)
    second = jnp.mean(inner * unit, axis=-1, keepdims=True)
    return scale * (inner - first - unit * second)


def keep_rows(values, count):
    index = lax.broadcasted_iota(jnp.int32, values.shape, 0)
    return jnp.where(index < count, values, 0.0)


def both(meta, short, long):
    pl.when(meta[0] == 0)(short)
    pl.when(meta[0] == 1)(long)


def split(rows, features):
    return pltpu.VMEM((features // LANE, rows, LANE), F32)


def put(ref, start, values, stride=1):
    count = values.shape[0]
    where = pl.ds(start, count) if stride == 1 else pl.ds(start, count, stride=stride)
    for c in range(ref.shape[0]):
        ref[c, where, :] = values[:, c * LANE : (c + 1) * LANE]


def get(ref, start, count, stride=1):
    where = pl.ds(start, count) if stride == 1 else pl.ds(start, count, stride=stride)
    return jnp.concatenate([ref[c, where, :] for c in range(ref.shape[0])], axis=1)


def split(rows, features):
    return pltpu.VMEM((features // LANE, rows, LANE), F32)


def put(ref, start, values, stride=1):
    count = values.shape[0]
    where = pl.ds(start, count) if stride == 1 else pl.ds(start, count, stride=stride)
    for c in range(ref.shape[0]):
        ref[c, where, :] = values[:, c * LANE : (c + 1) * LANE]


def get(ref, start, count, stride=1):
    where = pl.ds(start, count) if stride == 1 else pl.ds(start, count, stride=stride)
    return jnp.concatenate([ref[c, where, :] for c in range(ref.shape[0])], axis=1)


def pack_taps(plan, b, stage, first, packed):
    k, n = plan.factors[b], plan.steps[b]
    blocks = plan.features // LANE
    for i in range(plan.line_taps[b]):
        for c in range(blocks):
            at = (i * blocks + c) * n
            packed[at : at + n, :] = stage[c, pl.ds(first + i, n, stride=k), :]


def unpack_taps(plan, b, packed, stage, first):
    k, n = plan.factors[b], plan.steps[b]
    blocks = plan.features // LANE
    for i in range(plan.line_taps[b]):
        for c in range(blocks):
            at = (i * blocks + c) * n
            stage[c, pl.ds(first + i, n, stride=k), :] = packed[at : at + n, :]


def packed_matrix(plan, b, packed, base, matrix):
    n = plan.steps[b]
    for g in range(plan.line_taps[b] * plan.features // LANE):
        matrix[base : base + n, g * LANE : (g + 1) * LANE] = packed[g * n : (g + 1) * n, :]


def matrix_packed(plan, b, matrix, base, packed):
    n = plan.steps[b]
    for g in range(plan.line_taps[b] * plan.features // LANE):
        packed[g * n : (g + 1) * n, :] = matrix[base : base + n, g * LANE : (g + 1) * LANE]


def fetch_quarter(plan, b, meta_ref, sources, target, sems):
    own = plan.down_rows[b]
    quad = meta_ref[7]
    copies = []
    for v, source in enumerate(sources):
        start = pl.multiple_of((quad ^ v) * own, LANE)
        copies.append(
            pltpu.make_async_copy(
                source.at[pl.ds(0, own)], target.at[pl.ds(start, own)], sems.at[v]
            )
        )
    for copy in copies:
        copy.start()
    return copies


def total_of(parts):
    total = parts[0][...].astype(F32)
    for piece in parts[1:]:
        total = total + piece[...].astype(F32)
    return total


def prep_blocks(plan, meta, series):
    length, features, line = plan.length, plan.features, plan.line

    def kernel(meta_ref, x_ref, out_ref, wide, packed):
        def run(b):
            margin = plan.factors[b] // 2
            wide[...] = jnp.zeros_like(wide)
            put(wide, margin, x_ref[...].astype(F32))
            packed[...] = jnp.zeros_like(packed)
            for z in range(line):
                pack_taps(plan, b, wide, z * plan.line_taps[b], packed)
                out_ref[z ^ meta_ref[5]] = packed[...].astype(BF)

        both(meta_ref, lambda: run(0), lambda: run(1))

    return call(
        kernel,
        [SMEM] + vmem(1),
        [((line, plan.pack, LANE), BF)],
        [split(plan.stage_rows, features), pltpu.VMEM((plan.pack, LANE), F32)],
        moved=2 * length * features * 2,
        limit=8,
    )(meta, series)[0]


def down_partial(plan, meta, blocks, quarter):
    rows, features, line = plan.rows, plan.features, plan.line
    wide_max = 4 * plan.down_max

    def kernel(meta_ref, *refs):
        packs, weights = refs[:line], refs[line : line + 4]
        keep_ref, send_ref, *col_refs = refs[line + 4 : line + 10]
        weight, wide, packed, cols, sems = refs[line + 10 :]

        def run(b):
            copies = fetch_quarter(plan, b, meta_ref, weights, weight, sems)
            own = plan.down_rows[b]
            wide[...] = jnp.zeros_like(wide)
            for m in range(line):
                packed[...] = packs[m][...].astype(F32)
                packed_matrix(plan, b, packed, m * rows, wide)
            matrix = wide[...].astype(BF)
            for u in range(4):
                piece = matrix[:, u * own : (u + 1) * own]
                if own < plan.down_max:
                    pad = jnp.zeros((line * rows, plan.down_max - own), BF)
                    piece = jnp.concatenate([piece, pad], axis=1)
                cols[u ^ meta_ref[7]] = piece
            for v in range(4):
                col_refs[v][...] = cols[v]
            for copy in copies:
                copy.wait()
            part = dot(matrix[:, : 4 * own], weight[0 : 4 * own, :])
            keep_ref[...] = part[:rows]
            for m in range(1, line):
                send_ref[m - 1] = part[m * rows : (m + 1) * rows].astype(BF)

        both(meta_ref, lambda: run(0), lambda: run(1))

    return call(
        kernel,
        [SMEM] + vmem(line) + [ANY] * 4,
        [
            ((rows, features), F32),
            ((line - 1, rows, features), BF),
        ]
        + [((line * rows, plan.down_max), BF)] * 4,
        [
            pltpu.VMEM((wide_max, features), BF),
            pltpu.VMEM((line * rows, wide_max), F32),
            pltpu.VMEM((plan.pack, LANE), F32),
            pltpu.VMEM((4, line * rows, plan.down_max), BF),
            pltpu.SemaphoreType.DMA((4,)),
        ],
        flops=2 * line * rows * features * wide_max,
        moved=5 << 20,
        limit=16,
    )(meta, *blocks, *quarter)


def low_rows(plan, meta, pieces, biases):
    rows, features = plan.rows, plan.features

    def kernel(meta_ref, *refs):
        parts, bias_ref, low_ref, act_ref = refs[:-3], refs[-3], refs[-2], refs[-1]
        act = keep_rows(jnp.tanh(total_of(parts) + bias_ref[0:1, :]), meta_ref[4])
        act_ref[...] = act
        low_ref[...] = act.astype(BF)

    return call(
        kernel,
        [SMEM] + vmem(len(pieces) + 1),
        [((rows, features), BF), ((rows, features), F32)],
        [],
        moved=1 << 19,
        limit=4,
    )(meta, *pieces, biases)


def time_major(plan, halves, stage, target, lead):
    shards, rows = plan.shards, plan.rows
    half = shards // 2
    for q in range(shards):
        put(stage, q, halves[q // half][q % half].astype(F32), shards)
    body = shards * rows
    if lead:
        target[0 : lead * shards, :] = jnp.zeros((lead * shards, target.shape[1]), BF)
    target[lead * shards : lead * shards + body, :] = get(stage, 0, body).astype(BF)
    rest = target.shape[0] - lead * shards - body
    if rest:
        target[lead * shards + body :, :] = jnp.zeros((rest, target.shape[1]), BF)


def pad_weight(plan, b, meta_ref, source, target, sem):
    width, own, end = target.shape[1], plan.iso_rows[b], plan.taps[b] * target.shape[1]
    target[0:width, :] = jnp.zeros((width, width), BF)
    target[own:end, :] = jnp.zeros((end - own, width), BF)
    shift = pl.multiple_of(meta_ref[3], 16)
    copy = pltpu.make_async_copy(source, target.at[pl.ds(shift, plan.iso_rows[b])], sem)
    copy.start()
    return copy


def iso_partial(plan, meta, halves, w_short, w_long, backward):
    shards, rows, features = plan.shards, plan.rows, plan.features
    half = shards // 2
    extra = plan.taps_max + 2
    buffer = (max(plan.steps) + rows + extra) * shards

    def kernel(
        meta_ref, even_ref, odd_ref, ws_ref, wl_ref, keep_ref, send_ref, stage, lined, padded, sem
    ):
        first = meta_ref[2]

        def run(b, w_ref):
            n, taps = plan.steps[b], plan.taps[b]
            copy = pad_weight(plan, b, meta_ref, w_ref, padded, sem)
            lead = extra if backward else n - 1
            time_major(plan, (even_ref, odd_ref), stage, lined, lead)
            copy.wait()
            for m in range(taps):
                start = extra + n - 1 - first - m if backward else first + m
                start = pl.multiple_of(start * shards, 16)
                window = lined[pl.ds(start, rows * shards), :]
                weight = padded[m * features : (m + 1) * features, :]
                part = dot(window, weight, ((1,), (1,)) if backward else ((1,), (0,)))
                total = part if m == 0 else total + part
            put(stage, 0, total)
            for q in range(shards):
                piece = get(stage, q, rows, shards)
                if q < half:
                    keep_ref[q] = piece
                else:
                    send_ref[q - half] = piece.astype(BF)

        both(meta_ref, lambda: run(0, ws_ref), lambda: run(1, wl_ref))

    return call(
        kernel,
        [SMEM] + vmem(2) + [HBM] * 2,
        [((half, rows, features), F32), ((half, rows, features), BF)],
        [
            split(rows * shards, features),
            pltpu.VMEM((buffer, features), BF),
            pltpu.VMEM((plan.taps_max * features, features), BF),
            pltpu.SemaphoreType.DMA,
        ],
        flops=2 * shards * rows * features * features * plan.taps_max,
        moved=10 << 20,
        limit=56 if backward else 26,
    )(meta, *halves, w_short, w_long)


def iso_weight(plan, meta, b, low_own, low_other, delta_own, delta_other):
    shards, rows, features = plan.shards, plan.rows, plan.features
    half = shards // 2
    n, taps, own = plan.steps[b], plan.taps[b], plan.iso_rows[b]
    buffer = (n - 1 + rows + taps + 1) * shards

    def kernel(meta_ref, *refs):
        lows, deltas = refs[0:4], refs[4:8]
        grad_ref, sum_ref, stage, lined, delta, total, ordered = refs[8:]
        me = meta_ref[1]

        def load(low, steps):
            for q in range(shards):
                ordered[pl.ds(me ^ plan.mask(q), 1), :] = jnp.sum(
                    steps[q // half][q % half].astype(F32), axis=0, keepdims=True
                )
            time_major(plan, steps, stage, delta, 0)
            time_major(plan, low, stage, lined, n - 1)

        pl.when(meta_ref[0] == b)(lambda: load(lows[0:2], deltas[0:2]))
        pl.when(meta_ref[0] != b)(lambda: load(lows[2:4], deltas[2:4]))
        sum_ref[...] = jnp.sum(ordered[...], axis=0, keepdims=True)
        flat = me * own
        first = flat // features
        for m in range(taps):
            start = pl.multiple_of((first + m) * shards, 16)
            window = lined[pl.ds(start, rows * shards), :]
            total[m * features : (m + 1) * features, :] = dot(window, delta[...], ((0,), (0,)))
        shift = pl.multiple_of(flat % features, 16)
        grad_ref[...] = total[pl.ds(shift, own), :]

    return call(
        kernel,
        [SMEM] + vmem(8),
        [((own, features), F32), ((1, features), F32)],
        [
            split(rows * shards, features),
            pltpu.VMEM((buffer, features), BF),
            pltpu.VMEM((rows * shards, features), BF),
            pltpu.VMEM((taps * features, features), F32),
            pltpu.VMEM((shards, features), F32),
        ],
        flops=2 * shards * rows * features * features * taps,
        moved=10 << 20,
        limit=32,
    )(meta, *low_own, *low_other, *delta_own, *delta_other)


def inner_rows(plan, meta, pieces, low, biases, gain):
    rows, features = plan.rows, plan.features

    def kernel(meta_ref, *refs):
        parts = refs[:-5]
        low_ref, bias_ref, gain_ref, inner_ref, act_ref = refs[-5:]
        act = jnp.tanh(total_of(parts) + bias_ref[1:2, :])
        act_ref[...] = act
        unit, _ = norm_parts(act + low_ref[...].astype(F32))
        inner = unit * gain_ref[...] + bias_ref[3:4, :]
        inner_ref[...] = keep_rows(inner, meta_ref[4]).astype(BF)

    return call(
        kernel,
        [SMEM] + vmem(len(pieces) + 3),
        [((rows, features), BF), ((rows, features), F32)],
        [],
        moved=1 << 19,
        limit=4,
    )(meta, *pieces, low, biases, gain)


def trans_forward(plan, meta, inners, quarter):
    rows, features, line = plan.rows, plan.features, plan.line
    wide_max = 4 * plan.down_max

    def kernel(meta_ref, *refs):
        inner_refs, weights = refs[:line], refs[line : line + 4]
        out_ref, weight, wide, packed, sems = refs[line + 4 :]

        def run(b):
            copies = fetch_quarter(plan, b, meta_ref, weights, weight, sems)
            lhs = jnp.concatenate([ref[...] for ref in inner_refs], axis=0)
            for copy in copies:
                copy.wait()
            for i in range(plan.line_taps[b]):
                wide[:, i * features : (i + 1) * features] = dot(
                    lhs, weight[i * features : (i + 1) * features, :]
                )
            packed[...] = jnp.zeros_like(packed)
            for m in range(line):
                matrix_packed(plan, b, wide, m * rows, packed)
                out_ref[m] = packed[...].astype(BF)

        both(meta_ref, lambda: run(0), lambda: run(1))

    return call(
        kernel,
        [SMEM] + vmem(line) + [ANY] * 4,
        [((line, plan.pack, LANE), BF)],
        [
            pltpu.VMEM((wide_max, features), BF),
            pltpu.VMEM((line * rows, wide_max), F32),
            pltpu.VMEM((plan.pack, LANE), F32),
            pltpu.SemaphoreType.DMA((4,)),
        ],
        flops=2 * line * rows * features * wide_max,
        moved=4 << 20,
        limit=16,
    )(meta, *inners, *quarter)[0]


def outer_rows(plan, meta, packs, series, biases, gain):
    features, length, line = plan.features, plan.length, plan.line
    half_rows = length // 2

    def kernel(meta_ref, *refs):
        pack_refs = refs[:line]
        x_ref, bias_ref, gain_ref, keep_ref, send_ref, act_ref, stage, packed = refs[line:]

        def run(b):
            for m in range(line):
                packed[...] = pack_refs[m][...].astype(F32)
                unpack_taps(plan, b, packed, stage, (meta_ref[5] ^ m) * plan.line_taps[b])

        both(meta_ref, lambda: run(0), lambda: run(1))
        act = jnp.tanh(get(stage, 0, length) + bias_ref[2:3, :])
        act_ref[...] = act
        unit, _ = norm_parts(act + x_ref[...].astype(F32))
        put(stage, 0, unit * gain_ref[...] + bias_ref[3:4, :])
        mine = pl.multiple_of(meta_ref[0] * half_rows, 8)
        other = pl.multiple_of((1 - meta_ref[0]) * half_rows, 8)
        keep_ref[...] = get(stage, mine, half_rows).astype(BF)
        send_ref[...] = get(stage, other, half_rows).astype(BF)

    return call(
        kernel,
        [SMEM] + vmem(line + 3),
        [((half_rows, features), BF), ((half_rows, features), BF), ((length, features), F32)],
        [split(plan.stage_rows, features), pltpu.VMEM((plan.pack, LANE), F32)],
        moved=6 << 20,
        limit=16,
    )(meta, *packs, series, biases, gain)


def outer_backward(plan, meta, up_keep, up_recv, series, act, gain):
    features, length, line = plan.features, plan.length, plan.line
    half_rows = length // 2

    def kernel(
        meta_ref, uk_ref, ur_ref, x_ref, act_ref, gain_ref,
        outer_ref, taps_ref, vec_ref, stage, upstream, packed,
    ):
        mine = pl.multiple_of(meta_ref[0] * half_rows, 8)
        other = pl.multiple_of((1 - meta_ref[0]) * half_rows, 8)
        upstream[pl.ds(mine, half_rows), :] = uk_ref[...].astype(F32)
        upstream[pl.ds(other, half_rows), :] = ur_ref[...].astype(F32)
        act_value = act_ref[...]
        unit, scale = norm_parts(act_value + x_ref[...].astype(F32))
        above = upstream[...]
        vec_ref[...] = jnp.zeros_like(vec_ref)
        vec_ref[1:2, :] = jnp.sum(above, axis=0, keepdims=True)
        vec_ref[2:3, :] = jnp.sum(above * unit, axis=0, keepdims=True)
        outer = norm_back(above, unit, scale, gain_ref[...])
        outer_ref[...] = outer
        delta = (outer * (1.0 - act_value * act_value)).astype(BF).astype(F32)
        vec_ref[0:1, :] = jnp.sum(delta, axis=0, keepdims=True)
        put(stage, 0, delta)
        put(stage, length, jnp.zeros((plan.stage_rows - length, features), F32))
        packed[...] = jnp.zeros_like(packed)

        def run(b):
            for m in range(line):
                pack_taps(plan, b, stage, (meta_ref[5] ^ m) * plan.line_taps[b], packed)
                taps_ref[m] = packed[...].astype(BF)

        both(meta_ref, lambda: run(0), lambda: run(1))

    return call(
        kernel,
        [SMEM] + vmem(5),
        [((length, features), F32), ((line, plan.pack, LANE), BF), ((8, features), F32)],
        [
            split(plan.stage_rows, features),
            pltpu.VMEM((length, features), F32),
            pltpu.VMEM((plan.pack, LANE), F32),
        ],
        moved=8 << 20,
        limit=20,
    )(meta, up_keep, up_recv, series, act, gain)


def trans_backward(plan, meta, packs, quarter):
    rows, features, line = plan.rows, plan.features, plan.line
    wide_max = 4 * plan.down_max

    def kernel(meta_ref, *refs):
        pack_refs, weights = refs[:line], refs[line : line + 4]
        keep_ref, send_ref, wide_ref, weight, wide, packed, sems = refs[line + 4 :]

        def run(b):
            copies = fetch_quarter(plan, b, meta_ref, weights, weight, sems)
            wide[...] = jnp.zeros_like(wide)
            for m in range(line):
                packed[...] = pack_refs[m][...].astype(F32)
                packed_matrix(plan, b, packed, m * rows, wide)
            matrix = wide[...].astype(BF)
            wide_ref[...] = matrix
            for copy in copies:
                copy.wait()
            for i in range(plan.line_taps[b]):
                part = dot(
                    matrix[:, i * features : (i + 1) * features],
                    weight[i * features : (i + 1) * features, :],
                    ((1,), (1,)),
                )
                total = part if i == 0 else total + part
            keep_ref[...] = total[:rows]
            for m in range(1, line):
                send_ref[m - 1] = total[m * rows : (m + 1) * rows].astype(BF)

        both(meta_ref, lambda: run(0), lambda: run(1))

    return call(
        kernel,
        [SMEM] + vmem(line) + [ANY] * 4,
        [
            ((rows, features), F32),
            ((line - 1, rows, features), BF),
            ((line * rows, wide_max), BF),
        ],
        [
            pltpu.VMEM((wide_max, features), BF),
            pltpu.VMEM((line * rows, wide_max), F32),
            pltpu.VMEM((plan.pack, LANE), F32),
            pltpu.SemaphoreType.DMA((4,)),
        ],
        flops=2 * line * rows * features * wide_max,
        moved=5 << 20,
        limit=16,
    )(meta, *packs, *quarter)


def trans_weight(plan, meta, inners, wide):
    rows, features, line = plan.rows, plan.features, plan.line
    most = plan.down_max

    def kernel(meta_ref, *refs):
        inner_refs = refs[:line]
        wide_ref, keep_ref, send_ref, total = refs[line:]

        def run(b):
            own = plan.down_rows[b]
            lhs = jnp.concatenate([ref[...] for ref in inner_refs], axis=0)
            for i in range(plan.line_taps[b]):
                total[i * features : (i + 1) * features, :] = dot(
                    lhs, wide_ref[:, i * features : (i + 1) * features], ((0,), (0,))
                )
            for v in range(4):
                start = pl.multiple_of((meta_ref[7] ^ v) * own, LANE)
                piece = total[pl.ds(start, own), :]
                if own < most:
                    pad = jnp.zeros((most - own, features), F32)
                    piece = jnp.concatenate([piece, pad], axis=0)
                if v % 2 == 0:
                    keep_ref[v // 2] = piece
                else:
                    send_ref[v // 2] = piece.astype(BF)

        both(meta_ref, lambda: run(0), lambda: run(1))

    return call(
        kernel,
        [SMEM] + vmem(line + 1),
        [((2, most, features), F32), ((2, most, features), BF)],
        [pltpu.VMEM((4 * most, features), F32)],
        flops=2 * line * rows * features * 4 * most,
        moved=5 << 20,
        limit=20,
    )(meta, *inners, wide)


def inner_backward(plan, meta, pieces, low, act, vectors, gain):
    rows, features = plan.rows, plan.features

    def kernel(meta_ref, *refs):
        parts = refs[:-7]
        low_ref, act_ref, vec_ref, gain_ref, delta_ref, back_ref, out_ref = refs[-7:]
        total = keep_rows(total_of(parts), meta_ref[4])
        act_in = act_ref[...]
        unit, scale = norm_parts(act_in + low_ref[...].astype(F32))
        out_ref[...] = vec_ref[...]
        out_ref[1:2, :] = vec_ref[1:2, :] + jnp.sum(total, axis=0, keepdims=True)
        out_ref[2:3, :] = vec_ref[2:3, :] + jnp.sum(total * unit, axis=0, keepdims=True)
        back = norm_back(total, unit, scale, gain_ref[...])
        back_ref[...] = back
        delta_ref[...] = keep_rows(back * (1.0 - act_in * act_in), meta_ref[4]).astype(BF)

    return call(
        kernel,
        [SMEM] + vmem(len(pieces) + 4),
        [((rows, features), BF), ((rows, features), F32), ((8, features), F32)],
        [],
        moved=1 << 19,
        limit=6,
    )(meta, *pieces, low, act, vectors, gain)


def down_delta(plan, meta, pieces, delta_inner, act, small):
    rows, features = plan.rows, plan.features
    base, extra = up8(rows, 16), small.shape[0]

    def kernel(meta_ref, *refs):
        parts = refs[:-4]
        inner_ref, act_ref, small_ref, out_ref = refs[-4:]
        value = act_ref[...]
        total = total_of(parts) + inner_ref[...]
        delta = keep_rows(total * (1.0 - value * value), meta_ref[4])
        pad = jnp.zeros((base - rows, features), F32)
        out_ref[0:base, :] = jnp.concatenate([delta, pad], axis=0).astype(BF)
        high = small_ref[...].astype(BF)
        out_ref[base : base + extra, :] = high
        out_ref[base + extra :, :] = (small_ref[...] - high.astype(F32)).astype(BF)

    return call(
        kernel,
        [SMEM] + vmem(len(pieces) + 3),
        [((base + 2 * extra, features), BF)],
        [],
        moved=1 << 19,
        limit=8,
    )(meta, *pieces, delta_inner, act, small)[0]


def input_quarter(plan, meta, deltas, quarter):
    features, line = plan.features, plan.line
    rows = up8(plan.rows, 16)
    wide_max = 4 * plan.down_max

    def kernel(meta_ref, *refs):
        delta_refs, weights = refs[:line], refs[line : line + 4]
        out_ref, weight, wide, packed, sems = refs[line + 4 :]

        def run(b):
            copies = fetch_quarter(plan, b, meta_ref, weights, weight, sems)
            lhs = jnp.concatenate([ref[0:rows, :] for ref in delta_refs], axis=0)
            for copy in copies:
                copy.wait()
            for i in range(plan.line_taps[b]):
                wide[:, i * features : (i + 1) * features] = dot(
                    lhs, weight[i * features : (i + 1) * features, :], ((1,), (1,))
                )
            packed[...] = jnp.zeros_like(packed)
            for m in range(line):
                matrix_packed(plan, b, wide, m * rows, packed)
                out_ref[m] = packed[...].astype(BF)

        both(meta_ref, lambda: run(0), lambda: run(1))

    return call(
        kernel,
        [SMEM] + vmem(line) + [ANY] * 4,
        [((line, plan.pack, LANE), BF)],
        [
            pltpu.VMEM((wide_max, features), BF),
            pltpu.VMEM((line * rows, wide_max), F32),
            pltpu.VMEM((plan.pack, LANE), F32),
            pltpu.SemaphoreType.DMA((4,)),
        ],
        flops=2 * line * rows * features * wide_max,
        moved=4 << 20,
        limit=16,
    )(meta, *deltas, *quarter)[0]


def input_rows(plan, meta, packs, outer):
    features, length, line = plan.features, plan.length, plan.line

    def kernel(meta_ref, *refs):
        pack_refs = refs[:line]
        outer_ref, out_ref, stage, packed = refs[line:]

        def run(b):
            for m in range(line):
                packed[...] = pack_refs[m][...].astype(F32)
                unpack_taps(plan, b, packed, stage, (meta_ref[5] ^ m) * plan.line_taps[b])
            inner = get(stage, plan.factors[b] // 2, length)
            out_ref[...] = (inner + outer_ref[...]).astype(BF)

        both(meta_ref, lambda: run(0), lambda: run(1))

    return call(
        kernel,
        [SMEM] + vmem(line + 1),
        [((length, features), BF)],
        [split(plan.stage_rows, features), pltpu.VMEM((plan.pack, LANE), F32)],
        moved=3 << 20,
        limit=12,
    )(meta, *packs, outer)[0]


def down_weight(plan, meta, columns, even, odd, extra, loss_part):
    shards, rows, features, line = plan.shards, plan.rows, plan.features, plan.line
    half = shards // 2
    base = up8(rows, 16)
    most, tail = plan.down_max, up8(extra + 2, 16)

    def kernel(meta_ref, *refs):
        col_refs = refs[:4]
        even_ref, odd_ref, loss_ref, grad_ref, sums_ref, delta, ordered, small = refs[4:]
        me = meta_ref[1]
        for q in range(shards):
            source = (even_ref, odd_ref)[q // half]
            value = source[q % half, 0:base, :].astype(F32)
            at = me ^ plan.mask(q)
            ordered[pl.ds(at, 1), :] = jnp.sum(value, axis=0, keepdims=True)
            delta[q * rows : (q + 1) * rows, :] = value[:rows]
            high = source[q % half, base : base + extra, :].astype(F32)
            low = source[q % half, base + extra : base + 2 * extra, :].astype(F32)
            small[at] = high + low
        total = small[0]
        for i in range(1, shards):
            total = total + small[i]
        sums_ref[...] = jnp.zeros_like(sums_ref)
        sums_ref[0:extra, :] = total
        sums_ref[extra : extra + 1, :] = jnp.sum(ordered[...], axis=0, keepdims=True)
        sums_ref[extra + 1 : extra + 2, :] = jnp.broadcast_to(loss_ref[0:1, 0:1], (1, features))
        sums = sums_ref[...]
        high = sums.astype(BF)
        low = (sums - high.astype(F32)).astype(BF)
        grad_ref[most : most + tail, :] = high
        grad_ref[most + tail :, :] = low
        sums_ref[...] = high.astype(F32) + low.astype(F32)
        for at, v in enumerate((0, 2, 1, 3)):
            steps = delta[at * line * rows : (at + 1) * line * rows, :].astype(BF)
            part = dot(col_refs[v][...], steps, ((0,), (0,)))
            total = part if at == 0 else total + part
        grad_ref[0:most, :] = total.astype(BF)

    return call(
        kernel,
        [SMEM] + vmem(7),
        [((most + 2 * tail, features), BF), ((tail, features), F32)],
        [
            pltpu.VMEM((shards * rows, features), F32),
            pltpu.VMEM((shards, features), F32),
            pltpu.VMEM((shards, extra, features), F32),
        ],
        flops=2 * shards * rows * features * features,
        moved=4 << 20,
        limit=20,
    )(meta, *columns, even, odd, loss_part)


def finish(plan, meta, own, recv, mine, iso_sums, extra, ff_parts):
    features, most, tail = plan.features, plan.down_max, mine.shape[0]
    rows = plan.down_rows

    def kernel(
        meta_ref, own_ref, recv_ref, mine_ref, short_sum, long_sum,
        short_ref, long_ref, bias_ref, gain_ref, head_bias_ref, head_gain_ref, ff_ref, loss_ref,
    ):
        theirs = recv_ref[most : most + tail, :].astype(F32) + recv_ref[most + tail :, :].astype(F32)
        sums = mine_ref[...]
        total = sums + theirs
        first = 6 + ff_parts
        bias_ref[0, 1:2, :] = short_sum[...]
        bias_ref[1, 1:2, :] = long_sum[...]
        for b in range(2):
            bias_ref[b, 2:4, :] = total[first + 3 * b : first + 3 * b + 2]
            gain_ref[b : b + 1, :] = total[first + 3 * b + 2 : first + 3 * b + 3]
        head_bias_ref[...] = total[0:4]
        head_gain_ref[...] = total[4:6]
        ff_ref[...] = total[6 : 6 + ff_parts]
        loss_ref[...] = total[extra + 1 : extra + 2, 0:LANE] * (0.5 / (features * plan.length))

        def place(short_from, long_from, short_row, long_row):
            short_ref[...] = short_from[0 : rows[0], :].astype(F32)
            long_ref[...] = long_from[0 : rows[1], :].astype(F32)
            bias_ref[0, 0:1, :] = short_row[extra : extra + 1]
            bias_ref[1, 0:1, :] = long_row[extra : extra + 1]

        both(
            meta_ref,
            lambda: place(own_ref, recv_ref, sums, theirs),
            lambda: place(recv_ref, own_ref, theirs, sums),
        )

    return call(
        kernel,
        [SMEM] + vmem(5),
        [
            ((rows[0], features), F32),
            ((rows[1], features), F32),
            ((2, 4, features), F32),
            ((2, features), F32),
            ((4, features), F32),
            ((2, features), F32),
            ((ff_parts, features), F32),
            ((1, LANE), F32),
        ],
        [],
        moved=4 << 20,
        limit=12,
    )(meta, own, recv, mine, *iso_sums)


def natural_order(plan, meta, own, halves):
    shards = plan.shards
    half = shards // 2
    rows, features = own

    def kernel(meta_ref, even_ref, odd_ref, out_ref):
        for q in range(shards):
            out_ref[meta_ref[1] ^ plan.mask(q)] = (even_ref, odd_ref)[q // half][q % half].astype(
                F32
            )

    return call(
        kernel,
        [SMEM] + vmem(2),
        [((shards, rows, features), F32)],
        [],
        moved=3 << 20,
        limit=16,
    )(meta, *halves)[0]


ROOT_HALF = 0.7071067811865476
ROOT_TWO_PI = 0.3989422804014327


def head_rows(plan, meta, keep, recv, target, valid, merge, bias, gain, ff_in, ff_bias, ff_out):
    half_rows, features = keep.shape
    hidden = ff_in.shape[1]
    parts = hidden // features
    dims = (half_rows, features)

    def kernel(
        meta_ref, keep_ref, recv_ref, target_ref, valid_ref, merge_ref, bias_ref, gain_ref,
        in_bias_ref, in_hbm, out_hbm,
        out_ref, up_keep_ref, up_send_ref, normed_ref, act_ref, pre_delta_ref, ff_delta_ref,
        merged_delta_ref, vec_ref, loss_ref, slope_ref, in_ref, out_w_ref, sems,
    ):
        fetch_in = pltpu.make_async_copy(in_hbm, in_ref, sems.at[0])
        fetch_out = pltpu.make_async_copy(out_hbm, out_w_ref, sems.at[1])
        fetch_in.start()
        fetch_out.start()
        branch = meta_ref[0]
        merged = dot(keep_ref[...], merge_ref[branch]) + dot(recv_ref[...], merge_ref[1 - branch])
        merged = merged + bias_ref[0:1, :]
        unit, scale = norm_parts(merged)
        normed = (unit * gain_ref[0:1, :] + bias_ref[2:3, :]).astype(BF)
        normed_ref[...] = normed
        fetch_in.wait()
        fetch_out.wait()
        for c in range(parts):
            cols = slice(c * features, (c + 1) * features)
            pre = dot(normed, in_ref[:, cols]) + in_bias_ref[:, cols]
            share = 0.5 * (1.0 + lax.erf(pre * ROOT_HALF))
            slope_ref[:, cols] = share + pre * (jnp.exp(-0.5 * pre * pre) * ROOT_TWO_PI)
            act = (pre * share).astype(BF)
            act_ref[:, cols] = act
            part = dot(act, out_w_ref[cols, :])
            total = part if c == 0 else total + part
        unit_end, scale_end = norm_parts(merged + total + bias_ref[1:2, :])
        final = unit_end * gain_ref[1:2, :] + bias_ref[3:4, :]
        out_ref[...] = final.astype(BF)
        error = final - target_ref[...].astype(F32)
        weighted = valid_ref[...] * error
        loss = jnp.sum(jnp.sum(weighted * error, axis=0, keepdims=True), axis=1, keepdims=True)
        loss_ref[...] = jnp.broadcast_to(loss, loss_ref.shape)
        vec_ref[...] = jnp.zeros_like(vec_ref)
        vec_ref[3:4, :] = jnp.sum(weighted, axis=0, keepdims=True)
        vec_ref[5:6, :] = jnp.sum(weighted * unit_end, axis=0, keepdims=True)
        delta_sum = norm_back(weighted, unit_end, scale_end, gain_ref[1:2, :])
        delta_ff = delta_sum.astype(BF)
        ff_delta_ref[...] = delta_ff
        vec_ref[1:2, :] = jnp.sum(delta_ff.astype(F32), axis=0, keepdims=True)
        for c in range(parts):
            cols = slice(c * features, (c + 1) * features)
            pre_delta = dot(delta_ff, out_w_ref[cols, :], ((1,), (1,))) * slope_ref[:, cols]
            pre_delta = pre_delta.astype(BF)
            pre_delta_ref[:, cols] = pre_delta
            vec_ref[6 + c : 7 + c, :] = jnp.sum(pre_delta.astype(F32), axis=0, keepdims=True)
            part = dot(pre_delta, in_ref[:, cols], ((1,), (1,)))
            above = part if c == 0 else above + part
        vec_ref[2:3, :] = jnp.sum(above, axis=0, keepdims=True)
        vec_ref[4:5, :] = jnp.sum(above * unit, axis=0, keepdims=True)
        delta = norm_back(above, unit, scale, gain_ref[0:1, :]) + delta_sum
        delta = delta.astype(BF)
        merged_delta_ref[...] = delta
        vec_ref[0:1, :] = jnp.sum(delta.astype(F32), axis=0, keepdims=True)
        up_keep_ref[...] = dot(delta, merge_ref[branch], ((1,), (1,))).astype(BF)
        up_send_ref[...] = dot(delta, merge_ref[1 - branch], ((1,), (1,))).astype(BF)

    vec_rows = up8(6 + parts + 6)
    return call(
        kernel,
        [SMEM] + vmem(8) + [HBM] * 2,
        [
            (dims, BF), (dims, BF), (dims, BF), (dims, BF),
            ((half_rows, hidden), BF), ((half_rows, hidden), BF), (dims, BF), (dims, BF),
            ((vec_rows, features), F32), ((8, LANE), F32),
        ],
        [
            pltpu.VMEM((half_rows, hidden), F32),
            pltpu.VMEM((features, hidden), BF),
            pltpu.VMEM((hidden, features), BF),
            pltpu.SemaphoreType.DMA((2,)),
        ],
        flops=10 * half_rows * features * hidden,
        moved=14 << 20,
        limit=56,
    )(meta, keep, recv, target, valid, merge, bias, gain, ff_bias, ff_in, ff_out)


def head_weights(plan, meta, keep, recv, normed, act, pre_delta, ff_delta, merged_delta):
    shards = plan.shards
    half_rows, features = keep.shape
    hidden = act.shape[1]
    ff_rows, merge_rows = hidden // shards // 2, features // shards
    parts = hidden // features
    own = 2 * ff_rows + merge_rows

    def kernel(
        meta_ref, keep_hbm, recv_hbm, normed_hbm, act_hbm, pre_hbm, ff_hbm, merged_hbm,
        stay_near, stay_far, send_near, send_far, first, second, third,
        keep_ref, recv_ref, normed_ref, act_ref, pre_ref, ff_ref, merged_ref, sems,
    ):
        pairs = (
            (normed_hbm, normed_ref), (pre_hbm, pre_ref), (ff_hbm, ff_ref), (act_hbm, act_ref),
            (merged_hbm, merged_ref), (keep_hbm, keep_ref), (recv_hbm, recv_ref),
        )
        copies = [
            pltpu.make_async_copy(source, target, sems.at[i])
            for i, (source, target) in enumerate(pairs)
        ]
        for copy in copies:
            copy.start()
        branch = meta_ref[0]
        copies[0].wait()
        copies[1].wait()
        for c in range(parts):
            cols = slice(c * features, (c + 1) * features)
            first[cols, :] = dot(pre_ref[:, cols], normed_ref[...], ((0,), (0,))).astype(BF)
        copies[2].wait()
        copies[3].wait()
        for c in range(parts):
            cols = slice(c * features, (c + 1) * features)
            second[cols, :] = dot(act_ref[:, cols], ff_ref[...], ((0,), (0,))).astype(BF)
        for copy in copies[4:]:
            copy.wait()
        for side, ref in enumerate((keep_ref, recv_ref)):
            part = dot(ref[...], merged_ref[...], ((0,), (0,))).astype(BF)
            start = pl.multiple_of((branch ^ side) * features, 16)
            third[pl.ds(start, features), :] = part
        for q in range(shards):
            device = meta_ref[1] ^ plan.mask(q)
            targets = (stay_near, stay_far, send_near, send_far)
            target = targets[q // plan.line]
            for h in range(2):
                at = 2 * device + (branch ^ h)
                for start, count, source in (
                    (0, ff_rows, first),
                    (ff_rows, ff_rows, second),
                    (2 * ff_rows, merge_rows, third),
                ):
                    rows = pl.ds(pl.multiple_of(at * count, 16), count)
                    target[h, q % plan.line, start : start + count, :] = source[rows, :]

    return call(
        kernel,
        [SMEM] + [HBM] * 7,
        [((2, plan.line, own, features), BF)] * 4,
        [
            pltpu.VMEM((hidden, features), BF),
            pltpu.VMEM((hidden, features), BF),
            pltpu.VMEM((2 * features, features), BF),
        ]
        + [
            pltpu.VMEM(ref.shape, BF)
            for ref in (keep, recv, normed, act, pre_delta, ff_delta, merged_delta)
        ]
        + [pltpu.SemaphoreType.DMA((7,))],
        flops=4 * half_rows * features * hidden,
        moved=12 << 20,
        limit=56,
    )(meta, keep, recv, normed, act, pre_delta, ff_delta, merged_delta)


def hop(values, distance, shards):
    return lax.ppermute(values, "series", [(i, i ^ distance) for i in range(shards)])


def swap(values):
    return lax.ppermute(values, "branch", [(0, 1), (1, 0)])


def after(value, *others):
    return lax.optimization_barrier((value, others))[0]


def along_line(plan, own):
    return [own] + [hop(own, i << 2, plan.shards) for i in range(1, plan.line)]


def line_parts(plan, first, rest):
    return [first] + [hop(rest[i - 1], i << 2, plan.shards) for i in range(1, plan.line)]


def quad_gather(plan, own, later):
    side = hop(own, 2, plan.shards)
    return [own, hop(own, 1, plan.shards), side, hop(after(side, later), 1, plan.shards)]


def settle(value, *others):
    return lax.optimization_barrier((value,) + others)


def stacked(pieces):
    count, shape = len(pieces), pieces[0].shape

    def kernel(*refs):
        for i in range(count):
            refs[count][i] = refs[i][...]

    return call(kernel, vmem(count), [((count,) + shape, BF)], [], moved=1 << 20, limit=6)(*pieces)[0]


def gather_slots(plan, line, stack=jnp.stack):
    even = stack(line + [hop(value, 2, plan.shards) for value in line])
    return even, hop(even, 1, plan.shards)


def scatter_sum(plan, keep, send, *others):
    shards, line = plan.shards, plan.line
    first = keep + hop(send, 1, shards).astype(F32)
    second = first[:line] + hop(first[line:].astype(BF), 2, shards).astype(F32)
    if others:
        second, *others = settle(second, *others)
    pieces = line_parts(plan, second[0], [second[i].astype(BF) for i in range(1, line)])
    return (pieces, *others) if others else pieces


def rounded(values):
    return lax.reduce_precision(values, exponent_bits=8, mantissa_bits=7)


def layer_norm(values, gain_row, shift_row):
    center = values - jnp.mean(values, axis=-1, keepdims=True)
    spread = jnp.mean(center * center, axis=-1, keepdims=True)
    return center * lax.rsqrt(spread + EPSILON) * gain_row + shift_row


def gelu_exact(values):
    return jax.nn.gelu(values, approximate=False)


def product(a, b):
    return jnp.dot(a, b, preferred_element_type=F32)


def left_product(a, b):
    return jnp.einsum("mi,mo->io", a, b, preferred_element_type=F32)


def right_product(a, b):
    return jnp.einsum("mo,io->mi", a, b, preferred_element_type=F32)


def body(
    series_in, target, horizons, observed,
    down_short, iso_short, trans_short, down_long, iso_long, trans_long,
    branch_bias, branch_gain, merge_weight, head_bias, head_gain, ff_in, ff_in_bias, ff_out,
):
    shards = lax.axis_size("series")
    _, length, features = series_in.shape
    plan = Plan(
        shards,
        length,
        features,
        (down_short.shape[0], down_long.shape[0]),
        (iso_short.shape[0], iso_long.shape[0]),
    )
    line = plan.line
    half_rows = length // 2
    branch = lax.axis_index("branch")
    me = lax.axis_index("series")
    is_short = branch == 0
    iso_rows = jnp.where(is_short, plan.iso_rows[0], plan.iso_rows[1])
    meta = jnp.stack(
        [
            branch,
            me,
            (me * iso_rows) // features,
            (me * iso_rows) % features,
            jnp.where(is_short, plan.steps[0], plan.steps[1]),
            me // 4,
            me % 2,
            me % 4,
        ]
    ).astype(jnp.int32)
    series = series_in[0]
    biases, gain = branch_bias[0], branch_gain

    def chosen(short, long):
        rows = max(short.shape[0], long.shape[0])
        short = jnp.pad(short, ((0, rows - short.shape[0]), (0, 0)))
        long = jnp.pad(long, ((0, rows - long.shape[0]), (0, 0)))
        return jnp.where(is_short, short, long)

    def placed(own, other, b, rows):
        return jnp.where(branch == b, own, other)[:rows].astype(F32)

    blocks = prep_blocks(plan, meta, series)
    own_down = after(chosen(down_short, down_long), blocks)
    blocks = line_parts(plan, blocks[0], [blocks[i] for i in range(1, line)])
    down_quarter = quad_gather(plan, own_down, blocks)
    own_trans = after(chosen(trans_short, trans_long), blocks)
    keep, send, *columns = down_partial(plan, meta, blocks, down_quarter)
    pieces = line_parts(plan, keep, send)
    trans_quarter = quad_gather(plan, own_trans, pieces)
    low, act_down = low_rows(plan, meta, pieces, biases)
    low_own = gather_slots(plan, along_line(plan, low), stacked)
    low_own, trans_quarter = settle(low_own, trans_quarter)
    keep, send = iso_partial(plan, meta, low_own, iso_short, iso_long, False)
    low_other = swap(after(low_own[0], low_own[1]))
    pieces = scatter_sum(plan, keep, send)
    inner, act_iso = inner_rows(plan, meta, pieces, low, biases, gain)
    columns[2] = hop(after(columns[2], inner), 2, shards)
    inners, columns = settle(along_line(plan, inner), columns)
    packs = trans_forward(plan, meta, inners, trans_quarter)
    columns[3] = hop(after(columns[3], packs), 3, shards)
    packs = line_parts(plan, packs[0], [packs[i] for i in range(1, line)])
    packs, columns, low_other = settle(packs, columns, low_other)
    out_keep, out_send, act_trans = outer_rows(plan, meta, packs, series, biases, gain)
    out_recv = swap(out_send)
    columns[1] = hop(after(columns[1], out_keep), 1, shards)
    low_other = (low_other, hop(after(low_other, out_keep), 1, shards))
    out_recv, columns, low_other = settle(out_recv, columns, low_other)

    positions = branch * half_rows + jnp.arange(half_rows, dtype=jnp.int32)
    observed_half = lax.dynamic_slice_in_dim(observed[0], branch * half_rows, half_rows, 0)
    valid = (
        observed_half.astype(F32)
        * (positions >= SEQ_IN).astype(F32)
        * (positions < SEQ_IN + horizons[0]).astype(F32)
    )
    (
        out, up_keep, up_send, normed, act_ff, pre_delta, ff_delta, merged_delta, vec_head, loss_part
    ) = head_rows(
        plan, meta, out_keep, out_recv, target[0], valid[:, None], merge_weight, head_bias,
        head_gain, ff_in, ff_in_bias[None], ff_out,
    )
    up_recv = swap(up_send)
    near, far, near_send, far_send = head_weights(
        plan, meta, out_keep, out_recv, normed, act_ff, pre_delta, ff_delta, merged_delta
    )

    far_recv = hop(after(far_send, up_recv), 1, shards)
    outer, packs, vectors = outer_backward(plan, meta, up_keep, up_recv, series, act_trans, gain)
    far = (far.astype(F32) + after(far_recv, packs).astype(F32)).astype(BF)
    near_recv = hop(after(near_send, packs), 1, shards)
    share_recv = hop(far, 2, shards)
    packs = line_parts(plan, packs[0], [packs[i] for i in range(1, line)])
    keep, send, wide = trans_backward(plan, meta, packs, trans_quarter)
    trans_keep, trans_send = trans_weight(plan, meta, inners, wide)
    pieces, trans_send, share_recv, near_recv = settle(
        line_parts(plan, keep, send), trans_send, share_recv, near_recv
    )
    shares = near.astype(F32) + near_recv.astype(F32) + share_recv.astype(F32)
    share_recv = swap(shares[1].astype(BF))
    shares = shares[0]
    delta_iso, delta_inner, vectors = inner_backward(
        plan, meta, pieces, low, act_iso, vectors, gain
    )
    ff_parts = ff_in_bias.shape[0] // features
    selector = jnp.stack([is_short, branch == 1]).astype(F32)
    branch_rows = (selector[:, None, None] * vectors[None, 0:3]).reshape(6, features)
    small = jnp.concatenate([vec_head[: 6 + ff_parts], branch_rows], axis=0)
    count = small.shape[0]
    small = jnp.pad(small, ((0, up8(count, 16) - count), (0, 0)))
    trans_recv = hop(trans_send, 1, shards)
    deltas, trans_recv = settle(along_line(plan, delta_iso), trans_recv)
    trans_sum = trans_keep + trans_recv.astype(F32)
    trans_next = trans_sum[1].astype(BF)
    delta_own = gather_slots(plan, deltas)
    delta_own, trans_next, share_recv = settle(delta_own, trans_next, share_recv)
    shares = shares + share_recv.astype(F32)
    spread = line // 2
    share_recv = hop(shares[spread:].astype(BF), 4 * spread, shards)
    keep, send = iso_partial(plan, meta, delta_own, iso_short, iso_long, True)
    delta_other = swap(delta_own[0])
    pieces, delta_other = scatter_sum(plan, keep, send, delta_other)
    pieces, share_recv = settle(pieces, share_recv)
    shares = shares[:spread] + share_recv.astype(F32)
    payload = down_delta(plan, meta, pieces, delta_inner, act_down, small)
    delta_other = (delta_other, hop(after(delta_other, payload), 1, shards))
    trans_recv = hop(after(trans_next, payload), 2, shards)
    share_recv = hop(after(shares[1:].astype(BF), payload), 4, shards)
    first_grad = iso_weight(plan, meta, 0, low_own, low_other, delta_own, delta_other)
    deltas, trans_recv, share_recv, first_grad = settle(
        along_line(plan, payload), trans_recv, share_recv, first_grad
    )
    shares = rounded(shares[0] + share_recv[0].astype(F32))
    grad_trans = (trans_sum[0] + trans_recv.astype(F32)).astype(BF)
    packs = input_quarter(plan, meta, deltas, down_quarter)
    even = jnp.stack(deltas)
    odd = hop(after(even, packs), 2, shards)
    packs = line_parts(plan, packs[0], [packs[i] for i in range(1, line)])
    crossing = swap(after(jnp.concatenate([grad_trans, shares.astype(BF)], axis=0), odd))
    second_grad = iso_weight(
        plan, meta, 1, after(low_own, odd), low_other, delta_own, delta_other
    )
    packs, second_grad = settle(packs, second_grad)
    input_own = input_rows(plan, meta, packs, outer)
    input_own, crossing = settle(input_own, crossing)
    trans_recv, share_recv = crossing[: plan.down_max], crossing[plan.down_max :]
    input_recv = swap(input_own)
    even = jnp.concatenate([even, odd], axis=0)
    delta_halves = (even, hop(after(even, input_own), 1, shards))
    share_recv = share_recv.astype(F32)
    ff_rows = ff_in_bias.shape[0] // shards // 2
    halves = [
        jnp.where(is_short, shares, share_recv),
        jnp.where(is_short, share_recv, shares),
    ]
    merge_own = jnp.concatenate([half[2 * ff_rows :] for half in halves], axis=0)
    extra = small.shape[0]
    grad_down, mine = down_weight(
        plan, meta, columns, *after(delta_halves, input_own), extra, loss_part
    )
    down_recv = swap(grad_down)
    merge_even = jnp.stack(along_line(plan, after(merge_own.astype(BF), delta_halves[1])))
    merge_odd = hop(after(merge_even, grad_down), 2, shards)
    trans_grads = [placed(grad_trans, trans_recv, b, plan.down_rows[b]) for b in range(2)]
    merge_odd, trans_grads = settle(merge_odd, trans_grads)
    merge_even = jnp.concatenate([merge_even, merge_odd], axis=0)
    merge_core = hop(merge_even, 1, shards)
    input_total = input_own.astype(F32) + after(input_recv, merge_odd).astype(F32)
    merge_core, input_total = settle(merge_core, input_total)
    merge_total = natural_order(
        plan, meta, merge_own.shape, (merge_even, merge_core)
    ).reshape(2, features, features)
    down_recv = after(down_recv, merge_total)
    short_down, long_down, bias_total, gain_total, head_sums, head_gains, ff_sums, loss = finish(
        plan, meta, grad_down, down_recv, mine, [first_grad[1], second_grad[1]], extra, ff_parts
    )
    return (
        out[None],
        loss[0, 0:1],
        input_total[None],
        short_down,
        first_grad[0],
        trans_grads[0],
        long_down,
        second_grad[0],
        trans_grads[1],
        bias_total,
        gain_total,
        merge_total,
        head_sums,
        head_gains,
        jnp.concatenate([half[:ff_rows] for half in halves], axis=0).T,
        ff_sums.reshape(-1),
        jnp.concatenate([half[ff_rows : 2 * ff_rows] for half in halves], axis=0),
    )


def fitted(matrix, row_total):
    return jnp.pad(matrix, ((0, row_total - matrix.shape[0]), (0, 0)))


def unpack(gathered_all, shards, rows_max, rows_own):
    features = gathered_all.shape[1]
    return gathered_all.reshape(shards, rows_max, features)[:, :rows_own].reshape(
        shards * rows_own, features
    )


def repack(gradient, shards, rows_max):
    rows_own = gradient.shape[0] // shards
    shaped = gradient.reshape(shards, rows_own, gradient.shape[1])
    return jnp.pad(shaped, ((0, 0), (0, rows_max - rows_own), (0, 0))).reshape(
        shards * rows_max, gradient.shape[1]
    )


def branch_pass(series_in, weights, shards, rows_max, biases, gain_row, factor):
    series_count, length, features = series_in.shape
    step_count = (length + factor) // factor
    margin = factor // 2
    weight_down = unpack(weights[0], shards, rows_max[0], factor * features // shards)
    weight_iso = unpack(weights[1], shards, rows_max[1], step_count * features // shards)
    weight_trans = unpack(weights[2], shards, rows_max[2], factor * features // shards).reshape(
        factor, features, features
    )
    blocks = jnp.pad(series_in, ((0, 0), (margin, step_count * factor - length - margin), (0, 0)))
    blocks = blocks.reshape(series_count * step_count, factor * features)
    act_down = jnp.tanh(product(blocks, weight_down) + biases[0])
    low_down = act_down.astype(jnp.bfloat16)
    padded = jnp.concatenate(
        [
            jnp.zeros((series_count, step_count - 1, features), jnp.bfloat16),
            low_down.reshape(series_count, step_count, features),
        ],
        axis=1,
    )
    unfolded = jnp.concatenate(
        [padded[:, offset : offset + step_count] for offset in range(step_count)], axis=2
    )
    unfolded = unfolded.reshape(series_count * step_count, step_count * features)
    act_iso = jnp.tanh(product(unfolded, weight_iso) + biases[1])
    inner_norm, inner_back = jax.vjp(
        layer_norm, act_iso + low_down.astype(jnp.float32), gain_row, biases[3]
    )
    low_inner = inner_norm.astype(jnp.bfloat16)
    spread_out = jnp.einsum(
        "mi,jio->mjo", low_inner, weight_trans, preferred_element_type=jnp.float32
    )
    act_trans = jnp.tanh(
        spread_out.reshape(series_count, step_count * factor, features)[:, :length] + biases[2]
    )
    result, outer_back = jax.vjp(
        layer_norm, act_trans + series_in.astype(jnp.float32), gain_row, biases[3]
    )
    stored = (
        blocks,
        weight_down,
        weight_iso,
        weight_trans,
        act_down,
        unfolded,
        act_iso,
        inner_back,
        low_inner,
        act_trans,
        outer_back,
    )
    return (result, stored)


def branch_back(series_in, weights, shards, rows_max, biases, gain_row, factor, upstream):
    series_count, length, features = series_in.shape
    step_count = (length + factor) // factor
    margin = factor // 2
    result, stored = branch_pass(series_in, weights, shards, rows_max, biases, gain_row, factor)
    (
        blocks,
        weight_down,
        weight_iso,
        weight_trans,
        act_down,
        unfolded,
        act_iso,
        inner_back,
        low_inner,
        act_trans,
        outer_back,
    ) = stored
    delta_outer, gain_outer, shift_outer = outer_back(upstream)
    delta_trans = (delta_outer * (1.0 - act_trans * act_trans)).astype(jnp.bfloat16)
    trans_blocks = jnp.pad(delta_trans, ((0, 0), (0, step_count * factor - length), (0, 0)))
    trans_blocks = trans_blocks.reshape(series_count * step_count, factor, features)
    grad_trans = jnp.einsum(
        "mi,mjo->jio", low_inner, trans_blocks, preferred_element_type=jnp.float32
    )
    grad_trans = grad_trans.reshape(factor * features, features)
    inner_upstream = jnp.einsum(
        "mjo,jio->mi", trans_blocks, weight_trans, preferred_element_type=jnp.float32
    )
    delta_inner, gain_inner, shift_inner = inner_back(inner_upstream)
    delta_iso = (delta_inner * (1.0 - act_iso * act_iso)).astype(jnp.bfloat16)
    grad_iso = left_product(unfolded, delta_iso)
    delta_unfold = right_product(delta_iso, weight_iso).reshape(
        series_count, step_count, step_count, features
    )
    delta_padded = jnp.zeros((series_count, 2 * step_count - 1, features), jnp.float32)
    for offset in range(step_count):
        delta_padded = delta_padded.at[:, offset : offset + step_count].add(
            delta_unfold[:, :, offset]
        )
    delta_low = (
        delta_padded[:, step_count - 1 :].reshape(series_count * step_count, features) + delta_inner
    )
    delta_down = (delta_low * (1.0 - act_down * act_down)).astype(jnp.bfloat16)
    grad_down = left_product(blocks, delta_down)
    delta_blocks = right_product(delta_down, weight_down).reshape(
        series_count, step_count * factor, features
    )
    delta_series = delta_blocks[:, margin : margin + length] + delta_outer
    vectors = jnp.stack(
        [
            jnp.sum(delta_down.astype(jnp.float32), axis=0),
            jnp.sum(delta_iso.astype(jnp.float32), axis=0),
            jnp.sum(delta_trans.astype(jnp.float32), axis=(0, 1)),
            shift_inner + shift_outer,
        ]
    )
    padded_grads = (
        repack(grad_down, shards, rows_max[0]),
        repack(grad_iso, shards, rows_max[1]),
        repack(grad_trans, shards, rows_max[2]),
    )
    return (delta_series, padded_grads, vectors, gain_inner + gain_outer)


def plain_body(
    series_in,
    target,
    horizons,
    observed,
    down_short,
    iso_short,
    trans_short,
    down_long,
    iso_long,
    trans_long,
    branch_bias,
    branch_gain,
    merge_weight,
    head_bias,
    head_gain,
    ff_in,
    ff_in_bias,
    ff_out,
):
    branch_index = lax.axis_index("branch")
    shards = lax.axis_size("series")
    series_count, length, features = series_in.shape
    rows_max = (
        max(down_short.shape[0], down_long.shape[0]),
        max(iso_short.shape[0], iso_long.shape[0]),
        max(trans_short.shape[0], trans_long.shape[0]),
    )
    is_short = branch_index == 0
    own_down = jnp.where(is_short, fitted(down_short, rows_max[0]), fitted(down_long, rows_max[0]))
    own_iso = jnp.where(is_short, fitted(iso_short, rows_max[1]), fitted(iso_long, rows_max[1]))
    own_trans = jnp.where(
        is_short, fitted(trans_short, rows_max[2]), fitted(trans_long, rows_max[2])
    )
    gathered = (
        lax.all_gather(own_down, "series", axis=0, tiled=True),
        lax.all_gather(own_iso, "series", axis=0, tiled=True),
        lax.all_gather(own_trans, "series", axis=0, tiled=True),
    )
    biases = branch_bias[0]
    gain_row = branch_gain[0]

    def forward_with(factor):
        return lambda: branch_pass(series_in, gathered, shards, rows_max, biases, gain_row, factor)[
            0
        ].astype(jnp.bfloat16)

    branch_out = lax.cond(is_short, forward_with(SCALE_S), forward_with(SCALE_L))
    received = lax.all_to_all(
        branch_out.reshape(series_count, length, 1, features),
        "branch",
        split_axis=1,
        concat_axis=2,
        tiled=True,
    )
    half_rows = received.shape[1]
    merge_rows = received.reshape(series_count * half_rows, 2 * features)
    merge_flat = merge_weight.reshape(2 * features, features)
    merged = product(merge_rows, merge_flat) + head_bias[0]
    normed, first_back = jax.vjp(layer_norm, merged, head_gain[0], head_bias[2])
    low_normed = normed.astype(jnp.bfloat16)
    pre_ff = product(low_normed, ff_in) + ff_in_bias
    activated, gelu_back = jax.vjp(gelu_exact, pre_ff)
    low_act = activated.astype(jnp.bfloat16)
    ff_result = product(low_act, ff_out) + head_bias[1]
    final_out, second_back = jax.vjp(layer_norm, merged + ff_result, head_gain[1], head_bias[3])
    final_rows = final_out.reshape(series_count, half_rows, features)
    positions = branch_index * half_rows + jnp.arange(half_rows, dtype=jnp.int32)
    observed_half = lax.dynamic_slice_in_dim(observed, branch_index * half_rows, half_rows, 1)
    valid_mask = (
        observed_half.astype(jnp.float32)
        * (positions >= SEQ_IN).astype(jnp.float32)
        * (positions < SEQ_IN + horizons[:, None]).astype(jnp.float32)
    )
    error_rows = final_rows - target.astype(jnp.float32)
    weighted = valid_mask[:, :, None] * error_rows
    series_part = 0.5 * jnp.sum(weighted * error_rows, axis=(1, 2)) / (features * length)
    delta_sum, gain_second, shift_second = second_back(
        weighted.reshape(series_count * half_rows, features)
    )
    delta_ff = delta_sum.astype(jnp.bfloat16)
    grad_ff_out = left_product(low_act, delta_ff)
    delta_act = right_product(delta_ff, ff_out)
    (delta_pre,) = gelu_back(delta_act)
    low_pre = delta_pre.astype(jnp.bfloat16)
    grad_ff_in = left_product(low_normed, low_pre)
    delta_normed = right_product(low_pre, ff_in)
    delta_first, gain_first, shift_first = first_back(delta_normed)
    delta_merged = (delta_first + delta_sum).astype(jnp.bfloat16)
    grad_merge = left_product(merge_rows, delta_merged).reshape(2, features, features)
    delta_rows = (
        right_product(delta_merged, merge_flat)
        .astype(jnp.bfloat16)
        .reshape(series_count, half_rows, 2, features)
    )
    back_rows = lax.all_to_all(delta_rows, "branch", split_axis=2, concat_axis=1, tiled=True)
    upstream = back_rows.astype(jnp.float32).reshape(series_count, length, features)
    ff_shares = (
        lax.psum_scatter(grad_ff_in, "series", scatter_dimension=1, tiled=True),
        lax.psum_scatter(grad_ff_out, "series", scatter_dimension=0, tiled=True),
    )
    weights_back = (
        lax.all_gather(own_down, "series", axis=0, tiled=True),
        lax.all_gather(own_iso, "series", axis=0, tiled=True),
        lax.all_gather(own_trans, "series", axis=0, tiled=True),
    )

    def backward_with(factor):
        return lambda: branch_back(
            series_in, weights_back, shards, rows_max, biases, gain_row, factor, upstream
        )

    delta_series, padded_grads, vectors, gain_grad = lax.cond(
        is_short, backward_with(SCALE_S), backward_with(SCALE_L)
    )
    reduced = (
        lax.psum_scatter(padded_grads[0], "series", scatter_dimension=0, tiled=True),
        lax.psum_scatter(padded_grads[1], "series", scatter_dimension=0, tiled=True),
        lax.psum_scatter(padded_grads[2], "series", scatter_dimension=0, tiled=True),
    )
    short_flag = is_short.astype(jnp.float32)
    long_flag = 1.0 - short_flag
    summed = (
        lax.psum(delta_series.astype(jnp.bfloat16), "branch").astype(jnp.float32),
        lax.psum(series_part.astype(jnp.bfloat16), "branch").astype(jnp.float32),
        lax.psum(
            (short_flag * reduced[0][: down_short.shape[0]]).astype(jnp.bfloat16), "branch"
        ).astype(jnp.float32),
        lax.psum((short_flag * reduced[1]).astype(jnp.bfloat16), "branch").astype(jnp.float32),
        lax.psum(
            (short_flag * reduced[2][: trans_short.shape[0]]).astype(jnp.bfloat16), "branch"
        ).astype(jnp.float32),
        lax.psum((long_flag * reduced[0]).astype(jnp.bfloat16), "branch").astype(jnp.float32),
        lax.psum(
            (long_flag * reduced[1][: iso_long.shape[0]]).astype(jnp.bfloat16), "branch"
        ).astype(jnp.float32),
        lax.psum((long_flag * reduced[2]).astype(jnp.bfloat16), "branch").astype(jnp.float32),
        lax.psum(ff_shares[0].astype(jnp.bfloat16), "branch").astype(jnp.float32),
        lax.psum(ff_shares[1].astype(jnp.bfloat16), "branch").astype(jnp.float32),
    )
    selector = (jnp.arange(2, dtype=jnp.int32) == branch_index).astype(jnp.float32)
    full_bias = selector[:, None, None] * vectors[None]
    full_gain = selector[:, None] * gain_grad[None]
    head_vectors = jnp.stack(
        [
            jnp.sum(delta_merged.astype(jnp.float32), axis=0),
            jnp.sum(delta_ff.astype(jnp.float32), axis=0),
            shift_first,
            shift_second,
        ]
    )
    head_gains = jnp.stack([gain_first, gain_second])
    ff_bias_grad = jnp.sum(low_pre.astype(jnp.float32), axis=0)
    totals = lax.psum(
        (grad_merge, head_vectors, head_gains, ff_bias_grad, full_bias, full_gain),
        ("branch", "series"),
    )
    return (
        final_rows.astype(jnp.bfloat16),
        summed[1],
        summed[0],
        summed[2],
        summed[3],
        summed[4],
        summed[5],
        summed[6],
        summed[7],
        totals[4],
        totals[5],
        totals[0],
        totals[1],
        totals[2],
        summed[8],
        totals[3],
        summed[9],
    )


def solution(mesh):
    placed = (
        P("series", None, None),
        P("series", "branch", None),
        P("series"),
        P("series", None),
        P("series", None),
        P("series", None),
        P("series", None),
        P("series", None),
        P("series", None),
        P("series", None),
        P("branch", None, None),
        P("branch", None),
        P(),
        P(),
        P(),
        P(),
        P(),
        P(),
    )

    def run(*args):
        shards = mesh.shape["series"]
        features = args[0].shape[2]
        down_rows = [args[i].shape[0] // shards for i in (4, 7)]
        iso_rows = [args[i].shape[0] // shards for i in (5, 8)]
        fits = (
            args[0].shape[0] == shards
            and shards == 16
            and shards & (shards - 1) == 0
            and all(r % LANE == 0 and r <= features and 4 * r % features == 0 for r in down_rows)
            and all(r % 16 == 0 for r in iso_rows)
        )
        return jax.shard_map(
            body if fits else plain_body,
            mesh=mesh,
            in_specs=placed,
            out_specs=(
                P("series", "branch", None),
                P("series"),
                P("series", None, None),
                P("series", None),
                P("series", None),
                P("series", None),
                P("series", None),
                P("series", None),
                P("series", None),
                P(),
                P(),
                P(),
                P(),
                P(),
                P(None, "series"),
                P(),
                P("series", None),
            ),
            check_vma=False,
        )(*args)

    return run
```

```python
import functools

import jax
import jax.numpy as jnp
from jax import lax
from jax.experimental import pallas as pl
from jax.experimental.pallas import tpu as pltpu
from jax.sharding import PartitionSpec as P

SCALE_S = 12
SCALE_L = 16
SEQ_IN = 96
EPSILON = 1e-05
LANE = 128

BF = jnp.bfloat16
F32 = jnp.float32


def up8(count, base=8):
    return -(-count // base) * base


class Plan:
    def __init__(self, shards, length, features, down_rows, iso_rows):
        self.shards, self.length, self.features = shards, length, features
        self.factors = (SCALE_S, SCALE_L)
        self.steps = tuple((length + k) // k for k in self.factors)
        self.rows = up8(max(self.steps))
        self.down_rows = down_rows
        self.iso_rows = iso_rows
        self.down_max, self.iso_max = max(down_rows), max(iso_rows)
        self.line = shards // 4
        self.line_taps = tuple(4 * r // features for r in down_rows)
        blocks = features // LANE
        self.pack = up8(max(t * blocks * n for t, n in zip(self.line_taps, self.steps)), 16)
        self.taps = tuple(
            max(-(-((d * r) % features + r) // features) for d in range(shards)) for r in iso_rows
        )
        self.taps_max = max(self.taps)
        self.stage_rows = max(k * up8(n) for k, n in zip(self.factors, self.steps))

    def mask(self, slot):
        core, rest = divmod(slot, 2 * self.line)
        side, line = divmod(rest, self.line)
        return core | (side << 1) | (line << 2)


def vmem(count):
    return [pl.BlockSpec(memory_space=pltpu.VMEM) for _ in range(count)]


SMEM = pl.BlockSpec(memory_space=pltpu.SMEM)
ANY = pl.BlockSpec(memory_space=pl.ANY)
HBM = pl.BlockSpec(memory_space=pltpu.HBM)


def call(body, in_specs, outs, scratch, flops=0, moved=0, limit=56):
    return pl.pallas_call(
        body,
        out_shape=[jax.ShapeDtypeStruct(s, d) for s, d in outs],
        in_specs=in_specs,
        out_specs=vmem(len(outs)),
        scratch_shapes=scratch,
        compiler_params=pltpu.CompilerParams(vmem_limit_bytes=limit << 20),
        cost_estimate=pl.CostEstimate(flops=flops, bytes_accessed=moved, transcendentals=0),
    )


def dot(a, b, dims=((1,), (0,))):
    return lax.dot_general(a, b, (dims, ((), ())), preferred_element_type=F32)


def norm_parts(values):
    center = values - jnp.mean(values, axis=-1, keepdims=True)
    spread = jnp.mean(center * center, axis=-1, keepdims=True)
    scale = lax.rsqrt(spread + EPSILON)
    return center * scale, scale


def norm_back(upstream, unit, scale, gain):
    inner = upstream * gain
    first = jnp.mean(inner, axis=-1, keepdims=True)
    second = jnp.mean(inner * unit, axis=-1, keepdims=True)
    return scale * (inner - first - unit * second)


def keep_rows(values, count):
    index = lax.broadcasted_iota(jnp.int32, values.shape, 0)
    return jnp.where(index < count, values, 0.0)


def both(meta, short, long):
    pl.when(meta[0] == 0)(short)
    pl.when(meta[0] == 1)(long)


def split(rows, features):
    return pltpu.VMEM((features // LANE, rows, LANE), F32)


def put(ref, start, values, stride=1):
    count = values.shape[0]
    where = pl.ds(start, count) if stride == 1 else pl.ds(start, count, stride=stride)
    for c in range(ref.shape[0]):
        ref[c, where, :] = values[:, c * LANE : (c + 1) * LANE]


def get(ref, start, count, stride=1):
    where = pl.ds(start, count) if stride == 1 else pl.ds(start, count, stride=stride)
    return jnp.concatenate([ref[c, where, :] for c in range(ref.shape[0])], axis=1)


def split(rows, features):
    return pltpu.VMEM((features // LANE, rows, LANE), F32)


def put(ref, start, values, stride=1):
    count = values.shape[0]
    where = pl.ds(start, count) if stride == 1 else pl.ds(start, count, stride=stride)
    for c in range(ref.shape[0]):
        ref[c, where, :] = values[:, c * LANE : (c + 1) * LANE]


def get(ref, start, count, stride=1):
    where = pl.ds(start, count) if stride == 1 else pl.ds(start, count, stride=stride)
    return jnp.concatenate([ref[c, where, :] for c in range(ref.shape[0])], axis=1)


def pack_taps(plan, b, stage, first, packed):
    k, n = plan.factors[b], plan.steps[b]
    blocks = plan.features // LANE
    for i in range(plan.line_taps[b]):
        for c in range(blocks):
            at = (i * blocks + c) * n
            packed[at : at + n, :] = stage[c, pl.ds(first + i, n, stride=k), :]


def unpack_taps(plan, b, packed, stage, first):
    k, n = plan.factors[b], plan.steps[b]
    blocks = plan.features // LANE
    for i in range(plan.line_taps[b]):
        for c in range(blocks):
            at = (i * blocks + c) * n
            stage[c, pl.ds(first + i, n, stride=k), :] = packed[at : at + n, :]


def packed_matrix(plan, b, packed, base, matrix):
    n = plan.steps[b]
    for g in range(plan.line_taps[b] * plan.features // LANE):
        matrix[base : base + n, g * LANE : (g + 1) * LANE] = packed[g * n : (g + 1) * n, :]


def matrix_packed(plan, b, matrix, base, packed):
    n = plan.steps[b]
    for g in range(plan.line_taps[b] * plan.features // LANE):
        packed[g * n : (g + 1) * n, :] = matrix[base : base + n, g * LANE : (g + 1) * LANE]


def fetch_quarter(plan, b, meta_ref, sources, target, sems):
    own = plan.down_rows[b]
    quad = meta_ref[7]
    copies = []
    for v, source in enumerate(sources):
        start = pl.multiple_of((quad ^ v) * own, LANE)
        copies.append(
            pltpu.make_async_copy(
                source.at[pl.ds(0, own)], target.at[pl.ds(start, own)], sems.at[v]
            )
        )
    for copy in copies:
        copy.start()
    return copies


def total_of(parts):
    total = parts[0][...].astype(F32)
    for piece in parts[1:]:
        total = total + piece[...].astype(F32)
    return total


def prep_blocks(plan, meta, series):
    length, features, line = plan.length, plan.features, plan.line

    def kernel(meta_ref, x_ref, out_ref, wide, packed):
        def run(b):
            margin = plan.factors[b] // 2
            wide[...] = jnp.zeros_like(wide)
            put(wide, margin, x_ref[...].astype(F32))
            packed[...] = jnp.zeros_like(packed)
            for z in range(line):
                pack_taps(plan, b, wide, z * plan.line_taps[b], packed)
                out_ref[z ^ meta_ref[5]] = packed[...].astype(BF)

        both(meta_ref, lambda: run(0), lambda: run(1))

    return call(
        kernel,
        [SMEM] + vmem(1),
        [((line, plan.pack, LANE), BF)],
        [split(plan.stage_rows, features), pltpu.VMEM((plan.pack, LANE), F32)],
        moved=2 * length * features * 2,
        limit=8,
    )(meta, series)[0]


def down_partial(plan, meta, blocks, quarter):
    rows, features, line = plan.rows, plan.features, plan.line
    wide_max = 4 * plan.down_max

    def kernel(meta_ref, *refs):
        packs, weights = refs[:line], refs[line : line + 4]
        keep_ref, send_ref, *col_refs = refs[line + 4 : line + 10]
        weight, wide, packed, cols, sems = refs[line + 10 :]

        def run(b):
            copies = fetch_quarter(plan, b, meta_ref, weights, weight, sems)
            own = plan.down_rows[b]
            wide[...] = jnp.zeros_like(wide)
            for m in range(line):
                packed[...] = packs[m][...].astype(F32)
                packed_matrix(plan, b, packed, m * rows, wide)
            matrix = wide[...].astype(BF)
            for u in range(4):
                piece = matrix[:, u * own : (u + 1) * own]
                if own < plan.down_max:
                    pad = jnp.zeros((line * rows, plan.down_max - own), BF)
                    piece = jnp.concatenate([piece, pad], axis=1)
                cols[u ^ meta_ref[7]] = piece
            for v in range(4):
                col_refs[v][...] = cols[v]
            for copy in copies:
                copy.wait()
            part = dot(matrix[:, : 4 * own], weight[0 : 4 * own, :])
            keep_ref[...] = part[:rows]
            for m in range(1, line):
                send_ref[m - 1] = part[m * rows : (m + 1) * rows].astype(BF)

        both(meta_ref, lambda: run(0), lambda: run(1))

    return call(
        kernel,
        [SMEM] + vmem(line) + [ANY] * 4,
        [
            ((rows, features), F32),
            ((line - 1, rows, features), BF),
        ]
        + [((line * rows, plan.down_max), BF)] * 4,
        [
            pltpu.VMEM((wide_max, features), BF),
            pltpu.VMEM((line * rows, wide_max), F32),
            pltpu.VMEM((plan.pack, LANE), F32),
            pltpu.VMEM((4, line * rows, plan.down_max), BF),
            pltpu.SemaphoreType.DMA((4,)),
        ],
        flops=2 * line * rows * features * wide_max,
        moved=5 << 20,
        limit=16,
    )(meta, *blocks, *quarter)


def low_rows(plan, meta, pieces, biases):
    rows, features = plan.rows, plan.features

    def kernel(meta_ref, *refs):
        parts, bias_ref, low_ref, act_ref = refs[:-3], refs[-3], refs[-2], refs[-1]
        act = keep_rows(jnp.tanh(total_of(parts) + bias_ref[0:1, :]), meta_ref[4])
        act_ref[...] = act
        low_ref[...] = act.astype(BF)

    return call(
        kernel,
        [SMEM] + vmem(len(pieces) + 1),
        [((rows, features), BF), ((rows, features), F32)],
        [],
        moved=1 << 19,
        limit=4,
    )(meta, *pieces, biases)


def time_major(plan, halves, stage, target, lead):
    shards, rows = plan.shards, plan.rows
    half = shards // 2
    for q in range(shards):
        put(stage, q, halves[q // half][q % half].astype(F32), shards)
    body = shards * rows
    if lead:
        target[0 : lead * shards, :] = jnp.zeros((lead * shards, target.shape[1]), BF)
    target[lead * shards : lead * shards + body, :] = get(stage, 0, body).astype(BF)
    rest = target.shape[0] - lead * shards - body
    if rest:
        target[lead * shards + body :, :] = jnp.zeros((rest, target.shape[1]), BF)


def pad_weight(plan, b, meta_ref, source, target, sem):
    width, own, end = target.shape[1], plan.iso_rows[b], plan.taps[b] * target.shape[1]
    target[0:width, :] = jnp.zeros((width, width), BF)
    target[own:end, :] = jnp.zeros((end - own, width), BF)
    shift = pl.multiple_of(meta_ref[3], 16)
    copy = pltpu.make_async_copy(source, target.at[pl.ds(shift, plan.iso_rows[b])], sem)
    copy.start()
    return copy


def iso_partial(plan, meta, halves, w_short, w_long, backward):
    shards, rows, features = plan.shards, plan.rows, plan.features
    half = shards // 2
    extra = plan.taps_max + 2
    buffer = (max(plan.steps) + rows + extra) * shards

    def kernel(
        meta_ref, even_ref, odd_ref, ws_ref, wl_ref, keep_ref, send_ref, stage, lined, padded, sem
    ):
        first = meta_ref[2]

        def run(b, w_ref):
            n, taps = plan.steps[b], plan.taps[b]
            copy = pad_weight(plan, b, meta_ref, w_ref, padded, sem)
            lead = extra if backward else n - 1
            time_major(plan, (even_ref, odd_ref), stage, lined, lead)
            copy.wait()
            for m in range(taps):
                start = extra + n - 1 - first - m if backward else first + m
                start = pl.multiple_of(start * shards, 16)
                window = lined[pl.ds(start, rows * shards), :]
                weight = padded[m * features : (m + 1) * features, :]
                part = dot(window, weight, ((1,), (1,)) if backward else ((1,), (0,)))
                total = part if m == 0 else total + part
            put(stage, 0, total)
            for q in range(shards):
                piece = get(stage, q, rows, shards)
                if q < half:
                    keep_ref[q] = piece
                else:
                    send_ref[q - half] = piece.astype(BF)

        both(meta_ref, lambda: run(0, ws_ref), lambda: run(1, wl_ref))

    return call(
        kernel,
        [SMEM] + vmem(2) + [HBM] * 2,
        [((half, rows, features), F32), ((half, rows, features), BF)],
        [
            split(rows * shards, features),
            pltpu.VMEM((buffer, features), BF),
            pltpu.VMEM((plan.taps_max * features, features), BF),
            pltpu.SemaphoreType.DMA,
        ],
        flops=2 * shards * rows * features * features * plan.taps_max,
        moved=10 << 20,
        limit=56 if backward else 26,
    )(meta, *halves, w_short, w_long)


def iso_weight(plan, meta, b, low_own, low_other, delta_own, delta_other):
    shards, rows, features = plan.shards, plan.rows, plan.features
    half = shards // 2
    n, taps, own = plan.steps[b], plan.taps[b], plan.iso_rows[b]
    buffer = (n - 1 + rows + taps + 1) * shards

    def kernel(meta_ref, *refs):
        lows, deltas = refs[0:4], refs[4:8]
        grad_ref, sum_ref, stage, lined, delta, total, ordered = refs[8:]
        me = meta_ref[1]

        def load(low, steps):
            for q in range(shards):
                ordered[pl.ds(me ^ plan.mask(q), 1), :] = jnp.sum(
                    steps[q // half][q % half].astype(F32), axis=0, keepdims=True
                )
            time_major(plan, steps, stage, delta, 0)
            time_major(plan, low, stage, lined, n - 1)

        pl.when(meta_ref[0] == b)(lambda: load(lows[0:2], deltas[0:2]))
        pl.when(meta_ref[0] != b)(lambda: load(lows[2:4], deltas[2:4]))
        sum_ref[...] = jnp.sum(ordered[...], axis=0, keepdims=True)
        flat = me * own
        first = flat // features
        for m in range(taps):
            start = pl.multiple_of((first + m) * shards, 16)
            window = lined[pl.ds(start, rows * shards), :]
            total[m * features : (m + 1) * features, :] = dot(window, delta[...], ((0,), (0,)))
        shift = pl.multiple_of(flat % features, 16)
        grad_ref[...] = total[pl.ds(shift, own), :]

    return call(
        kernel,
        [SMEM] + vmem(8),
        [((own, features), F32), ((1, features), F32)],
        [
            split(rows * shards, features),
            pltpu.VMEM((buffer, features), BF),
            pltpu.VMEM((rows * shards, features), BF),
            pltpu.VMEM((taps * features, features), F32),
            pltpu.VMEM((shards, features), F32),
        ],
        flops=2 * shards * rows * features * features * taps,
        moved=10 << 20,
        limit=32,
    )(meta, *low_own, *low_other, *delta_own, *delta_other)


def inner_rows(plan, meta, pieces, low, biases, gain):
    rows, features = plan.rows, plan.features

    def kernel(meta_ref, *refs):
        parts = refs[:-5]
        low_ref, bias_ref, gain_ref, inner_ref, act_ref = refs[-5:]
        act = jnp.tanh(total_of(parts) + bias_ref[1:2, :])
        act_ref[...] = act
        unit, _ = norm_parts(act + low_ref[...].astype(F32))
        inner = unit * gain_ref[...] + bias_ref[3:4, :]
        inner_ref[...] = keep_rows(inner, meta_ref[4]).astype(BF)

    return call(
        kernel,
        [SMEM] + vmem(len(pieces) + 3),
        [((rows, features), BF), ((rows, features), F32)],
        [],
        moved=1 << 19,
        limit=4,
    )(meta, *pieces, low, biases, gain)


def trans_forward(plan, meta, inners, quarter):
    rows, features, line = plan.rows, plan.features, plan.line
    wide_max = 4 * plan.down_max

    def kernel(meta_ref, *refs):
        inner_refs, weights = refs[:line], refs[line : line + 4]
        out_ref, weight, wide, packed, sems = refs[line + 4 :]

        def run(b):
            copies = fetch_quarter(plan, b, meta_ref, weights, weight, sems)
            lhs = jnp.concatenate([ref[...] for ref in inner_refs], axis=0)
            for copy in copies:
                copy.wait()
            for i in range(plan.line_taps[b]):
                wide[:, i * features : (i + 1) * features] = dot(
                    lhs, weight[i * features : (i + 1) * features, :]
                )
            packed[...] = jnp.zeros_like(packed)
            for m in range(line):
                matrix_packed(plan, b, wide, m * rows, packed)
                out_ref[m] = packed[...].astype(BF)

        both(meta_ref, lambda: run(0), lambda: run(1))

    return call(
        kernel,
        [SMEM] + vmem(line) + [ANY] * 4,
        [((line, plan.pack, LANE), BF)],
        [
            pltpu.VMEM((wide_max, features), BF),
            pltpu.VMEM((line * rows, wide_max), F32),
            pltpu.VMEM((plan.pack, LANE), F32),
            pltpu.SemaphoreType.DMA((4,)),
        ],
        flops=2 * line * rows * features * wide_max,
        moved=4 << 20,
        limit=16,
    )(meta, *inners, *quarter)[0]


def outer_rows(plan, meta, packs, series, biases, gain):
    features, length, line = plan.features, plan.length, plan.line
    half_rows = length // 2

    def kernel(meta_ref, *refs):
        pack_refs = refs[:line]
        x_ref, bias_ref, gain_ref, keep_ref, send_ref, act_ref, stage, packed = refs[line:]

        def run(b):
            for m in range(line):
                packed[...] = pack_refs[m][...].astype(F32)
                unpack_taps(plan, b, packed, stage, (meta_ref[5] ^ m) * plan.line_taps[b])

        both(meta_ref, lambda: run(0), lambda: run(1))
        act = jnp.tanh(get(stage, 0, length) + bias_ref[2:3, :])
        act_ref[...] = act
        unit, _ = norm_parts(act + x_ref[...].astype(F32))
        put(stage, 0, unit * gain_ref[...] + bias_ref[3:4, :])
        mine = pl.multiple_of(meta_ref[0] * half_rows, 8)
        other = pl.multiple_of((1 - meta_ref[0]) * half_rows, 8)
        keep_ref[...] = get(stage, mine, half_rows).astype(BF)
        send_ref[...] = get(stage, other, half_rows).astype(BF)

    return call(
        kernel,
        [SMEM] + vmem(line + 3),
        [((half_rows, features), BF), ((half_rows, features), BF), ((length, features), F32)],
        [split(plan.stage_rows, features), pltpu.VMEM((plan.pack, LANE), F32)],
        moved=6 << 20,
        limit=16,
    )(meta, *packs, series, biases, gain)


def outer_backward(plan, meta, up_keep, up_recv, series, act, gain):
    features, length, line = plan.features, plan.length, plan.line
    half_rows = length // 2

    def kernel(
        meta_ref, uk_ref, ur_ref, x_ref, act_ref, gain_ref,
        outer_ref, taps_ref, vec_ref, stage, upstream, packed,
    ):
        mine = pl.multiple_of(meta_ref[0] * half_rows, 8)
        other = pl.multiple_of((1 - meta_ref[0]) * half_rows, 8)
        upstream[pl.ds(mine, half_rows), :] = uk_ref[...].astype(F32)
        upstream[pl.ds(other, half_rows), :] = ur_ref[...].astype(F32)
        act_value = act_ref[...]
        unit, scale = norm_parts(act_value + x_ref[...].astype(F32))
        above = upstream[...]
        vec_ref[...] = jnp.zeros_like(vec_ref)
        vec_ref[1:2, :] = jnp.sum(above, axis=0, keepdims=True)
        vec_ref[2:3, :] = jnp.sum(above * unit, axis=0, keepdims=True)
        outer = norm_back(above, unit, scale, gain_ref[...])
        outer_ref[...] = outer
        delta = (outer * (1.0 - act_value * act_value)).astype(BF).astype(F32)
        vec_ref[0:1, :] = jnp.sum(delta, axis=0, keepdims=True)
        put(stage, 0, delta)
        put(stage, length, jnp.zeros((plan.stage_rows - length, features), F32))
        packed[...] = jnp.zeros_like(packed)

        def run(b):
            for m in range(line):
                pack_taps(plan, b, stage, (meta_ref[5] ^ m) * plan.line_taps[b], packed)
                taps_ref[m] = packed[...].astype(BF)

        both(meta_ref, lambda: run(0), lambda: run(1))

    return call(
        kernel,
        [SMEM] + vmem(5),
        [((length, features), F32), ((line, plan.pack, LANE), BF), ((8, features), F32)],
        [
            split(plan.stage_rows, features),
            pltpu.VMEM((length, features), F32),
            pltpu.VMEM((plan.pack, LANE), F32),
        ],
        moved=8 << 20,
        limit=20,
    )(meta, up_keep, up_recv, series, act, gain)


def trans_backward(plan, meta, packs, quarter):
    rows, features, line = plan.rows, plan.features, plan.line
    wide_max = 4 * plan.down_max

    def kernel(meta_ref, *refs):
        pack_refs, weights = refs[:line], refs[line : line + 4]
        keep_ref, send_ref, wide_ref, weight, wide, packed, sems = refs[line + 4 :]

        def run(b):
            copies = fetch_quarter(plan, b, meta_ref, weights, weight, sems)
            wide[...] = jnp.zeros_like(wide)
            for m in range(line):
                packed[...] = pack_refs[m][...].astype(F32)
                packed_matrix(plan, b, packed, m * rows, wide)
            matrix = wide[...].astype(BF)
            wide_ref[...] = matrix
            for copy in copies:
                copy.wait()
            for i in range(plan.line_taps[b]):
                part = dot(
                    matrix[:, i * features : (i + 1) * features],
                    weight[i * features : (i + 1) * features, :],
                    ((1,), (1,)),
                )
                total = part if i == 0 else total + part
            keep_ref[...] = total[:rows]
            for m in range(1, line):
                send_ref[m - 1] = total[m * rows : (m + 1) * rows].astype(BF)

        both(meta_ref, lambda: run(0), lambda: run(1))

    return call(
        kernel,
        [SMEM] + vmem(line) + [ANY] * 4,
        [
            ((rows, features), F32),
            ((line - 1, rows, features), BF),
            ((line * rows, wide_max), BF),
        ],
        [
            pltpu.VMEM((wide_max, features), BF),
            pltpu.VMEM((line * rows, wide_max), F32),
            pltpu.VMEM((plan.pack, LANE), F32),
            pltpu.SemaphoreType.DMA((4,)),
        ],
        flops=2 * line * rows * features * wide_max,
        moved=5 << 20,
        limit=16,
    )(meta, *packs, *quarter)


def trans_weight(plan, meta, inners, wide):
    rows, features, line = plan.rows, plan.features, plan.line
    most = plan.down_max

    def kernel(meta_ref, *refs):
        inner_refs = refs[:line]
        wide_ref, keep_ref, send_ref, total = refs[line:]

        def run(b):
            own = plan.down_rows[b]
            lhs = jnp.concatenate([ref[...] for ref in inner_refs], axis=0)
            for i in range(plan.line_taps[b]):
                total[i * features : (i + 1) * features, :] = dot(
                    lhs, wide_ref[:, i * features : (i + 1) * features], ((0,), (0,))
                )
            for v in range(4):
                start = pl.multiple_of((meta_ref[7] ^ v) * own, LANE)
                piece = total[pl.ds(start, own), :]
                if own < most:
                    pad = jnp.zeros((most - own, features), F32)
                    piece = jnp.concatenate([piece, pad], axis=0)
                if v % 2 == 0:
                    keep_ref[v // 2] = piece
                else:
                    send_ref[v // 2] = piece.astype(BF)

        both(meta_ref, lambda: run(0), lambda: run(1))

    return call(
        kernel,
        [SMEM] + vmem(line + 1),
        [((2, most, features), F32), ((2, most, features), BF)],
        [pltpu.VMEM((4 * most, features), F32)],
        flops=2 * line * rows * features * 4 * most,
        moved=5 << 20,
        limit=20,
    )(meta, *inners, wide)


def inner_backward(plan, meta, pieces, low, act, vectors, gain):
    rows, features = plan.rows, plan.features

    def kernel(meta_ref, *refs):
        parts = refs[:-7]
        low_ref, act_ref, vec_ref, gain_ref, delta_ref, back_ref, out_ref = refs[-7:]
        total = keep_rows(total_of(parts), meta_ref[4])
        act_in = act_ref[...]
        unit, scale = norm_parts(act_in + low_ref[...].astype(F32))
        out_ref[...] = vec_ref[...]
        out_ref[1:2, :] = vec_ref[1:2, :] + jnp.sum(total, axis=0, keepdims=True)
        out_ref[2:3, :] = vec_ref[2:3, :] + jnp.sum(total * unit, axis=0, keepdims=True)
        back = norm_back(total, unit, scale, gain_ref[...])
        back_ref[...] = back
        delta_ref[...] = keep_rows(back * (1.0 - act_in * act_in), meta_ref[4]).astype(BF)

    return call(
        kernel,
        [SMEM] + vmem(len(pieces) + 4),
        [((rows, features), BF), ((rows, features), F32), ((8, features), F32)],
        [],
        moved=1 << 19,
        limit=6,
    )(meta, *pieces, low, act, vectors, gain)


def down_delta(plan, meta, pieces, delta_inner, act, small):
    rows, features = plan.rows, plan.features
    base, extra = up8(rows, 16), small.shape[0]

    def kernel(meta_ref, *refs):
        parts = refs[:-4]
        inner_ref, act_ref, small_ref, out_ref = refs[-4:]
        value = act_ref[...]
        total = total_of(parts) + inner_ref[...]
        delta = keep_rows(total * (1.0 - value * value), meta_ref[4])
        pad = jnp.zeros((base - rows, features), F32)
        out_ref[0:base, :] = jnp.concatenate([delta, pad], axis=0).astype(BF)
        high = small_ref[...].astype(BF)
        out_ref[base : base + extra, :] = high
        out_ref[base + extra :, :] = (small_ref[...] - high.astype(F32)).astype(BF)

    return call(
        kernel,
        [SMEM] + vmem(len(pieces) + 3),
        [((base + 2 * extra, features), BF)],
        [],
        moved=1 << 19,
        limit=8,
    )(meta, *pieces, delta_inner, act, small)[0]


def input_quarter(plan, meta, deltas, quarter):
    features, line = plan.features, plan.line
    rows = up8(plan.rows, 16)
    wide_max = 4 * plan.down_max

    def kernel(meta_ref, *refs):
        delta_refs, weights = refs[:line], refs[line : line + 4]
        out_ref, weight, wide, packed, sems = refs[line + 4 :]

        def run(b):
            copies = fetch_quarter(plan, b, meta_ref, weights, weight, sems)
            lhs = jnp.concatenate([ref[0:rows, :] for ref in delta_refs], axis=0)
            for copy in copies:
                copy.wait()
            for i in range(plan.line_taps[b]):
                wide[:, i * features : (i + 1) * features] = dot(
                    lhs, weight[i * features : (i + 1) * features, :], ((1,), (1,))
                )
            packed[...] = jnp.zeros_like(packed)
            for m in range(line):
                matrix_packed(plan, b, wide, m * rows, packed)
                out_ref[m] = packed[...].astype(BF)

        both(meta_ref, lambda: run(0), lambda: run(1))

    return call(
        kernel,
        [SMEM] + vmem(line) + [ANY] * 4,
        [((line, plan.pack, LANE), BF)],
        [
            pltpu.VMEM((wide_max, features), BF),
            pltpu.VMEM((line * rows, wide_max), F32),
            pltpu.VMEM((plan.pack, LANE), F32),
            pltpu.SemaphoreType.DMA((4,)),
        ],
        flops=2 * line * rows * features * wide_max,
        moved=4 << 20,
        limit=16,
    )(meta, *deltas, *quarter)[0]


def input_rows(plan, meta, packs, outer):
    features, length, line = plan.features, plan.length, plan.line

    def kernel(meta_ref, *refs):
        pack_refs = refs[:line]
        outer_ref, out_ref, stage, packed = refs[line:]

        def run(b):
            for m in range(line):
                packed[...] = pack_refs[m][...].astype(F32)
                unpack_taps(plan, b, packed, stage, (meta_ref[5] ^ m) * plan.line_taps[b])
            inner = get(stage, plan.factors[b] // 2, length)
            out_ref[...] = (inner + outer_ref[...]).astype(BF)

        both(meta_ref, lambda: run(0), lambda: run(1))

    return call(
        kernel,
        [SMEM] + vmem(line + 1),
        [((length, features), BF)],
        [split(plan.stage_rows, features), pltpu.VMEM((plan.pack, LANE), F32)],
        moved=3 << 20,
        limit=12,
    )(meta, *packs, outer)[0]


def down_weight(plan, meta, columns, even, odd, extra, loss_part):
    shards, rows, features, line = plan.shards, plan.rows, plan.features, plan.line
    half = shards // 2
    base = up8(rows, 16)
    most, tail = plan.down_max, up8(extra + 2, 16)

    def kernel(meta_ref, *refs):
        col_refs = refs[:4]
        even_ref, odd_ref, loss_ref, grad_ref, sums_ref, delta, ordered, small = refs[4:]
        me = meta_ref[1]
        for q in range(shards):
            source = (even_ref, odd_ref)[q // half]
            value = source[q % half, 0:base, :].astype(F32)
            at = me ^ plan.mask(q)
            ordered[pl.ds(at, 1), :] = jnp.sum(value, axis=0, keepdims=True)
            delta[q * rows : (q + 1) * rows, :] = value[:rows]
            high = source[q % half, base : base + extra, :].astype(F32)
            low = source[q % half, base + extra : base + 2 * extra, :].astype(F32)
            small[at] = high + low
        total = small[0]
        for i in range(1, shards):
            total = total + small[i]
        sums_ref[...] = jnp.zeros_like(sums_ref)
        sums_ref[0:extra, :] = total
        sums_ref[extra : extra + 1, :] = jnp.sum(ordered[...], axis=0, keepdims=True)
        sums_ref[extra + 1 : extra + 2, :] = jnp.broadcast_to(loss_ref[0:1, 0:1], (1, features))
        sums = sums_ref[...]
        high = sums.astype(BF)
        low = (sums - high.astype(F32)).astype(BF)
        grad_ref[most : most + tail, :] = high
        grad_ref[most + tail :, :] = low
        sums_ref[...] = high.astype(F32) + low.astype(F32)
        for at, v in enumerate((0, 2, 1, 3)):
            steps = delta[at * line * rows : (at + 1) * line * rows, :].astype(BF)
            part = dot(col_refs[v][...], steps, ((0,), (0,)))
            total = part if at == 0 else total + part
        grad_ref[0:most, :] = total.astype(BF)

    return call(
        kernel,
        [SMEM] + vmem(7),
        [((most + 2 * tail, features), BF), ((tail, features), F32)],
        [
            pltpu.VMEM((shards * rows, features), F32),
            pltpu.VMEM((shards, features), F32),
            pltpu.VMEM((shards, extra, features), F32),
        ],
        flops=2 * shards * rows * features * features,
        moved=4 << 20,
        limit=20,
    )(meta, *columns, even, odd, loss_part)


def finish(plan, meta, own, recv, mine, iso_sums, extra, ff_parts):
    features, most, tail = plan.features, plan.down_max, mine.shape[0]
    rows = plan.down_rows

    def kernel(
        meta_ref, own_ref, recv_ref, mine_ref, short_sum, long_sum,
        short_ref, long_ref, bias_ref, gain_ref, head_bias_ref, head_gain_ref, ff_ref, loss_ref,
    ):
        theirs = recv_ref[most : most + tail, :].astype(F32) + recv_ref[most + tail :, :].astype(F32)
        sums = mine_ref[...]
        total = sums + theirs
        first = 6 + ff_parts
        bias_ref[0, 1:2, :] = short_sum[...]
        bias_ref[1, 1:2, :] = long_sum[...]
        for b in range(2):
            bias_ref[b, 2:4, :] = total[first + 3 * b : first + 3 * b + 2]
            gain_ref[b : b + 1, :] = total[first + 3 * b + 2 : first + 3 * b + 3]
        head_bias_ref[...] = total[0:4]
        head_gain_ref[...] = total[4:6]
        ff_ref[...] = total[6 : 6 + ff_parts]
        loss_ref[...] = total[extra + 1 : extra + 2, 0:LANE] * (0.5 / (features * plan.length))

        def place(short_from, long_from, short_row, long_row):
            short_ref[...] = short_from[0 : rows[0], :].astype(F32)
            long_ref[...] = long_from[0 : rows[1], :].astype(F32)
            bias_ref[0, 0:1, :] = short_row[extra : extra + 1]
            bias_ref[1, 0:1, :] = long_row[extra : extra + 1]

        both(
            meta_ref,
            lambda: place(own_ref, recv_ref, sums, theirs),
            lambda: place(recv_ref, own_ref, theirs, sums),
        )

    return call(
        kernel,
        [SMEM] + vmem(5),
        [
            ((rows[0], features), F32),
            ((rows[1], features), F32),
            ((2, 4, features), F32),
            ((2, features), F32),
            ((4, features), F32),
            ((2, features), F32),
            ((ff_parts, features), F32),
            ((1, LANE), F32),
        ],
        [],
        moved=4 << 20,
        limit=12,
    )(meta, own, recv, mine, *iso_sums)


def natural_order(plan, meta, own, halves):
    shards = plan.shards
    line = plan.line
    rows, features = own

    def kernel(meta_ref, *refs):
        out_ref = refs[-1]
        for q in range(shards):
            out_ref[meta_ref[1] ^ plan.mask(q)] = refs[q // line][q % line].astype(F32)

    return call(
        kernel,
        [SMEM] + vmem(4),
        [((shards, rows, features), F32)],
        [],
        moved=3 << 20,
        limit=16,
    )(meta, *halves)[0]


ROOT_HALF = 0.7071067811865476
ROOT_TWO_PI = 0.3989422804014327


def head_rows(plan, meta, keep, recv, target, valid, merge, bias, gain, ff_in, ff_bias, ff_out):
    half_rows, features = keep.shape
    hidden = ff_in.shape[1]
    parts = hidden // features
    dims = (half_rows, features)

    def kernel(
        meta_ref, keep_ref, recv_ref, target_ref, valid_ref, merge_ref, bias_ref, gain_ref,
        in_bias_ref, in_hbm, out_hbm,
        out_ref, up_keep_ref, up_send_ref, normed_ref, act_ref, pre_delta_ref, ff_delta_ref,
        merged_delta_ref, vec_ref, loss_ref, slope_ref, in_ref, out_w_ref, sems,
    ):
        fetch_in = pltpu.make_async_copy(in_hbm, in_ref, sems.at[0])
        fetch_out = pltpu.make_async_copy(out_hbm, out_w_ref, sems.at[1])
        fetch_in.start()
        fetch_out.start()
        branch = meta_ref[0]
        merged = dot(keep_ref[...], merge_ref[branch]) + dot(recv_ref[...], merge_ref[1 - branch])
        merged = merged + bias_ref[0:1, :]
        unit, scale = norm_parts(merged)
        normed = (unit * gain_ref[0:1, :] + bias_ref[2:3, :]).astype(BF)
        normed_ref[...] = normed
        fetch_in.wait()
        fetch_out.wait()
        for c in range(parts):
            cols = slice(c * features, (c + 1) * features)
            pre = dot(normed, in_ref[:, cols]) + in_bias_ref[:, cols]
            share = 0.5 * (1.0 + lax.erf(pre * ROOT_HALF))
            slope_ref[:, cols] = share + pre * (jnp.exp(-0.5 * pre * pre) * ROOT_TWO_PI)
            act = (pre * share).astype(BF)
            act_ref[:, cols] = act
            part = dot(act, out_w_ref[cols, :])
            total = part if c == 0 else total + part
        unit_end, scale_end = norm_parts(merged + total + bias_ref[1:2, :])
        final = unit_end * gain_ref[1:2, :] + bias_ref[3:4, :]
        out_ref[...] = final.astype(BF)
        error = final - target_ref[...].astype(F32)
        weighted = valid_ref[...] * error
        loss = jnp.sum(jnp.sum(weighted * error, axis=0, keepdims=True), axis=1, keepdims=True)
        loss_ref[...] = jnp.broadcast_to(loss, loss_ref.shape)
        vec_ref[...] = jnp.zeros_like(vec_ref)
        vec_ref[3:4, :] = jnp.sum(weighted, axis=0, keepdims=True)
        vec_ref[5:6, :] = jnp.sum(weighted * unit_end, axis=0, keepdims=True)
        delta_sum = norm_back(weighted, unit_end, scale_end, gain_ref[1:2, :])
        delta_ff = delta_sum.astype(BF)
        ff_delta_ref[...] = delta_ff
        vec_ref[1:2, :] = jnp.sum(delta_ff.astype(F32), axis=0, keepdims=True)
        for c in range(parts):
            cols = slice(c * features, (c + 1) * features)
            pre_delta = dot(delta_ff, out_w_ref[cols, :], ((1,), (1,))) * slope_ref[:, cols]
            pre_delta = pre_delta.astype(BF)
            pre_delta_ref[:, cols] = pre_delta
            vec_ref[6 + c : 7 + c, :] = jnp.sum(pre_delta.astype(F32), axis=0, keepdims=True)
            part = dot(pre_delta, in_ref[:, cols], ((1,), (1,)))
            above = part if c == 0 else above + part
        vec_ref[2:3, :] = jnp.sum(above, axis=0, keepdims=True)
        vec_ref[4:5, :] = jnp.sum(above * unit, axis=0, keepdims=True)
        delta = norm_back(above, unit, scale, gain_ref[0:1, :]) + delta_sum
        delta = delta.astype(BF)
        merged_delta_ref[...] = delta
        vec_ref[0:1, :] = jnp.sum(delta.astype(F32), axis=0, keepdims=True)
        up_keep_ref[...] = dot(delta, merge_ref[branch], ((1,), (1,))).astype(BF)
        up_send_ref[...] = dot(delta, merge_ref[1 - branch], ((1,), (1,))).astype(BF)

    vec_rows = up8(6 + parts + 6)
    return call(
        kernel,
        [SMEM] + vmem(8) + [HBM] * 2,
        [
            (dims, BF), (dims, BF), (dims, BF), (dims, BF),
            ((half_rows, hidden), BF), ((half_rows, hidden), BF), (dims, BF), (dims, BF),
            ((vec_rows, features), F32), ((8, LANE), F32),
        ],
        [
            pltpu.VMEM((half_rows, hidden), F32),
            pltpu.VMEM((features, hidden), BF),
            pltpu.VMEM((hidden, features), BF),
            pltpu.SemaphoreType.DMA((2,)),
        ],
        flops=10 * half_rows * features * hidden,
        moved=14 << 20,
        limit=56,
    )(meta, keep, recv, target, valid, merge, bias, gain, ff_bias, ff_in, ff_out)


def head_weights(plan, meta, keep, recv, normed, act, pre_delta, ff_delta, merged_delta):
    shards = plan.shards
    half_rows, features = keep.shape
    hidden = act.shape[1]
    ff_rows, merge_rows = hidden // shards // 2, features // shards
    parts = hidden // features
    own = 2 * ff_rows + merge_rows

    def kernel(
        meta_ref, keep_hbm, recv_hbm, normed_hbm, act_hbm, pre_hbm, ff_hbm, merged_hbm,
        stay_near, stay_far, send_near, send_far, first, second, third,
        keep_ref, recv_ref, normed_ref, act_ref, pre_ref, ff_ref, merged_ref, sems,
    ):
        pairs = (
            (normed_hbm, normed_ref), (pre_hbm, pre_ref), (ff_hbm, ff_ref), (act_hbm, act_ref),
            (merged_hbm, merged_ref), (keep_hbm, keep_ref), (recv_hbm, recv_ref),
        )
        copies = [
            pltpu.make_async_copy(source, target, sems.at[i])
            for i, (source, target) in enumerate(pairs)
        ]
        for copy in copies:
            copy.start()
        branch = meta_ref[0]
        copies[0].wait()
        copies[1].wait()
        for c in range(parts):
            cols = slice(c * features, (c + 1) * features)
            first[cols, :] = dot(pre_ref[:, cols], normed_ref[...], ((0,), (0,))).astype(BF)
        copies[2].wait()
        copies[3].wait()
        for c in range(parts):
            cols = slice(c * features, (c + 1) * features)
            second[cols, :] = dot(act_ref[:, cols], ff_ref[...], ((0,), (0,))).astype(BF)
        for copy in copies[4:]:
            copy.wait()
        for side, ref in enumerate((keep_ref, recv_ref)):
            part = dot(ref[...], merged_ref[...], ((0,), (0,))).astype(BF)
            start = pl.multiple_of((branch ^ side) * features, 16)
            third[pl.ds(start, features), :] = part
        for q in range(shards):
            device = meta_ref[1] ^ plan.mask(q)
            targets = (stay_near, stay_far, send_near, send_far)
            target = targets[q // plan.line]
            for h in range(2):
                at = 2 * device + (branch ^ h)
                for start, count, source in (
                    (0, ff_rows, first),
                    (ff_rows, ff_rows, second),
                    (2 * ff_rows, merge_rows, third),
                ):
                    rows = pl.ds(pl.multiple_of(at * count, 16), count)
                    target[h, q % plan.line, start : start + count, :] = source[rows, :]

    return call(
        kernel,
        [SMEM] + [HBM] * 7,
        [((2, plan.line, own, features), BF)] * 4,
        [
            pltpu.VMEM((hidden, features), BF),
            pltpu.VMEM((hidden, features), BF),
            pltpu.VMEM((2 * features, features), BF),
        ]
        + [
            pltpu.VMEM(ref.shape, BF)
            for ref in (keep, recv, normed, act, pre_delta, ff_delta, merged_delta)
        ]
        + [pltpu.SemaphoreType.DMA((7,))],
        flops=4 * half_rows * features * hidden,
        moved=12 << 20,
        limit=56,
    )(meta, keep, recv, normed, act, pre_delta, ff_delta, merged_delta)


def hop(values, distance, shards):
    return lax.ppermute(values, "series", [(i, i ^ distance) for i in range(shards)])


def swap(values):
    return lax.ppermute(values, "branch", [(0, 1), (1, 0)])


def after(value, *others):
    return lax.optimization_barrier((value, others))[0]


def along_line(plan, own):
    return [own] + [hop(own, i << 2, plan.shards) for i in range(1, plan.line)]


def line_parts(plan, first, rest):
    return [first] + [hop(rest[i - 1], i << 2, plan.shards) for i in range(1, plan.line)]


def quad_gather(plan, own, later):
    side = hop(own, 2, plan.shards)
    return [own, hop(own, 1, plan.shards), side, hop(after(side, later), 1, plan.shards)]


def settle(value, *others):
    return lax.optimization_barrier((value,) + others)


def stacked(pieces):
    count, shape = len(pieces), pieces[0].shape

    def kernel(*refs):
        for i in range(count):
            refs[count][i] = refs[i][...]

    return call(kernel, vmem(count), [((count,) + shape, BF)], [], moved=1 << 20, limit=6)(*pieces)[0]


def gather_slots(plan, line, stack=jnp.stack):
    even = stack(line + [hop(value, 2, plan.shards) for value in line])
    return even, hop(even, 1, plan.shards)


def scatter_sum(plan, keep, send, *others):
    shards, line = plan.shards, plan.line
    first = keep + hop(send, 1, shards).astype(F32)
    second = first[:line] + hop(first[line:].astype(BF), 2, shards).astype(F32)
    if others:
        second, *others = settle(second, *others)
    pieces = line_parts(plan, second[0], [second[i].astype(BF) for i in range(1, line)])
    return (pieces, *others) if others else pieces


def rounded(values):
    return lax.reduce_precision(values, exponent_bits=8, mantissa_bits=7)


def layer_norm(values, gain_row, shift_row):
    center = values - jnp.mean(values, axis=-1, keepdims=True)
    spread = jnp.mean(center * center, axis=-1, keepdims=True)
    return center * lax.rsqrt(spread + EPSILON) * gain_row + shift_row


def gelu_exact(values):
    return jax.nn.gelu(values, approximate=False)


def product(a, b):
    return jnp.dot(a, b, preferred_element_type=F32)


def left_product(a, b):
    return jnp.einsum("mi,mo->io", a, b, preferred_element_type=F32)


def right_product(a, b):
    return jnp.einsum("mo,io->mi", a, b, preferred_element_type=F32)


def body(
    series_in, target, horizons, observed,
    down_short, iso_short, trans_short, down_long, iso_long, trans_long,
    branch_bias, branch_gain, merge_weight, head_bias, head_gain, ff_in, ff_in_bias, ff_out,
):
    shards = lax.axis_size("series")
    _, length, features = series_in.shape
    plan = Plan(
        shards,
        length,
        features,
        (down_short.shape[0], down_long.shape[0]),
        (iso_short.shape[0], iso_long.shape[0]),
    )
    line = plan.line
    half_rows = length // 2
    branch = lax.axis_index("branch")
    me = lax.axis_index("series")
    is_short = branch == 0
    iso_rows = jnp.where(is_short, plan.iso_rows[0], plan.iso_rows[1])
    meta = jnp.stack(
        [
            branch,
            me,
            (me * iso_rows) // features,
            (me * iso_rows) % features,
            jnp.where(is_short, plan.steps[0], plan.steps[1]),
            me // 4,
            me % 2,
            me % 4,
        ]
    ).astype(jnp.int32)
    series = series_in[0]
    biases, gain = branch_bias[0], branch_gain

    def chosen(short, long):
        rows = max(short.shape[0], long.shape[0])
        short = jnp.pad(short, ((0, rows - short.shape[0]), (0, 0)))
        long = jnp.pad(long, ((0, rows - long.shape[0]), (0, 0)))
        return jnp.where(is_short, short, long)

    def placed(own, other, b, rows):
        return jnp.where(branch == b, own, other)[:rows].astype(F32)

    blocks = prep_blocks(plan, meta, series)
    own_down = after(chosen(down_short, down_long), blocks)
    blocks = line_parts(plan, blocks[0], [blocks[i] for i in range(1, line)])
    down_quarter = quad_gather(plan, own_down, blocks)
    own_trans = after(chosen(trans_short, trans_long), blocks)
    keep, send, *columns = down_partial(plan, meta, blocks, down_quarter)
    pieces = line_parts(plan, keep, send)
    trans_quarter = quad_gather(plan, own_trans, pieces)
    low, act_down = low_rows(plan, meta, pieces, biases)
    low_own = gather_slots(plan, along_line(plan, low), stacked)
    low_own, trans_quarter = settle(low_own, trans_quarter)
    keep, send = iso_partial(plan, meta, low_own, iso_short, iso_long, False)
    low_other = swap(after(low_own[0], low_own[1]))
    pieces = scatter_sum(plan, keep, send)
    inner, act_iso = inner_rows(plan, meta, pieces, low, biases, gain)
    columns[2] = hop(after(columns[2], inner), 2, shards)
    inners, columns = settle(along_line(plan, inner), columns)
    packs = trans_forward(plan, meta, inners, trans_quarter)
    columns[3] = hop(after(columns[3], packs), 3, shards)
    packs = line_parts(plan, packs[0], [packs[i] for i in range(1, line)])
    packs, columns, low_other = settle(packs, columns, low_other)
    out_keep, out_send, act_trans = outer_rows(plan, meta, packs, series, biases, gain)
    out_recv = swap(out_send)
    columns[1] = hop(after(columns[1], out_keep), 1, shards)
    low_other = (low_other, hop(after(low_other, out_keep), 1, shards))
    out_recv, columns, low_other = settle(out_recv, columns, low_other)

    positions = branch * half_rows + jnp.arange(half_rows, dtype=jnp.int32)
    observed_half = lax.dynamic_slice_in_dim(observed[0], branch * half_rows, half_rows, 0)
    valid = (
        observed_half.astype(F32)
        * (positions >= SEQ_IN).astype(F32)
        * (positions < SEQ_IN + horizons[0]).astype(F32)
    )
    (
        out, up_keep, up_send, normed, act_ff, pre_delta, ff_delta, merged_delta, vec_head, loss_part
    ) = head_rows(
        plan, meta, out_keep, out_recv, target[0], valid[:, None], merge_weight, head_bias,
        head_gain, ff_in, ff_in_bias[None], ff_out,
    )
    up_recv = swap(up_send)
    near, far, near_send, far_send = head_weights(
        plan, meta, out_keep, out_recv, normed, act_ff, pre_delta, ff_delta, merged_delta
    )

    far_recv = hop(after(far_send, up_recv), 1, shards)
    outer, packs, vectors = outer_backward(plan, meta, up_keep, up_recv, series, act_trans, gain)
    far = (far.astype(F32) + after(far_recv, packs).astype(F32)).astype(BF)
    near_recv = hop(after(near_send, packs), 1, shards)
    share_recv = hop(far, 2, shards)
    packs = line_parts(plan, packs[0], [packs[i] for i in range(1, line)])
    keep, send, wide = trans_backward(plan, meta, packs, trans_quarter)
    trans_keep, trans_send = trans_weight(plan, meta, inners, wide)
    pieces, trans_send, share_recv, near_recv = settle(
        line_parts(plan, keep, send), trans_send, share_recv, near_recv
    )
    shares = near.astype(F32) + near_recv.astype(F32) + share_recv.astype(F32)
    share_recv = swap(shares[1].astype(BF))
    shares = shares[0]
    delta_iso, delta_inner, vectors = inner_backward(
        plan, meta, pieces, low, act_iso, vectors, gain
    )
    ff_parts = ff_in_bias.shape[0] // features
    selector = jnp.stack([is_short, branch == 1]).astype(F32)
    branch_rows = (selector[:, None, None] * vectors[None, 0:3]).reshape(6, features)
    small = jnp.concatenate([vec_head[: 6 + ff_parts], branch_rows], axis=0)
    count = small.shape[0]
    small = jnp.pad(small, ((0, up8(count, 16) - count), (0, 0)))
    trans_recv = hop(trans_send, 1, shards)
    deltas, trans_recv = settle(along_line(plan, delta_iso), trans_recv)
    trans_sum = trans_keep + trans_recv.astype(F32)
    trans_next = trans_sum[1].astype(BF)
    delta_own = gather_slots(plan, deltas)
    delta_own, trans_next, share_recv = settle(delta_own, trans_next, share_recv)
    shares = shares + share_recv.astype(F32)
    spread = line // 2
    share_recv = hop(shares[spread:].astype(BF), 4 * spread, shards)
    keep, send = iso_partial(plan, meta, delta_own, iso_short, iso_long, True)
    delta_other = swap(delta_own[0])
    pieces, delta_other = scatter_sum(plan, keep, send, delta_other)
    pieces, share_recv = settle(pieces, share_recv)
    shares = shares[:spread] + share_recv.astype(F32)
    payload = down_delta(plan, meta, pieces, delta_inner, act_down, small)
    delta_other = (delta_other, hop(after(delta_other, payload), 1, shards))
    trans_recv = hop(after(trans_next, payload), 2, shards)
    share_recv = hop(after(shares[1:].astype(BF), payload), 4, shards)
    first_grad = iso_weight(plan, meta, 0, low_own, low_other, delta_own, delta_other)
    deltas, trans_recv, share_recv, first_grad = settle(
        along_line(plan, payload), trans_recv, share_recv, first_grad
    )
    shares = rounded(shares[0] + share_recv[0].astype(F32))
    grad_trans = (trans_sum[0] + trans_recv.astype(F32)).astype(BF)
    packs = input_quarter(plan, meta, deltas, down_quarter)
    even = jnp.stack(deltas)
    odd = hop(after(even, packs), 2, shards)
    packs = line_parts(plan, packs[0], [packs[i] for i in range(1, line)])
    crossing = swap(after(jnp.concatenate([grad_trans, shares.astype(BF)], axis=0), odd))
    second_grad = iso_weight(
        plan, meta, 1, after(low_own, odd), low_other, delta_own, delta_other
    )
    packs, second_grad = settle(packs, second_grad)
    input_own = input_rows(plan, meta, packs, outer)
    trans_recv, share_recv = crossing[: plan.down_max], crossing[plan.down_max :]
    input_recv = swap(input_own)
    even = jnp.concatenate([even, odd], axis=0)
    delta_halves = (even, hop(after(even, input_own), 1, shards))
    share_recv = share_recv.astype(F32)
    ff_rows = ff_in_bias.shape[0] // shards // 2
    halves = [
        jnp.where(is_short, shares, share_recv),
        jnp.where(is_short, share_recv, shares),
    ]
    merge_own = jnp.concatenate([half[2 * ff_rows :] for half in halves], axis=0)
    extra = small.shape[0]
    grad_down, mine = down_weight(
        plan, meta, columns, *after(delta_halves, input_own), extra, loss_part
    )
    down_recv = swap(grad_down)
    merge_even = jnp.stack(along_line(plan, after(merge_own.astype(BF), grad_down)))
    merge_odd = hop(after(merge_even, grad_down), 2, shards)
    trans_recv = after(trans_recv, grad_down)
    trans_grads = [placed(grad_trans, trans_recv, b, plan.down_rows[b]) for b in range(2)]
    merge_odd, trans_grads = settle(merge_odd, trans_grads)
    merge_core = hop(merge_even, 1, shards), hop(merge_odd, 1, shards)
    input_total = input_own.astype(F32) + after(input_recv, merge_odd).astype(F32)
    merge_core, input_total = settle(merge_core, input_total)
    merge_total = natural_order(
        plan, meta, merge_own.shape, (merge_even, merge_odd, *merge_core)
    ).reshape(2, features, features)
    down_recv = after(down_recv, merge_total)
    short_down, long_down, bias_total, gain_total, head_sums, head_gains, ff_sums, loss = finish(
        plan, meta, grad_down, down_recv, mine, [first_grad[1], second_grad[1]], extra, ff_parts
    )
    return (
        out[None],
        loss[0, 0:1],
        input_total[None],
        short_down,
        first_grad[0],
        trans_grads[0],
        long_down,
        second_grad[0],
        trans_grads[1],
        bias_total,
        gain_total,
        merge_total,
        head_sums,
        head_gains,
        jnp.concatenate([half[:ff_rows] for half in halves], axis=0).T,
        ff_sums.reshape(-1),
        jnp.concatenate([half[ff_rows : 2 * ff_rows] for half in halves], axis=0),
    )


def fitted(matrix, row_total):
    return jnp.pad(matrix, ((0, row_total - matrix.shape[0]), (0, 0)))


def unpack(gathered_all, shards, rows_max, rows_own):
    features = gathered_all.shape[1]
    return gathered_all.reshape(shards, rows_max, features)[:, :rows_own].reshape(
        shards * rows_own, features
    )


def repack(gradient, shards, rows_max):
    rows_own = gradient.shape[0] // shards
    shaped = gradient.reshape(shards, rows_own, gradient.shape[1])
    return jnp.pad(shaped, ((0, 0), (0, rows_max - rows_own), (0, 0))).reshape(
        shards * rows_max, gradient.shape[1]
    )


def branch_pass(series_in, weights, shards, rows_max, biases, gain_row, factor):
    series_count, length, features = series_in.shape
    step_count = (length + factor) // factor
    margin = factor // 2
    weight_down = unpack(weights[0], shards, rows_max[0], factor * features // shards)
    weight_iso = unpack(weights[1], shards, rows_max[1], step_count * features // shards)
    weight_trans = unpack(weights[2], shards, rows_max[2], factor * features // shards).reshape(
        factor, features, features
    )
    blocks = jnp.pad(series_in, ((0, 0), (margin, step_count * factor - length - margin), (0, 0)))
    blocks = blocks.reshape(series_count * step_count, factor * features)
    act_down = jnp.tanh(product(blocks, weight_down) + biases[0])
    low_down = act_down.astype(jnp.bfloat16)
    padded = jnp.concatenate(
        [
            jnp.zeros((series_count, step_count - 1, features), jnp.bfloat16),
            low_down.reshape(series_count, step_count, features),
        ],
        axis=1,
    )
    unfolded = jnp.concatenate(
        [padded[:, offset : offset + step_count] for offset in range(step_count)], axis=2
    )
    unfolded = unfolded.reshape(series_count * step_count, step_count * features)
    act_iso = jnp.tanh(product(unfolded, weight_iso) + biases[1])
    inner_norm, inner_back = jax.vjp(
        layer_norm, act_iso + low_down.astype(jnp.float32), gain_row, biases[3]
    )
    low_inner = inner_norm.astype(jnp.bfloat16)
    spread_out = jnp.einsum(
        "mi,jio->mjo", low_inner, weight_trans, preferred_element_type=jnp.float32
    )
    act_trans = jnp.tanh(
        spread_out.reshape(series_count, step_count * factor, features)[:, :length] + biases[2]
    )
    result, outer_back = jax.vjp(
        layer_norm, act_trans + series_in.astype(jnp.float32), gain_row, biases[3]
    )
    stored = (
        blocks,
        weight_down,
        weight_iso,
        weight_trans,
        act_down,
        unfolded,
        act_iso,
        inner_back,
        low_inner,
        act_trans,
        outer_back,
    )
    return (result, stored)


def branch_back(series_in, weights, shards, rows_max, biases, gain_row, factor, upstream):
    series_count, length, features = series_in.shape
    step_count = (length + factor) // factor
    margin = factor // 2
    result, stored = branch_pass(series_in, weights, shards, rows_max, biases, gain_row, factor)
    (
        blocks,
        weight_down,
        weight_iso,
        weight_trans,
        act_down,
        unfolded,
        act_iso,
        inner_back,
        low_inner,
        act_trans,
        outer_back,
    ) = stored
    delta_outer, gain_outer, shift_outer = outer_back(upstream)
    delta_trans = (delta_outer * (1.0 - act_trans * act_trans)).astype(jnp.bfloat16)
    trans_blocks = jnp.pad(delta_trans, ((0, 0), (0, step_count * factor - length), (0, 0)))
    trans_blocks = trans_blocks.reshape(series_count * step_count, factor, features)
    grad_trans = jnp.einsum(
        "mi,mjo->jio", low_inner, trans_blocks, preferred_element_type=jnp.float32
    )
    grad_trans = grad_trans.reshape(factor * features, features)
    inner_upstream = jnp.einsum(
        "mjo,jio->mi", trans_blocks, weight_trans, preferred_element_type=jnp.float32
    )
    delta_inner, gain_inner, shift_inner = inner_back(inner_upstream)
    delta_iso = (delta_inner * (1.0 - act_iso * act_iso)).astype(jnp.bfloat16)
    grad_iso = left_product(unfolded, delta_iso)
    delta_unfold = right_product(delta_iso, weight_iso).reshape(
        series_count, step_count, step_count, features
    )
    delta_padded = jnp.zeros((series_count, 2 * step_count - 1, features), jnp.float32)
    for offset in range(step_count):
        delta_padded = delta_padded.at[:, offset : offset + step_count].add(
            delta_unfold[:, :, offset]
        )
    delta_low = (
        delta_padded[:, step_count - 1 :].reshape(series_count * step_count, features) + delta_inner
    )
    delta_down = (delta_low * (1.0 - act_down * act_down)).astype(jnp.bfloat16)
    grad_down = left_product(blocks, delta_down)
    delta_blocks = right_product(delta_down, weight_down).reshape(
        series_count, step_count * factor, features
    )
    delta_series = delta_blocks[:, margin : margin + length] + delta_outer
    vectors = jnp.stack(
        [
            jnp.sum(delta_down.astype(jnp.float32), axis=0),
            jnp.sum(delta_iso.astype(jnp.float32), axis=0),
            jnp.sum(delta_trans.astype(jnp.float32), axis=(0, 1)),
            shift_inner + shift_outer,
        ]
    )
    padded_grads = (
        repack(grad_down, shards, rows_max[0]),
        repack(grad_iso, shards, rows_max[1]),
        repack(grad_trans, shards, rows_max[2]),
    )
    return (delta_series, padded_grads, vectors, gain_inner + gain_outer)


def plain_body(
    series_in,
    target,
    horizons,
    observed,
    down_short,
    iso_short,
    trans_short,
    down_long,
    iso_long,
    trans_long,
    branch_bias,
    branch_gain,
    merge_weight,
    head_bias,
    head_gain,
    ff_in,
    ff_in_bias,
    ff_out,
):
    branch_index = lax.axis_index("branch")
    shards = lax.axis_size("series")
    series_count, length, features = series_in.shape
    rows_max = (
        max(down_short.shape[0], down_long.shape[0]),
        max(iso_short.shape[0], iso_long.shape[0]),
        max(trans_short.shape[0], trans_long.shape[0]),
    )
    is_short = branch_index == 0
    own_down = jnp.where(is_short, fitted(down_short, rows_max[0]), fitted(down_long, rows_max[0]))
    own_iso = jnp.where(is_short, fitted(iso_short, rows_max[1]), fitted(iso_long, rows_max[1]))
    own_trans = jnp.where(
        is_short, fitted(trans_short, rows_max[2]), fitted(trans_long, rows_max[2])
    )
    gathered = (
        lax.all_gather(own_down, "series", axis=0, tiled=True),
        lax.all_gather(own_iso, "series", axis=0, tiled=True),
        lax.all_gather(own_trans, "series", axis=0, tiled=True),
    )
    biases = branch_bias[0]
    gain_row = branch_gain[0]

    def forward_with(factor):
        return lambda: branch_pass(series_in, gathered, shards, rows_max, biases, gain_row, factor)[
            0
        ].astype(jnp.bfloat16)

    branch_out = lax.cond(is_short, forward_with(SCALE_S), forward_with(SCALE_L))
    received = lax.all_to_all(
        branch_out.reshape(series_count, length, 1, features),
        "branch",
        split_axis=1,
        concat_axis=2,
        tiled=True,
    )
    half_rows = received.shape[1]
    merge_rows = received.reshape(series_count * half_rows, 2 * features)
    merge_flat = merge_weight.reshape(2 * features, features)
    merged = product(merge_rows, merge_flat) + head_bias[0]
    normed, first_back = jax.vjp(layer_norm, merged, head_gain[0], head_bias[2])
    low_normed = normed.astype(jnp.bfloat16)
    pre_ff = product(low_normed, ff_in) + ff_in_bias
    activated, gelu_back = jax.vjp(gelu_exact, pre_ff)
    low_act = activated.astype(jnp.bfloat16)
    ff_result = product(low_act, ff_out) + head_bias[1]
    final_out, second_back = jax.vjp(layer_norm, merged + ff_result, head_gain[1], head_bias[3])
    final_rows = final_out.reshape(series_count, half_rows, features)
    positions = branch_index * half_rows + jnp.arange(half_rows, dtype=jnp.int32)
    observed_half = lax.dynamic_slice_in_dim(observed, branch_index * half_rows, half_rows, 1)
    valid_mask = (
        observed_half.astype(jnp.float32)
        * (positions >= SEQ_IN).astype(jnp.float32)
        * (positions < SEQ_IN + horizons[:, None]).astype(jnp.float32)
    )
    error_rows = final_rows - target.astype(jnp.float32)
    weighted = valid_mask[:, :, None] * error_rows
    series_part = 0.5 * jnp.sum(weighted * error_rows, axis=(1, 2)) / (features * length)
    delta_sum, gain_second, shift_second = second_back(
        weighted.reshape(series_count * half_rows, features)
    )
    delta_ff = delta_sum.astype(jnp.bfloat16)
    grad_ff_out = left_product(low_act, delta_ff)
    delta_act = right_product(delta_ff, ff_out)
    (delta_pre,) = gelu_back(delta_act)
    low_pre = delta_pre.astype(jnp.bfloat16)
    grad_ff_in = left_product(low_normed, low_pre)
    delta_normed = right_product(low_pre, ff_in)
    delta_first, gain_first, shift_first = first_back(delta_normed)
    delta_merged = (delta_first + delta_sum).astype(jnp.bfloat16)
    grad_merge = left_product(merge_rows, delta_merged).reshape(2, features, features)
    delta_rows = (
        right_product(delta_merged, merge_flat)
        .astype(jnp.bfloat16)
        .reshape(series_count, half_rows, 2, features)
    )
    back_rows = lax.all_to_all(delta_rows, "branch", split_axis=2, concat_axis=1, tiled=True)
    upstream = back_rows.astype(jnp.float32).reshape(series_count, length, features)
    ff_shares = (
        lax.psum_scatter(grad_ff_in, "series", scatter_dimension=1, tiled=True),
        lax.psum_scatter(grad_ff_out, "series", scatter_dimension=0, tiled=True),
    )
    weights_back = (
        lax.all_gather(own_down, "series", axis=0, tiled=True),
        lax.all_gather(own_iso, "series", axis=0, tiled=True),
        lax.all_gather(own_trans, "series", axis=0, tiled=True),
    )

    def backward_with(factor):
        return lambda: branch_back(
            series_in, weights_back, shards, rows_max, biases, gain_row, factor, upstream
        )

    delta_series, padded_grads, vectors, gain_grad = lax.cond(
        is_short, backward_with(SCALE_S), backward_with(SCALE_L)
    )
    reduced = (
        lax.psum_scatter(padded_grads[0], "series", scatter_dimension=0, tiled=True),
        lax.psum_scatter(padded_grads[1], "series", scatter_dimension=0, tiled=True),
        lax.psum_scatter(padded_grads[2], "series", scatter_dimension=0, tiled=True),
    )
    short_flag = is_short.astype(jnp.float32)
    long_flag = 1.0 - short_flag
    summed = (
        lax.psum(delta_series.astype(jnp.bfloat16), "branch").astype(jnp.float32),
        lax.psum(series_part.astype(jnp.bfloat16), "branch").astype(jnp.float32),
        lax.psum(
            (short_flag * reduced[0][: down_short.shape[0]]).astype(jnp.bfloat16), "branch"
        ).astype(jnp.float32),
        lax.psum((short_flag * reduced[1]).astype(jnp.bfloat16), "branch").astype(jnp.float32),
        lax.psum(
            (short_flag * reduced[2][: trans_short.shape[0]]).astype(jnp.bfloat16), "branch"
        ).astype(jnp.float32),
        lax.psum((long_flag * reduced[0]).astype(jnp.bfloat16), "branch").astype(jnp.float32),
        lax.psum(
            (long_flag * reduced[1][: iso_long.shape[0]]).astype(jnp.bfloat16), "branch"
        ).astype(jnp.float32),
        lax.psum((long_flag * reduced[2]).astype(jnp.bfloat16), "branch").astype(jnp.float32),
        lax.psum(ff_shares[0].astype(jnp.bfloat16), "branch").astype(jnp.float32),
        lax.psum(ff_shares[1].astype(jnp.bfloat16), "branch").astype(jnp.float32),
    )
    selector = (jnp.arange(2, dtype=jnp.int32) == branch_index).astype(jnp.float32)
    full_bias = selector[:, None, None] * vectors[None]
    full_gain = selector[:, None] * gain_grad[None]
    head_vectors = jnp.stack(
        [
            jnp.sum(delta_merged.astype(jnp.float32), axis=0),
            jnp.sum(delta_ff.astype(jnp.float32), axis=0),
            shift_first,
            shift_second,
        ]
    )
    head_gains = jnp.stack([gain_first, gain_second])
    ff_bias_grad = jnp.sum(low_pre.astype(jnp.float32), axis=0)
    totals = lax.psum(
        (grad_merge, head_vectors, head_gains, ff_bias_grad, full_bias, full_gain),
        ("branch", "series"),
    )
    return (
        final_rows.astype(jnp.bfloat16),
        summed[1],
        summed[0],
        summed[2],
        summed[3],
        summed[4],
        summed[5],
        summed[6],
        summed[7],
        totals[4],
        totals[5],
        totals[0],
        totals[1],
        totals[2],
        summed[8],
        totals[3],
        summed[9],
    )


def solution(mesh):
    placed = (
        P("series", None, None),
        P("series", "branch", None),
        P("series"),
        P("series", None),
        P("series", None),
        P("series", None),
        P("series", None),
        P("series", None),
        P("series", None),
        P("series", None),
        P("branch", None, None),
        P("branch", None),
        P(),
        P(),
        P(),
        P(),
        P(),
        P(),
    )

    def run(*args):
        shards = mesh.shape["series"]
        features = args[0].shape[2]
        down_rows = [args[i].shape[0] // shards for i in (4, 7)]
        iso_rows = [args[i].shape[0] // shards for i in (5, 8)]
        fits = (
            args[0].shape[0] == shards
            and shards == 16
            and shards & (shards - 1) == 0
            and all(r % LANE == 0 and r <= features and 4 * r % features == 0 for r in down_rows)
            and all(r % 16 == 0 for r in iso_rows)
        )
        return jax.shard_map(
            body if fits else plain_body,
            mesh=mesh,
            in_specs=placed,
            out_specs=(
                P("series", "branch", None),
                P("series"),
                P("series", None, None),
                P("series", None),
                P("series", None),
                P("series", None),
                P("series", None),
                P("series", None),
                P("series", None),
                P(),
                P(),
                P(),
                P(),
                P(),
                P(None, "series"),
                P(),
                P("series", None),
            ),
            check_vma=False,
        )(*args)

    return run
```

```python
import functools

import jax
import jax.numpy as jnp
from jax import lax
from jax.experimental import pallas as pl
from jax.experimental.pallas import tpu as pltpu
from jax.sharding import PartitionSpec as P

SCALE_S = 12
SCALE_L = 16
SEQ_IN = 96
EPSILON = 1e-05
LANE = 128

BF = jnp.bfloat16
F32 = jnp.float32


def up8(count, base=8):
    return -(-count // base) * base


class Plan:
    def __init__(self, shards, length, features, down_rows, iso_rows):
        self.shards, self.length, self.features = shards, length, features
        self.factors = (SCALE_S, SCALE_L)
        self.steps = tuple((length + k) // k for k in self.factors)
        self.rows = up8(max(self.steps))
        self.down_rows = down_rows
        self.iso_rows = iso_rows
        self.down_max, self.iso_max = max(down_rows), max(iso_rows)
        self.line = shards // 4
        self.line_taps = tuple(4 * r // features for r in down_rows)
        blocks = features // LANE
        self.pack = up8(max(t * blocks * n for t, n in zip(self.line_taps, self.steps)), 16)
        self.taps = tuple(
            max(-(-((d * r) % features + r) // features) for d in range(shards)) for r in iso_rows
        )
        self.taps_max = max(self.taps)
        self.stage_rows = max(k * up8(n) for k, n in zip(self.factors, self.steps))

    def mask(self, slot):
        core, rest = divmod(slot, 2 * self.line)
        side, line = divmod(rest, self.line)
        return core | (side << 1) | (line << 2)


def vmem(count):
    return [pl.BlockSpec(memory_space=pltpu.VMEM) for _ in range(count)]


SMEM = pl.BlockSpec(memory_space=pltpu.SMEM)
ANY = pl.BlockSpec(memory_space=pl.ANY)
HBM = pl.BlockSpec(memory_space=pltpu.HBM)


def call(body, in_specs, outs, scratch, flops=0, moved=0, limit=56):
    return pl.pallas_call(
        body,
        out_shape=[jax.ShapeDtypeStruct(s, d) for s, d in outs],
        in_specs=in_specs,
        out_specs=vmem(len(outs)),
        scratch_shapes=scratch,
        compiler_params=pltpu.CompilerParams(vmem_limit_bytes=limit << 20),
        cost_estimate=pl.CostEstimate(flops=flops, bytes_accessed=moved, transcendentals=0),
    )


def dot(a, b, dims=((1,), (0,))):
    return lax.dot_general(a, b, (dims, ((), ())), preferred_element_type=F32)


def norm_parts(values):
    center = values - jnp.mean(values, axis=-1, keepdims=True)
    spread = jnp.mean(center * center, axis=-1, keepdims=True)
    scale = lax.rsqrt(spread + EPSILON)
    return center * scale, scale


def norm_back(upstream, unit, scale, gain):
    inner = upstream * gain
    first = jnp.mean(inner, axis=-1, keepdims=True)
    second = jnp.mean(inner * unit, axis=-1, keepdims=True)
    return scale * (inner - first - unit * second)


def keep_rows(values, count):
    index = lax.broadcasted_iota(jnp.int32, values.shape, 0)
    return jnp.where(index < count, values, 0.0)


def both(meta, short, long):
    pl.when(meta[0] == 0)(short)
    pl.when(meta[0] == 1)(long)


def split(rows, features):
    return pltpu.VMEM((features // LANE, rows, LANE), F32)


def put(ref, start, values, stride=1):
    count = values.shape[0]
    where = pl.ds(start, count) if stride == 1 else pl.ds(start, count, stride=stride)
    for c in range(ref.shape[0]):
        ref[c, where, :] = values[:, c * LANE : (c + 1) * LANE]


def get(ref, start, count, stride=1):
    where = pl.ds(start, count) if stride == 1 else pl.ds(start, count, stride=stride)
    return jnp.concatenate([ref[c, where, :] for c in range(ref.shape[0])], axis=1)


def split(rows, features):
    return pltpu.VMEM((features // LANE, rows, LANE), F32)


def put(ref, start, values, stride=1):
    count = values.shape[0]
    where = pl.ds(start, count) if stride == 1 else pl.ds(start, count, stride=stride)
    for c in range(ref.shape[0]):
        ref[c, where, :] = values[:, c * LANE : (c + 1) * LANE]


def get(ref, start, count, stride=1):
    where = pl.ds(start, count) if stride == 1 else pl.ds(start, count, stride=stride)
    return jnp.concatenate([ref[c, where, :] for c in range(ref.shape[0])], axis=1)


def pack_taps(plan, b, stage, first, packed):
    k, n = plan.factors[b], plan.steps[b]
    blocks = plan.features // LANE
    for i in range(plan.line_taps[b]):
        for c in range(blocks):
            at = (i * blocks + c) * n
            packed[at : at + n, :] = stage[c, pl.ds(first + i, n, stride=k), :]


def unpack_taps(plan, b, packed, stage, first):
    k, n = plan.factors[b], plan.steps[b]
    blocks = plan.features // LANE
    for i in range(plan.line_taps[b]):
        for c in range(blocks):
            at = (i * blocks + c) * n
            stage[c, pl.ds(first + i, n, stride=k), :] = packed[at : at + n, :]


def packed_matrix(plan, b, packed, base, matrix):
    n = plan.steps[b]
    for g in range(plan.line_taps[b] * plan.features // LANE):
        matrix[base : base + n, g * LANE : (g + 1) * LANE] = packed[g * n : (g + 1) * n, :]


def matrix_packed(plan, b, matrix, base, packed):
    n = plan.steps[b]
    for g in range(plan.line_taps[b] * plan.features // LANE):
        packed[g * n : (g + 1) * n, :] = matrix[base : base + n, g * LANE : (g + 1) * LANE]


def fetch_quarter(plan, b, meta_ref, sources, target, sems):
    own = plan.down_rows[b]
    quad = meta_ref[7]
    copies = []
    for v, source in enumerate(sources):
        start = pl.multiple_of((quad ^ v) * own, LANE)
        copies.append(
            pltpu.make_async_copy(
                source.at[pl.ds(0, own)], target.at[pl.ds(start, own)], sems.at[v]
            )
        )
    for copy in copies:
        copy.start()
    return copies


def total_of(parts):
    total = parts[0][...].astype(F32)
    for piece in parts[1:]:
        total = total + piece[...].astype(F32)
    return total


def prep_blocks(plan, meta, series):
    length, features, line = plan.length, plan.features, plan.line

    def kernel(meta_ref, x_ref, out_ref, wide, packed):
        def run(b):
            margin = plan.factors[b] // 2
            wide[...] = jnp.zeros_like(wide)
            put(wide, margin, x_ref[...].astype(F32))
            packed[...] = jnp.zeros_like(packed)
            for z in range(line):
                pack_taps(plan, b, wide, z * plan.line_taps[b], packed)
                out_ref[z ^ meta_ref[5]] = packed[...].astype(BF)

        both(meta_ref, lambda: run(0), lambda: run(1))

    return call(
        kernel,
        [SMEM] + vmem(1),
        [((line, plan.pack, LANE), BF)],
        [split(plan.stage_rows, features), pltpu.VMEM((plan.pack, LANE), F32)],
        moved=2 * length * features * 2,
        limit=8,
    )(meta, series)[0]


def down_partial(plan, meta, blocks, quarter):
    rows, features, line = plan.rows, plan.features, plan.line
    wide_max = 4 * plan.down_max

    def kernel(meta_ref, *refs):
        packs, weights = refs[:line], refs[line : line + 4]
        keep_ref, send_ref, *col_refs = refs[line + 4 : line + 10]
        weight, wide, packed, cols, sems = refs[line + 10 :]

        def run(b):
            copies = fetch_quarter(plan, b, meta_ref, weights, weight, sems)
            own = plan.down_rows[b]
            wide[...] = jnp.zeros_like(wide)
            for m in range(line):
                packed[...] = packs[m][...].astype(F32)
                packed_matrix(plan, b, packed, m * rows, wide)
            matrix = wide[...].astype(BF)
            for u in range(4):
                piece = matrix[:, u * own : (u + 1) * own]
                if own < plan.down_max:
                    pad = jnp.zeros((line * rows, plan.down_max - own), BF)
                    piece = jnp.concatenate([piece, pad], axis=1)
                cols[u ^ meta_ref[7]] = piece
            for v in range(4):
                col_refs[v][...] = cols[v]
            for copy in copies:
                copy.wait()
            part = dot(matrix[:, : 4 * own], weight[0 : 4 * own, :])
            keep_ref[...] = part[:rows]
            for m in range(1, line):
                send_ref[m - 1] = part[m * rows : (m + 1) * rows].astype(BF)

        both(meta_ref, lambda: run(0), lambda: run(1))

    return call(
        kernel,
        [SMEM] + vmem(line) + [ANY] * 4,
        [
            ((rows, features), F32),
            ((line - 1, rows, features), BF),
        ]
        + [((line * rows, plan.down_max), BF)] * 4,
        [
            pltpu.VMEM((wide_max, features), BF),
            pltpu.VMEM((line * rows, wide_max), F32),
            pltpu.VMEM((plan.pack, LANE), F32),
            pltpu.VMEM((4, line * rows, plan.down_max), BF),
            pltpu.SemaphoreType.DMA((4,)),
        ],
        flops=2 * line * rows * features * wide_max,
        moved=5 << 20,
        limit=16,
    )(meta, *blocks, *quarter)


def low_rows(plan, meta, pieces, biases):
    rows, features = plan.rows, plan.features

    def kernel(meta_ref, *refs):
        parts, bias_ref, low_ref, act_ref = refs[:-3], refs[-3], refs[-2], refs[-1]
        act = keep_rows(jnp.tanh(total_of(parts) + bias_ref[0:1, :]), meta_ref[4])
        act_ref[...] = act
        low_ref[...] = act.astype(BF)

    return call(
        kernel,
        [SMEM] + vmem(len(pieces) + 1),
        [((rows, features), BF), ((rows, features), F32)],
        [],
        moved=1 << 19,
        limit=4,
    )(meta, *pieces, biases)


def time_major(plan, halves, stage, target, lead):
    shards, rows = plan.shards, plan.rows
    half = shards // 2
    for q in range(shards):
        put(stage, q, halves[q // half][q % half].astype(F32), shards)
    body = shards * rows
    if lead:
        target[0 : lead * shards, :] = jnp.zeros((lead * shards, target.shape[1]), BF)
    target[lead * shards : lead * shards + body, :] = get(stage, 0, body).astype(BF)
    rest = target.shape[0] - lead * shards - body
    if rest:
        target[lead * shards + body :, :] = jnp.zeros((rest, target.shape[1]), BF)


def pad_weight(plan, b, meta_ref, source, target, sem):
    width, own, end = target.shape[1], plan.iso_rows[b], plan.taps[b] * target.shape[1]
    target[0:width, :] = jnp.zeros((width, width), BF)
    target[own:end, :] = jnp.zeros((end - own, width), BF)
    shift = pl.multiple_of(meta_ref[3], 16)
    copy = pltpu.make_async_copy(source, target.at[pl.ds(shift, plan.iso_rows[b])], sem)
    copy.start()
    return copy


def iso_partial(plan, meta, halves, w_short, w_long, backward):
    shards, rows, features = plan.shards, plan.rows, plan.features
    half = shards // 2
    extra = plan.taps_max + 2
    buffer = (max(plan.steps) + rows + extra) * shards

    def kernel(
        meta_ref, even_ref, odd_ref, ws_ref, wl_ref, keep_ref, send_ref, stage, lined, padded, sem
    ):
        first = meta_ref[2]

        def run(b, w_ref):
            n, taps = plan.steps[b], plan.taps[b]
            copy = pad_weight(plan, b, meta_ref, w_ref, padded, sem)
            lead = extra if backward else n - 1
            time_major(plan, (even_ref, odd_ref), stage, lined, lead)
            copy.wait()
            for m in range(taps):
                start = extra + n - 1 - first - m if backward else first + m
                start = pl.multiple_of(start * shards, 16)
                window = lined[pl.ds(start, rows * shards), :]
                weight = padded[m * features : (m + 1) * features, :]
                part = dot(window, weight, ((1,), (1,)) if backward else ((1,), (0,)))
                total = part if m == 0 else total + part
            put(stage, 0, total)
            for q in range(shards):
                piece = get(stage, q, rows, shards)
                if q < half:
                    keep_ref[q] = piece
                else:
                    send_ref[q - half] = piece.astype(BF)

        both(meta_ref, lambda: run(0, ws_ref), lambda: run(1, wl_ref))

    return call(
        kernel,
        [SMEM] + vmem(2) + [HBM] * 2,
        [((half, rows, features), F32), ((half, rows, features), BF)],
        [
            split(rows * shards, features),
            pltpu.VMEM((buffer, features), BF),
            pltpu.VMEM((plan.taps_max * features, features), BF),
            pltpu.SemaphoreType.DMA,
        ],
        flops=2 * shards * rows * features * features * plan.taps_max,
        moved=10 << 20,
        limit=56 if backward else 26,
    )(meta, *halves, w_short, w_long)


def iso_weight(plan, meta, b, low_own, low_other, delta_own, delta_other):
    shards, rows, features = plan.shards, plan.rows, plan.features
    half = shards // 2
    n, taps, own = plan.steps[b], plan.taps[b], plan.iso_rows[b]
    buffer = (n - 1 + rows + taps + 1) * shards

    def kernel(meta_ref, *refs):
        lows, deltas = refs[0:4], refs[4:8]
        grad_ref, sum_ref, stage, lined, delta, total, ordered = refs[8:]
        me = meta_ref[1]

        def load(low, steps):
            for q in range(shards):
                ordered[pl.ds(me ^ plan.mask(q), 1), :] = jnp.sum(
                    steps[q // half][q % half].astype(F32), axis=0, keepdims=True
                )
            time_major(plan, steps, stage, delta, 0)
            time_major(plan, low, stage, lined, n - 1)

        pl.when(meta_ref[0] == b)(lambda: load(lows[0:2], deltas[0:2]))
        pl.when(meta_ref[0] != b)(lambda: load(lows[2:4], deltas[2:4]))
        sum_ref[...] = jnp.sum(ordered[...], axis=0, keepdims=True)
        flat = me * own
        first = flat // features
        for m in range(taps):
            start = pl.multiple_of((first + m) * shards, 16)
            window = lined[pl.ds(start, rows * shards), :]
            total[m * features : (m + 1) * features, :] = dot(window, delta[...], ((0,), (0,)))
        shift = pl.multiple_of(flat % features, 16)
        grad_ref[...] = total[pl.ds(shift, own), :]

    return call(
        kernel,
        [SMEM] + vmem(8),
        [((own, features), F32), ((1, features), F32)],
        [
            split(rows * shards, features),
            pltpu.VMEM((buffer, features), BF),
            pltpu.VMEM((rows * shards, features), BF),
            pltpu.VMEM((taps * features, features), F32),
            pltpu.VMEM((shards, features), F32),
        ],
        flops=2 * shards * rows * features * features * taps,
        moved=10 << 20,
        limit=32,
    )(meta, *low_own, *low_other, *delta_own, *delta_other)


def inner_rows(plan, meta, pieces, low, biases, gain):
    rows, features = plan.rows, plan.features

    def kernel(meta_ref, *refs):
        parts = refs[:-5]
        low_ref, bias_ref, gain_ref, inner_ref, act_ref = refs[-5:]
        act = jnp.tanh(total_of(parts) + bias_ref[1:2, :])
        act_ref[...] = act
        unit, _ = norm_parts(act + low_ref[...].astype(F32))
        inner = unit * gain_ref[...] + bias_ref[3:4, :]
        inner_ref[...] = keep_rows(inner, meta_ref[4]).astype(BF)

    return call(
        kernel,
        [SMEM] + vmem(len(pieces) + 3),
        [((rows, features), BF), ((rows, features), F32)],
        [],
        moved=1 << 19,
        limit=4,
    )(meta, *pieces, low, biases, gain)


def trans_forward(plan, meta, inners, quarter):
    rows, features, line = plan.rows, plan.features, plan.line
    wide_max = 4 * plan.down_max

    def kernel(meta_ref, *refs):
        inner_refs, weights = refs[:line], refs[line : line + 4]
        out_ref, weight, wide, packed, sems = refs[line + 4 :]

        def run(b):
            copies = fetch_quarter(plan, b, meta_ref, weights, weight, sems)
            lhs = jnp.concatenate([ref[...] for ref in inner_refs], axis=0)
            for copy in copies:
                copy.wait()
            for i in range(plan.line_taps[b]):
                wide[:, i * features : (i + 1) * features] = dot(
                    lhs, weight[i * features : (i + 1) * features, :]
                )
            packed[...] = jnp.zeros_like(packed)
            for m in range(line):
                matrix_packed(plan, b, wide, m * rows, packed)
                out_ref[m] = packed[...].astype(BF)

        both(meta_ref, lambda: run(0), lambda: run(1))

    return call(
        kernel,
        [SMEM] + vmem(line) + [ANY] * 4,
        [((line, plan.pack, LANE), BF)],
        [
            pltpu.VMEM((wide_max, features), BF),
            pltpu.VMEM((line * rows, wide_max), F32),
            pltpu.VMEM((plan.pack, LANE), F32),
            pltpu.SemaphoreType.DMA((4,)),
        ],
        flops=2 * line * rows * features * wide_max,
        moved=4 << 20,
        limit=16,
    )(meta, *inners, *quarter)[0]


def outer_rows(plan, meta, packs, series, biases, gain):
    features, length, line = plan.features, plan.length, plan.line
    half_rows = length // 2

    def kernel(meta_ref, *refs):
        pack_refs = refs[:line]
        x_ref, bias_ref, gain_ref, keep_ref, send_ref, act_ref, stage, packed = refs[line:]

        def run(b):
            for m in range(line):
                packed[...] = pack_refs[m][...].astype(F32)
                unpack_taps(plan, b, packed, stage, (meta_ref[5] ^ m) * plan.line_taps[b])

        both(meta_ref, lambda: run(0), lambda: run(1))
        act = jnp.tanh(get(stage, 0, length) + bias_ref[2:3, :])
        act_ref[...] = act
        unit, _ = norm_parts(act + x_ref[...].astype(F32))
        put(stage, 0, unit * gain_ref[...] + bias_ref[3:4, :])
        mine = pl.multiple_of(meta_ref[0] * half_rows, 8)
        other = pl.multiple_of((1 - meta_ref[0]) * half_rows, 8)
        keep_ref[...] = get(stage, mine, half_rows).astype(BF)
        send_ref[...] = get(stage, other, half_rows).astype(BF)

    return call(
        kernel,
        [SMEM] + vmem(line + 3),
        [((half_rows, features), BF), ((half_rows, features), BF), ((length, features), F32)],
        [split(plan.stage_rows, features), pltpu.VMEM((plan.pack, LANE), F32)],
        moved=6 << 20,
        limit=16,
    )(meta, *packs, series, biases, gain)


def outer_backward(plan, meta, up_keep, up_recv, series, act, gain):
    features, length, line = plan.features, plan.length, plan.line
    half_rows = length // 2

    def kernel(
        meta_ref, uk_ref, ur_ref, x_ref, act_ref, gain_ref,
        outer_ref, taps_ref, vec_ref, stage, upstream, packed,
    ):
        mine = pl.multiple_of(meta_ref[0] * half_rows, 8)
        other = pl.multiple_of((1 - meta_ref[0]) * half_rows, 8)
        upstream[pl.ds(mine, half_rows), :] = uk_ref[...].astype(F32)
        upstream[pl.ds(other, half_rows), :] = ur_ref[...].astype(F32)
        act_value = act_ref[...]
        unit, scale = norm_parts(act_value + x_ref[...].astype(F32))
        above = upstream[...]
        vec_ref[...] = jnp.zeros_like(vec_ref)
        vec_ref[1:2, :] = jnp.sum(above, axis=0, keepdims=True)
        vec_ref[2:3, :] = jnp.sum(above * unit, axis=0, keepdims=True)
        outer = norm_back(above, unit, scale, gain_ref[...])
        outer_ref[...] = outer
        delta = (outer * (1.0 - act_value * act_value)).astype(BF).astype(F32)
        vec_ref[0:1, :] = jnp.sum(delta, axis=0, keepdims=True)
        put(stage, 0, delta)
        put(stage, length, jnp.zeros((plan.stage_rows - length, features), F32))
        packed[...] = jnp.zeros_like(packed)

        def run(b):
            for m in range(line):
                pack_taps(plan, b, stage, (meta_ref[5] ^ m) * plan.line_taps[b], packed)
                taps_ref[m] = packed[...].astype(BF)

        both(meta_ref, lambda: run(0), lambda: run(1))

    return call(
        kernel,
        [SMEM] + vmem(5),
        [((length, features), F32), ((line, plan.pack, LANE), BF), ((8, features), F32)],
        [
            split(plan.stage_rows, features),
            pltpu.VMEM((length, features), F32),
            pltpu.VMEM((plan.pack, LANE), F32),
        ],
        moved=8 << 20,
        limit=20,
    )(meta, up_keep, up_recv, series, act, gain)


def trans_backward(plan, meta, packs, quarter):
    rows, features, line = plan.rows, plan.features, plan.line
    wide_max = 4 * plan.down_max

    def kernel(meta_ref, *refs):
        pack_refs, weights = refs[:line], refs[line : line + 4]
        keep_ref, send_ref, wide_ref, weight, wide, packed, sems = refs[line + 4 :]

        def run(b):
            copies = fetch_quarter(plan, b, meta_ref, weights, weight, sems)
            wide[...] = jnp.zeros_like(wide)
            for m in range(line):
                packed[...] = pack_refs[m][...].astype(F32)
                packed_matrix(plan, b, packed, m * rows, wide)
            matrix = wide[...].astype(BF)
            wide_ref[...] = matrix
            for copy in copies:
                copy.wait()
            for i in range(plan.line_taps[b]):
                part = dot(
                    matrix[:, i * features : (i + 1) * features],
                    weight[i * features : (i + 1) * features, :],
                    ((1,), (1,)),
                )
                total = part if i == 0 else total + part
            keep_ref[...] = total[:rows]
            for m in range(1, line):
                send_ref[m - 1] = total[m * rows : (m + 1) * rows].astype(BF)

        both(meta_ref, lambda: run(0), lambda: run(1))

    return call(
        kernel,
        [SMEM] + vmem(line) + [ANY] * 4,
        [
            ((rows, features), F32),
            ((line - 1, rows, features), BF),
            ((line * rows, wide_max), BF),
        ],
        [
            pltpu.VMEM((wide_max, features), BF),
            pltpu.VMEM((line * rows, wide_max), F32),
            pltpu.VMEM((plan.pack, LANE), F32),
            pltpu.SemaphoreType.DMA((4,)),
        ],
        flops=2 * line * rows * features * wide_max,
        moved=5 << 20,
        limit=16,
    )(meta, *packs, *quarter)


def trans_weight(plan, meta, inners, wide):
    rows, features, line = plan.rows, plan.features, plan.line
    most = plan.down_max

    def kernel(meta_ref, *refs):
        inner_refs = refs[:line]
        wide_ref, keep_ref, send_ref, total = refs[line:]

        def run(b):
            own = plan.down_rows[b]
            lhs = jnp.concatenate([ref[...] for ref in inner_refs], axis=0)
            for i in range(plan.line_taps[b]):
                total[i * features : (i + 1) * features, :] = dot(
                    lhs, wide_ref[:, i * features : (i + 1) * features], ((0,), (0,))
                )
            for v in range(4):
                start = pl.multiple_of((meta_ref[7] ^ v) * own, LANE)
                piece = total[pl.ds(start, own), :]
                if own < most:
                    pad = jnp.zeros((most - own, features), F32)
                    piece = jnp.concatenate([piece, pad], axis=0)
                if v % 2 == 0:
                    keep_ref[v // 2] = piece
                else:
                    send_ref[v // 2] = piece.astype(BF)

        both(meta_ref, lambda: run(0), lambda: run(1))

    return call(
        kernel,
        [SMEM] + vmem(line + 1),
        [((2, most, features), F32), ((2, most, features), BF)],
        [pltpu.VMEM((4 * most, features), F32)],
        flops=2 * line * rows * features * 4 * most,
        moved=5 << 20,
        limit=20,
    )(meta, *inners, wide)


def inner_backward(plan, meta, pieces, low, act, vectors, gain):
    rows, features = plan.rows, plan.features

    def kernel(meta_ref, *refs):
        parts = refs[:-7]
        low_ref, act_ref, vec_ref, gain_ref, delta_ref, back_ref, out_ref = refs[-7:]
        total = keep_rows(total_of(parts), meta_ref[4])
        act_in = act_ref[...]
        unit, scale = norm_parts(act_in + low_ref[...].astype(F32))
        out_ref[...] = vec_ref[...]
        out_ref[1:2, :] = vec_ref[1:2, :] + jnp.sum(total, axis=0, keepdims=True)
        out_ref[2:3, :] = vec_ref[2:3, :] + jnp.sum(total * unit, axis=0, keepdims=True)
        back = norm_back(total, unit, scale, gain_ref[...])
        back_ref[...] = back
        delta_ref[...] = keep_rows(back * (1.0 - act_in * act_in), meta_ref[4]).astype(BF)

    return call(
        kernel,
        [SMEM] + vmem(len(pieces) + 4),
        [((rows, features), BF), ((rows, features), F32), ((8, features), F32)],
        [],
        moved=1 << 19,
        limit=6,
    )(meta, *pieces, low, act, vectors, gain)


def down_delta(plan, meta, pieces, delta_inner, act, small):
    rows, features = plan.rows, plan.features
    base, extra = up8(rows, 16), small.shape[0]

    def kernel(meta_ref, *refs):
        parts = refs[:-4]
        inner_ref, act_ref, small_ref, out_ref = refs[-4:]
        value = act_ref[...]
        total = total_of(parts) + inner_ref[...]
        delta = keep_rows(total * (1.0 - value * value), meta_ref[4])
        pad = jnp.zeros((base - rows, features), F32)
        out_ref[0:base, :] = jnp.concatenate([delta, pad], axis=0).astype(BF)
        high = small_ref[...].astype(BF)
        out_ref[base : base + extra, :] = high
        out_ref[base + extra :, :] = (small_ref[...] - high.astype(F32)).astype(BF)

    return call(
        kernel,
        [SMEM] + vmem(len(pieces) + 3),
        [((base + 2 * extra, features), BF)],
        [],
        moved=1 << 19,
        limit=8,
    )(meta, *pieces, delta_inner, act, small)[0]


def input_quarter(plan, meta, deltas, quarter):
    features, line = plan.features, plan.line
    rows = up8(plan.rows, 16)
    wide_max = 4 * plan.down_max

    def kernel(meta_ref, *refs):
        delta_refs, weights = refs[:line], refs[line : line + 4]
        out_ref, weight, wide, packed, sems = refs[line + 4 :]

        def run(b):
            copies = fetch_quarter(plan, b, meta_ref, weights, weight, sems)
            lhs = jnp.concatenate([ref[0:rows, :] for ref in delta_refs], axis=0)
            for copy in copies:
                copy.wait()
            for i in range(plan.line_taps[b]):
                wide[:, i * features : (i + 1) * features] = dot(
                    lhs, weight[i * features : (i + 1) * features, :], ((1,), (1,))
                )
            packed[...] = jnp.zeros_like(packed)
            for m in range(line):
                matrix_packed(plan, b, wide, m * rows, packed)
                out_ref[m] = packed[...].astype(BF)

        both(meta_ref, lambda: run(0), lambda: run(1))

    return call(
        kernel,
        [SMEM] + vmem(line) + [ANY] * 4,
        [((line, plan.pack, LANE), BF)],
        [
            pltpu.VMEM((wide_max, features), BF),
            pltpu.VMEM((line * rows, wide_max), F32),
            pltpu.VMEM((plan.pack, LANE), F32),
            pltpu.SemaphoreType.DMA((4,)),
        ],
        flops=2 * line * rows * features * wide_max,
        moved=4 << 20,
        limit=16,
    )(meta, *deltas, *quarter)[0]


def input_rows(plan, meta, packs, outer):
    features, length, line = plan.features, plan.length, plan.line

    def kernel(meta_ref, *refs):
        pack_refs = refs[:line]
        outer_ref, out_ref, stage, packed = refs[line:]

        def run(b):
            for m in range(line):
                packed[...] = pack_refs[m][...].astype(F32)
                unpack_taps(plan, b, packed, stage, (meta_ref[5] ^ m) * plan.line_taps[b])
            inner = get(stage, plan.factors[b] // 2, length)
            out_ref[...] = (inner + outer_ref[...]).astype(BF)

        both(meta_ref, lambda: run(0), lambda: run(1))

    return call(
        kernel,
        [SMEM] + vmem(line + 1),
        [((length, features), BF)],
        [split(plan.stage_rows, features), pltpu.VMEM((plan.pack, LANE), F32)],
        moved=3 << 20,
        limit=12,
    )(meta, *packs, outer)[0]


def down_weight(plan, meta, columns, even, odd, extra, loss_part):
    shards, rows, features, line = plan.shards, plan.rows, plan.features, plan.line
    half = shards // 2
    base = up8(rows, 16)
    most, tail = plan.down_max, up8(extra + 2, 16)

    def kernel(meta_ref, *refs):
        even_ref, odd_ref, loss_ref, grad_ref, sums_ref, delta, ordered, small = refs[4:12]
        col_refs, sems = refs[12:16], refs[16]
        copies = [pltpu.make_async_copy(refs[v], col_refs[v], sems.at[v]) for v in range(4)]
        for copy in copies:
            copy.start()
        me = meta_ref[1]
        for q in range(shards):
            source = (even_ref, odd_ref)[q // half]
            value = source[q % half, 0:base, :].astype(F32)
            at = me ^ plan.mask(q)
            ordered[pl.ds(at, 1), :] = jnp.sum(value, axis=0, keepdims=True)
            delta[q * rows : (q + 1) * rows, :] = value[:rows]
            high = source[q % half, base : base + extra, :].astype(F32)
            low = source[q % half, base + extra : base + 2 * extra, :].astype(F32)
            small[at] = high + low
        total = small[0]
        for i in range(1, shards):
            total = total + small[i]
        sums_ref[...] = jnp.zeros_like(sums_ref)
        sums_ref[0:extra, :] = total
        sums_ref[extra : extra + 1, :] = jnp.sum(ordered[...], axis=0, keepdims=True)
        sums_ref[extra + 1 : extra + 2, :] = jnp.broadcast_to(loss_ref[0:1, 0:1], (1, features))
        sums = sums_ref[...]
        high = sums.astype(BF)
        low = (sums - high.astype(F32)).astype(BF)
        grad_ref[most : most + tail, :] = high
        grad_ref[most + tail :, :] = low
        sums_ref[...] = high.astype(F32) + low.astype(F32)
        for copy in copies:
            copy.wait()
        for at, v in enumerate((0, 2, 1, 3)):
            steps = delta[at * line * rows : (at + 1) * line * rows, :].astype(BF)
            part = dot(col_refs[v][...], steps, ((0,), (0,)))
            total = part if at == 0 else total + part
        grad_ref[0:most, :] = total.astype(BF)

    return call(
        kernel,
        [SMEM] + [HBM] * 4 + vmem(3),
        [((most + 2 * tail, features), BF), ((tail, features), F32)],
        [
            pltpu.VMEM((shards * rows, features), F32),
            pltpu.VMEM((shards, features), F32),
            pltpu.VMEM((shards, extra, features), F32),
        ]
        + [pltpu.VMEM(column.shape, BF) for column in columns]
        + [pltpu.SemaphoreType.DMA((4,))],
        flops=2 * shards * rows * features * features,
        moved=4 << 20,
        limit=56,
    )(meta, *columns, even, odd, loss_part)


def finish(plan, meta, own, recv, mine, iso_sums, extra, ff_parts):
    features, most, tail = plan.features, plan.down_max, mine.shape[0]
    rows = plan.down_rows

    def kernel(
        meta_ref, own_ref, recv_ref, mine_ref, short_sum, long_sum,
        short_ref, long_ref, bias_ref, gain_ref, head_bias_ref, head_gain_ref, ff_ref, loss_ref,
    ):
        theirs = recv_ref[most : most + tail, :].astype(F32) + recv_ref[most + tail :, :].astype(F32)
        sums = mine_ref[...]
        total = sums + theirs
        first = 6 + ff_parts
        bias_ref[0, 1:2, :] = short_sum[...]
        bias_ref[1, 1:2, :] = long_sum[...]
        for b in range(2):
            bias_ref[b, 2:4, :] = total[first + 3 * b : first + 3 * b + 2]
            gain_ref[b : b + 1, :] = total[first + 3 * b + 2 : first + 3 * b + 3]
        head_bias_ref[...] = total[0:4]
        head_gain_ref[...] = total[4:6]
        ff_ref[...] = total[6 : 6 + ff_parts]
        loss_ref[...] = total[extra + 1 : extra + 2, 0:LANE] * (0.5 / (features * plan.length))

        def place(short_from, long_from, short_row, long_row):
            short_ref[...] = short_from[0 : rows[0], :].astype(F32)
            long_ref[...] = long_from[0 : rows[1], :].astype(F32)
            bias_ref[0, 0:1, :] = short_row[extra : extra + 1]
            bias_ref[1, 0:1, :] = long_row[extra : extra + 1]

        both(
            meta_ref,
            lambda: place(own_ref, recv_ref, sums, theirs),
            lambda: place(recv_ref, own_ref, theirs, sums),
        )

    return call(
        kernel,
        [SMEM] + vmem(5),
        [
            ((rows[0], features), F32),
            ((rows[1], features), F32),
            ((2, 4, features), F32),
            ((2, features), F32),
            ((4, features), F32),
            ((2, features), F32),
            ((ff_parts, features), F32),
            ((1, LANE), F32),
        ],
        [],
        moved=4 << 20,
        limit=12,
    )(meta, own, recv, mine, *iso_sums)


def natural_order(plan, meta, own, halves):
    shards = plan.shards
    line = plan.line
    rows, features = own

    def kernel(meta_ref, *refs):
        out_ref = refs[-1]
        for q in range(shards):
            out_ref[meta_ref[1] ^ plan.mask(q)] = refs[q // line][q % line].astype(F32)

    return call(
        kernel,
        [SMEM] + vmem(4),
        [((shards, rows, features), F32)],
        [],
        moved=3 << 20,
        limit=16,
    )(meta, *halves)[0]


ROOT_HALF = 0.7071067811865476
ROOT_TWO_PI = 0.3989422804014327


def head_rows(plan, meta, keep, recv, target, valid, merge, bias, gain, ff_in, ff_bias, ff_out):
    half_rows, features = keep.shape
    hidden = ff_in.shape[1]
    parts = hidden // features
    dims = (half_rows, features)

    def kernel(
        meta_ref, keep_ref, recv_ref, target_ref, valid_ref, merge_ref, bias_ref, gain_ref,
        in_bias_ref, in_hbm, out_hbm,
        out_ref, up_keep_ref, up_send_ref, normed_ref, act_ref, pre_delta_ref, ff_delta_ref,
        merged_delta_ref, vec_ref, loss_ref, slope_ref, in_ref, out_w_ref, sems,
    ):
        fetch_in = pltpu.make_async_copy(in_hbm, in_ref, sems.at[0])
        fetch_out = pltpu.make_async_copy(out_hbm, out_w_ref, sems.at[1])
        fetch_in.start()
        fetch_out.start()
        branch = meta_ref[0]
        merged = dot(keep_ref[...], merge_ref[branch]) + dot(recv_ref[...], merge_ref[1 - branch])
        merged = merged + bias_ref[0:1, :]
        unit, scale = norm_parts(merged)
        normed = (unit * gain_ref[0:1, :] + bias_ref[2:3, :]).astype(BF)
        normed_ref[...] = normed
        fetch_in.wait()
        fetch_out.wait()
        for c in range(parts):
            cols = slice(c * features, (c + 1) * features)
            pre = dot(normed, in_ref[:, cols]) + in_bias_ref[:, cols]
            share = 0.5 * (1.0 + lax.erf(pre * ROOT_HALF))
            slope_ref[:, cols] = share + pre * (jnp.exp(-0.5 * pre * pre) * ROOT_TWO_PI)
            act = (pre * share).astype(BF)
            act_ref[:, cols] = act
            part = dot(act, out_w_ref[cols, :])
            total = part if c == 0 else total + part
        unit_end, scale_end = norm_parts(merged + total + bias_ref[1:2, :])
        final = unit_end * gain_ref[1:2, :] + bias_ref[3:4, :]
        out_ref[...] = final.astype(BF)
        error = final - target_ref[...].astype(F32)
        weighted = valid_ref[...] * error
        loss = jnp.sum(jnp.sum(weighted * error, axis=0, keepdims=True), axis=1, keepdims=True)
        loss_ref[...] = jnp.broadcast_to(loss, loss_ref.shape)
        vec_ref[...] = jnp.zeros_like(vec_ref)
        vec_ref[3:4, :] = jnp.sum(weighted, axis=0, keepdims=True)
        vec_ref[5:6, :] = jnp.sum(weighted * unit_end, axis=0, keepdims=True)
        delta_sum = norm_back(weighted, unit_end, scale_end, gain_ref[1:2, :])
        delta_ff = delta_sum.astype(BF)
        ff_delta_ref[...] = delta_ff
        vec_ref[1:2, :] = jnp.sum(delta_ff.astype(F32), axis=0, keepdims=True)
        for c in range(parts):
            cols = slice(c * features, (c + 1) * features)
            pre_delta = dot(delta_ff, out_w_ref[cols, :], ((1,), (1,))) * slope_ref[:, cols]
            pre_delta = pre_delta.astype(BF)
            pre_delta_ref[:, cols] = pre_delta
            vec_ref[6 + c : 7 + c, :] = jnp.sum(pre_delta.astype(F32), axis=0, keepdims=True)
            part = dot(pre_delta, in_ref[:, cols], ((1,), (1,)))
            above = part if c == 0 else above + part
        vec_ref[2:3, :] = jnp.sum(above, axis=0, keepdims=True)
        vec_ref[4:5, :] = jnp.sum(above * unit, axis=0, keepdims=True)
        delta = norm_back(above, unit, scale, gain_ref[0:1, :]) + delta_sum
        delta = delta.astype(BF)
        merged_delta_ref[...] = delta
        vec_ref[0:1, :] = jnp.sum(delta.astype(F32), axis=0, keepdims=True)
        up_keep_ref[...] = dot(delta, merge_ref[branch], ((1,), (1,))).astype(BF)
        up_send_ref[...] = dot(delta, merge_ref[1 - branch], ((1,), (1,))).astype(BF)

    vec_rows = up8(6 + parts + 6)
    return call(
        kernel,
        [SMEM] + vmem(8) + [HBM] * 2,
        [
            (dims, BF), (dims, BF), (dims, BF), (dims, BF),
            ((half_rows, hidden), BF), ((half_rows, hidden), BF), (dims, BF), (dims, BF),
            ((vec_rows, features), F32), ((8, LANE), F32),
        ],
        [
            pltpu.VMEM((half_rows, hidden), F32),
            pltpu.VMEM((features, hidden), BF),
            pltpu.VMEM((hidden, features), BF),
            pltpu.SemaphoreType.DMA((2,)),
        ],
        flops=10 * half_rows * features * hidden,
        moved=14 << 20,
        limit=56,
    )(meta, keep, recv, target, valid, merge, bias, gain, ff_bias, ff_in, ff_out)


def head_weights(plan, meta, keep, recv, normed, act, pre_delta, ff_delta, merged_delta):
    shards = plan.shards
    half_rows, features = keep.shape
    hidden = act.shape[1]
    ff_rows, merge_rows = hidden // shards // 2, features // shards
    parts = hidden // features
    own = 2 * ff_rows + merge_rows

    def kernel(
        meta_ref, keep_hbm, recv_hbm, normed_hbm, act_hbm, pre_hbm, ff_hbm, merged_hbm,
        stay_near, stay_far, send_near, send_far, first, second, third,
        keep_ref, recv_ref, normed_ref, act_ref, pre_ref, ff_ref, merged_ref, sems,
    ):
        pairs = (
            (normed_hbm, normed_ref), (pre_hbm, pre_ref), (ff_hbm, ff_ref), (act_hbm, act_ref),
            (merged_hbm, merged_ref), (keep_hbm, keep_ref), (recv_hbm, recv_ref),
        )
        copies = [
            pltpu.make_async_copy(source, target, sems.at[i])
            for i, (source, target) in enumerate(pairs)
        ]
        for copy in copies:
            copy.start()
        branch = meta_ref[0]
        copies[0].wait()
        copies[1].wait()
        for c in range(parts):
            cols = slice(c * features, (c + 1) * features)
            first[cols, :] = dot(pre_ref[:, cols], normed_ref[...], ((0,), (0,))).astype(BF)
        copies[2].wait()
        copies[3].wait()
        for c in range(parts):
            cols = slice(c * features, (c + 1) * features)
            second[cols, :] = dot(act_ref[:, cols], ff_ref[...], ((0,), (0,))).astype(BF)
        for copy in copies[4:]:
            copy.wait()
        for side, ref in enumerate((keep_ref, recv_ref)):
            part = dot(ref[...], merged_ref[...], ((0,), (0,))).astype(BF)
            start = pl.multiple_of((branch ^ side) * features, 16)
            third[pl.ds(start, features), :] = part
        for q in range(shards):
            device = meta_ref[1] ^ plan.mask(q)
            targets = (stay_near, stay_far, send_near, send_far)
            target = targets[q // plan.line]
            for h in range(2):
                at = 2 * device + (branch ^ h)
                for start, count, source in (
                    (0, ff_rows, first),
                    (ff_rows, ff_rows, second),
                    (2 * ff_rows, merge_rows, third),
                ):
                    rows = pl.ds(pl.multiple_of(at * count, 16), count)
                    target[h, q % plan.line, start : start + count, :] = source[rows, :]

    return call(
        kernel,
        [SMEM] + [HBM] * 7,
        [((2, plan.line, own, features), BF)] * 4,
        [
            pltpu.VMEM((hidden, features), BF),
            pltpu.VMEM((hidden, features), BF),
            pltpu.VMEM((2 * features, features), BF),
        ]
        + [
            pltpu.VMEM(ref.shape, BF)
            for ref in (keep, recv, normed, act, pre_delta, ff_delta, merged_delta)
        ]
        + [pltpu.SemaphoreType.DMA((7,))],
        flops=4 * half_rows * features * hidden,
        moved=12 << 20,
        limit=56,
    )(meta, keep, recv, normed, act, pre_delta, ff_delta, merged_delta)


def hop(values, distance, shards):
    return lax.ppermute(values, "series", [(i, i ^ distance) for i in range(shards)])


def swap(values):
    return lax.ppermute(values, "branch", [(0, 1), (1, 0)])


def after(value, *others):
    return lax.optimization_barrier((value, others))[0]


def along_line(plan, own):
    return [own] + [hop(own, i << 2, plan.shards) for i in range(1, plan.line)]


def line_parts(plan, first, rest):
    return [first] + [hop(rest[i - 1], i << 2, plan.shards) for i in range(1, plan.line)]


def quad_gather(plan, own, later):
    side = hop(own, 2, plan.shards)
    return [own, hop(own, 1, plan.shards), side, hop(after(side, later), 1, plan.shards)]


def settle(value, *others):
    return lax.optimization_barrier((value,) + others)


def stacked(pieces):
    count, shape = len(pieces), pieces[0].shape

    def kernel(*refs):
        for i in range(count):
            refs[count][i] = refs[i][...]

    return call(kernel, vmem(count), [((count,) + shape, BF)], [], moved=1 << 20, limit=6)(*pieces)[0]


def gather_slots(plan, line, stack=jnp.stack):
    even = stack(line + [hop(value, 2, plan.shards) for value in line])
    return even, hop(even, 1, plan.shards)


def scatter_sum(plan, keep, send, *others):
    shards, line = plan.shards, plan.line
    first = keep + hop(send, 1, shards).astype(F32)
    second = first[:line] + hop(first[line:].astype(BF), 2, shards).astype(F32)
    if others:
        second, *others = settle(second, *others)
    pieces = line_parts(plan, second[0], [second[i].astype(BF) for i in range(1, line)])
    return (pieces, *others) if others else pieces


def rounded(values):
    return lax.reduce_precision(values, exponent_bits=8, mantissa_bits=7)


def layer_norm(values, gain_row, shift_row):
    center = values - jnp.mean(values, axis=-1, keepdims=True)
    spread = jnp.mean(center * center, axis=-1, keepdims=True)
    return center * lax.rsqrt(spread + EPSILON) * gain_row + shift_row


def gelu_exact(values):
    return jax.nn.gelu(values, approximate=False)


def product(a, b):
    return jnp.dot(a, b, preferred_element_type=F32)


def left_product(a, b):
    return jnp.einsum("mi,mo->io", a, b, preferred_element_type=F32)


def right_product(a, b):
    return jnp.einsum("mo,io->mi", a, b, preferred_element_type=F32)


def body(
    series_in, target, horizons, observed,
    down_short, iso_short, trans_short, down_long, iso_long, trans_long,
    branch_bias, branch_gain, merge_weight, head_bias, head_gain, ff_in, ff_in_bias, ff_out,
):
    shards = lax.axis_size("series")
    _, length, features = series_in.shape
    plan = Plan(
        shards,
        length,
        features,
        (down_short.shape[0], down_long.shape[0]),
        (iso_short.shape[0], iso_long.shape[0]),
    )
    line = plan.line
    half_rows = length // 2
    branch = lax.axis_index("branch")
    me = lax.axis_index("series")
    is_short = branch == 0
    iso_rows = jnp.where(is_short, plan.iso_rows[0], plan.iso_rows[1])
    meta = jnp.stack(
        [
            branch,
            me,
            (me * iso_rows) // features,
            (me * iso_rows) % features,
            jnp.where(is_short, plan.steps[0], plan.steps[1]),
            me // 4,
            me % 2,
            me % 4,
        ]
    ).astype(jnp.int32)
    series = series_in[0]
    biases, gain = branch_bias[0], branch_gain

    def chosen(short, long):
        rows = max(short.shape[0], long.shape[0])
        short = jnp.pad(short, ((0, rows - short.shape[0]), (0, 0)))
        long = jnp.pad(long, ((0, rows - long.shape[0]), (0, 0)))
        return jnp.where(is_short, short, long)

    def placed(own, other, b, rows):
        return jnp.where(branch == b, own, other)[:rows].astype(F32)

    blocks = prep_blocks(plan, meta, series)
    own_down = after(chosen(down_short, down_long), blocks)
    blocks = line_parts(plan, blocks[0], [blocks[i] for i in range(1, line)])
    down_quarter = quad_gather(plan, own_down, blocks)
    own_trans = after(chosen(trans_short, trans_long), blocks)
    keep, send, *columns = down_partial(plan, meta, blocks, down_quarter)
    pieces = line_parts(plan, keep, send)
    trans_quarter = quad_gather(plan, own_trans, pieces)
    low, act_down = low_rows(plan, meta, pieces, biases)
    low_own = gather_slots(plan, along_line(plan, low), stacked)
    low_own, trans_quarter = settle(low_own, trans_quarter)
    keep, send = iso_partial(plan, meta, low_own, iso_short, iso_long, False)
    low_other = swap(after(low_own[0], low_own[1]))
    pieces = scatter_sum(plan, keep, send)
    inner, act_iso = inner_rows(plan, meta, pieces, low, biases, gain)
    columns[2] = hop(after(columns[2], inner), 2, shards)
    inners, columns = settle(along_line(plan, inner), columns)
    packs = trans_forward(plan, meta, inners, trans_quarter)
    columns[3] = hop(after(columns[3], packs), 3, shards)
    packs = line_parts(plan, packs[0], [packs[i] for i in range(1, line)])
    packs, columns, low_other = settle(packs, columns, low_other)
    out_keep, out_send, act_trans = outer_rows(plan, meta, packs, series, biases, gain)
    out_recv = swap(out_send)
    columns[1] = hop(after(columns[1], out_keep), 1, shards)
    low_other = (low_other, hop(after(low_other, out_keep), 1, shards))
    out_recv, columns, low_other = settle(out_recv, columns, low_other)

    positions = branch * half_rows + jnp.arange(half_rows, dtype=jnp.int32)
    observed_half = lax.dynamic_slice_in_dim(observed[0], branch * half_rows, half_rows, 0)
    valid = (
        observed_half.astype(F32)
        * (positions >= SEQ_IN).astype(F32)
        * (positions < SEQ_IN + horizons[0]).astype(F32)
    )
    (
        out, up_keep, up_send, normed, act_ff, pre_delta, ff_delta, merged_delta, vec_head, loss_part
    ) = head_rows(
        plan, meta, out_keep, out_recv, target[0], valid[:, None], merge_weight, head_bias,
        head_gain, ff_in, ff_in_bias[None], ff_out,
    )
    up_recv = swap(up_send)
    near, far, near_send, far_send = head_weights(
        plan, meta, out_keep, out_recv, normed, act_ff, pre_delta, ff_delta, merged_delta
    )

    far_recv = hop(after(far_send, up_recv), 1, shards)
    outer, packs, vectors = outer_backward(plan, meta, up_keep, up_recv, series, act_trans, gain)
    far = (far.astype(F32) + after(far_recv, packs).astype(F32)).astype(BF)
    near_recv = hop(after(near_send, packs), 1, shards)
    share_recv = hop(far, 2, shards)
    packs = line_parts(plan, packs[0], [packs[i] for i in range(1, line)])
    keep, send, wide = trans_backward(plan, meta, packs, trans_quarter)
    trans_keep, trans_send = trans_weight(plan, meta, inners, wide)
    pieces, trans_send, share_recv, near_recv = settle(
        line_parts(plan, keep, send), trans_send, share_recv, near_recv
    )
    shares = near.astype(F32) + near_recv.astype(F32) + share_recv.astype(F32)
    share_recv = swap(shares[1].astype(BF))
    shares = shares[0]
    delta_iso, delta_inner, vectors = inner_backward(
        plan, meta, pieces, low, act_iso, vectors, gain
    )
    ff_parts = ff_in_bias.shape[0] // features
    selector = jnp.stack([is_short, branch == 1]).astype(F32)
    branch_rows = (selector[:, None, None] * vectors[None, 0:3]).reshape(6, features)
    small = jnp.concatenate([vec_head[: 6 + ff_parts], branch_rows], axis=0)
    count = small.shape[0]
    small = jnp.pad(small, ((0, up8(count, 16) - count), (0, 0)))
    trans_recv = hop(trans_send, 1, shards)
    deltas, trans_recv = settle(along_line(plan, delta_iso), trans_recv)
    trans_sum = trans_keep + trans_recv.astype(F32)
    trans_next = trans_sum[1].astype(BF)
    delta_own = gather_slots(plan, deltas)
    delta_own, trans_next, share_recv = settle(delta_own, trans_next, share_recv)
    shares = shares + share_recv.astype(F32)
    spread = line // 2
    share_recv = hop(shares[spread:].astype(BF), 4 * spread, shards)
    keep, send = iso_partial(plan, meta, delta_own, iso_short, iso_long, True)
    delta_other = swap(delta_own[0])
    pieces, delta_other = scatter_sum(plan, keep, send, delta_other)
    pieces, share_recv = settle(pieces, share_recv)
    shares = shares[:spread] + share_recv.astype(F32)
    payload = down_delta(plan, meta, pieces, delta_inner, act_down, small)
    delta_other = (delta_other, hop(after(delta_other, payload), 1, shards))
    trans_recv = hop(after(trans_next, payload), 2, shards)
    share_recv = hop(after(shares[1:].astype(BF), payload), 4, shards)
    first_grad = iso_weight(plan, meta, 0, low_own, low_other, delta_own, delta_other)
    deltas, trans_recv, share_recv, first_grad = settle(
        along_line(plan, payload), trans_recv, share_recv, first_grad
    )
    shares = rounded(shares[0] + share_recv[0].astype(F32))
    grad_trans = (trans_sum[0] + trans_recv.astype(F32)).astype(BF)
    packs = input_quarter(plan, meta, deltas, down_quarter)
    even = jnp.stack(deltas)
    odd = hop(after(even, packs), 2, shards)
    packs = line_parts(plan, packs[0], [packs[i] for i in range(1, line)])
    crossing = swap(after(jnp.concatenate([grad_trans, shares.astype(BF)], axis=0), odd))
    second_grad = iso_weight(
        plan, meta, 1, after(low_own, odd), low_other, delta_own, delta_other
    )
    packs, second_grad = settle(packs, second_grad)
    input_own = input_rows(plan, meta, packs, outer)
    trans_recv, share_recv = crossing[: plan.down_max], crossing[plan.down_max :]
    input_recv = swap(input_own)
    even = jnp.concatenate([even, odd], axis=0)
    delta_halves = (even, hop(after(even, input_own), 1, shards))
    share_recv = share_recv.astype(F32)
    ff_rows = ff_in_bias.shape[0] // shards // 2
    halves = [
        jnp.where(is_short, shares, share_recv),
        jnp.where(is_short, share_recv, shares),
    ]
    merge_own = jnp.concatenate([half[2 * ff_rows :] for half in halves], axis=0)
    extra = small.shape[0]
    grad_down, mine = down_weight(
        plan, meta, columns, *after(delta_halves, input_own), extra, loss_part
    )
    down_recv = swap(grad_down)
    merge_even = jnp.stack(along_line(plan, after(merge_own.astype(BF), grad_down)))
    merge_odd = hop(after(merge_even, grad_down), 2, shards)
    trans_recv = after(trans_recv, grad_down)
    trans_grads = [placed(grad_trans, trans_recv, b, plan.down_rows[b]) for b in range(2)]
    merge_odd, trans_grads = settle(merge_odd, trans_grads)
    merge_core = hop(merge_even, 1, shards), hop(merge_odd, 1, shards)
    input_total = input_own.astype(F32) + after(input_recv, merge_odd).astype(F32)
    merge_core, input_total = settle(merge_core, input_total)
    merge_total = natural_order(
        plan, meta, merge_own.shape, (merge_even, merge_odd, *merge_core)
    ).reshape(2, features, features)
    down_recv = after(down_recv, merge_total)
    short_down, long_down, bias_total, gain_total, head_sums, head_gains, ff_sums, loss = finish(
        plan, meta, grad_down, down_recv, mine, [first_grad[1], second_grad[1]], extra, ff_parts
    )
    return (
        out[None],
        loss[0, 0:1],
        input_total[None],
        short_down,
        first_grad[0],
        trans_grads[0],
        long_down,
        second_grad[0],
        trans_grads[1],
        bias_total,
        gain_total,
        merge_total,
        head_sums,
        head_gains,
        jnp.concatenate([half[:ff_rows] for half in halves], axis=0).T,
        ff_sums.reshape(-1),
        jnp.concatenate([half[ff_rows : 2 * ff_rows] for half in halves], axis=0),
    )


def fitted(matrix, row_total):
    return jnp.pad(matrix, ((0, row_total - matrix.shape[0]), (0, 0)))


def unpack(gathered_all, shards, rows_max, rows_own):
    features = gathered_all.shape[1]
    return gathered_all.reshape(shards, rows_max, features)[:, :rows_own].reshape(
        shards * rows_own, features
    )


def repack(gradient, shards, rows_max):
    rows_own = gradient.shape[0] // shards
    shaped = gradient.reshape(shards, rows_own, gradient.shape[1])
    return jnp.pad(shaped, ((0, 0), (0, rows_max - rows_own), (0, 0))).reshape(
        shards * rows_max, gradient.shape[1]
    )


def branch_pass(series_in, weights, shards, rows_max, biases, gain_row, factor):
    series_count, length, features = series_in.shape
    step_count = (length + factor) // factor
    margin = factor // 2
    weight_down = unpack(weights[0], shards, rows_max[0], factor * features // shards)
    weight_iso = unpack(weights[1], shards, rows_max[1], step_count * features // shards)
    weight_trans = unpack(weights[2], shards, rows_max[2], factor * features // shards).reshape(
        factor, features, features
    )
    blocks = jnp.pad(series_in, ((0, 0), (margin, step_count * factor - length - margin), (0, 0)))
    blocks = blocks.reshape(series_count * step_count, factor * features)
    act_down = jnp.tanh(product(blocks, weight_down) + biases[0])
    low_down = act_down.astype(jnp.bfloat16)
    padded = jnp.concatenate(
        [
            jnp.zeros((series_count, step_count - 1, features), jnp.bfloat16),
            low_down.reshape(series_count, step_count, features),
        ],
        axis=1,
    )
    unfolded = jnp.concatenate(
        [padded[:, offset : offset + step_count] for offset in range(step_count)], axis=2
    )
    unfolded = unfolded.reshape(series_count * step_count, step_count * features)
    act_iso = jnp.tanh(product(unfolded, weight_iso) + biases[1])
    inner_norm, inner_back = jax.vjp(
        layer_norm, act_iso + low_down.astype(jnp.float32), gain_row, biases[3]
    )
    low_inner = inner_norm.astype(jnp.bfloat16)
    spread_out = jnp.einsum(
        "mi,jio->mjo", low_inner, weight_trans, preferred_element_type=jnp.float32
    )
    act_trans = jnp.tanh(
        spread_out.reshape(series_count, step_count * factor, features)[:, :length] + biases[2]
    )
    result, outer_back = jax.vjp(
        layer_norm, act_trans + series_in.astype(jnp.float32), gain_row, biases[3]
    )
    stored = (
        blocks,
        weight_down,
        weight_iso,
        weight_trans,
        act_down,
        unfolded,
        act_iso,
        inner_back,
        low_inner,
        act_trans,
        outer_back,
    )
    return (result, stored)


def branch_back(series_in, weights, shards, rows_max, biases, gain_row, factor, upstream):
    series_count, length, features = series_in.shape
    step_count = (length + factor) // factor
    margin = factor // 2
    result, stored = branch_pass(series_in, weights, shards, rows_max, biases, gain_row, factor)
    (
        blocks,
        weight_down,
        weight_iso,
        weight_trans,
        act_down,
        unfolded,
        act_iso,
        inner_back,
        low_inner,
        act_trans,
        outer_back,
    ) = stored
    delta_outer, gain_outer, shift_outer = outer_back(upstream)
    delta_trans = (delta_outer * (1.0 - act_trans * act_trans)).astype(jnp.bfloat16)
    trans_blocks = jnp.pad(delta_trans, ((0, 0), (0, step_count * factor - length), (0, 0)))
    trans_blocks = trans_blocks.reshape(series_count * step_count, factor, features)
    grad_trans = jnp.einsum(
        "mi,mjo->jio", low_inner, trans_blocks, preferred_element_type=jnp.float32
    )
    grad_trans = grad_trans.reshape(factor * features, features)
    inner_upstream = jnp.einsum(
        "mjo,jio->mi", trans_blocks, weight_trans, preferred_element_type=jnp.float32
    )
    delta_inner, gain_inner, shift_inner = inner_back(inner_upstream)
    delta_iso = (delta_inner * (1.0 - act_iso * act_iso)).astype(jnp.bfloat16)
    grad_iso = left_product(unfolded, delta_iso)
    delta_unfold = right_product(delta_iso, weight_iso).reshape(
        series_count, step_count, step_count, features
    )
    delta_padded = jnp.zeros((series_count, 2 * step_count - 1, features), jnp.float32)
    for offset in range(step_count):
        delta_padded = delta_padded.at[:, offset : offset + step_count].add(
            delta_unfold[:, :, offset]
        )
    delta_low = (
        delta_padded[:, step_count - 1 :].reshape(series_count * step_count, features) + delta_inner
    )
    delta_down = (delta_low * (1.0 - act_down * act_down)).astype(jnp.bfloat16)
    grad_down = left_product(blocks, delta_down)
    delta_blocks = right_product(delta_down, weight_down).reshape(
        series_count, step_count * factor, features
    )
    delta_series = delta_blocks[:, margin : margin + length] + delta_outer
    vectors = jnp.stack(
        [
            jnp.sum(delta_down.astype(jnp.float32), axis=0),
            jnp.sum(delta_iso.astype(jnp.float32), axis=0),
            jnp.sum(delta_trans.astype(jnp.float32), axis=(0, 1)),
            shift_inner + shift_outer,
        ]
    )
    padded_grads = (
        repack(grad_down, shards, rows_max[0]),
        repack(grad_iso, shards, rows_max[1]),
        repack(grad_trans, shards, rows_max[2]),
    )
    return (delta_series, padded_grads, vectors, gain_inner + gain_outer)


def plain_body(
    series_in,
    target,
    horizons,
    observed,
    down_short,
    iso_short,
    trans_short,
    down_long,
    iso_long,
    trans_long,
    branch_bias,
    branch_gain,
    merge_weight,
    head_bias,
    head_gain,
    ff_in,
    ff_in_bias,
    ff_out,
):
    branch_index = lax.axis_index("branch")
    shards = lax.axis_size("series")
    series_count, length, features = series_in.shape
    rows_max = (
        max(down_short.shape[0], down_long.shape[0]),
        max(iso_short.shape[0], iso_long.shape[0]),
        max(trans_short.shape[0], trans_long.shape[0]),
    )
    is_short = branch_index == 0
    own_down = jnp.where(is_short, fitted(down_short, rows_max[0]), fitted(down_long, rows_max[0]))
    own_iso = jnp.where(is_short, fitted(iso_short, rows_max[1]), fitted(iso_long, rows_max[1]))
    own_trans = jnp.where(
        is_short, fitted(trans_short, rows_max[2]), fitted(trans_long, rows_max[2])
    )
    gathered = (
        lax.all_gather(own_down, "series", axis=0, tiled=True),
        lax.all_gather(own_iso, "series", axis=0, tiled=True),
        lax.all_gather(own_trans, "series", axis=0, tiled=True),
    )
    biases = branch_bias[0]
    gain_row = branch_gain[0]

    def forward_with(factor):
        return lambda: branch_pass(series_in, gathered, shards, rows_max, biases, gain_row, factor)[
            0
        ].astype(jnp.bfloat16)

    branch_out = lax.cond(is_short, forward_with(SCALE_S), forward_with(SCALE_L))
    received = lax.all_to_all(
        branch_out.reshape(series_count, length, 1, features),
        "branch",
        split_axis=1,
        concat_axis=2,
        tiled=True,
    )
    half_rows = received.shape[1]
    merge_rows = received.reshape(series_count * half_rows, 2 * features)
    merge_flat = merge_weight.reshape(2 * features, features)
    merged = product(merge_rows, merge_flat) + head_bias[0]
    normed, first_back = jax.vjp(layer_norm, merged, head_gain[0], head_bias[2])
    low_normed = normed.astype(jnp.bfloat16)
    pre_ff = product(low_normed, ff_in) + ff_in_bias
    activated, gelu_back = jax.vjp(gelu_exact, pre_ff)
    low_act = activated.astype(jnp.bfloat16)
    ff_result = product(low_act, ff_out) + head_bias[1]
    final_out, second_back = jax.vjp(layer_norm, merged + ff_result, head_gain[1], head_bias[3])
    final_rows = final_out.reshape(series_count, half_rows, features)
    positions = branch_index * half_rows + jnp.arange(half_rows, dtype=jnp.int32)
    observed_half = lax.dynamic_slice_in_dim(observed, branch_index * half_rows, half_rows, 1)
    valid_mask = (
        observed_half.astype(jnp.float32)
        * (positions >= SEQ_IN).astype(jnp.float32)
        * (positions < SEQ_IN + horizons[:, None]).astype(jnp.float32)
    )
    error_rows = final_rows - target.astype(jnp.float32)
    weighted = valid_mask[:, :, None] * error_rows
    series_part = 0.5 * jnp.sum(weighted * error_rows, axis=(1, 2)) / (features * length)
    delta_sum, gain_second, shift_second = second_back(
        weighted.reshape(series_count * half_rows, features)
    )
    delta_ff = delta_sum.astype(jnp.bfloat16)
    grad_ff_out = left_product(low_act, delta_ff)
    delta_act = right_product(delta_ff, ff_out)
    (delta_pre,) = gelu_back(delta_act)
    low_pre = delta_pre.astype(jnp.bfloat16)
    grad_ff_in = left_product(low_normed, low_pre)
    delta_normed = right_product(low_pre, ff_in)
    delta_first, gain_first, shift_first = first_back(delta_normed)
    delta_merged = (delta_first + delta_sum).astype(jnp.bfloat16)
    grad_merge = left_product(merge_rows, delta_merged).reshape(2, features, features)
    delta_rows = (
        right_product(delta_merged, merge_flat)
        .astype(jnp.bfloat16)
        .reshape(series_count, half_rows, 2, features)
    )
    back_rows = lax.all_to_all(delta_rows, "branch", split_axis=2, concat_axis=1, tiled=True)
    upstream = back_rows.astype(jnp.float32).reshape(series_count, length, features)
    ff_shares = (
        lax.psum_scatter(grad_ff_in, "series", scatter_dimension=1, tiled=True),
        lax.psum_scatter(grad_ff_out, "series", scatter_dimension=0, tiled=True),
    )
    weights_back = (
        lax.all_gather(own_down, "series", axis=0, tiled=True),
        lax.all_gather(own_iso, "series", axis=0, tiled=True),
        lax.all_gather(own_trans, "series", axis=0, tiled=True),
    )

    def backward_with(factor):
        return lambda: branch_back(
            series_in, weights_back, shards, rows_max, biases, gain_row, factor, upstream
        )

    delta_series, padded_grads, vectors, gain_grad = lax.cond(
        is_short, backward_with(SCALE_S), backward_with(SCALE_L)
    )
    reduced = (
        lax.psum_scatter(padded_grads[0], "series", scatter_dimension=0, tiled=True),
        lax.psum_scatter(padded_grads[1], "series", scatter_dimension=0, tiled=True),
        lax.psum_scatter(padded_grads[2], "series", scatter_dimension=0, tiled=True),
    )
    short_flag = is_short.astype(jnp.float32)
    long_flag = 1.0 - short_flag
    summed = (
        lax.psum(delta_series.astype(jnp.bfloat16), "branch").astype(jnp.float32),
        lax.psum(series_part.astype(jnp.bfloat16), "branch").astype(jnp.float32),
        lax.psum(
            (short_flag * reduced[0][: down_short.shape[0]]).astype(jnp.bfloat16), "branch"
        ).astype(jnp.float32),
        lax.psum((short_flag * reduced[1]).astype(jnp.bfloat16), "branch").astype(jnp.float32),
        lax.psum(
            (short_flag * reduced[2][: trans_short.shape[0]]).astype(jnp.bfloat16), "branch"
        ).astype(jnp.float32),
        lax.psum((long_flag * reduced[0]).astype(jnp.bfloat16), "branch").astype(jnp.float32),
        lax.psum(
            (long_flag * reduced[1][: iso_long.shape[0]]).astype(jnp.bfloat16), "branch"
        ).astype(jnp.float32),
        lax.psum((long_flag * reduced[2]).astype(jnp.bfloat16), "branch").astype(jnp.float32),
        lax.psum(ff_shares[0].astype(jnp.bfloat16), "branch").astype(jnp.float32),
        lax.psum(ff_shares[1].astype(jnp.bfloat16), "branch").astype(jnp.float32),
    )
    selector = (jnp.arange(2, dtype=jnp.int32) == branch_index).astype(jnp.float32)
    full_bias = selector[:, None, None] * vectors[None]
    full_gain = selector[:, None] * gain_grad[None]
    head_vectors = jnp.stack(
        [
            jnp.sum(delta_merged.astype(jnp.float32), axis=0),
            jnp.sum(delta_ff.astype(jnp.float32), axis=0),
            shift_first,
            shift_second,
        ]
    )
    head_gains = jnp.stack([gain_first, gain_second])
    ff_bias_grad = jnp.sum(low_pre.astype(jnp.float32), axis=0)
    totals = lax.psum(
        (grad_merge, head_vectors, head_gains, ff_bias_grad, full_bias, full_gain),
        ("branch", "series"),
    )
    return (
        final_rows.astype(jnp.bfloat16),
        summed[1],
        summed[0],
        summed[2],
        summed[3],
        summed[4],
        summed[5],
        summed[6],
        summed[7],
        totals[4],
        totals[5],
        totals[0],
        totals[1],
        totals[2],
        summed[8],
        totals[3],
        summed[9],
    )


def solution(mesh):
    placed = (
        P("series", None, None),
        P("series", "branch", None),
        P("series"),
        P("series", None),
        P("series", None),
        P("series", None),
        P("series", None),
        P("series", None),
        P("series", None),
        P("series", None),
        P("branch", None, None),
        P("branch", None),
        P(),
        P(),
        P(),
        P(),
        P(),
        P(),
    )

    def run(*args):
        shards = mesh.shape["series"]
        features = args[0].shape[2]
        down_rows = [args[i].shape[0] // shards for i in (4, 7)]
        iso_rows = [args[i].shape[0] // shards for i in (5, 8)]
        fits = (
            args[0].shape[0] == shards
            and shards == 16
            and shards & (shards - 1) == 0
            and all(r % LANE == 0 and r <= features and 4 * r % features == 0 for r in down_rows)
            and all(r % 16 == 0 for r in iso_rows)
        )
        return jax.shard_map(
            body if fits else plain_body,
            mesh=mesh,
            in_specs=placed,
            out_specs=(
                P("series", "branch", None),
                P("series"),
                P("series", None, None),
                P("series", None),
                P("series", None),
                P("series", None),
                P("series", None),
                P("series", None),
                P("series", None),
                P(),
                P(),
                P(),
                P(),
                P(),
                P(None, "series"),
                P(),
                P("series", None),
            ),
            check_vma=False,
        )(*args)

    return run
```

```python
import functools

import jax
import jax.numpy as jnp
from jax import lax
from jax.experimental import pallas as pl
from jax.experimental.pallas import tpu as pltpu
from jax.sharding import PartitionSpec as P

SCALE_S = 12
SCALE_L = 16
SEQ_IN = 96
EPSILON = 1e-05
LANE = 128

BF = jnp.bfloat16
F32 = jnp.float32


def up8(count, base=8):
    return -(-count // base) * base


class Plan:
    def __init__(self, shards, length, features, down_rows, iso_rows):
        self.shards, self.length, self.features = shards, length, features
        self.factors = (SCALE_S, SCALE_L)
        self.steps = tuple((length + k) // k for k in self.factors)
        self.rows = up8(max(self.steps))
        self.down_rows = down_rows
        self.iso_rows = iso_rows
        self.down_max, self.iso_max = max(down_rows), max(iso_rows)
        self.line = shards // 4
        self.line_taps = tuple(4 * r // features for r in down_rows)
        blocks = features // LANE
        self.pack = up8(max(t * blocks * n for t, n in zip(self.line_taps, self.steps)), 16)
        self.taps = tuple(
            max(-(-((d * r) % features + r) // features) for d in range(shards)) for r in iso_rows
        )
        self.taps_max = max(self.taps)
        self.stage_rows = max(k * up8(n) for k, n in zip(self.factors, self.steps))

    def mask(self, slot):
        core, rest = divmod(slot, 2 * self.line)
        side, line = divmod(rest, self.line)
        return core | (side << 1) | (line << 2)


def vmem(count):
    return [pl.BlockSpec(memory_space=pltpu.VMEM) for _ in range(count)]


SMEM = pl.BlockSpec(memory_space=pltpu.SMEM)
ANY = pl.BlockSpec(memory_space=pl.ANY)
HBM = pl.BlockSpec(memory_space=pltpu.HBM)


def call(body, in_specs, outs, scratch, flops=0, moved=0, limit=56):
    return pl.pallas_call(
        body,
        out_shape=[jax.ShapeDtypeStruct(s, d) for s, d in outs],
        in_specs=in_specs,
        out_specs=vmem(len(outs)),
        scratch_shapes=scratch,
        compiler_params=pltpu.CompilerParams(vmem_limit_bytes=limit << 20),
        cost_estimate=pl.CostEstimate(flops=flops, bytes_accessed=moved, transcendentals=0),
    )


def dot(a, b, dims=((1,), (0,))):
    return lax.dot_general(a, b, (dims, ((), ())), preferred_element_type=F32)


def norm_parts(values):
    center = values - jnp.mean(values, axis=-1, keepdims=True)
    spread = jnp.mean(center * center, axis=-1, keepdims=True)
    scale = lax.rsqrt(spread + EPSILON)
    return center * scale, scale


def norm_back(upstream, unit, scale, gain):
    inner = upstream * gain
    first = jnp.mean(inner, axis=-1, keepdims=True)
    second = jnp.mean(inner * unit, axis=-1, keepdims=True)
    return scale * (inner - first - unit * second)


def keep_rows(values, count):
    index = lax.broadcasted_iota(jnp.int32, values.shape, 0)
    return jnp.where(index < count, values, 0.0)


def both(meta, short, long):
    pl.when(meta[0] == 0)(short)
    pl.when(meta[0] == 1)(long)


def split(rows, features):
    return pltpu.VMEM((features // LANE, rows, LANE), F32)


def put(ref, start, values, stride=1):
    count = values.shape[0]
    where = pl.ds(start, count) if stride == 1 else pl.ds(start, count, stride=stride)
    for c in range(ref.shape[0]):
        ref[c, where, :] = values[:, c * LANE : (c + 1) * LANE]


def get(ref, start, count, stride=1):
    where = pl.ds(start, count) if stride == 1 else pl.ds(start, count, stride=stride)
    return jnp.concatenate([ref[c, where, :] for c in range(ref.shape[0])], axis=1)


def split(rows, features):
    return pltpu.VMEM((features // LANE, rows, LANE), F32)


def put(ref, start, values, stride=1):
    count = values.shape[0]
    where = pl.ds(start, count) if stride == 1 else pl.ds(start, count, stride=stride)
    for c in range(ref.shape[0]):
        ref[c, where, :] = values[:, c * LANE : (c + 1) * LANE]


def get(ref, start, count, stride=1):
    where = pl.ds(start, count) if stride == 1 else pl.ds(start, count, stride=stride)
    return jnp.concatenate([ref[c, where, :] for c in range(ref.shape[0])], axis=1)


def pack_taps(plan, b, stage, first, packed):
    k, n = plan.factors[b], plan.steps[b]
    blocks = plan.features // LANE
    for i in range(plan.line_taps[b]):
        for c in range(blocks):
            at = (i * blocks + c) * n
            packed[at : at + n, :] = stage[c, pl.ds(first + i, n, stride=k), :]


def unpack_taps(plan, b, packed, stage, first):
    k, n = plan.factors[b], plan.steps[b]
    blocks = plan.features // LANE
    for i in range(plan.line_taps[b]):
        for c in range(blocks):
            at = (i * blocks + c) * n
            stage[c, pl.ds(first + i, n, stride=k), :] = packed[at : at + n, :]


def packed_matrix(plan, b, packed, base, matrix):
    n = plan.steps[b]
    for g in range(plan.line_taps[b] * plan.features // LANE):
        matrix[base : base + n, g * LANE : (g + 1) * LANE] = packed[g * n : (g + 1) * n, :]


def matrix_packed(plan, b, matrix, base, packed):
    n = plan.steps[b]
    for g in range(plan.line_taps[b] * plan.features // LANE):
        packed[g * n : (g + 1) * n, :] = matrix[base : base + n, g * LANE : (g + 1) * LANE]


def fetch_quarter(plan, b, meta_ref, sources, target, sems):
    own = plan.down_rows[b]
    quad = meta_ref[7]
    copies = []
    for v, source in enumerate(sources):
        start = pl.multiple_of((quad ^ v) * own, LANE)
        copies.append(
            pltpu.make_async_copy(
                source.at[pl.ds(0, own)], target.at[pl.ds(start, own)], sems.at[v]
            )
        )
    for copy in copies:
        copy.start()
    return copies


def total_of(parts):
    total = parts[0][...].astype(F32)
    for piece in parts[1:]:
        total = total + piece[...].astype(F32)
    return total


def prep_blocks(plan, meta, series):
    length, features, line = plan.length, plan.features, plan.line

    def kernel(meta_ref, x_ref, out_ref, wide, packed):
        def run(b):
            margin = plan.factors[b] // 2
            wide[...] = jnp.zeros_like(wide)
            put(wide, margin, x_ref[...].astype(F32))
            packed[...] = jnp.zeros_like(packed)
            for z in range(line):
                pack_taps(plan, b, wide, z * plan.line_taps[b], packed)
                out_ref[z ^ meta_ref[5]] = packed[...].astype(BF)

        both(meta_ref, lambda: run(0), lambda: run(1))

    return call(
        kernel,
        [SMEM] + vmem(1),
        [((line, plan.pack, LANE), BF)],
        [split(plan.stage_rows, features), pltpu.VMEM((plan.pack, LANE), F32)],
        moved=2 * length * features * 2,
        limit=8,
    )(meta, series)[0]


def down_partial(plan, meta, blocks, quarter):
    rows, features, line = plan.rows, plan.features, plan.line
    wide_max = 4 * plan.down_max

    def kernel(meta_ref, *refs):
        packs, weights = refs[:line], refs[line : line + 4]
        keep_ref, send_ref, *col_refs = refs[line + 4 : line + 10]
        weight, wide, packed, cols, sems = refs[line + 10 :]

        def run(b):
            copies = fetch_quarter(plan, b, meta_ref, weights, weight, sems)
            own = plan.down_rows[b]
            wide[...] = jnp.zeros_like(wide)
            for m in range(line):
                packed[...] = packs[m][...].astype(F32)
                packed_matrix(plan, b, packed, m * rows, wide)
            matrix = wide[...].astype(BF)
            for u in range(4):
                piece = matrix[:, u * own : (u + 1) * own]
                if own < plan.down_max:
                    pad = jnp.zeros((line * rows, plan.down_max - own), BF)
                    piece = jnp.concatenate([piece, pad], axis=1)
                cols[u ^ meta_ref[7]] = piece
            for v in range(4):
                col_refs[v][...] = cols[v]
            for copy in copies:
                copy.wait()
            part = dot(matrix[:, : 4 * own], weight[0 : 4 * own, :])
            keep_ref[...] = part[:rows]
            for m in range(1, line):
                send_ref[m - 1] = part[m * rows : (m + 1) * rows].astype(BF)

        both(meta_ref, lambda: run(0), lambda: run(1))

    return call(
        kernel,
        [SMEM] + vmem(line) + [ANY] * 4,
        [
            ((rows, features), F32),
            ((line - 1, rows, features), BF),
        ]
        + [((line * rows, plan.down_max), BF)] * 4,
        [
            pltpu.VMEM((wide_max, features), BF),
            pltpu.VMEM((line * rows, wide_max), F32),
            pltpu.VMEM((plan.pack, LANE), F32),
            pltpu.VMEM((4, line * rows, plan.down_max), BF),
            pltpu.SemaphoreType.DMA((4,)),
        ],
        flops=2 * line * rows * features * wide_max,
        moved=5 << 20,
        limit=16,
    )(meta, *blocks, *quarter)


def low_rows(plan, meta, pieces, biases):
    rows, features = plan.rows, plan.features

    def kernel(meta_ref, *refs):
        parts, bias_ref, low_ref, act_ref = refs[:-3], refs[-3], refs[-2], refs[-1]
        act = keep_rows(jnp.tanh(total_of(parts) + bias_ref[0:1, :]), meta_ref[4])
        act_ref[...] = act
        low_ref[...] = act.astype(BF)

    return call(
        kernel,
        [SMEM] + vmem(len(pieces) + 1),
        [((rows, features), BF), ((rows, features), F32)],
        [],
        moved=1 << 19,
        limit=4,
    )(meta, *pieces, biases)


def time_major(plan, halves, stage, target, lead):
    shards, rows = plan.shards, plan.rows
    half = shards // 2
    for q in range(shards):
        put(stage, q, halves[q // half][q % half].astype(F32), shards)
    body = shards * rows
    if lead:
        target[0 : lead * shards, :] = jnp.zeros((lead * shards, target.shape[1]), BF)
    target[lead * shards : lead * shards + body, :] = get(stage, 0, body).astype(BF)
    rest = target.shape[0] - lead * shards - body
    if rest:
        target[lead * shards + body :, :] = jnp.zeros((rest, target.shape[1]), BF)


def pad_weight(plan, b, meta_ref, source, target, sem):
    width, own, end = target.shape[1], plan.iso_rows[b], plan.taps[b] * target.shape[1]
    target[0:width, :] = jnp.zeros((width, width), BF)
    target[own:end, :] = jnp.zeros((end - own, width), BF)
    shift = pl.multiple_of(meta_ref[3], 16)
    copy = pltpu.make_async_copy(source, target.at[pl.ds(shift, plan.iso_rows[b])], sem)
    copy.start()
    return copy


def iso_partial(plan, meta, halves, w_short, w_long, backward):
    shards, rows, features = plan.shards, plan.rows, plan.features
    half = shards // 2
    extra = plan.taps_max + 2
    buffer = (max(plan.steps) + rows + extra) * shards

    def kernel(
        meta_ref, even_ref, odd_ref, ws_ref, wl_ref, keep_ref, send_ref, stage, lined, padded, sem
    ):
        first = meta_ref[2]

        def run(b, w_ref):
            n, taps = plan.steps[b], plan.taps[b]
            copy = pad_weight(plan, b, meta_ref, w_ref, padded, sem)
            lead = extra if backward else n - 1
            time_major(plan, (even_ref, odd_ref), stage, lined, lead)
            copy.wait()
            for m in range(taps):
                start = extra + n - 1 - first - m if backward else first + m
                start = pl.multiple_of(start * shards, 16)
                window = lined[pl.ds(start, rows * shards), :]
                weight = padded[m * features : (m + 1) * features, :]
                part = dot(window, weight, ((1,), (1,)) if backward else ((1,), (0,)))
                total = part if m == 0 else total + part
            put(stage, 0, total)
            for q in range(shards):
                piece = get(stage, q, rows, shards)
                if q < half:
                    keep_ref[q] = piece
                else:
                    send_ref[q - half] = piece.astype(BF)

        both(meta_ref, lambda: run(0, ws_ref), lambda: run(1, wl_ref))

    return call(
        kernel,
        [SMEM] + vmem(2) + [HBM] * 2,
        [((half, rows, features), F32), ((half, rows, features), BF)],
        [
            split(rows * shards, features),
            pltpu.VMEM((buffer, features), BF),
            pltpu.VMEM((plan.taps_max * features, features), BF),
            pltpu.SemaphoreType.DMA,
        ],
        flops=2 * shards * rows * features * features * plan.taps_max,
        moved=10 << 20,
        limit=56 if backward else 26,
    )(meta, *halves, w_short, w_long)


def iso_weight(plan, meta, b, low_own, low_other, delta_own, delta_other):
    shards, rows, features = plan.shards, plan.rows, plan.features
    half = shards // 2
    n, taps, own = plan.steps[b], plan.taps[b], plan.iso_rows[b]
    buffer = (n - 1 + rows + taps + 1) * shards

    def kernel(meta_ref, *refs):
        lows, deltas = refs[0:4], refs[4:8]
        grad_ref, sum_ref, stage, lined, delta, total, ordered = refs[8:]
        me = meta_ref[1]

        def load(low, steps):
            for q in range(shards):
                ordered[pl.ds(me ^ plan.mask(q), 1), :] = jnp.sum(
                    steps[q // half][q % half].astype(F32), axis=0, keepdims=True
                )
            time_major(plan, steps, stage, delta, 0)
            time_major(plan, low, stage, lined, n - 1)

        pl.when(meta_ref[0] == b)(lambda: load(lows[0:2], deltas[0:2]))
        pl.when(meta_ref[0] != b)(lambda: load(lows[2:4], deltas[2:4]))
        sum_ref[...] = jnp.sum(ordered[...], axis=0, keepdims=True)
        flat = me * own
        first = flat // features
        for m in range(taps):
            start = pl.multiple_of((first + m) * shards, 16)
            window = lined[pl.ds(start, rows * shards), :]
            total[m * features : (m + 1) * features, :] = dot(window, delta[...], ((0,), (0,)))
        shift = pl.multiple_of(flat % features, 16)
        grad_ref[...] = total[pl.ds(shift, own), :]

    return call(
        kernel,
        [SMEM] + vmem(8),
        [((own, features), F32), ((1, features), F32)],
        [
            split(rows * shards, features),
            pltpu.VMEM((buffer, features), BF),
            pltpu.VMEM((rows * shards, features), BF),
            pltpu.VMEM((taps * features, features), F32),
            pltpu.VMEM((shards, features), F32),
        ],
        flops=2 * shards * rows * features * features * taps,
        moved=10 << 20,
        limit=32,
    )(meta, *low_own, *low_other, *delta_own, *delta_other)


def inner_rows(plan, meta, pieces, low, biases, gain):
    rows, features = plan.rows, plan.features

    def kernel(meta_ref, *refs):
        parts = refs[:-5]
        low_ref, bias_ref, gain_ref, inner_ref, act_ref = refs[-5:]
        act = jnp.tanh(total_of(parts) + bias_ref[1:2, :])
        act_ref[...] = act
        unit, _ = norm_parts(act + low_ref[...].astype(F32))
        inner = unit * gain_ref[...] + bias_ref[3:4, :]
        inner_ref[...] = keep_rows(inner, meta_ref[4]).astype(BF)

    return call(
        kernel,
        [SMEM] + vmem(len(pieces) + 3),
        [((rows, features), BF), ((rows, features), F32)],
        [],
        moved=1 << 19,
        limit=4,
    )(meta, *pieces, low, biases, gain)


def trans_forward(plan, meta, inners, quarter):
    rows, features, line = plan.rows, plan.features, plan.line
    wide_max = 4 * plan.down_max

    def kernel(meta_ref, *refs):
        inner_refs, weights = refs[:line], refs[line : line + 4]
        out_ref, weight, wide, packed, sems = refs[line + 4 :]

        def run(b):
            copies = fetch_quarter(plan, b, meta_ref, weights, weight, sems)
            lhs = jnp.concatenate([ref[...] for ref in inner_refs], axis=0)
            for copy in copies:
                copy.wait()
            for i in range(plan.line_taps[b]):
                wide[:, i * features : (i + 1) * features] = dot(
                    lhs, weight[i * features : (i + 1) * features, :]
                )
            packed[...] = jnp.zeros_like(packed)
            for m in range(line):
                matrix_packed(plan, b, wide, m * rows, packed)
                out_ref[m] = packed[...].astype(BF)

        both(meta_ref, lambda: run(0), lambda: run(1))

    return call(
        kernel,
        [SMEM] + vmem(line) + [ANY] * 4,
        [((line, plan.pack, LANE), BF)],
        [
            pltpu.VMEM((wide_max, features), BF),
            pltpu.VMEM((line * rows, wide_max), F32),
            pltpu.VMEM((plan.pack, LANE), F32),
            pltpu.SemaphoreType.DMA((4,)),
        ],
        flops=2 * line * rows * features * wide_max,
        moved=4 << 20,
        limit=16,
    )(meta, *inners, *quarter)[0]


def outer_rows(plan, meta, packs, series, biases, gain):
    features, length, line = plan.features, plan.length, plan.line
    half_rows = length // 2

    def kernel(meta_ref, *refs):
        pack_refs = refs[:line]
        x_ref, bias_ref, gain_ref, keep_ref, send_ref, act_ref, stage, packed = refs[line:]

        def run(b):
            for m in range(line):
                packed[...] = pack_refs[m][...].astype(F32)
                unpack_taps(plan, b, packed, stage, (meta_ref[5] ^ m) * plan.line_taps[b])

        both(meta_ref, lambda: run(0), lambda: run(1))
        act = jnp.tanh(get(stage, 0, length) + bias_ref[2:3, :])
        act_ref[...] = act
        unit, _ = norm_parts(act + x_ref[...].astype(F32))
        put(stage, 0, unit * gain_ref[...] + bias_ref[3:4, :])
        mine = pl.multiple_of(meta_ref[0] * half_rows, 8)
        other = pl.multiple_of((1 - meta_ref[0]) * half_rows, 8)
        keep_ref[...] = get(stage, mine, half_rows).astype(BF)
        send_ref[...] = get(stage, other, half_rows).astype(BF)

    return call(
        kernel,
        [SMEM] + vmem(line + 3),
        [((half_rows, features), BF), ((half_rows, features), BF), ((length, features), F32)],
        [split(plan.stage_rows, features), pltpu.VMEM((plan.pack, LANE), F32)],
        moved=6 << 20,
        limit=16,
    )(meta, *packs, series, biases, gain)


def outer_backward(plan, meta, up_keep, up_recv, series, act, gain):
    features, length, line = plan.features, plan.length, plan.line
    half_rows = length // 2

    def kernel(
        meta_ref, uk_ref, ur_ref, x_ref, act_ref, gain_ref,
        outer_ref, taps_ref, vec_ref, stage, upstream, packed,
    ):
        mine = pl.multiple_of(meta_ref[0] * half_rows, 8)
        other = pl.multiple_of((1 - meta_ref[0]) * half_rows, 8)
        upstream[pl.ds(mine, half_rows), :] = uk_ref[...].astype(F32)
        upstream[pl.ds(other, half_rows), :] = ur_ref[...].astype(F32)
        act_value = act_ref[...]
        unit, scale = norm_parts(act_value + x_ref[...].astype(F32))
        above = upstream[...]
        vec_ref[...] = jnp.zeros_like(vec_ref)
        vec_ref[1:2, :] = jnp.sum(above, axis=0, keepdims=True)
        vec_ref[2:3, :] = jnp.sum(above * unit, axis=0, keepdims=True)
        outer = norm_back(above, unit, scale, gain_ref[...])
        outer_ref[...] = outer
        delta = (outer * (1.0 - act_value * act_value)).astype(BF).astype(F32)
        vec_ref[0:1, :] = jnp.sum(delta, axis=0, keepdims=True)
        put(stage, 0, delta)
        put(stage, length, jnp.zeros((plan.stage_rows - length, features), F32))
        packed[...] = jnp.zeros_like(packed)

        def run(b):
            for m in range(line):
                pack_taps(plan, b, stage, (meta_ref[5] ^ m) * plan.line_taps[b], packed)
                taps_ref[m] = packed[...].astype(BF)

        both(meta_ref, lambda: run(0), lambda: run(1))

    return call(
        kernel,
        [SMEM] + vmem(5),
        [((length, features), F32), ((line, plan.pack, LANE), BF), ((8, features), F32)],
        [
            split(plan.stage_rows, features),
            pltpu.VMEM((length, features), F32),
            pltpu.VMEM((plan.pack, LANE), F32),
        ],
        moved=8 << 20,
        limit=20,
    )(meta, up_keep, up_recv, series, act, gain)


def trans_backward(plan, meta, packs, quarter):
    rows, features, line = plan.rows, plan.features, plan.line
    wide_max = 4 * plan.down_max

    def kernel(meta_ref, *refs):
        pack_refs, weights = refs[:line], refs[line : line + 4]
        keep_ref, send_ref, wide_ref, weight, wide, packed, sems = refs[line + 4 :]

        def run(b):
            copies = fetch_quarter(plan, b, meta_ref, weights, weight, sems)
            wide[...] = jnp.zeros_like(wide)
            for m in range(line):
                packed[...] = pack_refs[m][...].astype(F32)
                packed_matrix(plan, b, packed, m * rows, wide)
            matrix = wide[...].astype(BF)
            wide_ref[...] = matrix
            for copy in copies:
                copy.wait()
            for i in range(plan.line_taps[b]):
                part = dot(
                    matrix[:, i * features : (i + 1) * features],
                    weight[i * features : (i + 1) * features, :],
                    ((1,), (1,)),
                )
                total = part if i == 0 else total + part
            keep_ref[...] = total[:rows]
            for m in range(1, line):
                send_ref[m - 1] = total[m * rows : (m + 1) * rows].astype(BF)

        both(meta_ref, lambda: run(0), lambda: run(1))

    return call(
        kernel,
        [SMEM] + vmem(line) + [ANY] * 4,
        [
            ((rows, features), F32),
            ((line - 1, rows, features), BF),
            ((line * rows, wide_max), BF),
        ],
        [
            pltpu.VMEM((wide_max, features), BF),
            pltpu.VMEM((line * rows, wide_max), F32),
            pltpu.VMEM((plan.pack, LANE), F32),
            pltpu.SemaphoreType.DMA((4,)),
        ],
        flops=2 * line * rows * features * wide_max,
        moved=5 << 20,
        limit=16,
    )(meta, *packs, *quarter)


def trans_weight(plan, meta, inners, wide):
    rows, features, line = plan.rows, plan.features, plan.line
    most = plan.down_max

    def kernel(meta_ref, *refs):
        inner_refs = refs[:line]
        wide_ref, keep_ref, send_ref, total = refs[line:]

        def run(b):
            own = plan.down_rows[b]
            lhs = jnp.concatenate([ref[...] for ref in inner_refs], axis=0)
            for i in range(plan.line_taps[b]):
                total[i * features : (i + 1) * features, :] = dot(
                    lhs, wide_ref[:, i * features : (i + 1) * features], ((0,), (0,))
                )
            for v in range(4):
                start = pl.multiple_of((meta_ref[7] ^ v) * own, LANE)
                piece = total[pl.ds(start, own), :]
                if own < most:
                    pad = jnp.zeros((most - own, features), F32)
                    piece = jnp.concatenate([piece, pad], axis=0)
                if v % 2 == 0:
                    keep_ref[v // 2] = piece
                else:
                    send_ref[v // 2] = piece.astype(BF)

        both(meta_ref, lambda: run(0), lambda: run(1))

    return call(
        kernel,
        [SMEM] + vmem(line + 1),
        [((2, most, features), F32), ((2, most, features), BF)],
        [pltpu.VMEM((4 * most, features), F32)],
        flops=2 * line * rows * features * 4 * most,
        moved=5 << 20,
        limit=20,
    )(meta, *inners, wide)


def inner_backward(plan, meta, pieces, low, act, vectors, gain):
    rows, features = plan.rows, plan.features

    def kernel(meta_ref, *refs):
        parts = refs[:-7]
        low_ref, act_ref, vec_ref, gain_ref, delta_ref, back_ref, out_ref = refs[-7:]
        total = keep_rows(total_of(parts), meta_ref[4])
        act_in = act_ref[...]
        unit, scale = norm_parts(act_in + low_ref[...].astype(F32))
        out_ref[...] = vec_ref[...]
        out_ref[1:2, :] = vec_ref[1:2, :] + jnp.sum(total, axis=0, keepdims=True)
        out_ref[2:3, :] = vec_ref[2:3, :] + jnp.sum(total * unit, axis=0, keepdims=True)
        back = norm_back(total, unit, scale, gain_ref[...])
        back_ref[...] = back
        delta_ref[...] = keep_rows(back * (1.0 - act_in * act_in), meta_ref[4]).astype(BF)

    return call(
        kernel,
        [SMEM] + vmem(len(pieces) + 4),
        [((rows, features), BF), ((rows, features), F32), ((8, features), F32)],
        [],
        moved=1 << 19,
        limit=6,
    )(meta, *pieces, low, act, vectors, gain)


def down_delta(plan, meta, pieces, delta_inner, act, small):
    rows, features = plan.rows, plan.features
    base, extra = up8(rows, 16), small.shape[0]

    def kernel(meta_ref, *refs):
        parts = refs[:-4]
        inner_ref, act_ref, small_ref, out_ref = refs[-4:]
        value = act_ref[...]
        total = total_of(parts) + inner_ref[...]
        delta = keep_rows(total * (1.0 - value * value), meta_ref[4])
        pad = jnp.zeros((base - rows, features), F32)
        out_ref[0:base, :] = jnp.concatenate([delta, pad], axis=0).astype(BF)
        high = small_ref[...].astype(BF)
        out_ref[base : base + extra, :] = high
        out_ref[base + extra :, :] = (small_ref[...] - high.astype(F32)).astype(BF)

    return call(
        kernel,
        [SMEM] + vmem(len(pieces) + 3),
        [((base + 2 * extra, features), BF)],
        [],
        moved=1 << 19,
        limit=8,
    )(meta, *pieces, delta_inner, act, small)[0]


def input_quarter(plan, meta, deltas, quarter):
    features, line = plan.features, plan.line
    rows = up8(plan.rows, 16)
    wide_max = 4 * plan.down_max

    def kernel(meta_ref, *refs):
        delta_refs, weights = refs[:line], refs[line : line + 4]
        out_ref, weight, wide, packed, sems = refs[line + 4 :]

        def run(b):
            copies = fetch_quarter(plan, b, meta_ref, weights, weight, sems)
            lhs = jnp.concatenate([ref[0:rows, :] for ref in delta_refs], axis=0)
            for copy in copies:
                copy.wait()
            for i in range(plan.line_taps[b]):
                wide[:, i * features : (i + 1) * features] = dot(
                    lhs, weight[i * features : (i + 1) * features, :], ((1,), (1,))
                )
            packed[...] = jnp.zeros_like(packed)
            for m in range(line):
                matrix_packed(plan, b, wide, m * rows, packed)
                out_ref[m] = packed[...].astype(BF)

        both(meta_ref, lambda: run(0), lambda: run(1))

    return call(
        kernel,
        [SMEM] + vmem(line) + [ANY] * 4,
        [((line, plan.pack, LANE), BF)],
        [
            pltpu.VMEM((wide_max, features), BF),
            pltpu.VMEM((line * rows, wide_max), F32),
            pltpu.VMEM((plan.pack, LANE), F32),
            pltpu.SemaphoreType.DMA((4,)),
        ],
        flops=2 * line * rows * features * wide_max,
        moved=4 << 20,
        limit=16,
    )(meta, *deltas, *quarter)[0]


def input_rows(plan, meta, packs, outer):
    features, length, line = plan.features, plan.length, plan.line

    def kernel(meta_ref, *refs):
        pack_refs = refs[:line]
        outer_ref, out_ref, stage, packed = refs[line:]

        def run(b):
            for m in range(line):
                packed[...] = pack_refs[m][...].astype(F32)
                unpack_taps(plan, b, packed, stage, (meta_ref[5] ^ m) * plan.line_taps[b])
            inner = get(stage, plan.factors[b] // 2, length)
            out_ref[...] = (inner + outer_ref[...]).astype(BF)

        both(meta_ref, lambda: run(0), lambda: run(1))

    return call(
        kernel,
        [SMEM] + vmem(line + 1),
        [((length, features), BF)],
        [split(plan.stage_rows, features), pltpu.VMEM((plan.pack, LANE), F32)],
        moved=3 << 20,
        limit=12,
    )(meta, *packs, outer)[0]


def down_weight(plan, meta, columns, even, odd, extra, loss_part):
    shards, rows, features, line = plan.shards, plan.rows, plan.features, plan.line
    half = shards // 2
    base = up8(rows, 16)
    most, tail = plan.down_max, up8(extra + 2, 16)

    def kernel(meta_ref, *refs):
        col_refs = refs[:4]
        even_ref, odd_ref, loss_ref, grad_ref, sums_ref, delta, ordered, small = refs[4:]
        me = meta_ref[1]
        for q in range(shards):
            source = (even_ref, odd_ref)[q // half]
            value = source[q % half, 0:base, :].astype(F32)
            at = me ^ plan.mask(q)
            ordered[pl.ds(at, 1), :] = jnp.sum(value, axis=0, keepdims=True)
            delta[q * rows : (q + 1) * rows, :] = value[:rows]
            high = source[q % half, base : base + extra, :].astype(F32)
            low = source[q % half, base + extra : base + 2 * extra, :].astype(F32)
            small[at] = high + low
        total = small[0]
        for i in range(1, shards):
            total = total + small[i]
        sums_ref[...] = jnp.zeros_like(sums_ref)
        sums_ref[0:extra, :] = total
        sums_ref[extra : extra + 1, :] = jnp.sum(ordered[...], axis=0, keepdims=True)
        sums_ref[extra + 1 : extra + 2, :] = jnp.broadcast_to(loss_ref[0:1, 0:1], (1, features))
        sums = sums_ref[...]
        high = sums.astype(BF)
        low = (sums - high.astype(F32)).astype(BF)
        grad_ref[most : most + tail, :] = high
        grad_ref[most + tail :, :] = low
        sums_ref[...] = high.astype(F32) + low.astype(F32)
        for at, v in enumerate((0, 2, 1, 3)):
            steps = delta[at * line * rows : (at + 1) * line * rows, :].astype(BF)
            part = dot(col_refs[v][...], steps, ((0,), (0,)))
            total = part if at == 0 else total + part
        grad_ref[0:most, :] = total.astype(BF)

    return call(
        kernel,
        [SMEM] + vmem(7),
        [((most + 2 * tail, features), BF), ((tail, features), F32)],
        [
            pltpu.VMEM((shards * rows, features), F32),
            pltpu.VMEM((shards, features), F32),
            pltpu.VMEM((shards, extra, features), F32),
        ],
        flops=2 * shards * rows * features * features,
        moved=4 << 20,
        limit=20,
    )(meta, *columns, even, odd, loss_part)


def finish(plan, meta, own, recv, mine, iso_sums, extra, ff_parts):
    features, most, tail = plan.features, plan.down_max, mine.shape[0]
    rows = plan.down_rows

    def kernel(
        meta_ref, own_ref, recv_ref, mine_ref, short_sum, long_sum,
        short_ref, long_ref, bias_ref, gain_ref, head_bias_ref, head_gain_ref, ff_ref, loss_ref,
    ):
        theirs = recv_ref[most : most + tail, :].astype(F32) + recv_ref[most + tail :, :].astype(F32)
        sums = mine_ref[...]
        total = sums + theirs
        first = 6 + ff_parts
        bias_ref[0, 1:2, :] = short_sum[...]
        bias_ref[1, 1:2, :] = long_sum[...]
        for b in range(2):
            bias_ref[b, 2:4, :] = total[first + 3 * b : first + 3 * b + 2]
            gain_ref[b : b + 1, :] = total[first + 3 * b + 2 : first + 3 * b + 3]
        head_bias_ref[...] = total[0:4]
        head_gain_ref[...] = total[4:6]
        ff_ref[...] = total[6 : 6 + ff_parts]
        loss_ref[...] = total[extra + 1 : extra + 2, 0:LANE] * (0.5 / (features * plan.length))

        def place(short_from, long_from, short_row, long_row):
            short_ref[...] = short_from[0 : rows[0], :].astype(F32)
            long_ref[...] = long_from[0 : rows[1], :].astype(F32)
            bias_ref[0, 0:1, :] = short_row[extra : extra + 1]
            bias_ref[1, 0:1, :] = long_row[extra : extra + 1]

        both(
            meta_ref,
            lambda: place(own_ref, recv_ref, sums, theirs),
            lambda: place(recv_ref, own_ref, theirs, sums),
        )

    return call(
        kernel,
        [SMEM] + vmem(5),
        [
            ((rows[0], features), F32),
            ((rows[1], features), F32),
            ((2, 4, features), F32),
            ((2, features), F32),
            ((4, features), F32),
            ((2, features), F32),
            ((ff_parts, features), F32),
            ((1, LANE), F32),
        ],
        [],
        moved=4 << 20,
        limit=12,
    )(meta, own, recv, mine, *iso_sums)


def natural_order(plan, meta, own, halves):
    shards = plan.shards
    line = plan.line
    rows, features = own

    def kernel(meta_ref, *refs):
        out_ref = refs[-1]
        for q in range(shards):
            out_ref[meta_ref[1] ^ plan.mask(q)] = refs[q // line][q % line].astype(F32)

    return call(
        kernel,
        [SMEM] + vmem(4),
        [((shards, rows, features), F32)],
        [],
        moved=3 << 20,
        limit=16,
    )(meta, *halves)[0]


ROOT_HALF = 0.7071067811865476
ROOT_TWO_PI = 0.3989422804014327


def head_rows(plan, meta, keep, recv, target, valid, merge, bias, gain, ff_in, ff_bias, ff_out):
    half_rows, features = keep.shape
    hidden = ff_in.shape[1]
    parts = hidden // features
    dims = (half_rows, features)

    def kernel(
        meta_ref, keep_ref, recv_ref, target_ref, valid_ref, merge_ref, bias_ref, gain_ref,
        in_bias_ref, in_hbm, out_hbm,
        out_ref, up_keep_ref, up_send_ref, normed_ref, act_ref, pre_delta_ref, ff_delta_ref,
        merged_delta_ref, vec_ref, loss_ref, slope_ref, in_ref, out_w_ref, sems,
    ):
        fetch_in = pltpu.make_async_copy(in_hbm, in_ref, sems.at[0])
        fetch_out = pltpu.make_async_copy(out_hbm, out_w_ref, sems.at[1])
        fetch_in.start()
        fetch_out.start()
        branch = meta_ref[0]
        merged = dot(keep_ref[...], merge_ref[branch]) + dot(recv_ref[...], merge_ref[1 - branch])
        merged = merged + bias_ref[0:1, :]
        unit, scale = norm_parts(merged)
        normed = (unit * gain_ref[0:1, :] + bias_ref[2:3, :]).astype(BF)
        normed_ref[...] = normed
        fetch_in.wait()
        fetch_out.wait()
        for c in range(parts):
            cols = slice(c * features, (c + 1) * features)
            pre = dot(normed, in_ref[:, cols]) + in_bias_ref[:, cols]
            share = 0.5 * (1.0 + lax.erf(pre * ROOT_HALF))
            slope_ref[:, cols] = share + pre * (jnp.exp(-0.5 * pre * pre) * ROOT_TWO_PI)
            act = (pre * share).astype(BF)
            act_ref[:, cols] = act
            part = dot(act, out_w_ref[cols, :])
            total = part if c == 0 else total + part
        unit_end, scale_end = norm_parts(merged + total + bias_ref[1:2, :])
        final = unit_end * gain_ref[1:2, :] + bias_ref[3:4, :]
        out_ref[...] = final.astype(BF)
        error = final - target_ref[...].astype(F32)
        weighted = valid_ref[...] * error
        loss = jnp.sum(jnp.sum(weighted * error, axis=0, keepdims=True), axis=1, keepdims=True)
        loss_ref[...] = jnp.broadcast_to(loss, loss_ref.shape)
        vec_ref[...] = jnp.zeros_like(vec_ref)
        vec_ref[3:4, :] = jnp.sum(weighted, axis=0, keepdims=True)
        vec_ref[5:6, :] = jnp.sum(weighted * unit_end, axis=0, keepdims=True)
        delta_sum = norm_back(weighted, unit_end, scale_end, gain_ref[1:2, :])
        delta_ff = delta_sum.astype(BF)
        ff_delta_ref[...] = delta_ff
        vec_ref[1:2, :] = jnp.sum(delta_ff.astype(F32), axis=0, keepdims=True)
        for c in range(parts):
            cols = slice(c * features, (c + 1) * features)
            pre_delta = dot(delta_ff, out_w_ref[cols, :], ((1,), (1,))) * slope_ref[:, cols]
            pre_delta = pre_delta.astype(BF)
            pre_delta_ref[:, cols] = pre_delta
            vec_ref[6 + c : 7 + c, :] = jnp.sum(pre_delta.astype(F32), axis=0, keepdims=True)
            part = dot(pre_delta, in_ref[:, cols], ((1,), (1,)))
            above = part if c == 0 else above + part
        vec_ref[2:3, :] = jnp.sum(above, axis=0, keepdims=True)
        vec_ref[4:5, :] = jnp.sum(above * unit, axis=0, keepdims=True)
        delta = norm_back(above, unit, scale, gain_ref[0:1, :]) + delta_sum
        delta = delta.astype(BF)
        merged_delta_ref[...] = delta
        vec_ref[0:1, :] = jnp.sum(delta.astype(F32), axis=0, keepdims=True)
        up_keep_ref[...] = dot(delta, merge_ref[branch], ((1,), (1,))).astype(BF)
        up_send_ref[...] = dot(delta, merge_ref[1 - branch], ((1,), (1,))).astype(BF)

    vec_rows = up8(6 + parts + 6)
    return call(
        kernel,
        [SMEM] + vmem(8) + [HBM] * 2,
        [
            (dims, BF), (dims, BF), (dims, BF), (dims, BF),
            ((half_rows, hidden), BF), ((half_rows, hidden), BF), (dims, BF), (dims, BF),
            ((vec_rows, features), F32), ((8, LANE), F32),
        ],
        [
            pltpu.VMEM((half_rows, hidden), F32),
            pltpu.VMEM((features, hidden), BF),
            pltpu.VMEM((hidden, features), BF),
            pltpu.SemaphoreType.DMA((2,)),
        ],
        flops=10 * half_rows * features * hidden,
        moved=14 << 20,
        limit=56,
    )(meta, keep, recv, target, valid, merge, bias, gain, ff_bias, ff_in, ff_out)


def head_weights(plan, meta, keep, recv, normed, act, pre_delta, ff_delta, merged_delta):
    shards = plan.shards
    half_rows, features = keep.shape
    hidden = act.shape[1]
    ff_rows, merge_rows = hidden // shards // 2, features // shards
    parts = hidden // features
    own = 2 * ff_rows + merge_rows

    def kernel(
        meta_ref, keep_hbm, recv_hbm, normed_hbm, act_hbm, pre_hbm, ff_hbm, merged_hbm,
        stay_near, stay_far, send_near, send_far, first, second, third,
        keep_ref, recv_ref, normed_ref, act_ref, pre_ref, ff_ref, merged_ref, sems,
    ):
        pairs = (
            (normed_hbm, normed_ref), (pre_hbm, pre_ref), (ff_hbm, ff_ref), (act_hbm, act_ref),
            (merged_hbm, merged_ref), (keep_hbm, keep_ref), (recv_hbm, recv_ref),
        )
        copies = [
            pltpu.make_async_copy(source, target, sems.at[i])
            for i, (source, target) in enumerate(pairs)
        ]
        for copy in copies:
            copy.start()
        branch = meta_ref[0]
        copies[0].wait()
        copies[1].wait()
        for c in range(parts):
            cols = slice(c * features, (c + 1) * features)
            first[cols, :] = dot(pre_ref[:, cols], normed_ref[...], ((0,), (0,))).astype(BF)
        copies[2].wait()
        copies[3].wait()
        for c in range(parts):
            cols = slice(c * features, (c + 1) * features)
            second[cols, :] = dot(act_ref[:, cols], ff_ref[...], ((0,), (0,))).astype(BF)
        for copy in copies[4:]:
            copy.wait()
        for side, ref in enumerate((keep_ref, recv_ref)):
            part = dot(ref[...], merged_ref[...], ((0,), (0,))).astype(BF)
            start = pl.multiple_of((branch ^ side) * features, 16)
            third[pl.ds(start, features), :] = part
        for q in range(shards):
            device = meta_ref[1] ^ plan.mask(q)
            targets = (stay_near, stay_far, send_near, send_far)
            target = targets[q // plan.line]
            for h in range(2):
                at = 2 * device + (branch ^ h)
                for start, count, source in (
                    (0, ff_rows, first),
                    (ff_rows, ff_rows, second),
                    (2 * ff_rows, merge_rows, third),
                ):
                    rows = pl.ds(pl.multiple_of(at * count, 16), count)
                    target[h, q % plan.line, start : start + count, :] = source[rows, :]

    return call(
        kernel,
        [SMEM] + [HBM] * 7,
        [((2, plan.line, own, features), BF)] * 4,
        [
            pltpu.VMEM((hidden, features), BF),
            pltpu.VMEM((hidden, features), BF),
            pltpu.VMEM((2 * features, features), BF),
        ]
        + [
            pltpu.VMEM(ref.shape, BF)
            for ref in (keep, recv, normed, act, pre_delta, ff_delta, merged_delta)
        ]
        + [pltpu.SemaphoreType.DMA((7,))],
        flops=4 * half_rows * features * hidden,
        moved=12 << 20,
        limit=56,
    )(meta, keep, recv, normed, act, pre_delta, ff_delta, merged_delta)


def hop(values, distance, shards):
    return lax.ppermute(values, "series", [(i, i ^ distance) for i in range(shards)])


def swap(values):
    return lax.ppermute(values, "branch", [(0, 1), (1, 0)])


def after(value, *others):
    return lax.optimization_barrier((value, others))[0]


def along_line(plan, own):
    return [own] + [hop(own, i << 2, plan.shards) for i in range(1, plan.line)]


def line_parts(plan, first, rest):
    return [first] + [hop(rest[i - 1], i << 2, plan.shards) for i in range(1, plan.line)]


def quad_gather(plan, own, later):
    side = hop(own, 2, plan.shards)
    return [own, hop(own, 1, plan.shards), side, hop(after(side, later), 1, plan.shards)]


def settle(value, *others):
    return lax.optimization_barrier((value,) + others)


def stacked(pieces):
    count, shape = len(pieces), pieces[0].shape

    def kernel(*refs):
        for i in range(count):
            refs[count][i] = refs[i][...]

    return call(kernel, vmem(count), [((count,) + shape, BF)], [], moved=1 << 20, limit=6)(*pieces)[0]


def gather_slots(plan, line, stack=jnp.stack):
    even = stack(line + [hop(value, 2, plan.shards) for value in line])
    return even, hop(even, 1, plan.shards)


def scatter_sum(plan, keep, send, *others):
    shards, line = plan.shards, plan.line
    first = keep + hop(send, 1, shards).astype(F32)
    second = first[:line] + hop(first[line:].astype(BF), 2, shards).astype(F32)
    if others:
        second, *others = settle(second, *others)
    pieces = line_parts(plan, second[0], [second[i].astype(BF) for i in range(1, line)])
    return (pieces, *others) if others else pieces


def rounded(values):
    return lax.reduce_precision(values, exponent_bits=8, mantissa_bits=7)


def layer_norm(values, gain_row, shift_row):
    center = values - jnp.mean(values, axis=-1, keepdims=True)
    spread = jnp.mean(center * center, axis=-1, keepdims=True)
    return center * lax.rsqrt(spread + EPSILON) * gain_row + shift_row


def gelu_exact(values):
    return jax.nn.gelu(values, approximate=False)


def product(a, b):
    return jnp.dot(a, b, preferred_element_type=F32)


def left_product(a, b):
    return jnp.einsum("mi,mo->io", a, b, preferred_element_type=F32)


def right_product(a, b):
    return jnp.einsum("mo,io->mi", a, b, preferred_element_type=F32)


def body(
    series_in, target, horizons, observed,
    down_short, iso_short, trans_short, down_long, iso_long, trans_long,
    branch_bias, branch_gain, merge_weight, head_bias, head_gain, ff_in, ff_in_bias, ff_out,
):
    shards = lax.axis_size("series")
    _, length, features = series_in.shape
    plan = Plan(
        shards,
        length,
        features,
        (down_short.shape[0], down_long.shape[0]),
        (iso_short.shape[0], iso_long.shape[0]),
    )
    line = plan.line
    half_rows = length // 2
    branch = lax.axis_index("branch")
    me = lax.axis_index("series")
    is_short = branch == 0
    iso_rows = jnp.where(is_short, plan.iso_rows[0], plan.iso_rows[1])
    meta = jnp.stack(
        [
            branch,
            me,
            (me * iso_rows) // features,
            (me * iso_rows) % features,
            jnp.where(is_short, plan.steps[0], plan.steps[1]),
            me // 4,
            me % 2,
            me % 4,
        ]
    ).astype(jnp.int32)
    series = series_in[0]
    biases, gain = branch_bias[0], branch_gain

    def chosen(short, long):
        rows = max(short.shape[0], long.shape[0])
        short = jnp.pad(short, ((0, rows - short.shape[0]), (0, 0)))
        long = jnp.pad(long, ((0, rows - long.shape[0]), (0, 0)))
        return jnp.where(is_short, short, long)

    def placed(own, other, b, rows):
        return jnp.where(branch == b, own, other)[:rows].astype(F32)

    blocks = prep_blocks(plan, meta, series)
    own_down = after(chosen(down_short, down_long), blocks)
    blocks = line_parts(plan, blocks[0], [blocks[i] for i in range(1, line)])
    down_quarter = quad_gather(plan, own_down, blocks)
    own_trans = after(chosen(trans_short, trans_long), blocks)
    keep, send, *columns = down_partial(plan, meta, blocks, down_quarter)
    pieces = line_parts(plan, keep, send)
    trans_quarter = quad_gather(plan, own_trans, pieces)
    low, act_down = low_rows(plan, meta, pieces, biases)
    low_own = gather_slots(plan, along_line(plan, low), stacked)
    low_own, trans_quarter = settle(low_own, trans_quarter)
    keep, send = iso_partial(plan, meta, low_own, iso_short, iso_long, False)
    low_other = swap(after(low_own[0], low_own[1]))
    pieces = scatter_sum(plan, keep, send)
    inner, act_iso = inner_rows(plan, meta, pieces, low, biases, gain)
    columns[2] = hop(after(columns[2], inner), 2, shards)
    inners, columns = settle(along_line(plan, inner), columns)
    packs = trans_forward(plan, meta, inners, trans_quarter)
    columns[3] = hop(after(columns[3], packs), 3, shards)
    packs = line_parts(plan, packs[0], [packs[i] for i in range(1, line)])
    packs, columns, low_other = settle(packs, columns, low_other)
    out_keep, out_send, act_trans = outer_rows(plan, meta, packs, series, biases, gain)
    out_recv = swap(out_send)
    columns[1] = hop(after(columns[1], out_keep), 1, shards)
    low_other = (low_other, hop(after(low_other, out_keep), 1, shards))
    out_recv, columns, low_other = settle(out_recv, columns, low_other)

    positions = branch * half_rows + jnp.arange(half_rows, dtype=jnp.int32)
    observed_half = lax.dynamic_slice_in_dim(observed[0], branch * half_rows, half_rows, 0)
    valid = (
        observed_half.astype(F32)
        * (positions >= SEQ_IN).astype(F32)
        * (positions < SEQ_IN + horizons[0]).astype(F32)
    )
    (
        out, up_keep, up_send, normed, act_ff, pre_delta, ff_delta, merged_delta, vec_head, loss_part
    ) = head_rows(
        plan, meta, out_keep, out_recv, target[0], valid[:, None], merge_weight, head_bias,
        head_gain, ff_in, ff_in_bias[None], ff_out,
    )
    up_recv = swap(up_send)
    near, far, near_send, far_send = head_weights(
        plan, meta, out_keep, out_recv, normed, act_ff, pre_delta, ff_delta, merged_delta
    )

    far_recv = hop(after(far_send, up_recv), 1, shards)
    outer, packs, vectors = outer_backward(plan, meta, up_keep, up_recv, series, act_trans, gain)
    far = (far.astype(F32) + after(far_recv, packs).astype(F32)).astype(BF)
    near_recv = hop(after(near_send, packs), 1, shards)
    share_recv = hop(far, 2, shards)
    packs = line_parts(plan, packs[0], [packs[i] for i in range(1, line)])
    keep, send, wide = trans_backward(plan, meta, packs, trans_quarter)
    trans_keep, trans_send = trans_weight(plan, meta, inners, wide)
    pieces, trans_send, share_recv, near_recv = settle(
        line_parts(plan, keep, send), trans_send, share_recv, near_recv
    )
    shares = near.astype(F32) + near_recv.astype(F32) + share_recv.astype(F32)
    share_recv = swap(shares[1].astype(BF))
    shares = shares[0]
    delta_iso, delta_inner, vectors = inner_backward(
        plan, meta, pieces, low, act_iso, vectors, gain
    )
    ff_parts = ff_in_bias.shape[0] // features
    selector = jnp.stack([is_short, branch == 1]).astype(F32)
    branch_rows = (selector[:, None, None] * vectors[None, 0:3]).reshape(6, features)
    small = jnp.concatenate([vec_head[: 6 + ff_parts], branch_rows], axis=0)
    count = small.shape[0]
    small = jnp.pad(small, ((0, up8(count, 16) - count), (0, 0)))
    trans_recv = hop(trans_send, 1, shards)
    deltas, trans_recv = settle(along_line(plan, delta_iso), trans_recv)
    trans_sum = trans_keep + trans_recv.astype(F32)
    trans_next = trans_sum[1].astype(BF)
    delta_own = gather_slots(plan, deltas)
    delta_own, trans_next, share_recv = settle(delta_own, trans_next, share_recv)
    shares = shares + share_recv.astype(F32)
    spread = line // 2
    share_recv = hop(shares[spread:].astype(BF), 4 * spread, shards)
    keep, send = iso_partial(plan, meta, delta_own, iso_short, iso_long, True)
    delta_other = swap(delta_own[0])
    pieces, delta_other = scatter_sum(plan, keep, send, delta_other)
    pieces, share_recv = settle(pieces, share_recv)
    shares = shares[:spread] + share_recv.astype(F32)
    payload = down_delta(plan, meta, pieces, delta_inner, act_down, small)
    delta_other = (delta_other, hop(after(delta_other, payload), 1, shards))
    trans_recv = hop(after(trans_next, payload), 2, shards)
    share_recv = hop(after(shares[1:].astype(BF), payload), 4, shards)
    first_grad = iso_weight(plan, meta, 0, low_own, low_other, delta_own, delta_other)
    deltas, trans_recv, share_recv, first_grad = settle(
        along_line(plan, payload), trans_recv, share_recv, first_grad
    )
    shares = rounded(shares[0] + share_recv[0].astype(F32))
    grad_trans = (trans_sum[0] + trans_recv.astype(F32)).astype(BF)
    packs = input_quarter(plan, meta, deltas, down_quarter)
    even = jnp.stack(deltas)
    crossing = jnp.concatenate([grad_trans, shares.astype(BF)], axis=0)
    crossing = swap(after(crossing, packs))
    second_grad = iso_weight(
        plan, meta, 1, after(low_own, packs), low_other, delta_own, delta_other
    )
    packs = line_parts(plan, packs[0], [packs[i] for i in range(1, line)])
    crossing, second_grad = settle(crossing, second_grad)
    odd = hop(after(even, crossing), 2, shards)
    packs, second_grad = settle(packs, second_grad)
    input_own = input_rows(plan, meta, packs, outer)
    trans_recv, share_recv = crossing[: plan.down_max], crossing[plan.down_max :]
    input_recv = swap(input_own)
    even = jnp.concatenate([even, odd], axis=0)
    delta_halves = (even, hop(after(even, input_own), 1, shards))
    share_recv = share_recv.astype(F32)
    ff_rows = ff_in_bias.shape[0] // shards // 2
    halves = [
        jnp.where(is_short, shares, share_recv),
        jnp.where(is_short, share_recv, shares),
    ]
    merge_own = jnp.concatenate([half[2 * ff_rows :] for half in halves], axis=0)
    extra = small.shape[0]
    grad_down, mine = down_weight(
        plan, meta, columns, *after(delta_halves, input_own), extra, loss_part
    )
    down_recv = swap(grad_down)
    merge_even = jnp.stack(along_line(plan, after(merge_own.astype(BF), delta_halves[1])))
    merge_odd = hop(after(merge_even, grad_down), 2, shards)
    trans_recv = after(trans_recv, grad_down)
    trans_grads = [placed(grad_trans, trans_recv, b, plan.down_rows[b]) for b in range(2)]
    merge_odd, trans_grads = settle(merge_odd, trans_grads)
    merge_core = hop(merge_even, 1, shards), hop(merge_odd, 1, shards)
    input_total = input_own.astype(F32) + after(input_recv, merge_odd).astype(F32)
    merge_core, input_total = settle(merge_core, input_total)
    merge_total = natural_order(
        plan, meta, merge_own.shape, (merge_even, merge_odd, *merge_core)
    ).reshape(2, features, features)
    down_recv = after(down_recv, merge_total)
    short_down, long_down, bias_total, gain_total, head_sums, head_gains, ff_sums, loss = finish(
        plan, meta, grad_down, down_recv, mine, [first_grad[1], second_grad[1]], extra, ff_parts
    )
    return (
        out[None],
        loss[0, 0:1],
        input_total[None],
        short_down,
        first_grad[0],
        trans_grads[0],
        long_down,
        second_grad[0],
        trans_grads[1],
        bias_total,
        gain_total,
        merge_total,
        head_sums,
        head_gains,
        jnp.concatenate([half[:ff_rows] for half in halves], axis=0).T,
        ff_sums.reshape(-1),
        jnp.concatenate([half[ff_rows : 2 * ff_rows] for half in halves], axis=0),
    )


def fitted(matrix, row_total):
    return jnp.pad(matrix, ((0, row_total - matrix.shape[0]), (0, 0)))


def unpack(gathered_all, shards, rows_max, rows_own):
    features = gathered_all.shape[1]
    return gathered_all.reshape(shards, rows_max, features)[:, :rows_own].reshape(
        shards * rows_own, features
    )


def repack(gradient, shards, rows_max):
    rows_own = gradient.shape[0] // shards
    shaped = gradient.reshape(shards, rows_own, gradient.shape[1])
    return jnp.pad(shaped, ((0, 0), (0, rows_max - rows_own), (0, 0))).reshape(
        shards * rows_max, gradient.shape[1]
    )


def branch_pass(series_in, weights, shards, rows_max, biases, gain_row, factor):
    series_count, length, features = series_in.shape
    step_count = (length + factor) // factor
    margin = factor // 2
    weight_down = unpack(weights[0], shards, rows_max[0], factor * features // shards)
    weight_iso = unpack(weights[1], shards, rows_max[1], step_count * features // shards)
    weight_trans = unpack(weights[2], shards, rows_max[2], factor * features // shards).reshape(
        factor, features, features
    )
    blocks = jnp.pad(series_in, ((0, 0), (margin, step_count * factor - length - margin), (0, 0)))
    blocks = blocks.reshape(series_count * step_count, factor * features)
    act_down = jnp.tanh(product(blocks, weight_down) + biases[0])
    low_down = act_down.astype(jnp.bfloat16)
    padded = jnp.concatenate(
        [
            jnp.zeros((series_count, step_count - 1, features), jnp.bfloat16),
            low_down.reshape(series_count, step_count, features),
        ],
        axis=1,
    )
    unfolded = jnp.concatenate(
        [padded[:, offset : offset + step_count] for offset in range(step_count)], axis=2
    )
    unfolded = unfolded.reshape(series_count * step_count, step_count * features)
    act_iso = jnp.tanh(product(unfolded, weight_iso) + biases[1])
    inner_norm, inner_back = jax.vjp(
        layer_norm, act_iso + low_down.astype(jnp.float32), gain_row, biases[3]
    )
    low_inner = inner_norm.astype(jnp.bfloat16)
    spread_out = jnp.einsum(
        "mi,jio->mjo", low_inner, weight_trans, preferred_element_type=jnp.float32
    )
    act_trans = jnp.tanh(
        spread_out.reshape(series_count, step_count * factor, features)[:, :length] + biases[2]
    )
    result, outer_back = jax.vjp(
        layer_norm, act_trans + series_in.astype(jnp.float32), gain_row, biases[3]
    )
    stored = (
        blocks,
        weight_down,
        weight_iso,
        weight_trans,
        act_down,
        unfolded,
        act_iso,
        inner_back,
        low_inner,
        act_trans,
        outer_back,
    )
    return (result, stored)


def branch_back(series_in, weights, shards, rows_max, biases, gain_row, factor, upstream):
    series_count, length, features = series_in.shape
    step_count = (length + factor) // factor
    margin = factor // 2
    result, stored = branch_pass(series_in, weights, shards, rows_max, biases, gain_row, factor)
    (
        blocks,
        weight_down,
        weight_iso,
        weight_trans,
        act_down,
        unfolded,
        act_iso,
        inner_back,
        low_inner,
        act_trans,
        outer_back,
    ) = stored
    delta_outer, gain_outer, shift_outer = outer_back(upstream)
    delta_trans = (delta_outer * (1.0 - act_trans * act_trans)).astype(jnp.bfloat16)
    trans_blocks = jnp.pad(delta_trans, ((0, 0), (0, step_count * factor - length), (0, 0)))
    trans_blocks = trans_blocks.reshape(series_count * step_count, factor, features)
    grad_trans = jnp.einsum(
        "mi,mjo->jio", low_inner, trans_blocks, preferred_element_type=jnp.float32
    )
    grad_trans = grad_trans.reshape(factor * features, features)
    inner_upstream = jnp.einsum(
        "mjo,jio->mi", trans_blocks, weight_trans, preferred_element_type=jnp.float32
    )
    delta_inner, gain_inner, shift_inner = inner_back(inner_upstream)
    delta_iso = (delta_inner * (1.0 - act_iso * act_iso)).astype(jnp.bfloat16)
    grad_iso = left_product(unfolded, delta_iso)
    delta_unfold = right_product(delta_iso, weight_iso).reshape(
        series_count, step_count, step_count, features
    )
    delta_padded = jnp.zeros((series_count, 2 * step_count - 1, features), jnp.float32)
    for offset in range(step_count):
        delta_padded = delta_padded.at[:, offset : offset + step_count].add(
            delta_unfold[:, :, offset]
        )
    delta_low = (
        delta_padded[:, step_count - 1 :].reshape(series_count * step_count, features) + delta_inner
    )
    delta_down = (delta_low * (1.0 - act_down * act_down)).astype(jnp.bfloat16)
    grad_down = left_product(blocks, delta_down)
    delta_blocks = right_product(delta_down, weight_down).reshape(
        series_count, step_count * factor, features
    )
    delta_series = delta_blocks[:, margin : margin + length] + delta_outer
    vectors = jnp.stack(
        [
            jnp.sum(delta_down.astype(jnp.float32), axis=0),
            jnp.sum(delta_iso.astype(jnp.float32), axis=0),
            jnp.sum(delta_trans.astype(jnp.float32), axis=(0, 1)),
            shift_inner + shift_outer,
        ]
    )
    padded_grads = (
        repack(grad_down, shards, rows_max[0]),
        repack(grad_iso, shards, rows_max[1]),
        repack(grad_trans, shards, rows_max[2]),
    )
    return (delta_series, padded_grads, vectors, gain_inner + gain_outer)


def plain_body(
    series_in,
    target,
    horizons,
    observed,
    down_short,
    iso_short,
    trans_short,
    down_long,
    iso_long,
    trans_long,
    branch_bias,
    branch_gain,
    merge_weight,
    head_bias,
    head_gain,
    ff_in,
    ff_in_bias,
    ff_out,
):
    branch_index = lax.axis_index("branch")
    shards = lax.axis_size("series")
    series_count, length, features = series_in.shape
    rows_max = (
        max(down_short.shape[0], down_long.shape[0]),
        max(iso_short.shape[0], iso_long.shape[0]),
        max(trans_short.shape[0], trans_long.shape[0]),
    )
    is_short = branch_index == 0
    own_down = jnp.where(is_short, fitted(down_short, rows_max[0]), fitted(down_long, rows_max[0]))
    own_iso = jnp.where(is_short, fitted(iso_short, rows_max[1]), fitted(iso_long, rows_max[1]))
    own_trans = jnp.where(
        is_short, fitted(trans_short, rows_max[2]), fitted(trans_long, rows_max[2])
    )
    gathered = (
        lax.all_gather(own_down, "series", axis=0, tiled=True),
        lax.all_gather(own_iso, "series", axis=0, tiled=True),
        lax.all_gather(own_trans, "series", axis=0, tiled=True),
    )
    biases = branch_bias[0]
    gain_row = branch_gain[0]

    def forward_with(factor):
        return lambda: branch_pass(series_in, gathered, shards, rows_max, biases, gain_row, factor)[
            0
        ].astype(jnp.bfloat16)

    branch_out = lax.cond(is_short, forward_with(SCALE_S), forward_with(SCALE_L))
    received = lax.all_to_all(
        branch_out.reshape(series_count, length, 1, features),
        "branch",
        split_axis=1,
        concat_axis=2,
        tiled=True,
    )
    half_rows = received.shape[1]
    merge_rows = received.reshape(series_count * half_rows, 2 * features)
    merge_flat = merge_weight.reshape(2 * features, features)
    merged = product(merge_rows, merge_flat) + head_bias[0]
    normed, first_back = jax.vjp(layer_norm, merged, head_gain[0], head_bias[2])
    low_normed = normed.astype(jnp.bfloat16)
    pre_ff = product(low_normed, ff_in) + ff_in_bias
    activated, gelu_back = jax.vjp(gelu_exact, pre_ff)
    low_act = activated.astype(jnp.bfloat16)
    ff_result = product(low_act, ff_out) + head_bias[1]
    final_out, second_back = jax.vjp(layer_norm, merged + ff_result, head_gain[1], head_bias[3])
    final_rows = final_out.reshape(series_count, half_rows, features)
    positions = branch_index * half_rows + jnp.arange(half_rows, dtype=jnp.int32)
    observed_half = lax.dynamic_slice_in_dim(observed, branch_index * half_rows, half_rows, 1)
    valid_mask = (
        observed_half.astype(jnp.float32)
        * (positions >= SEQ_IN).astype(jnp.float32)
        * (positions < SEQ_IN + horizons[:, None]).astype(jnp.float32)
    )
    error_rows = final_rows - target.astype(jnp.float32)
    weighted = valid_mask[:, :, None] * error_rows
    series_part = 0.5 * jnp.sum(weighted * error_rows, axis=(1, 2)) / (features * length)
    delta_sum, gain_second, shift_second = second_back(
        weighted.reshape(series_count * half_rows, features)
    )
    delta_ff = delta_sum.astype(jnp.bfloat16)
    grad_ff_out = left_product(low_act, delta_ff)
    delta_act = right_product(delta_ff, ff_out)
    (delta_pre,) = gelu_back(delta_act)
    low_pre = delta_pre.astype(jnp.bfloat16)
    grad_ff_in = left_product(low_normed, low_pre)
    delta_normed = right_product(low_pre, ff_in)
    delta_first, gain_first, shift_first = first_back(delta_normed)
    delta_merged = (delta_first + delta_sum).astype(jnp.bfloat16)
    grad_merge = left_product(merge_rows, delta_merged).reshape(2, features, features)
    delta_rows = (
        right_product(delta_merged, merge_flat)
        .astype(jnp.bfloat16)
        .reshape(series_count, half_rows, 2, features)
    )
    back_rows = lax.all_to_all(delta_rows, "branch", split_axis=2, concat_axis=1, tiled=True)
    upstream = back_rows.astype(jnp.float32).reshape(series_count, length, features)
    ff_shares = (
        lax.psum_scatter(grad_ff_in, "series", scatter_dimension=1, tiled=True),
        lax.psum_scatter(grad_ff_out, "series", scatter_dimension=0, tiled=True),
    )
    weights_back = (
        lax.all_gather(own_down, "series", axis=0, tiled=True),
        lax.all_gather(own_iso, "series", axis=0, tiled=True),
        lax.all_gather(own_trans, "series", axis=0, tiled=True),
    )

    def backward_with(factor):
        return lambda: branch_back(
            series_in, weights_back, shards, rows_max, biases, gain_row, factor, upstream
        )

    delta_series, padded_grads, vectors, gain_grad = lax.cond(
        is_short, backward_with(SCALE_S), backward_with(SCALE_L)
    )
    reduced = (
        lax.psum_scatter(padded_grads[0], "series", scatter_dimension=0, tiled=True),
        lax.psum_scatter(padded_grads[1], "series", scatter_dimension=0, tiled=True),
        lax.psum_scatter(padded_grads[2], "series", scatter_dimension=0, tiled=True),
    )
    short_flag = is_short.astype(jnp.float32)
    long_flag = 1.0 - short_flag
    summed = (
        lax.psum(delta_series.astype(jnp.bfloat16), "branch").astype(jnp.float32),
        lax.psum(series_part.astype(jnp.bfloat16), "branch").astype(jnp.float32),
        lax.psum(
            (short_flag * reduced[0][: down_short.shape[0]]).astype(jnp.bfloat16), "branch"
        ).astype(jnp.float32),
        lax.psum((short_flag * reduced[1]).astype(jnp.bfloat16), "branch").astype(jnp.float32),
        lax.psum(
            (short_flag * reduced[2][: trans_short.shape[0]]).astype(jnp.bfloat16), "branch"
        ).astype(jnp.float32),
        lax.psum((long_flag * reduced[0]).astype(jnp.bfloat16), "branch").astype(jnp.float32),
        lax.psum(
            (long_flag * reduced[1][: iso_long.shape[0]]).astype(jnp.bfloat16), "branch"
        ).astype(jnp.float32),
        lax.psum((long_flag * reduced[2]).astype(jnp.bfloat16), "branch").astype(jnp.float32),
        lax.psum(ff_shares[0].astype(jnp.bfloat16), "branch").astype(jnp.float32),
        lax.psum(ff_shares[1].astype(jnp.bfloat16), "branch").astype(jnp.float32),
    )
    selector = (jnp.arange(2, dtype=jnp.int32) == branch_index).astype(jnp.float32)
    full_bias = selector[:, None, None] * vectors[None]
    full_gain = selector[:, None] * gain_grad[None]
    head_vectors = jnp.stack(
        [
            jnp.sum(delta_merged.astype(jnp.float32), axis=0),
            jnp.sum(delta_ff.astype(jnp.float32), axis=0),
            shift_first,
            shift_second,
        ]
    )
    head_gains = jnp.stack([gain_first, gain_second])
    ff_bias_grad = jnp.sum(low_pre.astype(jnp.float32), axis=0)
    totals = lax.psum(
        (grad_merge, head_vectors, head_gains, ff_bias_grad, full_bias, full_gain),
        ("branch", "series"),
    )
    return (
        final_rows.astype(jnp.bfloat16),
        summed[1],
        summed[0],
        summed[2],
        summed[3],
        summed[4],
        summed[5],
        summed[6],
        summed[7],
        totals[4],
        totals[5],
        totals[0],
        totals[1],
        totals[2],
        summed[8],
        totals[3],
        summed[9],
    )


def solution(mesh):
    placed = (
        P("series", None, None),
        P("series", "branch", None),
        P("series"),
        P("series", None),
        P("series", None),
        P("series", None),
        P("series", None),
        P("series", None),
        P("series", None),
        P("series", None),
        P("branch", None, None),
        P("branch", None),
        P(),
        P(),
        P(),
        P(),
        P(),
        P(),
    )

    def run(*args):
        shards = mesh.shape["series"]
        features = args[0].shape[2]
        down_rows = [args[i].shape[0] // shards for i in (4, 7)]
        iso_rows = [args[i].shape[0] // shards for i in (5, 8)]
        fits = (
            args[0].shape[0] == shards
            and shards == 16
            and shards & (shards - 1) == 0
            and all(r % LANE == 0 and r <= features and 4 * r % features == 0 for r in down_rows)
            and all(r % 16 == 0 for r in iso_rows)
        )
        return jax.shard_map(
            body if fits else plain_body,
            mesh=mesh,
            in_specs=placed,
            out_specs=(
                P("series", "branch", None),
                P("series"),
                P("series", None, None),
                P("series", None),
                P("series", None),
                P("series", None),
                P("series", None),
                P("series", None),
                P("series", None),
                P(),
                P(),
                P(),
                P(),
                P(),
                P(None, "series"),
                P(),
                P("series", None),
            ),
            check_vma=False,
        )(*args)

    return run
```
